32 devices in a mesh: scene: 2 (over y), blk: 8 (over z, x), head: 2 (over core).
Axes of the slice: x: 2, y: 2, z: 4, core: 2. Of those that a mesh axis runs over, the one named last changes fastest.
Arguments:
- patch_rows: bfloat16 [32, 192, 1024], P(('scene', 'blk'), None, 'head'), parts along dimension 0
- special_rows: bfloat16 [32, 5, 1024], P(('scene', 'blk'), None, 'head'), parts along dimension 0, may hold values from -6 to 6
- role_first: bfloat16 [5, 1024], replicated, may hold values from -3 to 3
- role_rest: bfloat16 [5, 1024], replicated, may hold values from -3 to 3
- frame_order: int32 [32], P(('scene', 'blk')), parts along dimension 0, may hold values from 0 to 15, each once
- covisible: int32 [32, 16], P(('scene', 'blk')), parts along dimension 0, may hold values from 0 to 1, as said below
- w_qkv: bfloat16 [3, 1024, 1024], P(None, None, 'head')
- w_out: bfloat16 [1024, 1024], P('head'), may hold values from -0.1875 to 0.1875
Outputs:
- patch_out: bfloat16 [32, 192, 1024], P(('scene', 'blk'), None, 'head'), parts along dimension 0
- special_out: bfloat16 [32, 5, 1024], P(('scene', 'blk'), None, 'head'), parts along dimension 0
The draws below stay inside these ranges and needn't reach their ends.
There are 2 independent parts, one for each index of `scene`. The reference program is written for one: setup_inputs(seed, part) draws one part's arguments, and reference() takes and returns one part's arrays. A program takes and returns all parts, laid end to end along the dimension named above; an argument that names none is the same for every part. Nothing has to cross between parts.
Inputs may be any that keep to these rules, and one draw needn't show every extreme that they name: Image a sits on index a // 2 of blk. covisible[a, b] = covisible[b, a]; covisible[a, a] = 1; covisible[a, b] is 0 whenever the owners of a and b are more than 1 indices apart around the loop of blk, and that distance 1 is reached. `frame_order`: each capture index appears once.
All inputs are finite; a program needn't handle non-finite values.
Results may differ from the reference program's by a relative error of at most 0.012.
The reference program's roundings to bfloat16 on the way count: a program that leaves them out, or rounds other values in their place, can miss the bound.
Values may be sent and summed in bfloat16 or wider, within the bound.
No kernel may reach another device: no remote copies, remote signals or barrier semaphores. Data moves between devices by JAX's collectives and lax.ppermute only.
A program may use at most 128 MiB of HBM per device.

```python
import jax
import jax.numpy as jnp
from jax import lax

D = 1024
HEADS = 16
HEAD_DIM = 64
SPECIAL = 5
PATCH = 192
IMG_DEV = 2
NIMG = 16
REACH = 1
N_BLK = 8


def draw_patch_rows(key, part):
    key = jax.random.fold_in(key, 5)
    first_key = jax.random.fold_in(key, 0)
    values_out = jax.random.normal(first_key, (NIMG, PATCH, D), jnp.float32)
    return values_out.astype(jnp.bfloat16)


def draw_w_qkv(key, part):
    key = jax.random.fold_in(key, 7)
    weights = jax.random.normal(key, (3, D, D), jnp.float32) * D ** (-0.5)
    return weights.astype(jnp.bfloat16)


def draw_covisible(key, part):
    key = jax.random.fold_in(key, 11)
    first_key, second_key = jax.random.split(key)
    owners_count = NIMG // IMG_DEV
    indices = jnp.arange(NIMG, dtype=jnp.int32)
    owner = indices // IMG_DEV
    position = indices % IMG_DEV
    difference = (owner[:, None] - owner[None, :]) % owners_count
    distance = jnp.minimum(difference, owners_count - difference)
    threshold = jax.random.randint(first_key, (NIMG,), 4, 64)
    lottery = jax.random.randint(second_key, (NIMG, NIMG), 0, 64)
    chosen = lottery < threshold[:, None]
    chosen = chosen | chosen.T
    farthest = (distance == REACH) & (position[:, None] == 0) & (position[None, :] == 0)
    itself = indices[:, None] == indices[None, :]
    return ((chosen | farthest | itself) & (distance <= REACH)).astype(jnp.int32)


def block_scale(rng, shape, shards, low, top_value):
    gain, own = 1.0, jax.random.fold_in(rng, 6)
    for dim, blocks in shards:
        heights = jnp.exp(jax.random.uniform(jax.random.fold_in(own, dim), (blocks,), jnp.float32, low / len(shards), top_value / len(shards)))
        gain = gain * jnp.repeat(heights, shape[dim] // blocks).reshape([-1 if axis == dim else 1 for axis in range(len(shape))])
    return gain


def noise(stream_key, shape, width, limit, cuts=(), kind=jnp.bfloat16):
    entries = jax.random.normal(stream_key, shape, jnp.float32) * width
    if len(cuts) > 0:
        entries = block_scale(stream_key, shape, cuts, -0.22, 0.18) * entries
    return jnp.clip(entries, min=-limit, max=limit).astype(kind)


def setup_inputs(seed: int = 0, part: int = 0) -> dict:
    arg_keys = jax.random.split(jax.random.key(seed), 9)
    own_keys = jax.random.split(jax.random.fold_in(arg_keys[8], part), 9)
    return {
        "patch_rows": draw_patch_rows(jax.random.fold_in(jax.random.fold_in(arg_keys[8], part), 71), part),
        "special_rows": noise(own_keys[1], (NIMG, SPECIAL, D), 1.0, 6.0, ((0, 8), (2, 2))),
        "role_first": noise(arg_keys[2], (SPECIAL, D), 0.5, 3.0),
        "role_rest": noise(arg_keys[3], (SPECIAL, D), 0.5, 3.0),
        "frame_order": jax.random.permutation(own_keys[4], NIMG).astype(jnp.int32),
        "covisible": draw_covisible(jax.random.fold_in(jax.random.fold_in(arg_keys[8], part), 71), part),
        "w_qkv": draw_w_qkv(jax.random.fold_in(arg_keys[8], 71), part),
        "w_out": noise(arg_keys[7], (D, D), D ** -0.5, 0.1875, ((0, 2),)),
    }


def reference(patch_rows, special_rows, role_first, role_rest, frame_order, covisible, w_qkv, w_out):
    per_image = SPECIAL + PATCH
    dev_rows = IMG_DEV * per_image
    reference_frame = (frame_order == 0)[:, None, None]
    role_added = jnp.where(reference_frame, role_first.astype(jnp.float32)[None], role_rest.astype(jnp.float32)[None])
    specials = (special_rows.astype(jnp.float32) + role_added).astype(jnp.bfloat16)
    all_rows = jnp.concatenate([specials, patch_rows], axis=1).reshape(NIMG * per_image, D)
    projected = []
    for which in range(3):
        product = jnp.dot(all_rows, w_qkv[which], preferred_element_type=jnp.float32).astype(jnp.bfloat16)
        projected.append(product.reshape(NIMG, per_image, HEADS, HEAD_DIM))
    queries, keys_all, values_all = projected
    special_keys = keys_all[:, :SPECIAL].reshape(NIMG * SPECIAL, HEADS, HEAD_DIM).astype(jnp.float32)
    special_values = values_all[:, :SPECIAL].reshape(NIMG * SPECIAL, HEADS, HEAD_DIM).astype(jnp.float32)
    patch_keys = keys_all[:, SPECIAL:].reshape(N_BLK, IMG_DEV * PATCH, HEADS, HEAD_DIM)
    patch_values = values_all[:, SPECIAL:].reshape(N_BLK, IMG_DEV * PATCH, HEADS, HEAD_DIM)
    query_blocks = queries.reshape(N_BLK, dev_rows, HEADS, HEAD_DIM)
    mask_blocks = covisible.reshape(N_BLK, IMG_DEV, NIMG)
    offsets = jnp.arange(-REACH, REACH + 1, dtype=jnp.int32)
    scale = HEAD_DIM ** -0.5

    def one_device(device):
        owners = ((device + offsets) % N_BLK).astype(jnp.int32)
        near_keys = patch_keys[owners].reshape(-1, HEADS, HEAD_DIM).astype(jnp.float32)
        near_values = patch_values[owners].reshape(-1, HEADS, HEAD_DIM).astype(jnp.float32)
        query_block = query_blocks[device].astype(jnp.float32)
        key_images = (owners[:, None] * IMG_DEV + jnp.arange(IMG_DEV, dtype=jnp.int32)[None, :]).reshape(-1)
        block_mask = mask_blocks[device][:, key_images]
        allowed = jnp.repeat(jnp.repeat(block_mask > 0, per_image, 0), PATCH, 1)
        special_scores = jnp.einsum('rhd,khd->hrk', query_block, special_keys) * scale
        patch_scores = jnp.einsum('rhd,khd->hrk', query_block, near_keys) * scale
        patch_scores = jnp.where(allowed[None], patch_scores, -jnp.inf)
        scores = jnp.concatenate([special_scores, patch_scores], axis=2)
        largest = jnp.max(scores, axis=2, keepdims=True)
        weights = jnp.exp(scores - largest)
        denominator = jnp.sum(weights, axis=2, keepdims=True)
        rounded = lax.optimization_barrier(weights.astype(jnp.bfloat16)).astype(jnp.float32)
        mixed_values = jnp.concatenate([special_values, near_values], axis=0)
        numerator = jnp.einsum('hrk,khd->hrd', rounded, mixed_values)
        attended = (numerator / denominator).astype(jnp.bfloat16)
        return jnp.transpose(attended, (1, 0, 2)).reshape(dev_rows, D)

    attended_all = lax.map(one_device, jnp.arange(N_BLK, dtype=jnp.int32))
    output_rows = jnp.dot(attended_all.reshape(-1, D), w_out, preferred_element_type=jnp.float32)
    output_rows = output_rows.astype(jnp.bfloat16).reshape(NIMG, per_image, D)
    return output_rows[:, SPECIAL:], output_rows[:, :SPECIAL]
```

```python
import functools

import jax
import jax.numpy as jnp
from jax import lax
from jax.experimental import pallas as pl
from jax.experimental.pallas import tpu as pltpu
from jax.sharding import PartitionSpec as P

HEAD_DIM = 64
PAIR = 2 * HEAD_DIM
TILE_ROWS = 16
BLOCKED = -(2.0**127)
VMEM_BYTES = 32 * 1024 * 1024


def shifted(block, axis, distance):
    count = lax.axis_size(axis)
    route = [((i - distance) % count, i) for i in range(count)]
    return lax.ppermute(block, axis, route)


def swapped(block, axis, bit):
    count = lax.axis_size(axis)
    return lax.ppermute(block, axis, [(i ^ bit, i) for i in range(count)])


def project(own, other, w_ref, which, half):
    depth = own.shape[1]
    mine = pl.ds(pl.multiple_of(half * depth, depth), depth)
    theirs = pl.ds(pl.multiple_of((1 - half) * depth, depth), depth)
    return jnp.dot(own, w_ref[which, mine, :], preferred_element_type=jnp.float32) + jnp.dot(
        other, w_ref[which, theirs, :], preferred_element_type=jnp.float32
    )


def lanes_of(sub):
    lane = lax.broadcasted_iota(jnp.int32, (1, PAIR), 1)
    in_head = (lane >= sub * HEAD_DIM) & (lane < (sub + 1) * HEAD_DIM)
    return in_head, lane - (1 - sub) * HEAD_DIM


def image_bias(covisible, owner, images, sub):
    spare = lanes_of(sub)[1]
    rows = []
    for b in range(images):
        row = jnp.zeros((1, PAIR), jnp.float32)
        for a in range(images):
            seen = covisible[a, owner * images + b] > 0
            row = jnp.where(spare == a, jnp.where(seen, 0.0, BLOCKED), row)
        rows.append(row)
    return rows


def patch_key_head(keys_pair, covisible, owner, images, sub):
    in_head = lanes_of(sub)[0]
    per_image = keys_pair.shape[0] // images
    rows = image_bias(covisible, owner, images, sub)
    return jnp.concatenate(
        [
            jnp.where(in_head, keys_pair[b * per_image : (b + 1) * per_image], rows[b])
            for b in range(images)
        ],
        axis=0,
    ).astype(jnp.bfloat16)


def special_key_head(keys_pair, real_rows, images, sub):
    in_head, spare = lanes_of(sub)
    row = lax.broadcasted_iota(jnp.int32, keys_pair.shape, 0) % TILE_ROWS
    blocked = (row >= real_rows) & (spare >= 0) & (spare < images)
    return jnp.where(in_head, keys_pair, jnp.where(blocked, BLOCKED, 0.0)).astype(jnp.bfloat16)


def value_head(values_pair, sub):
    return jnp.where(lanes_of(sub)[0], values_pair, 1.0).astype(jnp.bfloat16)


def score(queries, keys):
    return lax.dot_general(
        queries, keys, (((1,), (1,)), ((), ())), preferred_element_type=jnp.float32
    )


def attend(queries, keys, values, state):
    scores = score(queries, keys)
    largest = jnp.max(scores, axis=1, keepdims=True)
    if state is not None:
        before, total = state
        largest = jnp.maximum(before[:, :1], largest)
    weights = jnp.exp(scores - largest).astype(jnp.bfloat16)
    added = jnp.dot(weights, values, preferred_element_type=jnp.float32)
    if state is not None:
        added = added + total * jnp.exp(before - largest)
    return largest, added


def first_kernel(
    images, special_count, covisible, own, other, own_special, other_special, w_qkv,
    queries_out, largest_out, total_out,
):
    half = lax.axis_index("head")
    owner = lax.axis_index("blk")
    patch_total = own.shape[0]
    per_image = patch_total // images
    own_rows = jnp.concatenate([own[...], own_special[...]], axis=0)
    other_rows = jnp.concatenate([other[...], other_special[...]], axis=0)
    queries = project(own_rows, other_rows, w_qkv, 0, half) * HEAD_DIM ** (-0.5)
    keys = project(own[...], other[...], w_qkv, 1, half)
    values = project(own[...], other[...], w_qkv, 2, half)
    rows = queries.shape[0]
    row = lax.broadcasted_iota(jnp.int32, (rows, PAIR), 0)
    image = jnp.where(
        row < patch_total, row // per_image, jnp.minimum((row - patch_total) // special_count, images - 1)
    )
    for pair in range(queries.shape[1] // PAIR):
        cols = slice(pair * PAIR, (pair + 1) * PAIR)
        for sub in range(2):
            head = 2 * pair + sub
            in_head, spare = lanes_of(sub)
            mark = jnp.where(spare == image, 1.0, 0.0)
            query_head = jnp.where(in_head, queries[:, cols], mark).astype(jnp.bfloat16)
            queries_out[head] = query_head
            largest, total = attend(
                query_head,
                patch_key_head(keys[:, cols], covisible, owner, images, sub),
                value_head(values[:, cols], sub),
                None,
            )
            largest_out[head] = jnp.broadcast_to(largest, total.shape)
            total_out[head] = total


def neighbour_kernel(
    images, offset, covisible, own, other, w_qkv, queries, largest_in, total_in,
    largest_out, total_out,
):
    half = lax.axis_index("head")
    count = lax.axis_size("blk")
    owner = lax.rem(lax.axis_index("blk") + offset + count, count)
    keys = project(own[...], other[...], w_qkv, 1, half)
    values = project(own[...], other[...], w_qkv, 2, half)
    for head in range(queries.shape[0]):
        pair, sub = head // 2, head % 2
        cols = slice(pair * PAIR, (pair + 1) * PAIR)
        largest, total = attend(
            queries[head],
            patch_key_head(keys[:, cols], covisible, owner, images, sub),
            value_head(values[:, cols], sub),
            (largest_in[head], total_in[head]),
        )
        largest_out[head] = jnp.broadcast_to(largest, total.shape)
        total_out[head] = total


def last_kernel(
    images, offset, real_rows, covisible, own, other, own_special, other_special, w_qkv, w_out,
    queries, largest_in, total_in, kept_out, sent_out,
):
    half = lax.axis_index("head")
    count = lax.axis_size("blk")
    owner = lax.rem(lax.axis_index("blk") + offset + count, count)
    patch_total = own.shape[0]
    own_rows = jnp.concatenate([own[...], own_special[...]], axis=0)
    other_rows = jnp.concatenate([other[...], other_special[...]], axis=0)
    keys = project(own_rows, other_rows, w_qkv, 1, half)
    values = project(own_rows, other_rows, w_qkv, 2, half)
    lane = lax.broadcasted_iota(jnp.int32, (1, PAIR), 1)
    attended = []
    for pair in range(queries.shape[0] // 2):
        cols = slice(pair * PAIR, (pair + 1) * PAIR)
        totals = []
        for sub in range(2):
            head = 2 * pair + sub
            key_head = jnp.concatenate(
                [
                    patch_key_head(keys[:patch_total, cols], covisible, owner, images, sub),
                    special_key_head(keys[patch_total:, cols], real_rows, images, sub),
                ],
                axis=0,
            )
            totals.append(
                attend(
                    queries[head],
                    key_head,
                    value_head(values[:, cols], sub),
                    (largest_in[head], total_in[head]),
                )[1]
            )
        numerator = jnp.where(lane < HEAD_DIM, totals[0], totals[1])
        denominator = pltpu.roll(jnp.where(lane < HEAD_DIM, totals[1], totals[0]), HEAD_DIM, 1)
        attended.append((numerator / denominator).astype(jnp.bfloat16))
    attended = jnp.concatenate(attended, axis=1)
    width = kept_out.shape[1]
    mine = pl.ds(pl.multiple_of(half * width, width), width)
    theirs = pl.ds(pl.multiple_of((1 - half) * width, width), width)
    sent_out[...] = jnp.dot(
        attended, w_out[:, theirs], preferred_element_type=jnp.float32
    ).astype(jnp.bfloat16)
    kept_out[...] = jnp.dot(attended, w_out[:, mine], preferred_element_type=jnp.float32)


def call(kernel, out_shape, *operands):
    smem = pl.BlockSpec(memory_space=pltpu.SMEM)
    vmem = pl.BlockSpec(memory_space=pltpu.VMEM)
    return pl.pallas_call(
        kernel,
        out_shape=out_shape,
        in_specs=[smem] + [vmem] * (len(operands) - 1),
        out_specs=[vmem] * len(out_shape),
        compiler_params=pltpu.CompilerParams(vmem_limit_bytes=VMEM_BYTES),
    )(*operands)


def gathered(block, axis):
    count = lax.axis_size(axis)
    if count & (count - 1):
        return lax.all_gather(block, axis, axis=0, tiled=True)
    bit = 1
    while bit < count:
        block = jnp.concatenate([block, swapped(block, axis, bit)], axis=0)
        bit *= 2
    return block


def per_device(
    patch_rows, special_rows, role_first, role_rest, frame_order, covisible, w_qkv, w_out
):
    images, patch_count, width = patch_rows.shape
    special_count = special_rows.shape[1]
    real_rows = images * special_count
    padding = -real_rows % TILE_ROWS
    half = lax.axis_index("head")
    owner_count = lax.axis_size("blk")
    reach = max(1, owner_count // 64)

    own = patch_rows.reshape(images * patch_count, width)
    other = swapped(own, "head", 1)
    role = jnp.where(
        (frame_order == 0)[:, None, None],
        lax.dynamic_slice_in_dim(role_first, half * width, width, 1)[None],
        lax.dynamic_slice_in_dim(role_rest, half * width, width, 1)[None],
    )
    specials = special_rows.astype(jnp.float32) + role.astype(jnp.float32)
    specials = specials.astype(jnp.bfloat16).reshape(real_rows, width)
    specials = jnp.pad(specials, ((0, padding), (0, 0)))
    other_specials = swapped(specials, "head", 1)
    all_specials = gathered(specials, "blk")
    all_other_specials = swapped(all_specials, "head", 1)

    near = []
    for distance in range(1, reach + 1):
        for offset in (-distance, distance):
            near_own = shifted(own, "blk", -offset)
            near.append((offset, near_own, swapped(near_own, "head", 1)))

    head_count = width // HEAD_DIM
    rows = images * patch_count + real_rows + padding
    wide = jax.ShapeDtypeStruct((head_count, rows, PAIR), jnp.float32)
    queries, largest, total = call(
        functools.partial(first_kernel, images, special_count),
        [jax.ShapeDtypeStruct((head_count, rows, PAIR), jnp.bfloat16), wide, wide],
        covisible, own, other, specials, other_specials, w_qkv,
    )
    for offset, near_own, near_other in near[:-1]:
        largest, total = call(
            functools.partial(neighbour_kernel, images, offset),
            [wide, wide],
            covisible, near_own, near_other, w_qkv, queries, largest, total,
        )
    offset, near_own, near_other = near[-1]
    kept, sent = call(
        functools.partial(last_kernel, images, offset, real_rows),
        [
            jax.ShapeDtypeStruct((rows, width), jnp.float32),
            jax.ShapeDtypeStruct((rows, width), jnp.bfloat16),
        ],
        covisible, near_own, near_other, all_specials, all_other_specials, w_qkv, w_out,
        queries, largest, total,
    )
    received = swapped(sent, "head", 1)
    out = (kept + received.astype(jnp.float32)).astype(jnp.bfloat16)
    patch_total = images * patch_count
    return (
        out[:patch_total].reshape(images, patch_count, width),
        out[patch_total : patch_total + real_rows].reshape(images, special_count, width),
    )


def solution(mesh):
    in_specs = (
        P(("scene", "blk"), None, "head"),
        P(("scene", "blk"), None, "head"),
        P(),
        P(),
        P(("scene", "blk")),
        P(("scene", "blk"), None),
        P(None, None, "head"),
        P("head", None),
    )
    out_specs = (P(("scene", "blk"), None, "head"), P(("scene", "blk"), None, "head"))
    return jax.shard_map(
        per_device, mesh=mesh, in_specs=in_specs, out_specs=out_specs, check_vma=False
    )
```

```python
import functools

import jax
import jax.numpy as jnp
from jax import lax
from jax.experimental import pallas as pl
from jax.experimental.pallas import tpu as pltpu
from jax.sharding import PartitionSpec as P

HEAD_DIM = 64
PAIR = 2 * HEAD_DIM
TILE_ROWS = 16
BLOCKED = -(2.0**127)
VMEM_BYTES = 32 * 1024 * 1024


def shifted(block, axis, distance):
    count = lax.axis_size(axis)
    route = [((i - distance) % count, i) for i in range(count)]
    return lax.ppermute(block, axis, route)


def swapped(block, axis, bit):
    count = lax.axis_size(axis)
    return lax.ppermute(block, axis, [(i ^ bit, i) for i in range(count)])


def project(own, other, w_ref, which, half):
    depth = own.shape[1]
    mine = pl.ds(pl.multiple_of(half * depth, depth), depth)
    theirs = pl.ds(pl.multiple_of((1 - half) * depth, depth), depth)
    return jnp.dot(own, w_ref[which, mine, :], preferred_element_type=jnp.float32) + jnp.dot(
        other, w_ref[which, theirs, :], preferred_element_type=jnp.float32
    )


def lanes_of(sub):
    lane = lax.broadcasted_iota(jnp.int32, (1, PAIR), 1)
    in_head = (lane >= sub * HEAD_DIM) & (lane < (sub + 1) * HEAD_DIM)
    return in_head, lane - (1 - sub) * HEAD_DIM


def image_bias(covisible, source, images, sub):
    owner, b = source
    spare = lanes_of(sub)[1]
    row = jnp.zeros((1, PAIR), jnp.float32)
    for a in range(images):
        seen = covisible[a, owner * images + b] > 0
        row = jnp.where(spare == a, jnp.where(seen, 0.0, BLOCKED), row)
    return row


def patch_key_head(keys_pair, covisible, sources, images, sub):
    in_head = lanes_of(sub)[0]
    per_image = keys_pair.shape[0] // len(sources)
    return jnp.concatenate(
        [
            jnp.where(
                in_head,
                keys_pair[i * per_image : (i + 1) * per_image],
                image_bias(covisible, source, images, sub),
            )
            for i, source in enumerate(sources)
        ],
        axis=0,
    ).astype(jnp.bfloat16)


def special_key_head(keys_pair, real_rows, images, sub):
    in_head, spare = lanes_of(sub)
    row = lax.broadcasted_iota(jnp.int32, keys_pair.shape, 0) % TILE_ROWS
    blocked = (row >= real_rows) & (spare >= 0) & (spare < images)
    return jnp.where(in_head, keys_pair, jnp.where(blocked, BLOCKED, 0.0)).astype(jnp.bfloat16)


def value_head(values_pair, sub):
    return jnp.where(lanes_of(sub)[0], values_pair, 1.0).astype(jnp.bfloat16)


def score(queries, keys):
    return lax.dot_general(
        queries, keys, (((1,), (1,)), ((), ())), preferred_element_type=jnp.float32
    )


def attend(queries, keys, values, state):
    scores = score(queries, keys)
    largest = jnp.max(scores, axis=1, keepdims=True)
    if state is not None:
        before, total = state
        largest = jnp.maximum(before[:, :1], largest)
    weights = jnp.exp(scores - largest).astype(jnp.bfloat16)
    added = jnp.dot(weights, values, preferred_element_type=jnp.float32)
    if state is not None:
        added = added + total * jnp.exp(before - largest)
    return largest, added


def start_kernel(
    special_count, frame_order, patches, specials, role_first, role_rest,
    own_out, early_out, late_out, special_out, copied,
):
    images, per_image, width = patches.shape
    copies = []
    for b in range(images):
        rows = pl.ds(b * per_image, per_image)
        copies.append(pltpu.make_async_copy(patches.at[b], own_out.at[rows], copied.at[2 * b]))
        target = early_out.at[pl.ds(0, per_image)] if b == 0 else late_out
        copies.append(pltpu.make_async_copy(patches.at[b], target, copied.at[2 * b + 1]))
    for copy in copies:
        copy.start()
    half = lax.axis_index("head")
    columns = pl.ds(pl.multiple_of(half * width, width), width)
    first = role_first[:, columns].astype(jnp.float32)
    rest = role_rest[:, columns].astype(jnp.float32)
    summed = [
        specials[:, b, :].astype(jnp.float32) + jnp.where(frame_order[b] == 0, first, rest)
        for b in range(images)
    ]
    padding = special_out.shape[0] - images * special_count
    summed.append(jnp.zeros((padding, width), jnp.float32))
    block = jnp.concatenate(summed, axis=0).astype(jnp.bfloat16)
    special_out[...] = block
    own_out[images * per_image :, :] = block
    early_out[per_image:, :] = block
    for copy in copies:
        copy.wait()


def first_kernel(
    images, special_count, patch_total, covisible, own, other, w_qkv,
    queries_out, largest_out, total_out,
):
    half = lax.axis_index("head")
    owner = lax.axis_index("blk")
    per_image = patch_total // images
    queries = project(own[...], other[...], w_qkv, 0, half) * HEAD_DIM ** (-0.5)
    keys = project(own[:patch_total, :], other[:patch_total, :], w_qkv, 1, half)
    values = project(own[:patch_total, :], other[:patch_total, :], w_qkv, 2, half)
    rows = queries.shape[0]
    row = lax.broadcasted_iota(jnp.int32, (rows, PAIR), 0)
    image = jnp.where(
        row < patch_total, row // per_image, jnp.minimum((row - patch_total) // special_count, images - 1)
    )
    for pair in range(queries.shape[1] // PAIR):
        cols = slice(pair * PAIR, (pair + 1) * PAIR)
        for sub in range(2):
            head = 2 * pair + sub
            in_head, spare = lanes_of(sub)
            mark = jnp.where(spare == image, 1.0, 0.0)
            query_head = jnp.where(in_head, queries[:, cols], mark).astype(jnp.bfloat16)
            queries_out[head] = query_head
            largest, total = attend(
                query_head,
                patch_key_head(keys[:, cols], covisible, [(owner, b) for b in range(images)], images, sub),
                value_head(values[:, cols], sub),
                None,
            )
            largest_out[head] = jnp.broadcast_to(largest, total.shape)
            total_out[head] = total


def owner_at(offset):
    count = lax.axis_size("blk")
    here = lax.axis_index("blk")
    if isinstance(offset, tuple):
        offset = jnp.where(lax.rem(here, 2) == 0, offset[0], offset[1])
    return lax.rem(here + offset + count, count)


def later_kernel(images, blocks, special_count, per_image, covisible, *refs):
    inputs, refs = refs[: 2 * len(blocks)], refs[2 * len(blocks) :]
    last = special_count > 0
    if last:
        own_special, other_special, w_qkv, w_out, queries, largest_in, total_in, kept_out, sent_out = refs
    else:
        w_qkv, queries, largest_in, total_in, largest_out, total_out = refs
    half = lax.axis_index("head")
    own_rows = [ref[:per_image, :] for ref in inputs[: len(blocks)]]
    other_rows = [ref[:per_image, :] for ref in inputs[len(blocks) :]]
    if last:
        own_rows.append(own_special[...])
        other_rows.append(other_special[...])
    own_rows = jnp.concatenate(own_rows, axis=0)
    other_rows = jnp.concatenate(other_rows, axis=0)
    keys = project(own_rows, other_rows, w_qkv, 1, half)
    values = project(own_rows, other_rows, w_qkv, 2, half)
    patch_total = per_image * len(blocks)
    sources = [(owner_at(offset), b) for offset, b in blocks]
    lane = lax.broadcasted_iota(jnp.int32, (1, PAIR), 1)
    attended = []
    for pair in range(queries.shape[0] // 2):
        cols = slice(pair * PAIR, (pair + 1) * PAIR)
        totals = []
        for sub in range(2):
            head = 2 * pair + sub
            key_head = patch_key_head(keys[:patch_total, cols], covisible, sources, images, sub)
            if last:
                special = special_key_head(keys[patch_total:, cols], images * special_count, images, sub)
                key_head = jnp.concatenate([key_head, special], axis=0)
            largest, total = attend(
                queries[head], key_head, value_head(values[:, cols], sub), (largest_in[head], total_in[head])
            )
            totals.append(total)
            if not last:
                largest_out[head] = jnp.broadcast_to(largest, total.shape)
                total_out[head] = total
        if last:
            numerator = jnp.where(lane < HEAD_DIM, totals[0], totals[1])
            denominator = pltpu.roll(jnp.where(lane < HEAD_DIM, totals[1], totals[0]), HEAD_DIM, 1)
            attended.append((numerator / denominator).astype(jnp.bfloat16))
    if last:
        attended = jnp.concatenate(attended, axis=1)
        width = kept_out.shape[1]
        mine = pl.ds(pl.multiple_of(half * width, width), width)
        theirs = pl.ds(pl.multiple_of((1 - half) * width, width), width)
        sent_out[...] = jnp.dot(
            attended, w_out[:, theirs], preferred_element_type=jnp.float32
        ).astype(jnp.bfloat16)
        kept_out[...] = jnp.dot(attended, w_out[:, mine], preferred_element_type=jnp.float32)


def end_kernel(images, kept, received, patch_out, special_out):
    patch_total = patch_out.shape[0]
    special_count = special_out.shape[0]
    patch_out[...] = (kept[:patch_total, :] + received[:patch_total, :].astype(jnp.float32)).astype(
        jnp.bfloat16
    )
    rest = kept[patch_total:, :] + received[patch_total:, :].astype(jnp.float32)
    rows = [rest[b * special_count : (b + 1) * special_count][:, None, :] for b in range(images)]
    special_out[...] = jnp.concatenate(rows, axis=1).astype(jnp.bfloat16)


SMEM = pl.BlockSpec(memory_space=pltpu.SMEM)
VMEM = pl.BlockSpec(memory_space=pltpu.VMEM)
HBM = pl.BlockSpec(memory_space=pl.ANY)


def call(kernel, out_shape, operands, in_specs=None, out_specs=None, scratch=()):
    return pl.pallas_call(
        kernel,
        out_shape=out_shape,
        in_specs=in_specs or [SMEM] + [VMEM] * (len(operands) - 1),
        out_specs=out_specs or [VMEM] * len(out_shape),
        scratch_shapes=scratch,
        compiler_params=pltpu.CompilerParams(vmem_limit_bytes=VMEM_BYTES),
    )(*operands)


def gathered(block, axis, bit):
    count = lax.axis_size(axis)
    if count & (count - 1):
        return lax.all_gather(block, axis, axis=0, tiled=True)
    while bit < count:
        block = jnp.concatenate([block, swapped(block, axis, bit)], axis=0)
        bit *= 2
    return block


def after(array, *others):
    return lax.optimization_barrier((array, *others))[0]


def relayed(block, axis):
    count = lax.axis_size(axis)
    return lax.ppermute(block, axis, [(i, (i + (2 if i % 2 == 0 else -2)) % count) for i in range(count)])


def per_device(
    patch_rows, special_rows, role_first, role_rest, frame_order, covisible, w_qkv, w_out
):
    images, per_image, width = patch_rows.shape
    special_count = special_rows.shape[1]
    real_rows = images * special_count
    special_block = real_rows + -real_rows % TILE_ROWS
    owner_count = lax.axis_size("blk")
    reach = max(1, owner_count // 64)
    patch_total = images * per_image
    rows = patch_total + special_block
    head_count = width // HEAD_DIM
    narrow = lambda count: jax.ShapeDtypeStruct((count, width), jnp.bfloat16)
    wide = jax.ShapeDtypeStruct((head_count, rows, PAIR), jnp.float32)

    own, early, late, specials = call(
        functools.partial(start_kernel, special_count),
        [narrow(rows), narrow(per_image + special_block), narrow(per_image), narrow(special_block)],
        (frame_order, patch_rows, jnp.transpose(special_rows, (1, 0, 2)), role_first, role_rest),
        in_specs=[SMEM, HBM, VMEM, VMEM, VMEM],
        scratch=[pltpu.SemaphoreType.DMA((2 * images,))],
    )

    def first():
        return call(
            functools.partial(first_kernel, images, special_count, patch_total),
            [jax.ShapeDtypeStruct((head_count, rows, PAIR), jnp.bfloat16), wide, wide],
            (covisible, own, swapped(own, "head", 1), w_qkv),
        )

    def later(blocks, sources, extra, state):
        pairs = [own_half for own_half, _ in sources] + [other for _, other in sources]
        return call(
            functools.partial(
                later_kernel, images, blocks, special_count if extra else 0, per_image
            ),
            [jax.ShapeDtypeStruct((rows, width), jnp.float32), narrow(rows)] if extra else [wide, wide],
            (covisible, *pairs, *extra[:2], w_qkv, *extra[2:], *state),
        )

    if reach == 1 and owner_count % 2 == 0 and images == 2:
        next_early = swapped(early, "blk", 1)
        next_late = swapped(late, "blk", 1)
        queries, largest, total = first()
        next_early = after(next_early, queries)
        far_early = relayed(next_early, "blk")
        pair = jnp.concatenate([specials, next_early[per_image:]], axis=0)
        all_specials = gathered(pair, "blk", 2)
        next_early = (next_early, swapped(next_early, "head", 1))
        beside, beyond = (1, -1), (-1, 1)
        largest, total = later(
            [(beside, 0)], [next_early], (), (queries, largest, total)
        )
        next_late = after(next_late, largest)
        far_late = relayed(next_late, "blk")
        next_late = (next_late, swapped(next_late, "head", 1))
        far_early = (far_early, swapped(far_early, "head", 1))
        all_specials = (all_specials, swapped(all_specials, "head", 1))
        largest, total = later(
            [(beside, 1), (beyond, 0)], [next_late, far_early], (), (queries, largest, total)
        )
        far_late = (far_late, swapped(far_late, "head", 1))
        blocks, sources = [(beyond, 1)], [far_late]
    else:
        near = []
        for distance in range(1, reach + 1):
            for offset in (-distance, distance):
                parts = [shifted(part, "blk", -offset) for part in (early, late)]
                sources = [(part, swapped(part, "head", 1)) for part in parts]
                near.append(([(offset, 0), (offset, 1)], sources))
        all_specials = gathered(specials, "blk", 1)
        all_specials = (all_specials, swapped(all_specials, "head", 1))
        queries, largest, total = first()
        for blocks, sources in near[:-1]:
            largest, total = later(blocks, sources, (), (queries, largest, total))
        blocks, sources = near[-1]
    kept, sent = later(blocks, sources, (*all_specials, w_out), (queries, largest, total))
    received = swapped(sent, "head", 1)
    patch_out, special_out = call(
        functools.partial(end_kernel, images),
        [narrow(patch_total), jax.ShapeDtypeStruct((special_count, images, width), jnp.bfloat16)],
        (kept, received),
        in_specs=[VMEM, VMEM],
        out_specs=[pl.BlockSpec(), pl.BlockSpec()],
    )
    return patch_out.reshape(patch_rows.shape), jnp.transpose(special_out, (1, 0, 2))


def solution(mesh):
    in_specs = (
        P(("scene", "blk"), None, "head"),
        P(("scene", "blk"), None, "head"),
        P(),
        P(),
        P(("scene", "blk")),
        P(("scene", "blk"), None),
        P(None, None, "head"),
        P("head", None),
    )
    out_specs = (P(("scene", "blk"), None, "head"), P(("scene", "blk"), None, "head"))
    return jax.shard_map(
        per_device, mesh=mesh, in_specs=in_specs, out_specs=out_specs, check_vma=False
    )
```

```python
import functools

import jax
import jax.numpy as jnp
from jax import lax
from jax.experimental import pallas as pl
from jax.experimental.pallas import tpu as pltpu
from jax.sharding import PartitionSpec as P

HEAD_DIM = 64
PAIR = 2 * HEAD_DIM
TILE_ROWS = 16
VMEM_BYTES = 32 * 1024 * 1024
SMEM = pl.BlockSpec(memory_space=pltpu.SMEM)
VMEM = pl.BlockSpec(memory_space=pltpu.VMEM)
HBM = pl.BlockSpec(memory_space=pltpu.HBM)


def shifted(block, axis, distance):
    count = lax.axis_size(axis)
    route = [((i - distance) % count, i) for i in range(count)]
    return lax.ppermute(block, axis, route)


def swapped(block, axis, bit):
    count = lax.axis_size(axis)
    return lax.ppermute(block, axis, [(i ^ bit, i) for i in range(count)])


def relayed(block, axis):
    count = lax.axis_size(axis)
    return lax.ppermute(block, axis, [(i, (i + (2 if i % 2 == 0 else -2)) % count) for i in range(count)])


def halves(width):
    half = lax.axis_index("head")
    mine = pl.ds(pl.multiple_of(half * width, width), width)
    theirs = pl.ds(pl.multiple_of((1 - half) * width, width), width)
    return mine, theirs


def product(left, right):
    return jnp.dot(left, right, preferred_element_type=jnp.float32)


def owner_at(offset):
    count = lax.axis_size("blk")
    here = lax.axis_index("blk")
    if isinstance(offset, tuple):
        offset = jnp.where(lax.rem(here, 2) == 0, offset[0], offset[1])
    return lax.rem(here + offset + count, count)


def start_kernel(
    offsets, frame_order, covisible, patches, specials, role_first, role_rest,
    own_out, pieces_out, special_out, mask_out, order, seen, special_rows, first_rows, rest_rows, copied,
):
    images, per_image, width = patches.shape
    special_count = specials.shape[0]
    patch_total = images * per_image
    small = [
        pltpu.make_async_copy(source, target, copied.at[i])
        for i, (source, target) in enumerate(
            [
                (specials, special_rows), (role_first, first_rows), (role_rest, rest_rows),
                (frame_order, order), (covisible, seen),
            ]
        )
    ]
    large = []
    for b in range(images):
        large.append((patches.at[b], pieces_out.at[b]))
        large.append((patches.at[b], own_out.at[pl.ds(b * per_image, per_image)]))
    large = [
        pltpu.make_async_copy(source, target, copied.at[len(small) + i])
        for i, (source, target) in enumerate(large)
    ]
    for copy in small + large:
        copy.start()
    for copy in small:
        copy.wait()
    mine, _ = halves(width)
    first = first_rows[:, mine].astype(jnp.float32)
    rest = rest_rows[:, mine].astype(jnp.float32)
    summed = [
        special_rows[:, b, :].astype(jnp.float32) + jnp.where(order[b] == 0, first, rest)
        for b in range(images)
    ]
    padding = special_out.shape[0] - images * special_count
    summed.append(jnp.zeros((padding, width), jnp.float32))
    block = jnp.concatenate(summed, axis=0).astype(jnp.bfloat16)
    special_out[...] = block
    own_out[patch_total:, :] = block
    lane = lax.broadcasted_iota(jnp.int32, (1, mask_out.shape[1]), 1)
    special_lane = lax.rem(lane - patch_total, special_out.shape[0])
    image = jnp.where(
        lane < patch_total, lane // per_image, jnp.minimum(special_lane // special_count, images - 1)
    )
    for i, offset in enumerate(offsets):
        for b in range(images):
            row = jnp.zeros(lane.shape, jnp.float32)
            for a in range(images):
                hidden = seen[a, owner_at(offset) * images + b] <= 0
                row = jnp.where((image == a) & hidden, -jnp.inf, row)
            mask_out[i * images + b : i * images + b + 1, :] = row
    for copy in large:
        copy.wait()


def partial_kernel(own, w_qkv, sums_out, weights_out, copied):
    width = own.shape[1]
    mine, theirs = halves(width)
    copies = [
        pltpu.make_async_copy(w_qkv.at[i, rows], weights_out.at[i, rows], copied.at[i, j])
        for j, rows in enumerate((mine, theirs))
        for i in range(3)
    ]
    for copy in copies:
        copy.start()
    for i in range(3):
        copies[i].wait()
        sums_out[i] = product(own[...], weights_out[i, mine, :])
    for i in range(3, 6):
        copies[i].wait()


def project(own, other, weights, which):
    mine, theirs = halves(own.shape[1])
    return product(own, weights[which, mine, :]) + product(other, weights[which, theirs, :])


def attend(scores, masks, state):
    largest = None if state is None else state
    start = 0
    for count, mask in masks:
        part = jnp.max(scores[start : start + count], axis=0, keepdims=True) + mask
        largest = part if largest is None else jnp.maximum(largest, part)
        start += count
    weights, start = [], 0
    for count, mask in masks:
        weights.append(jnp.exp(scores[start : start + count] - (largest - mask)).astype(jnp.bfloat16))
        start += count
    factor = None if state is None else jnp.exp(state - largest)
    return largest, factor, jnp.concatenate(weights, axis=0)


def attend_all(keys, values, masks, queries, special_queries, state, special_rows, special_real):
    pairs = queries.shape[0]
    rows = queries.shape[2] // 2
    count = keys.shape[0]
    values = jnp.transpose(values).astype(jnp.bfloat16)
    keys = keys.astype(jnp.bfloat16)
    ones = jnp.ones((TILE_ROWS, count), jnp.bfloat16)
    key_row = lax.broadcasted_iota(jnp.int32, (special_rows, 1), 0)
    real = lax.rem(key_row, TILE_ROWS) < special_real

    def scored(keys, queries):
        scores = product(keys, queries)
        if not special_rows:
            return scores
        cut = count - special_rows
        special = jnp.where(real, scores[cut:], -jnp.inf)
        return jnp.concatenate([scores[:cut], special], axis=0)

    for pair in range(pairs):
        scores = scored(keys[:, pair * PAIR : (pair + 1) * PAIR], queries[pair])
        both = [(n, jnp.concatenate([mask[:, :rows]] * 2, axis=1)) for n, mask in masks]
        largest, factor, weights = attend(scores, both, state and state.largest(pair))
        for sub in range(2):
            first = pair * PAIR + sub * HEAD_DIM
            lanes = slice(sub * rows, (sub + 1) * rows)
            left = jnp.concatenate([values[first : first + HEAD_DIM], ones], axis=0)
            added = product(left, weights[:, lanes])
            added = added[: HEAD_DIM + 1]
            if state is not None:
                before = jnp.concatenate([state.total(pair, sub), state.weight(pair, sub)], axis=0)
                added = added + before * factor[:, lanes]
            yield pair, sub, largest[:, lanes], added[:HEAD_DIM], added[HEAD_DIM:]
    only = [(n, mask[:, rows:]) for n, mask in masks]
    largest, factor, weights = attend(
        scored(keys, special_queries[...]), only, state and state.largest(pairs)
    )
    added = product(jnp.concatenate([values, ones], axis=0), weights)[: values.shape[0] + 1]
    if state is not None:
        before = jnp.concatenate([state.total(pairs, 0), state.weight(pairs, 0)], axis=0)
        added = added + before * factor
    yield pairs, 0, largest, added[:-1], added[-1:]


class State:
    def __init__(self, rows, refs):
        self.rows = rows
        self.largest_ref, self.weight_ref, self.total_ref, self.special_ref = refs

    def lanes(self, pair, sub):
        if pair == self.total_ref.shape[0]:
            return slice(0, self.special_ref.shape[1])
        return slice(sub * self.rows, (sub + 1) * self.rows)

    def largest(self, pair):
        stop = self.special_ref.shape[1] if pair == self.total_ref.shape[0] else 2 * self.rows
        return self.largest_ref[pair : pair + 1, 0:stop]

    def weight(self, pair, sub):
        return self.weight_ref[pair : pair + 1, self.lanes(pair, sub)]

    def total(self, pair, sub):
        if pair == self.total_ref.shape[0]:
            return self.special_ref[...]
        return self.total_ref[pair, :, self.lanes(pair, sub)]

    def put(self, pair, sub, largest, total, weight):
        lanes = self.lanes(pair, sub)
        self.largest_ref[pair : pair + 1, lanes] = largest
        self.weight_ref[pair : pair + 1, lanes] = weight
        if pair == self.total_ref.shape[0]:
            self.special_ref[...] = total
        else:
            self.total_ref[pair, :, lanes] = total


def first_kernel(
    images, patch_total, mask, sums, other, weights, queries_out, special_out, *state_out
):
    _, theirs = halves(other.shape[1])
    queries, keys, values = [sums[i] + product(other[...], weights[i, theirs, :]) for i in range(3)]
    queries = queries * HEAD_DIM ** (-0.5)
    columns = jnp.transpose(queries[:patch_total]).astype(jnp.bfloat16)
    zero = jnp.zeros((HEAD_DIM, patch_total), jnp.bfloat16)
    pairs = queries_out.shape[0]
    for pair in range(pairs):
        first = pair * PAIR
        upper = jnp.concatenate([columns[first : first + HEAD_DIM], zero], axis=1)
        lower = jnp.concatenate([zero, columns[first + HEAD_DIM : first + PAIR]], axis=1)
        queries_out[pair] = jnp.concatenate([upper, lower], axis=0)
    special = jnp.concatenate([queries[patch_total:]] * (2 * pairs), axis=0)
    row = lax.broadcasted_iota(jnp.int32, special.shape, 0) // (queries.shape[0] - patch_total)
    lane = lax.broadcasted_iota(jnp.int32, special.shape, 1) // HEAD_DIM
    special = jnp.where(row == lane, special, 0.0)
    special_out[...] = jnp.transpose(special).astype(jnp.bfloat16)
    per_image = patch_total // images
    masks = [(per_image, mask[b : b + 1, :]) for b in range(images)]
    state = State(patch_total, state_out)
    for result in attend_all(
        keys[:patch_total], values[:patch_total], masks, queries_out, special_out, None, 0, 0
    ):
        state.put(*result)


def later_kernel(sources, per_image, mask, *refs):
    count = len(sources)
    own = jnp.concatenate([ref[...] for ref in refs[:count]], axis=0)
    other = jnp.concatenate([ref[...] for ref in refs[count : 2 * count]], axis=0)
    weights, queries, special_queries = refs[2 * count : 2 * count + 3]
    state_in, state_out = refs[2 * count + 3 : 2 * count + 7], refs[2 * count + 7 :]
    rows = queries.shape[2] // 2
    keys = project(own, other, weights, 1)
    values = project(own, other, weights, 2)
    masks = [(per_image, mask[i : i + 1, :]) for i in sources]
    state = State(rows, state_out)
    for result in attend_all(
        keys, values, masks, queries, special_queries, State(rows, state_in), 0, 0
    ):
        state.put(*result)


def last_kernel(sources, per_image, special_real, mask, *refs):
    count = len(sources)
    own_special, other_special = refs[2 * count : 2 * count + 2]
    own = jnp.concatenate([ref[...] for ref in refs[:count]] + [own_special[...]], axis=0)
    other = jnp.concatenate([ref[...] for ref in refs[count : 2 * count]] + [other_special[...]], axis=0)
    weights, queries, special_queries = refs[2 * count + 2 : 2 * count + 5]
    state_in = refs[2 * count + 5 : 2 * count + 9]
    w_out, kept_out, sent_out, w_here, copied = refs[2 * count + 9 :]
    copy = pltpu.make_async_copy(w_out, w_here, copied)
    copy.start()
    pairs, rows = queries.shape[0], queries.shape[2] // 2
    keys = project(own, other, weights, 1)
    values = project(own, other, weights, 2)
    special_rows = own_special.shape[0]
    masks = [(per_image, mask[i : i + 1, :]) for i in sources]
    masks.append((special_rows, jnp.zeros((1, mask.shape[1]), jnp.float32)))
    columns = []
    for pair, _, _, total, weight in attend_all(
        keys, values, masks, queries, special_queries, State(rows, state_in), special_rows, special_real
    ):
        columns.append(total / weight)
    special = columns.pop()
    attended = jnp.transpose(jnp.concatenate(columns, axis=0))
    row = lax.broadcasted_iota(jnp.int32, special.shape, 0) // HEAD_DIM
    lane = lax.broadcasted_iota(jnp.int32, special.shape, 1) // TILE_ROWS
    special = jnp.transpose(jnp.where(row == lane, special, 0.0))
    special = sum(special[i * TILE_ROWS : (i + 1) * TILE_ROWS] for i in range(2 * pairs))
    attended = jnp.concatenate([attended, special], axis=0).astype(jnp.bfloat16)
    mine, theirs = halves(kept_out.shape[1])
    copy.wait()
    sent_out[...] = product(attended, w_here[:, theirs]).astype(jnp.bfloat16)
    kept_out[...] = product(attended, w_here[:, mine])


def end_kernel(images, kept, received, patch_out, special_out):
    patch_total = patch_out.shape[0]
    special_count = special_out.shape[0]
    patch_out[...] = (kept[:patch_total, :] + received[:patch_total, :].astype(jnp.float32)).astype(
        jnp.bfloat16
    )
    rest = kept[patch_total:, :] + received[patch_total:, :].astype(jnp.float32)
    rows = [rest[b * special_count : (b + 1) * special_count][:, None, :] for b in range(images)]
    special_out[...] = jnp.concatenate(rows, axis=1).astype(jnp.bfloat16)


def call(kernel, out_shape, operands, in_specs=None, out_specs=None, scratch=()):
    return pl.pallas_call(
        kernel,
        out_shape=out_shape,
        in_specs=in_specs or [VMEM] * len(operands),
        out_specs=out_specs or [VMEM] * len(out_shape),
        scratch_shapes=scratch,
        compiler_params=pltpu.CompilerParams(vmem_limit_bytes=VMEM_BYTES),
        cost_estimate=pl.CostEstimate(flops=0, transcendentals=0, bytes_accessed=0),
    )(*operands)


def gathered(block, axis):
    count = lax.axis_size(axis)
    if count & (count - 1):
        return lax.all_gather(block, axis, axis=0, tiled=True)
    bit = 1
    while bit < count:
        bit *= 2
        block = jnp.concatenate([block, swapped(block, axis, bit % count + bit // count)], axis=0)
    return block


def after(array, *others):
    return lax.optimization_barrier((array, *others))[0]


def per_device(
    patch_rows, special_rows, role_first, role_rest, frame_order, covisible, w_qkv, w_out
):
    images, per_image, width = patch_rows.shape
    special_count = special_rows.shape[1]
    real_rows = images * special_count
    special_block = real_rows + -real_rows % TILE_ROWS
    owner_count = lax.axis_size("blk")
    reach = max(1, owner_count // 64)
    patch_total = images * per_image
    rows = patch_total + special_block
    heads = width // HEAD_DIM
    pairs = heads // 2
    relay = reach == 1 and owner_count % 2 == 0

    if relay:
        offsets = [0, (1, -1), (-1, 1)]
    else:
        offsets = [0] + [sign * d for d in range(1, reach + 1) for sign in (-1, 1)]
    mask_rows = -(-len(offsets) * images // 8) * 8
    bf16 = lambda *shape: jax.ShapeDtypeStruct(shape, jnp.bfloat16)
    f32 = lambda *shape: jax.ShapeDtypeStruct(shape, jnp.float32)
    state_shape = [
        f32(8, 2 * patch_total),
        f32(8, 2 * patch_total),
        f32(pairs, HEAD_DIM, 2 * patch_total),
        f32(width, heads * special_block),
    ]

    turned = jnp.transpose(special_rows, (1, 0, 2))
    own, pieces, specials, mask = call(
        functools.partial(start_kernel, offsets),
        [
            bf16(rows, width),
            bf16(images, per_image, width),
            bf16(special_block, width),
            f32(mask_rows, patch_total + heads * special_block),
        ],
        (frame_order, covisible, patch_rows, turned, role_first, role_rest),
        in_specs=[HBM] * 6,
        scratch=[
            pltpu.SMEM(frame_order.shape, jnp.int32),
            pltpu.SMEM(covisible.shape, jnp.int32),
            pltpu.VMEM(turned.shape, jnp.bfloat16),
            pltpu.VMEM(role_first.shape, jnp.bfloat16),
            pltpu.VMEM(role_rest.shape, jnp.bfloat16),
            pltpu.SemaphoreType.DMA((5 + 2 * images,)),
        ],
    )
    pieces = [pieces[b] for b in range(images)]

    def later(sources, parts, *operands):
        halves_here = [part[0] for part in parts] + [part[1] for part in parts]
        return call(
            functools.partial(later_kernel, sources, per_image),
            state_shape,
            (mask, *halves_here, *operands),
        )

    near = [swapped(piece, "blk", 1) for piece in pieces] if relay else []
    other = swapped(own, "head", 1)
    all_specials = gathered(specials, "blk")
    sums, weights = call(
        partial_kernel,
        [f32(3, rows, width), bf16(*w_qkv.shape)],
        (own, w_qkv),
        in_specs=[VMEM, HBM],
        scratch=[pltpu.SemaphoreType.DMA((3, 2))],
    )
    queries, special_queries, *state = call(
        functools.partial(first_kernel, images, patch_total),
        [bf16(pairs, PAIR, 2 * patch_total), bf16(width, heads * special_block), *state_shape],
        (mask, sums, other, weights),
    )
    fixed = (weights, queries, special_queries)
    all_specials = (all_specials, swapped(all_specials, "head", 1))
    both = lambda part: (part, swapped(part, "head", 1))
    if relay:
        groups, far = [], []
        for b in range(images):
            near[b] = after(near[b], state[0])
            far.append(relayed(near[b], "blk"))
            if b == images - 1:
                far[:-1] = [both(part) for part in far[:-1]]
                last = later(
                    [images + b] + [2 * images + c for c in range(b)],
                    [both(near[b]), *far[:-1]], *fixed, *state,
                )
            else:
                state = later([images + b], [both(near[b])], *fixed, *state)
        state = last
        sources, parts = [3 * images - 1], [both(far[-1])]
    else:
        near = []
        for offset in offsets[1:]:
            near.append([both(shifted(piece, "blk", -offset)) for piece in pieces])
        for i, parts in enumerate(near[:-1]):
            state = later([(i + 1) * images + b for b in range(images)], parts, *fixed, *state)
        sources, parts = [len(near) * images + b for b in range(images)], near[-1]
    kept, sent = call(
        functools.partial(last_kernel, sources, per_image, real_rows),
        [f32(rows, width), bf16(rows, width)],
        (
            mask, *[part[0] for part in parts], *[part[1] for part in parts], *all_specials,
            *fixed, *state, w_out,
        ),
        in_specs=[VMEM] * (1 + 2 * len(parts) + 2 + len(fixed) + len(state)) + [HBM],
        scratch=[pltpu.VMEM(w_out.shape, jnp.bfloat16), pltpu.SemaphoreType.DMA],
    )
    received = swapped(sent, "head", 1)
    patch_out, special_out = call(
        functools.partial(end_kernel, images),
        [bf16(patch_total, width), bf16(special_count, images, width)],
        (kept, received),
        out_specs=[pl.BlockSpec(), pl.BlockSpec()],
    )
    return patch_out.reshape(patch_rows.shape), jnp.transpose(special_out, (1, 0, 2))


def solution(mesh):
    in_specs = (
        P(("scene", "blk"), None, "head"),
        P(("scene", "blk"), None, "head"),
        P(),
        P(),
        P(("scene", "blk")),
        P(("scene", "blk"), None),
        P(None, None, "head"),
        P("head", None),
    )
    out_specs = (P(("scene", "blk"), None, "head"), P(("scene", "blk"), None, "head"))
    return jax.shard_map(
        per_device, mesh=mesh, in_specs=in_specs, out_specs=out_specs, check_vma=False
    )
```

```python
import functools

import jax
import jax.numpy as jnp
from jax import lax
from jax.experimental import pallas as pl
from jax.experimental.pallas import tpu as pltpu
from jax.sharding import PartitionSpec as P

HEAD_DIM = 64
PAIR = 2 * HEAD_DIM
TILE_ROWS = 16
VMEM_BYTES = 32 * 1024 * 1024
SMEM = pl.BlockSpec(memory_space=pltpu.SMEM)
VMEM = pl.BlockSpec(memory_space=pltpu.VMEM)
HBM = pl.BlockSpec(memory_space=pltpu.HBM)


def shifted(block, axis, distance):
    count = lax.axis_size(axis)
    route = [((i - distance) % count, i) for i in range(count)]
    return lax.ppermute(block, axis, route)


def swapped(block, axis, bit):
    count = lax.axis_size(axis)
    return lax.ppermute(block, axis, [(i ^ bit, i) for i in range(count)])


def relayed(block, axis):
    count = lax.axis_size(axis)
    return lax.ppermute(block, axis, [(i, (i + (2 if i % 2 == 0 else -2)) % count) for i in range(count)])


def crossed(block, axis):
    count = lax.axis_size(axis)
    return lax.ppermute(block, axis, [(i, (i + (-1 if i % 2 == 0 else 1)) % count) for i in range(count)])


def halves(width):
    half = lax.axis_index("head")
    mine = pl.ds(pl.multiple_of(half * width, width), width)
    theirs = pl.ds(pl.multiple_of((1 - half) * width, width), width)
    return mine, theirs


def product(left, right):
    return jnp.dot(left, right, preferred_element_type=jnp.float32)


def owner_at(offset):
    count = lax.axis_size("blk")
    here = lax.axis_index("blk")
    if isinstance(offset, tuple):
        offset = jnp.where(lax.rem(here, 2) == 0, offset[0], offset[1])
    return lax.rem(here + offset + count, count)


def start_kernel(
    offsets, frame_order, covisible, patches, specials, role_first, role_rest,
    own_out, special_out, mask_out, *rest,
):
    images, per_image, width = patches.shape
    pieces_out, (order, seen, special_rows, first_rows, rest_rows, copied) = rest[:images], rest[images:]
    special_count = specials.shape[0]
    patch_total = images * per_image
    small = [
        pltpu.make_async_copy(source, target, copied.at[i])
        for i, (source, target) in enumerate(
            [
                (specials, special_rows), (role_first, first_rows), (role_rest, rest_rows),
                (frame_order, order), (covisible, seen),
            ]
        )
    ]
    large = []
    for b in range(images):
        large.append((patches.at[b], pieces_out[b]))
        large.append((patches.at[b], own_out.at[pl.ds(b * per_image, per_image)]))
    large = [
        pltpu.make_async_copy(source, target, copied.at[len(small) + i])
        for i, (source, target) in enumerate(large)
    ]
    for copy in small + large:
        copy.start()
    for copy in small:
        copy.wait()
    mine, _ = halves(width)
    first = first_rows[:, mine].astype(jnp.float32)
    rest = rest_rows[:, mine].astype(jnp.float32)
    summed = [
        special_rows[:, b, :].astype(jnp.float32) + jnp.where(order[b] == 0, first, rest)
        for b in range(images)
    ]
    padding = special_out.shape[0] - images * special_count
    summed.append(jnp.zeros((padding, width), jnp.float32))
    block = jnp.concatenate(summed, axis=0).astype(jnp.bfloat16)
    special_out[...] = block
    own_out[patch_total:, :] = block
    lane = lax.broadcasted_iota(jnp.int32, (1, mask_out.shape[1]), 1)
    special_lane = lax.rem(lane - patch_total, special_out.shape[0])
    image = jnp.where(
        lane < patch_total, lane // per_image, jnp.minimum(special_lane // special_count, images - 1)
    )
    for i, offset in enumerate(offsets):
        for b in range(images):
            row = jnp.zeros(lane.shape, jnp.float32)
            for a in range(images):
                hidden = seen[a, owner_at(offset) * images + b] <= 0
                row = jnp.where((image == a) & hidden, -jnp.inf, row)
            mask_out[i * images + b : i * images + b + 1, :] = row
    for copy in large:
        copy.wait()


def partial_kernel(own, w_qkv, sums_out, weights_out, copied):
    width = own.shape[1]
    mine, theirs = halves(width)
    copies = [
        pltpu.make_async_copy(w_qkv.at[i, rows], weights_out.at[i, rows], copied.at[i, j])
        for j, rows in enumerate((mine, theirs))
        for i in range(3)
    ]
    for copy in copies:
        copy.start()
    for i in range(3):
        copies[i].wait()
        sums_out[i] = product(own[...], weights_out[i, mine, :])
    for i in range(3, 6):
        copies[i].wait()


def project(own, other, weights, which):
    mine, theirs = halves(own.shape[1])
    return product(own, weights[which, mine, :]) + product(other, weights[which, theirs, :])


def attend(scores, masks, state):
    largest = None if state is None else state
    start = 0
    for count, mask in masks:
        part = jnp.max(scores[start : start + count], axis=0, keepdims=True) + mask
        largest = part if largest is None else jnp.maximum(largest, part)
        start += count
    weights, start = [], 0
    for count, mask in masks:
        weights.append(jnp.exp(scores[start : start + count] - (largest - mask)).astype(jnp.bfloat16))
        start += count
    factor = None if state is None else jnp.exp(state - largest)
    return largest, factor, jnp.concatenate(weights, axis=0)


def attend_all(keys, values, masks, queries, special_queries, state, special_rows, special_real):
    pairs = queries.shape[0]
    rows = queries.shape[2] // 2
    count = keys.shape[0]
    values = jnp.transpose(values).astype(jnp.bfloat16)
    keys = keys.astype(jnp.bfloat16)
    ones = jnp.ones((TILE_ROWS, count), jnp.bfloat16)
    key_row = lax.broadcasted_iota(jnp.int32, (special_rows, 1), 0)
    real = lax.rem(key_row, TILE_ROWS) < special_real

    def scored(keys, queries):
        scores = product(keys, queries)
        if not special_rows:
            return scores
        cut = count - special_rows
        special = jnp.where(real, scores[cut:], -jnp.inf)
        return jnp.concatenate([scores[:cut], special], axis=0)

    for pair in range(pairs):
        scores = scored(keys[:, pair * PAIR : (pair + 1) * PAIR], queries[pair])
        both = [(n, jnp.concatenate([mask[:, :rows]] * 2, axis=1)) for n, mask in masks]
        largest, factor, weights = attend(scores, both, state and state.largest(pair))
        for sub in range(2):
            first = pair * PAIR + sub * HEAD_DIM
            lanes = slice(sub * rows, (sub + 1) * rows)
            left = jnp.concatenate([values[first : first + HEAD_DIM], ones], axis=0)
            added = product(left, weights[:, lanes])
            added = added[: HEAD_DIM + 1]
            if state is not None:
                before = jnp.concatenate([state.total(pair, sub), state.weight(pair, sub)], axis=0)
                added = added + before * factor[:, lanes]
            yield pair, sub, largest[:, lanes], added[:HEAD_DIM], added[HEAD_DIM:]
    only = [(n, mask[:, rows:]) for n, mask in masks]
    largest, factor, weights = attend(
        scored(keys, special_queries[...]), only, state and state.largest(pairs)
    )
    added = product(jnp.concatenate([values, ones], axis=0), weights)[: values.shape[0] + 1]
    if state is not None:
        before = jnp.concatenate([state.total(pairs, 0), state.weight(pairs, 0)], axis=0)
        added = added + before * factor
    yield pairs, 0, largest, added[:-1], added[-1:]


class State:
    def __init__(self, rows, refs):
        self.rows = rows
        self.largest_ref, self.weight_ref, self.total_ref, self.special_ref = refs

    def lanes(self, pair, sub):
        if pair == self.total_ref.shape[0]:
            return slice(0, self.special_ref.shape[1])
        return slice(sub * self.rows, (sub + 1) * self.rows)

    def largest(self, pair):
        stop = self.special_ref.shape[1] if pair == self.total_ref.shape[0] else 2 * self.rows
        return self.largest_ref[pair : pair + 1, 0:stop]

    def weight(self, pair, sub):
        return self.weight_ref[pair : pair + 1, self.lanes(pair, sub)]

    def total(self, pair, sub):
        if pair == self.total_ref.shape[0]:
            return self.special_ref[...]
        return self.total_ref[pair, :, self.lanes(pair, sub)]

    def put(self, pair, sub, largest, total, weight):
        lanes = self.lanes(pair, sub)
        self.largest_ref[pair : pair + 1, lanes] = largest
        self.weight_ref[pair : pair + 1, lanes] = weight
        if pair == self.total_ref.shape[0]:
            self.special_ref[...] = total
        else:
            self.total_ref[pair, :, lanes] = total


def first_kernel(
    images, patch_total, mask, sums, other, weights, queries_out, special_out, *state_out
):
    _, theirs = halves(other.shape[1])
    queries, keys, values = [sums[i] + product(other[...], weights[i, theirs, :]) for i in range(3)]
    queries = queries * HEAD_DIM ** (-0.5)
    columns = jnp.transpose(queries[:patch_total]).astype(jnp.bfloat16)
    zero = jnp.zeros((HEAD_DIM, patch_total), jnp.bfloat16)
    pairs = queries_out.shape[0]
    for pair in range(pairs):
        first = pair * PAIR
        upper = jnp.concatenate([columns[first : first + HEAD_DIM], zero], axis=1)
        lower = jnp.concatenate([zero, columns[first + HEAD_DIM : first + PAIR]], axis=1)
        queries_out[pair] = jnp.concatenate([upper, lower], axis=0)
    special = jnp.concatenate([queries[patch_total:]] * (2 * pairs), axis=0)
    row = lax.broadcasted_iota(jnp.int32, special.shape, 0) // (queries.shape[0] - patch_total)
    lane = lax.broadcasted_iota(jnp.int32, special.shape, 1) // HEAD_DIM
    special = jnp.where(row == lane, special, 0.0)
    special_out[...] = jnp.transpose(special).astype(jnp.bfloat16)
    per_image = patch_total // images
    masks = [(per_image, mask[b : b + 1, :]) for b in range(images)]
    state = State(patch_total, state_out)
    for result in attend_all(
        keys[:patch_total], values[:patch_total], masks, queries_out, special_out, None, 0, 0
    ):
        state.put(*result)


def later_kernel(sources, per_image, mask, *refs):
    count = len(sources)
    own = jnp.concatenate([ref[...] for ref in refs[:count]], axis=0)
    other = jnp.concatenate([ref[...] for ref in refs[count : 2 * count]], axis=0)
    weights, queries, special_queries = refs[2 * count : 2 * count + 3]
    state_in, state_out = refs[2 * count + 3 : 2 * count + 7], refs[2 * count + 7 :]
    rows = queries.shape[2] // 2
    keys = project(own, other, weights, 1)
    values = project(own, other, weights, 2)
    masks = [(per_image, mask[i : i + 1, :]) for i in sources]
    state = State(rows, state_out)
    for result in attend_all(
        keys, values, masks, queries, special_queries, State(rows, state_in), 0, 0
    ):
        state.put(*result)


def last_kernel(sources, per_image, special_real, mask, *refs):
    count = len(sources)
    own_special, other_special = refs[2 * count : 2 * count + 2]
    own = jnp.concatenate([ref[...] for ref in refs[:count]] + [own_special[...]], axis=0)
    other = jnp.concatenate([ref[...] for ref in refs[count : 2 * count]] + [other_special[...]], axis=0)
    weights, queries, special_queries = refs[2 * count + 2 : 2 * count + 5]
    state_in = refs[2 * count + 5 : 2 * count + 9]
    w_out, kept_out, sent_out, w_here, copied = refs[2 * count + 9 :]
    copy = pltpu.make_async_copy(w_out, w_here, copied)
    copy.start()
    pairs, rows = queries.shape[0], queries.shape[2] // 2
    keys = project(own, other, weights, 1)
    values = project(own, other, weights, 2)
    special_rows = own_special.shape[0]
    masks = [(per_image, mask[i : i + 1, :]) for i in sources]
    masks.append((special_rows, jnp.zeros((1, mask.shape[1]), jnp.float32)))
    columns = []
    for pair, _, _, total, weight in attend_all(
        keys, values, masks, queries, special_queries, State(rows, state_in), special_rows, special_real
    ):
        columns.append(total / weight)
    special = columns.pop()
    attended = jnp.transpose(jnp.concatenate(columns, axis=0))
    row = lax.broadcasted_iota(jnp.int32, special.shape, 0) // HEAD_DIM
    lane = lax.broadcasted_iota(jnp.int32, special.shape, 1) // TILE_ROWS
    special = jnp.transpose(jnp.where(row == lane, special, 0.0))
    special = sum(special[i * TILE_ROWS : (i + 1) * TILE_ROWS] for i in range(2 * pairs))
    attended = jnp.concatenate([attended, special], axis=0).astype(jnp.bfloat16)
    mine, theirs = halves(kept_out.shape[1])
    copy.wait()
    sent_out[...] = product(attended, w_here[:, theirs]).astype(jnp.bfloat16)
    kept_out[...] = product(attended, w_here[:, mine])


def end_kernel(images, kept, received, patch_out, special_out):
    patch_total = patch_out.shape[0]
    special_count = special_out.shape[0]
    patch_out[...] = (kept[:patch_total, :] + received[:patch_total, :].astype(jnp.float32)).astype(
        jnp.bfloat16
    )
    rest = kept[patch_total:, :] + received[patch_total:, :].astype(jnp.float32)
    rows = [rest[b * special_count : (b + 1) * special_count][:, None, :] for b in range(images)]
    special_out[...] = jnp.concatenate(rows, axis=1).astype(jnp.bfloat16)


def call(kernel, out_shape, operands, in_specs=None, out_specs=None, scratch=()):
    if in_specs:
        operands = [
            pltpu.with_memory_space_constraint(operand, pltpu.HBM) if spec is HBM else operand
            for operand, spec in zip(operands, in_specs)
        ]
    return pl.pallas_call(
        kernel,
        out_shape=out_shape,
        in_specs=in_specs or [VMEM] * len(operands),
        out_specs=out_specs or [VMEM] * len(out_shape),
        scratch_shapes=scratch,
        compiler_params=pltpu.CompilerParams(vmem_limit_bytes=VMEM_BYTES),
        cost_estimate=pl.CostEstimate(flops=0, transcendentals=0, bytes_accessed=0),
    )(*operands)


def gathered(block, axis):
    copies = jnp.concatenate([block] * lax.axis_size(axis), axis=0)
    return lax.all_to_all(copies, axis, split_axis=0, concat_axis=0, tiled=True)


def after(array, *others):
    return lax.optimization_barrier((array, *others))[0]


def per_device(
    patch_rows, special_rows, role_first, role_rest, frame_order, covisible, w_qkv, w_out
):
    images, per_image, width = patch_rows.shape
    special_count = special_rows.shape[1]
    real_rows = images * special_count
    special_block = real_rows + -real_rows % TILE_ROWS
    owner_count = lax.axis_size("blk")
    reach = max(1, owner_count // 64)
    patch_total = images * per_image
    rows = patch_total + special_block
    heads = width // HEAD_DIM
    pairs = heads // 2
    relay = reach == 1 and owner_count % 2 == 0 and images > 1

    if relay:
        offsets = [0, (1, -1), (-1, 1)]
    else:
        offsets = [0] + [sign * d for d in range(1, reach + 1) for sign in (-1, 1)]
    mask_rows = -(-len(offsets) * images // 8) * 8
    bf16 = lambda *shape: jax.ShapeDtypeStruct(shape, jnp.bfloat16)
    f32 = lambda *shape: jax.ShapeDtypeStruct(shape, jnp.float32)
    state_shape = [
        f32(8, 2 * patch_total),
        f32(8, 2 * patch_total),
        f32(pairs, HEAD_DIM, 2 * patch_total),
        f32(width, heads * special_block),
    ]

    turned = jnp.transpose(special_rows, (1, 0, 2))
    own, specials, mask, *pieces = call(
        functools.partial(start_kernel, offsets),
        [
            bf16(rows, width),
            bf16(special_block, width),
            f32(mask_rows, patch_total + heads * special_block),
            *[bf16(per_image, width)] * images,
        ],
        (frame_order, covisible, patch_rows, turned, role_first, role_rest),
        in_specs=[HBM] * 6,
        scratch=[
            pltpu.SMEM(frame_order.shape, jnp.int32),
            pltpu.SMEM(covisible.shape, jnp.int32),
            pltpu.VMEM(turned.shape, jnp.bfloat16),
            pltpu.VMEM(role_first.shape, jnp.bfloat16),
            pltpu.VMEM(role_rest.shape, jnp.bfloat16),
            pltpu.SemaphoreType.DMA((5 + 2 * images,)),
        ],
    )

    def later(sources, parts, *operands):
        halves_here = [part[0] for part in parts] + [part[1] for part in parts]
        return call(
            functools.partial(later_kernel, sources, per_image),
            state_shape,
            (mask, *halves_here, *operands),
        )

    both = lambda part: (part, swapped(part, "head", 1))
    if relay:
        near = [swapped(piece, "blk", 1) for piece in pieces]
        far = [crossed(piece, "blk") for piece in pieces[1:]]
    other = swapped(own, "head", 1)
    all_specials = gathered(specials, "blk")
    sums, weights = call(
        partial_kernel,
        [f32(3, rows, width), bf16(*w_qkv.shape)],
        (own, w_qkv),
        in_specs=[VMEM, HBM],
        scratch=[pltpu.SemaphoreType.DMA((3, 2))],
    )
    if relay:
        near[0] = after(near[0], sums)
        far = [relayed(near[0], "blk"), *far]
        near[0] = both(near[0])
    queries, special_queries, *state = call(
        functools.partial(first_kernel, images, patch_total),
        [bf16(pairs, PAIR, 2 * patch_total), bf16(width, heads * special_block), *state_shape],
        (mask, sums, other, weights),
    )
    fixed = (weights, queries, special_queries)
    if relay:
        near[1:] = [both(after(part, state[0])) for part in near[1:]]
        state = later([images], near[:1], *fixed, *state)
        far = [both(after(part, state[0])) for part in far]
        all_specials = both(after(all_specials, state[0]))
        state = later([images + b for b in range(1, images)], near[1:], *fixed, *state)
        sources, parts = [2 * images + b for b in range(images)], far
    else:
        all_specials = both(all_specials)
        near = []
        for offset in offsets[1:]:
            near.append([both(shifted(piece, "blk", -offset)) for piece in pieces])
        for i, parts in enumerate(near[:-1]):
            state = later([(i + 1) * images + b for b in range(images)], parts, *fixed, *state)
        sources, parts = [len(near) * images + b for b in range(images)], near[-1]
    kept, sent = call(
        functools.partial(last_kernel, sources, per_image, real_rows),
        [f32(rows, width), bf16(rows, width)],
        (
            mask, *[part[0] for part in parts], *[part[1] for part in parts], *all_specials,
            *fixed, *state, w_out,
        ),
        in_specs=[VMEM] * (1 + 2 * len(parts) + 2 + len(fixed) + len(state)) + [HBM],
        scratch=[pltpu.VMEM(w_out.shape, jnp.bfloat16), pltpu.SemaphoreType.DMA],
    )
    received = swapped(sent, "head", 1)
    patch_out, special_out = call(
        functools.partial(end_kernel, images),
        [bf16(patch_total, width), bf16(special_count, images, width)],
        (kept, received),
        out_specs=[pl.BlockSpec(), pl.BlockSpec()],
    )
    return patch_out.reshape(patch_rows.shape), jnp.transpose(special_out, (1, 0, 2))


def solution(mesh):
    in_specs = (
        P(("scene", "blk"), None, "head"),
        P(("scene", "blk"), None, "head"),
        P(),
        P(),
        P(("scene", "blk")),
        P(("scene", "blk"), None),
        P(None, None, "head"),
        P("head", None),
    )
    out_specs = (P(("scene", "blk"), None, "head"), P(("scene", "blk"), None, "head"))
    return jax.shard_map(
        per_device, mesh=mesh, in_specs=in_specs, out_specs=out_specs, check_vma=False
    )
```

```python
import functools

import jax
import jax.numpy as jnp
from jax import lax
from jax.experimental import pallas as pl
from jax.experimental.pallas import tpu as pltpu
from jax.sharding import PartitionSpec as P

HEAD_DIM = 64
PAIR = 2 * HEAD_DIM
QUAD = 2 * PAIR
TILE_ROWS = 16
VMEM_BYTES = 32 * 1024 * 1024
SMEM = pl.BlockSpec(memory_space=pltpu.SMEM)
VMEM = pl.BlockSpec(memory_space=pltpu.VMEM)
HBM = pl.BlockSpec(memory_space=pltpu.HBM)


def shifted(block, axis, distance):
    count = lax.axis_size(axis)
    route = [((i - distance) % count, i) for i in range(count)]
    return lax.ppermute(block, axis, route)


def swapped(block, axis, bit):
    count = lax.axis_size(axis)
    return lax.ppermute(block, axis, [(i ^ bit, i) for i in range(count)])


def crossed(block, axis):
    count = lax.axis_size(axis)
    return lax.ppermute(block, axis, [(i, (i + (-1 if i % 2 == 0 else 1)) % count) for i in range(count)])


def halves(width):
    half = lax.axis_index("head")
    mine = pl.ds(pl.multiple_of(half * width, width), width)
    theirs = pl.ds(pl.multiple_of((1 - half) * width, width), width)
    return mine, theirs


def product(left, right):
    return jnp.dot(left, right, preferred_element_type=jnp.float32)


def owner_at(offset):
    count = lax.axis_size("blk")
    here = lax.axis_index("blk")
    if isinstance(offset, tuple):
        offset = jnp.where(lax.rem(here, 2) == 0, offset[0], offset[1])
    return lax.rem(here + offset + count, count)


def start_kernel(
    offsets, special_total, frame_order, covisible, patches, specials, other_specials, role_first, role_rest,
    w_qkv, own_out, special_out, mask_out, weights_out, order, seen, special_here, first_rows, rest_rows, copied,
):
    images, per_image, width = patches.shape
    special_count = specials.shape[0]
    patch_total = images * per_image
    moves = [
        (specials, special_here.at[0]), (other_specials, special_here.at[1]), (role_first, first_rows),
        (role_rest, rest_rows), (frame_order, order), (covisible, seen),
    ]
    small = len(moves)
    moves += [(patches.at[b], own_out.at[pl.ds(b * per_image, per_image)]) for b in range(images)]
    moves += [(w_qkv.at[i], weights_out.at[i]) for i in range(3)]
    copies = [
        pltpu.make_async_copy(source, target, copied.at[i]) for i, (source, target) in enumerate(moves)
    ]
    for copy in copies:
        copy.start()
    for copy in copies[:small]:
        copy.wait()
    for i, columns in enumerate(halves(width)):
        first = first_rows[:, columns].astype(jnp.float32)
        rest = rest_rows[:, columns].astype(jnp.float32)
        summed = [
            special_here[i, :, b, :].astype(jnp.float32) + jnp.where(order[b] == 0, first, rest)
            for b in range(images)
        ]
        summed.append(jnp.zeros((special_total - images * special_count, width), jnp.float32))
        special_out[i] = jnp.concatenate(summed, axis=0).astype(jnp.bfloat16)
    lane = lax.broadcasted_iota(jnp.int32, (1, mask_out.shape[1]), 1)
    special_lane = lax.rem(lane - patch_total, special_total)
    image = jnp.where(
        lane < patch_total, lane // per_image, jnp.minimum(special_lane // special_count, images - 1)
    )
    for i, offset in enumerate(offsets):
        for b in range(images):
            row = jnp.zeros(lane.shape, jnp.float32)
            for a in range(images):
                hidden = seen[a, owner_at(offset) * images + b] <= 0
                row = jnp.where((image == a) & hidden, -jnp.inf, row)
            mask_out[i * images + b : i * images + b + 1, :] = row
    for copy in copies[small:]:
        copy.wait()


def projector(own, other, weights):
    mine, theirs = halves(own.shape[1])

    def columns(which, quad):
        lanes = slice(quad * QUAD, (quad + 1) * QUAD)
        return product(own, weights[which, mine, lanes]) + product(other, weights[which, theirs, lanes])

    return columns


def attend(scores, masks, state):
    largest = state
    start = 0
    for count, mask in masks:
        part = jnp.max(scores[start : start + count], axis=0, keepdims=True)
        part = part if mask is None else part + mask
        largest = part if largest is None else jnp.maximum(largest, part)
        start += count
    weights, start = [], 0
    for count, mask in masks:
        level = largest if mask is None else largest - mask
        weights.append(jnp.exp(scores[start : start + count] - level).astype(jnp.bfloat16))
        start += count
    factor = None if state is None else jnp.exp(state - largest)
    return largest, factor, jnp.concatenate(weights, axis=0)


def attend_all(columns, masks, queries_of, special_queries, state, pairs, rows, special_real):
    keys, values = [], []

    def scored(keys, queries):
        scores = product(keys, queries)
        if all(mask is not None for _, mask in masks):
            return scores
        parts, start = [], 0
        for count, mask in masks:
            part = scores[start : start + count]
            if mask is None:
                key_row = lax.broadcasted_iota(jnp.int32, (count, 1), 0)
                part = jnp.where(lax.rem(key_row, TILE_ROWS) < special_real, part, -jnp.inf)
            parts.append(part)
            start += count
        return jnp.concatenate(parts, axis=0)

    def prepared(pair):
        if pair == pairs:
            return scored(jnp.concatenate(keys, axis=1), special_queries())
        if pair % 2 == 0:
            keys.append(columns(1, pair // 2).astype(jnp.bfloat16))
        lanes = slice((pair % 2) * PAIR, (pair % 2 + 1) * PAIR)
        return scored(keys[pair // 2][:, lanes], queries_of(pair))

    ones = jnp.ones((TILE_ROWS, sum(count for count, _ in masks)), jnp.bfloat16)
    both = [
        (count, None if mask is None else jnp.concatenate([mask[:, :rows]] * 2, axis=1))
        for count, mask in masks
    ]
    only = [(count, None if mask is None else mask[:, rows:]) for count, mask in masks]
    scores = prepared(0)
    for pair in range(pairs):
        if pair % 2 == 0:
            values.append(jnp.transpose(columns(2, pair // 2)).astype(jnp.bfloat16))
        following = prepared(pair + 1)
        largest, factor, weights = attend(scores, both, state and state.largest(pair))
        for sub in range(2):
            first = (pair % 2) * PAIR + sub * HEAD_DIM
            lanes = slice(sub * rows, (sub + 1) * rows)
            left = jnp.concatenate([values[pair // 2][first : first + HEAD_DIM], ones], axis=0)
            added = product(left, weights[:, lanes])[: HEAD_DIM + 1]
            if state is not None:
                before = jnp.concatenate([state.total(pair, sub), state.weight(pair, sub)], axis=0)
                added = added + before * factor[:, lanes]
            yield pair, sub, largest[:, lanes], added[:HEAD_DIM], added[HEAD_DIM:]
        scores = following
    largest, factor, weights = attend(scores, only, state and state.largest(pairs))
    added = product(jnp.concatenate(values + [ones], axis=0), weights)[: pairs * PAIR + 1]
    if state is not None:
        before = jnp.concatenate([state.total(pairs, 0), state.weight(pairs, 0)], axis=0)
        added = added + before * factor
    yield pairs, 0, largest, added[:-1], added[-1:]


class State:
    def __init__(self, rows, refs):
        self.rows = rows
        self.largest_ref, self.weight_ref, self.total_ref, self.special_ref = refs

    def lanes(self, pair, sub):
        if pair == self.total_ref.shape[0]:
            return slice(0, self.special_ref.shape[1])
        return slice(sub * self.rows, (sub + 1) * self.rows)

    def largest(self, pair):
        stop = self.special_ref.shape[1] if pair == self.total_ref.shape[0] else 2 * self.rows
        return self.largest_ref[pair : pair + 1, 0:stop]

    def weight(self, pair, sub):
        return self.weight_ref[pair : pair + 1, self.lanes(pair, sub)]

    def total(self, pair, sub):
        if pair == self.total_ref.shape[0]:
            return self.special_ref[...]
        return self.total_ref[pair, :, self.lanes(pair, sub)]

    def put(self, pair, sub, largest, total, weight):
        lanes = self.lanes(pair, sub)
        self.largest_ref[pair : pair + 1, lanes] = largest
        self.weight_ref[pair : pair + 1, lanes] = weight
        if pair == self.total_ref.shape[0]:
            self.special_ref[...] = total
        else:
            self.total_ref[pair, :, lanes] = total


def first_kernel(
    images, mask, own, other, special, weights, queries_out, special_out, *state_out
):
    patch_total = own.shape[0]
    columns = projector(
        jnp.concatenate([own[...], special[0]], axis=0),
        jnp.concatenate([other[...], special[1]], axis=0),
        weights,
    )
    pairs = queries_out.shape[0]
    zero = jnp.zeros((HEAD_DIM, patch_total), jnp.bfloat16)
    special_columns = []

    def patch_columns(which, quad):
        return columns(which, quad)[:patch_total]

    def queries_of(pair):
        if pair % 2 == 0:
            queries = columns(0, pair // 2) * HEAD_DIM ** (-0.5)
            special_columns.append(queries[patch_total:])
            turned = jnp.transpose(queries[:patch_total]).astype(jnp.bfloat16)
            for i in range(2):
                first = i * PAIR
                upper = jnp.concatenate([turned[first : first + HEAD_DIM], zero], axis=1)
                lower = jnp.concatenate([zero, turned[first + HEAD_DIM : first + PAIR]], axis=1)
                queries_out[pair + i] = jnp.concatenate([upper, lower], axis=0)
        return queries_out[pair]

    def special_queries():
        block = jnp.concatenate(special_columns, axis=1)
        count = block.shape[0]
        block = jnp.concatenate([block] * (2 * pairs), axis=0)
        row = lax.broadcasted_iota(jnp.int32, block.shape, 0) // count
        lane = lax.broadcasted_iota(jnp.int32, block.shape, 1) // HEAD_DIM
        block = jnp.transpose(jnp.where(row == lane, block, 0.0)).astype(jnp.bfloat16)
        special_out[...] = block
        return block

    per_image = patch_total // images
    masks = [(per_image, mask[b : b + 1, :]) for b in range(images)]
    state = State(patch_total, state_out)
    for result in attend_all(
        patch_columns, masks, queries_of, special_queries, None, pairs, patch_total, 0
    ):
        state.put(*result)


def joined(stretches, mask, refs):
    count = len(stretches)
    own = jnp.concatenate([ref[0] if len(ref.shape) > 2 else ref[...] for ref in refs[:count]], axis=0)
    other = jnp.concatenate(
        [ref[1] if len(ref.shape) > 2 else ref[...] for ref in refs[count : 2 * count]], axis=0
    )
    masks = [
        (rows, None if i is None else mask[i : i + 1, :]) for part in stretches for rows, i in part
    ]
    return own, other, masks, refs[2 * count :]


def later_kernel(stretches, special_real, mask, *refs):
    own, other, masks, refs = joined(stretches, mask, refs)
    weights, queries, special_queries = refs[:3]
    state_in, state_out = refs[3:7], refs[7:]
    pairs, rows = queries.shape[0], queries.shape[2] // 2
    state = State(rows, state_out)
    for result in attend_all(
        projector(own, other, weights), masks, lambda pair: queries[pair], lambda: special_queries[...],
        State(rows, state_in), pairs, rows, special_real,
    ):
        state.put(*result)


def last_kernel(stretches, special_real, mask, *refs):
    own, other, masks, refs = joined(stretches, mask, refs)
    weights, queries, special_queries = refs[:3]
    state_in = refs[3:7]
    w_out, kept_out, sent_out, w_here, copied = refs[7:]
    copy = pltpu.make_async_copy(w_out, w_here, copied)
    copy.start()
    pairs, rows = queries.shape[0], queries.shape[2] // 2
    columns = []
    for pair, _, _, total, weight in attend_all(
        projector(own, other, weights), masks, lambda pair: queries[pair], lambda: special_queries[...],
        State(rows, state_in), pairs, rows, special_real,
    ):
        columns.append(total / weight)
    special = columns.pop()
    attended = jnp.transpose(jnp.concatenate(columns, axis=0))
    row = lax.broadcasted_iota(jnp.int32, special.shape, 0) // HEAD_DIM
    lane = lax.broadcasted_iota(jnp.int32, special.shape, 1) // TILE_ROWS
    special = jnp.transpose(jnp.where(row == lane, special, 0.0))
    special = sum(special[i * TILE_ROWS : (i + 1) * TILE_ROWS] for i in range(2 * pairs))
    attended = jnp.concatenate([attended, special], axis=0).astype(jnp.bfloat16)
    mine, theirs = halves(kept_out.shape[1])
    copy.wait()
    sent_out[...] = product(attended, w_here[:, theirs]).astype(jnp.bfloat16)
    kept_out[...] = product(attended, w_here[:, mine])


def end_kernel(images, kept, received, patch_out, special_out):
    patch_total = patch_out.shape[0]
    special_count = special_out.shape[0]
    patch_out[...] = (kept[:patch_total, :] + received[:patch_total, :].astype(jnp.float32)).astype(
        jnp.bfloat16
    )
    rest = kept[patch_total:, :] + received[patch_total:, :].astype(jnp.float32)
    rows = [rest[b * special_count : (b + 1) * special_count][:, None, :] for b in range(images)]
    special_out[...] = jnp.concatenate(rows, axis=1).astype(jnp.bfloat16)


def call(kernel, out_shape, operands, in_specs=None, out_specs=None, scratch=(), cost=0):
    if in_specs:
        operands = [
            pltpu.with_memory_space_constraint(operand, pltpu.HBM) if spec is HBM else operand
            for operand, spec in zip(operands, in_specs)
        ]
    return pl.pallas_call(
        kernel,
        out_shape=out_shape,
        in_specs=in_specs or [VMEM] * len(operands),
        out_specs=out_specs or [VMEM] * len(out_shape),
        scratch_shapes=scratch,
        compiler_params=pltpu.CompilerParams(vmem_limit_bytes=VMEM_BYTES),
        cost_estimate=pl.CostEstimate(flops=cost, transcendentals=0, bytes_accessed=0),
    )(*operands)


def gathered(block, axis, bits):
    for bit in bits:
        block = jnp.concatenate([block, swapped(block, axis, bit)], axis=1)
    return block


def after(array, *others):
    return lax.optimization_barrier((array, *others))[0]


def per_device(
    patch_rows, special_rows, role_first, role_rest, frame_order, covisible, w_qkv, w_out
):
    images, per_image, width = patch_rows.shape
    special_count = special_rows.shape[1]
    real_rows = images * special_count
    special_block = real_rows + -real_rows % TILE_ROWS
    owner_count = lax.axis_size("blk")
    reach = max(1, owner_count // 64)
    patch_total = images * per_image
    rows = patch_total + special_block
    heads = width // HEAD_DIM
    pairs = heads // 2
    paired = reach == 1 and owner_count % 2 == 0

    if paired:
        offsets = [0, (1, -1), (-1, 1)]
    else:
        offsets = [0] + [sign * d for d in range(1, reach + 1) for sign in (-1, 1)]
    mask_rows = -(-len(offsets) * images // 8) * 8
    bf16 = lambda *shape: jax.ShapeDtypeStruct(shape, jnp.bfloat16)
    f32 = lambda *shape: jax.ShapeDtypeStruct(shape, jnp.float32)
    state_shape = [
        f32(8, 2 * patch_total),
        f32(8, 2 * patch_total),
        f32(pairs, HEAD_DIM, 2 * patch_total),
        f32(width, heads * special_block),
    ]

    both = lambda part: (part, swapped(part, "head", 1))
    patches = patch_rows.reshape(patch_total, width)
    turned = jnp.transpose(special_rows, (1, 0, 2))
    if paired:
        near = [swapped(patches, "blk", 1), crossed(patches, "blk")]
    else:
        near = [shifted(patches, "blk", -offset) for offset in offsets[1:]]
    other = swapped(patches, "head", 1)
    own, specials, mask, weights = call(
        functools.partial(start_kernel, offsets, special_block),
        [
            bf16(patch_total, width),
            bf16(2, special_block, width),
            f32(mask_rows, patch_total + heads * special_block),
            bf16(*w_qkv.shape),
        ],
        (
            frame_order, covisible, patch_rows, turned, swapped(turned, "head", 1),
            role_first, role_rest, w_qkv,
        ),
        in_specs=[HBM] * 8,
        scratch=[
            pltpu.SMEM(frame_order.shape, jnp.int32),
            pltpu.SMEM(covisible.shape, jnp.int32),
            pltpu.VMEM((2, *turned.shape), jnp.bfloat16),
            pltpu.VMEM(role_first.shape, jnp.bfloat16),
            pltpu.VMEM(role_rest.shape, jnp.bfloat16),
            pltpu.SemaphoreType.DMA((6 + images + 3,)),
        ],
    )
    if owner_count & (owner_count - 1):
        bits, everywhere = [], lax.all_gather(specials, "blk", axis=1, tiled=True)
    else:
        bits = [1 << i for i in range(1, owner_count.bit_length() - 1)] + [1]
        everywhere = gathered(specials, "blk", bits[:-1])
    queries, special_queries, *state = call(
        functools.partial(first_kernel, images),
        [bf16(pairs, PAIR, 2 * patch_total), bf16(width, heads * special_block), *state_shape],
        (mask, own, other, specials, weights),
    )
    fixed = (weights, queries, special_queries)

    def later(stretches, parts, state):
        return call(
            functools.partial(later_kernel, stretches, real_rows),
            state_shape,
            (mask, *[part[0] for part in parts], *[part[1] for part in parts], *fixed, *state),
        )

    image_rows = lambda owner: [(per_image, owner * images + b) for b in range(images)]
    for i, part in enumerate(near):
        part = after(part, state[0])
        stretches = [[image] for image in image_rows(i + 1)]
        parts = [both(part[b * per_image : (b + 1) * per_image]) for b in range(images)]
        if i < len(near) - 1:
            state = later(stretches, parts, state)
    everywhere = gathered(after(everywhere, state[0]), "blk", bits[-1:])
    stretches.append([(everywhere.shape[1], None)])
    parts.append((everywhere, everywhere))
    kept, sent = call(
        functools.partial(last_kernel, stretches, real_rows),
        [f32(rows, width), bf16(rows, width)],
        (
            mask, *[part[0] for part in parts], *[part[1] for part in parts], *fixed, *state, w_out,
        ),
        in_specs=[VMEM] * (1 + 2 * len(parts) + len(fixed) + len(state)) + [HBM],
        scratch=[pltpu.VMEM(w_out.shape, jnp.bfloat16), pltpu.SemaphoreType.DMA],
    )
    received = swapped(sent, "head", 1)
    patch_out, special_out = call(
        functools.partial(end_kernel, images),
        [bf16(patch_total, width), bf16(special_count, images, width)],
        (kept, received),
        out_specs=[pl.BlockSpec(), pl.BlockSpec()],
    )
    return patch_out.reshape(patch_rows.shape), jnp.transpose(special_out, (1, 0, 2))


def solution(mesh):
    in_specs = (
        P(("scene", "blk"), None, "head"),
        P(("scene", "blk"), None, "head"),
        P(),
        P(),
        P(("scene", "blk")),
        P(("scene", "blk"), None),
        P(None, None, "head"),
        P("head", None),
    )
    out_specs = (P(("scene", "blk"), None, "head"), P(("scene", "blk"), None, "head"))
    return jax.shard_map(
        per_device, mesh=mesh, in_specs=in_specs, out_specs=out_specs, check_vma=False
    )
```

```python
import functools

import jax
import jax.numpy as jnp
from jax import lax
from jax.experimental import pallas as pl
from jax.experimental.pallas import tpu as pltpu
from jax.sharding import PartitionSpec as P

HEAD_DIM = 64
PAIR = 2 * HEAD_DIM
QUAD = 2 * PAIR
TILE_ROWS = 16
VMEM_BYTES = 32 * 1024 * 1024
SMEM = pl.BlockSpec(memory_space=pltpu.SMEM)
VMEM = pl.BlockSpec(memory_space=pltpu.VMEM)
HBM = pl.BlockSpec(memory_space=pltpu.HBM)


def shifted(block, axis, distance):
    count = lax.axis_size(axis)
    route = [((i - distance) % count, i) for i in range(count)]
    return lax.ppermute(block, axis, route)


def swapped(block, axis, bit):
    count = lax.axis_size(axis)
    return lax.ppermute(block, axis, [(i ^ bit, i) for i in range(count)])


def crossed(block, axis):
    count = lax.axis_size(axis)
    return lax.ppermute(block, axis, [(i, (i + (-1 if i % 2 == 0 else 1)) % count) for i in range(count)])


def halves(width):
    half = lax.axis_index("head")
    mine = pl.ds(pl.multiple_of(half * width, width), width)
    theirs = pl.ds(pl.multiple_of((1 - half) * width, width), width)
    return mine, theirs


def product(left, right):
    return jnp.dot(left, right, preferred_element_type=jnp.float32)


def owner_at(offset):
    count = lax.axis_size("blk")
    here = lax.axis_index("blk")
    if isinstance(offset, tuple):
        offset = jnp.where(lax.rem(here, 2) == 0, offset[0], offset[1])
    return lax.rem(here + offset + count, count)


def start_kernel(
    offsets, special_total, frame_order, covisible, patches, specials, other_specials, role_first, role_rest,
    w_qkv, own_out, special_out, mask_out, weights_out, order, seen, special_here, first_rows, rest_rows, copied,
):
    images, per_image, width = patches.shape
    special_count = specials.shape[0]
    patch_total = images * per_image
    moves = [
        (specials, special_here.at[0]), (other_specials, special_here.at[1]), (role_first, first_rows),
        (role_rest, rest_rows), (frame_order, order), (covisible, seen),
    ]
    small = len(moves)
    moves += [(patches.at[b], own_out.at[pl.ds(b * per_image, per_image)]) for b in range(images)]
    moves += [(w_qkv.at[i], weights_out.at[i]) for i in range(3)]
    copies = [
        pltpu.make_async_copy(source, target, copied.at[i]) for i, (source, target) in enumerate(moves)
    ]
    for copy in copies:
        copy.start()
    for copy in copies[:small]:
        copy.wait()
    for i, columns in enumerate(halves(width)):
        first = first_rows[:, columns].astype(jnp.float32)
        rest = rest_rows[:, columns].astype(jnp.float32)
        summed = [
            special_here[i, :, b, :].astype(jnp.float32) + jnp.where(order[b] == 0, first, rest)
            for b in range(images)
        ]
        summed.append(jnp.zeros((special_total - images * special_count, width), jnp.float32))
        special_out[i] = jnp.concatenate(summed, axis=0).astype(jnp.bfloat16)
    lane = lax.broadcasted_iota(jnp.int32, (1, mask_out.shape[1]), 1)
    special_lane = lax.rem(lane - patch_total, special_total)
    image = jnp.where(
        lane < patch_total, lane // per_image, jnp.minimum(special_lane // special_count, images - 1)
    )
    for i, offset in enumerate(offsets):
        for b in range(images):
            row = jnp.zeros(lane.shape, jnp.float32)
            for a in range(images):
                hidden = seen[a, owner_at(offset) * images + b] <= 0
                row = jnp.where((image == a) & hidden, -jnp.inf, row)
            mask_out[i * images + b : i * images + b + 1, :] = row
    for copy in copies[small:]:
        copy.wait()


def projector(own, other, weights):
    mine, theirs = halves(own.shape[1])

    def columns(which, quad):
        lanes = slice(quad * QUAD, (quad + 1) * QUAD)
        return product(own, weights[which, mine, lanes]) + product(other, weights[which, theirs, lanes])

    return columns


def attend(scores, masks, state):
    largest = state
    start = 0
    for count, mask in masks:
        part = jnp.max(scores[start : start + count], axis=0, keepdims=True)
        part = part if mask is None else part + mask
        largest = part if largest is None else jnp.maximum(largest, part)
        start += count
    weights, start = [], 0
    for count, mask in masks:
        level = largest if mask is None else largest - mask
        weights.append(jnp.exp(scores[start : start + count] - level).astype(jnp.bfloat16))
        start += count
    factor = None if state is None else jnp.exp(state - largest)
    return largest, factor, jnp.concatenate(weights, axis=0)


def attend_all(columns, masks, queries_of, special_queries, state, pairs, rows, special_real):
    keys, values = [], []

    def scored(keys, queries):
        scores = product(keys, queries)
        if all(mask is not None for _, mask in masks):
            return scores
        parts, start = [], 0
        for count, mask in masks:
            part = scores[start : start + count]
            if mask is None:
                key_row = lax.broadcasted_iota(jnp.int32, (count, 1), 0)
                part = jnp.where(lax.rem(key_row, TILE_ROWS) < special_real, part, -jnp.inf)
            parts.append(part)
            start += count
        return jnp.concatenate(parts, axis=0)

    def prepared(pair):
        if pair == pairs:
            return scored(jnp.concatenate(keys, axis=1), special_queries())
        if pair % 2 == 0:
            keys.append(columns(1, pair // 2).astype(jnp.bfloat16))
        lanes = slice((pair % 2) * PAIR, (pair % 2 + 1) * PAIR)
        return scored(keys[pair // 2][:, lanes], queries_of(pair))

    ones = jnp.ones((TILE_ROWS, sum(count for count, _ in masks)), jnp.bfloat16)
    both = [
        (count, None if mask is None else jnp.concatenate([mask[:, :rows]] * 2, axis=1))
        for count, mask in masks
    ]
    only = [(count, None if mask is None else mask[:, rows:]) for count, mask in masks]
    scores = prepared(0)
    for pair in range(pairs):
        if pair % 2 == 0:
            values.append(jnp.transpose(columns(2, pair // 2)).astype(jnp.bfloat16))
        following = prepared(pair + 1)
        largest, factor, weights = attend(scores, both, state and state.largest(pair))
        for sub in range(2):
            first = (pair % 2) * PAIR + sub * HEAD_DIM
            lanes = slice(sub * rows, (sub + 1) * rows)
            left = jnp.concatenate([values[pair // 2][first : first + HEAD_DIM], ones], axis=0)
            added = product(left, weights[:, lanes])[: HEAD_DIM + 1]
            if state is not None:
                before = jnp.concatenate([state.total(pair, sub), state.weight(pair, sub)], axis=0)
                added = added + before * factor[:, lanes]
            yield pair, sub, largest[:, lanes], added[:HEAD_DIM], added[HEAD_DIM:]
        scores = following
    largest, factor, weights = attend(scores, only, state and state.largest(pairs))
    added = product(jnp.concatenate(values + [ones], axis=0), weights)[: pairs * PAIR + 1]
    if state is not None:
        before = jnp.concatenate([state.total(pairs, 0), state.weight(pairs, 0)], axis=0)
        added = added + before * factor
    yield pairs, 0, largest, added[:-1], added[-1:]


class State:
    def __init__(self, rows, refs):
        self.rows = rows
        self.largest_ref, self.weight_ref, self.total_ref, self.special_ref = refs

    def lanes(self, pair, sub):
        if pair == self.total_ref.shape[0]:
            return slice(0, self.special_ref.shape[1])
        return slice(sub * self.rows, (sub + 1) * self.rows)

    def largest(self, pair):
        stop = self.special_ref.shape[1] if pair == self.total_ref.shape[0] else 2 * self.rows
        return self.largest_ref[pair : pair + 1, 0:stop]

    def weight(self, pair, sub):
        return self.weight_ref[pair : pair + 1, self.lanes(pair, sub)]

    def total(self, pair, sub):
        if pair == self.total_ref.shape[0]:
            return self.special_ref[...]
        return self.total_ref[pair, :, self.lanes(pair, sub)]

    def put(self, pair, sub, largest, total, weight):
        lanes = self.lanes(pair, sub)
        self.largest_ref[pair : pair + 1, lanes] = largest
        self.weight_ref[pair : pair + 1, lanes] = weight
        if pair == self.total_ref.shape[0]:
            self.special_ref[...] = total
        else:
            self.total_ref[pair, :, lanes] = total


def first_kernel(
    images, mask, own, other, special, weights, queries_out, special_out, *state_out
):
    patch_total = own.shape[0]
    columns = projector(
        jnp.concatenate([own[...], special[0]], axis=0),
        jnp.concatenate([other[...], special[1]], axis=0),
        weights,
    )
    pairs = queries_out.shape[0]
    zero = jnp.zeros((HEAD_DIM, patch_total), jnp.bfloat16)
    special_columns = []

    def patch_columns(which, quad):
        return columns(which, quad)[:patch_total]

    def queries_of(pair):
        if pair % 2 == 0:
            queries = columns(0, pair // 2) * HEAD_DIM ** (-0.5)
            special_columns.append(queries[patch_total:])
            turned = jnp.transpose(queries[:patch_total]).astype(jnp.bfloat16)
            for i in range(2):
                first = i * PAIR
                upper = jnp.concatenate([turned[first : first + HEAD_DIM], zero], axis=1)
                lower = jnp.concatenate([zero, turned[first + HEAD_DIM : first + PAIR]], axis=1)
                queries_out[pair + i] = jnp.concatenate([upper, lower], axis=0)
        return queries_out[pair]

    def special_queries():
        block = jnp.concatenate(special_columns, axis=1)
        count = block.shape[0]
        block = jnp.concatenate([block] * (2 * pairs), axis=0)
        row = lax.broadcasted_iota(jnp.int32, block.shape, 0) // count
        lane = lax.broadcasted_iota(jnp.int32, block.shape, 1) // HEAD_DIM
        block = jnp.transpose(jnp.where(row == lane, block, 0.0)).astype(jnp.bfloat16)
        special_out[...] = block
        return block

    per_image = patch_total // images
    masks = [(per_image, mask[b : b + 1, :]) for b in range(images)]
    state = State(patch_total, state_out)
    for result in attend_all(
        patch_columns, masks, queries_of, special_queries, None, pairs, patch_total, 0
    ):
        state.put(*result)


def joined(stretches, mask, refs):
    count = len(stretches)
    own = jnp.concatenate([ref[0] if len(ref.shape) > 2 else ref[...] for ref in refs[:count]], axis=0)
    other = jnp.concatenate(
        [ref[1] if len(ref.shape) > 2 else ref[...] for ref in refs[count : 2 * count]], axis=0
    )
    masks = [
        (rows, None if i is None else mask[i : i + 1, :]) for part in stretches for rows, i in part
    ]
    return own, other, masks, refs[2 * count :]


def later_kernel(stretches, special_real, mask, *refs):
    own, other, masks, refs = joined(stretches, mask, refs)
    weights, queries, special_queries = refs[:3]
    state_in, state_out = refs[3:7], refs[7:]
    pairs, rows = queries.shape[0], queries.shape[2] // 2
    state = State(rows, state_out)
    for result in attend_all(
        projector(own, other, weights), masks, lambda pair: queries[pair], lambda: special_queries[...],
        State(rows, state_in), pairs, rows, special_real,
    ):
        state.put(*result)


def last_kernel(stretches, special_real, mask, *refs):
    own, other, masks, refs = joined(stretches, mask, refs)
    weights, queries, special_queries = refs[:3]
    state_in = refs[3:7]
    w_out, kept_out, sent_out, w_here, copied = refs[7:]
    copy = pltpu.make_async_copy(w_out, w_here, copied)
    copy.start()
    pairs, rows = queries.shape[0], queries.shape[2] // 2
    columns = []
    for pair, _, _, total, weight in attend_all(
        projector(own, other, weights), masks, lambda pair: queries[pair], lambda: special_queries[...],
        State(rows, state_in), pairs, rows, special_real,
    ):
        columns.append(total / weight)
    special = columns.pop()
    attended = jnp.transpose(jnp.concatenate(columns, axis=0))
    row = lax.broadcasted_iota(jnp.int32, special.shape, 0) // HEAD_DIM
    lane = lax.broadcasted_iota(jnp.int32, special.shape, 1) // TILE_ROWS
    special = jnp.transpose(jnp.where(row == lane, special, 0.0))
    special = sum(special[i * TILE_ROWS : (i + 1) * TILE_ROWS] for i in range(2 * pairs))
    attended = jnp.concatenate([attended, special], axis=0).astype(jnp.bfloat16)
    mine, theirs = halves(kept_out.shape[1])
    copy.wait()
    sent_out[...] = product(attended, w_here[:, theirs]).astype(jnp.bfloat16)
    kept_out[...] = product(attended, w_here[:, mine])


def end_kernel(images, kept, received, patch_out, special_out):
    patch_total = patch_out.shape[0]
    special_count = special_out.shape[0]
    patch_out[...] = (kept[:patch_total, :] + received[:patch_total, :].astype(jnp.float32)).astype(
        jnp.bfloat16
    )
    rest = kept[patch_total:, :] + received[patch_total:, :].astype(jnp.float32)
    rows = [rest[b * special_count : (b + 1) * special_count][:, None, :] for b in range(images)]
    special_out[...] = jnp.concatenate(rows, axis=1).astype(jnp.bfloat16)


def call(kernel, out_shape, operands, in_specs=None, out_specs=None, scratch=(), cost=0):
    if in_specs:
        operands = [
            pltpu.with_memory_space_constraint(operand, pltpu.HBM) if spec is HBM else operand
            for operand, spec in zip(operands, in_specs)
        ]
    return pl.pallas_call(
        kernel,
        out_shape=out_shape,
        in_specs=in_specs or [VMEM] * len(operands),
        out_specs=out_specs or [VMEM] * len(out_shape),
        scratch_shapes=scratch,
        compiler_params=pltpu.CompilerParams(vmem_limit_bytes=VMEM_BYTES),
        cost_estimate=pl.CostEstimate(flops=cost, transcendentals=0, bytes_accessed=0),
    )(*operands)


def gathered(block, axis, bits):
    for bit in bits:
        block = jnp.concatenate([block, swapped(block, axis, bit)], axis=1)
    return block


def after(array, *others):
    return lax.optimization_barrier((array, *others))[0]


def per_device(
    patch_rows, special_rows, role_first, role_rest, frame_order, covisible, w_qkv, w_out
):
    images, per_image, width = patch_rows.shape
    special_count = special_rows.shape[1]
    real_rows = images * special_count
    special_block = real_rows + -real_rows % TILE_ROWS
    owner_count = lax.axis_size("blk")
    reach = max(1, owner_count // 64)
    patch_total = images * per_image
    rows = patch_total + special_block
    heads = width // HEAD_DIM
    pairs = heads // 2
    paired = reach == 1 and owner_count % 2 == 0

    if paired:
        offsets = [0, (1, -1), (-1, 1)]
    else:
        offsets = [0] + [sign * d for d in range(1, reach + 1) for sign in (-1, 1)]
    mask_rows = -(-len(offsets) * images // 8) * 8
    bf16 = lambda *shape: jax.ShapeDtypeStruct(shape, jnp.bfloat16)
    f32 = lambda *shape: jax.ShapeDtypeStruct(shape, jnp.float32)
    state_shape = [
        f32(8, 2 * patch_total),
        f32(8, 2 * patch_total),
        f32(pairs, HEAD_DIM, 2 * patch_total),
        f32(width, heads * special_block),
    ]

    both = lambda part: (part, swapped(part, "head", 1))
    patches = patch_rows.reshape(patch_total, width)
    turned = jnp.transpose(special_rows, (1, 0, 2))
    if paired:
        near = [swapped(patches, "blk", 1), crossed(patches, "blk")]
    else:
        near = [shifted(patches, "blk", -offset) for offset in offsets[1:]]
    other = swapped(patches, "head", 1)
    own, specials, mask, weights = call(
        functools.partial(start_kernel, offsets, special_block),
        [
            bf16(patch_total, width),
            bf16(2, special_block, width),
            f32(mask_rows, patch_total + heads * special_block),
            bf16(*w_qkv.shape),
        ],
        (
            frame_order, covisible, patch_rows, turned, swapped(turned, "head", 1),
            role_first, role_rest, w_qkv,
        ),
        in_specs=[HBM] * 4 + [VMEM] + [HBM] * 3,
        scratch=[
            pltpu.SMEM(frame_order.shape, jnp.int32),
            pltpu.SMEM(covisible.shape, jnp.int32),
            pltpu.VMEM((2, *turned.shape), jnp.bfloat16),
            pltpu.VMEM(role_first.shape, jnp.bfloat16),
            pltpu.VMEM(role_rest.shape, jnp.bfloat16),
            pltpu.SemaphoreType.DMA((6 + images + 3,)),
        ],
    )
    power = owner_count & (owner_count - 1) == 0
    bits = [1 << i for i in range(1, owner_count.bit_length() - 1)] + [1] if power else []
    everywhere = gathered(specials, "blk", bits[:1])
    queries, special_queries, *state = call(
        functools.partial(first_kernel, images),
        [bf16(pairs, PAIR, 2 * patch_total), bf16(width, heads * special_block), *state_shape],
        (mask, own, other, specials, weights),
    )
    fixed = (weights, queries, special_queries)

    def later(stretches, parts, state):
        return call(
            functools.partial(later_kernel, stretches, real_rows),
            state_shape,
            (mask, *[part[0] for part in parts], *[part[1] for part in parts], *fixed, *state),
        )

    image_rows = lambda owner: [(per_image, owner * images + b) for b in range(images)]
    if power:
        everywhere = gathered(after(everywhere, state[0]), "blk", bits[1:])
    else:
        everywhere = lax.all_gather(specials, "blk", axis=1, tiled=True)
    for i, part in enumerate(near):
        part = after(part, state[0])
        stretches = [[image] for image in image_rows(i + 1)]
        parts = [both(part[b * per_image : (b + 1) * per_image]) for b in range(images)]
        if i == 0:
            stretches.append([(everywhere.shape[1], None)])
            parts.append((everywhere, everywhere))
        if i < len(near) - 1:
            state = later(stretches, parts, state)
    kept, sent = call(
        functools.partial(last_kernel, stretches, real_rows),
        [f32(rows, width), bf16(rows, width)],
        (
            mask, *[part[0] for part in parts], *[part[1] for part in parts], *fixed, *state, w_out,
        ),
        in_specs=[VMEM] * (1 + 2 * len(parts) + len(fixed) + len(state)) + [HBM],
        scratch=[pltpu.VMEM(w_out.shape, jnp.bfloat16), pltpu.SemaphoreType.DMA],
    )
    received = swapped(sent, "head", 1)
    patch_out, special_out = call(
        functools.partial(end_kernel, images),
        [bf16(patch_total, width), bf16(special_count, images, width)],
        (kept, received),
        out_specs=[pl.BlockSpec(), pl.BlockSpec()],
    )
    return patch_out.reshape(patch_rows.shape), jnp.transpose(special_out, (1, 0, 2))


def solution(mesh):
    in_specs = (
        P(("scene", "blk"), None, "head"),
        P(("scene", "blk"), None, "head"),
        P(),
        P(),
        P(("scene", "blk")),
        P(("scene", "blk"), None),
        P(None, None, "head"),
        P("head", None),
    )
    out_specs = (P(("scene", "blk"), None, "head"), P(("scene", "blk"), None, "head"))
    return jax.shard_map(
        per_device, mesh=mesh, in_specs=in_specs, out_specs=out_specs, check_vma=False
    )
```

```python
import functools

import jax
import jax.numpy as jnp
from jax import lax
from jax.experimental import pallas as pl
from jax.experimental.pallas import tpu as pltpu
from jax.sharding import PartitionSpec as P

HEAD_DIM = 64
PAIR = 2 * HEAD_DIM
QUAD = 2 * PAIR
TILE_ROWS = 16
LOG2_E = 1.4426950408889634
FIRST = 20_000_000_000
VMEM_BYTES = 32 * 1024 * 1024
SMEM = pl.BlockSpec(memory_space=pltpu.SMEM)
VMEM = pl.BlockSpec(memory_space=pltpu.VMEM)
HBM = pl.BlockSpec(memory_space=pltpu.HBM)


def shifted(block, axis, distance):
    count = lax.axis_size(axis)
    route = [((i - distance) % count, i) for i in range(count)]
    return lax.ppermute(block, axis, route)


def swapped(block, axis, bit):
    count = lax.axis_size(axis)
    return lax.ppermute(block, axis, [(i ^ bit, i) for i in range(count)])


def crossed(block, axis):
    count = lax.axis_size(axis)
    return lax.ppermute(block, axis, [(i, (i + (-1 if i % 2 == 0 else 1)) % count) for i in range(count)])


def halves(width):
    half = lax.axis_index("head")
    mine = pl.ds(pl.multiple_of(half * width, width), width)
    theirs = pl.ds(pl.multiple_of((1 - half) * width, width), width)
    return mine, theirs


def product(left, right):
    return jnp.dot(left, right, preferred_element_type=jnp.float32)


def owner_at(offset):
    count = lax.axis_size("blk")
    here = lax.axis_index("blk")
    if isinstance(offset, tuple):
        offset = jnp.where(lax.rem(here, 2) == 0, offset[0], offset[1])
    return lax.rem(here + offset + count, count)


def special_kernel(frame_order, specials, role_first, role_rest, special_out, order, here, first_rows, rest_rows, copied):
    special_count, images, width = specials.shape
    moves = [(specials, here), (role_first, first_rows), (role_rest, rest_rows), (frame_order, order)]
    copies = [
        pltpu.make_async_copy(source, target, copied.at[i]) for i, (source, target) in enumerate(moves)
    ]
    for copy in copies:
        copy.start()
    for copy in copies:
        copy.wait()
    mine, _ = halves(width)
    first = first_rows[:, mine].astype(jnp.float32)
    rest = rest_rows[:, mine].astype(jnp.float32)
    summed = [
        here[:, b, :].astype(jnp.float32) + jnp.where(order[b] == 0, first, rest) for b in range(images)
    ]
    summed.append(jnp.zeros((special_out.shape[0] - images * special_count, width), jnp.float32))
    special_out[...] = jnp.concatenate(summed, axis=0).astype(jnp.bfloat16)


def start_kernel(
    offsets, special_count, special_total, covisible, patches, w_qkv, own_out, mask_out, weights_out, seen, copied
):
    images, per_image, width = patches.shape
    patch_total = images * per_image
    moves = [(covisible, seen)]
    moves += [(patches.at[b], own_out.at[pl.ds(b * per_image, per_image)]) for b in range(images)]
    moves += [(w_qkv.at[i], weights_out.at[i]) for i in range(3)]
    copies = [
        pltpu.make_async_copy(source, target, copied.at[i]) for i, (source, target) in enumerate(moves)
    ]
    for copy in copies:
        copy.start()
    copies[0].wait()
    lane = lax.broadcasted_iota(jnp.int32, (1, mask_out.shape[1]), 1)
    special_lane = lax.rem(lane - patch_total, special_total)
    image = jnp.where(
        lane < patch_total, lane // per_image, jnp.minimum(special_lane // special_count, images - 1)
    )
    for i, offset in enumerate(offsets):
        for b in range(images):
            row = jnp.zeros(lane.shape, jnp.float32)
            for a in range(images):
                hidden = seen[a, owner_at(offset) * images + b] <= 0
                row = jnp.where((image == a) & hidden, -jnp.inf, row)
            mask_out[i * images + b : i * images + b + 1, :] = row
    for copy in copies[1:]:
        copy.wait()


def projector(own, other, weights):
    mine, theirs = halves(own.shape[1])

    def columns(which, quad):
        lanes = slice(quad * QUAD, (quad + 1) * QUAD)
        return product(own, weights[which, mine, lanes]) + product(other, weights[which, theirs, lanes])

    return columns


def attend(scores, masks, state):
    largest = state
    start = 0
    for count, mask in masks:
        part = jnp.max(scores[start : start + count], axis=0, keepdims=True)
        part = part if mask is None else part + mask
        largest = part if largest is None else jnp.maximum(largest, part)
        start += count
    weights, start = [], 0
    for count, mask in masks:
        level = largest if mask is None else largest - mask
        weights.append(jnp.exp2((scores[start : start + count] - level).astype(jnp.bfloat16)))
        start += count
    factor = None if state is None else jnp.exp2(state - largest)
    return largest, factor, jnp.concatenate(weights, axis=0)


def attend_all(columns, masks, queries_of, special_queries, state, pairs, rows, special_real):
    keys, values = {}, {}
    quads = pairs // 2

    def keys_of(quad):
        if quad not in keys:
            keys[quad] = columns(1, quad).astype(jnp.bfloat16)
        return keys[quad]

    def values_of(quad):
        if quad not in values:
            values[quad] = jnp.transpose(columns(2, quad)).astype(jnp.bfloat16)
        return values[quad]

    def prepared(pair):
        if pair == pairs:
            scores = product(
                jnp.concatenate([keys_of(quad) for quad in range(quads)], axis=1), special_queries()
            )
        else:
            lanes = slice((pair % 2) * PAIR, (pair % 2 + 1) * PAIR)
            scores = product(keys_of(pair // 2)[:, lanes], queries_of(pair))
        if all(mask is not None for _, mask in masks):
            return scores
        parts, start = [], 0
        for count, mask in masks:
            part = scores[start : start + count]
            if mask is None:
                key_row = lax.broadcasted_iota(jnp.int32, (count, 1), 0)
                part = jnp.where(lax.rem(key_row, TILE_ROWS) < special_real, part, -jnp.inf)
            parts.append(part)
            start += count
        return jnp.concatenate(parts, axis=0)

    ones = jnp.ones((TILE_ROWS, sum(count for count, _ in masks)), jnp.bfloat16)
    both = [
        (count, None if mask is None else jnp.concatenate([mask[:, :rows]] * 2, axis=1))
        for count, mask in masks
    ]
    only = [(count, None if mask is None else mask[:, rows:]) for count, mask in masks]
    order = list(range(pairs))
    order.insert(pairs - 2, pairs)
    scores = prepared(order[0])
    for step, pair in enumerate(order):
        if pair < pairs:
            left = [
                values_of(pair // 2)[first : first + HEAD_DIM]
                for first in ((pair % 2) * PAIR, (pair % 2) * PAIR + HEAD_DIM)
            ]
        else:
            left = [jnp.concatenate([values_of(quad) for quad in range(quads)], axis=0)]
        following = prepared(order[step + 1]) if step < pairs else None
        largest, factor, weights = attend(
            scores, both if pair < pairs else only, state and state.largest(pair)
        )
        width = scores.shape[1] // len(left)
        for sub, part in enumerate(left):
            lanes = slice(sub * width, (sub + 1) * width)
            added = product(jnp.concatenate([part, ones], axis=0), weights[:, lanes])
            total, weight = added[: part.shape[0]], added[part.shape[0] : part.shape[0] + 1]
            if state is not None:
                total = total + state.total(pair, sub) * factor[:, lanes]
                weight = weight + state.weight(pair, sub) * factor[:, lanes]
            yield pair, sub, largest[:, lanes], total, weight
        scores = following


class State:
    def __init__(self, rows, refs):
        self.rows = rows
        self.largest_ref, self.weight_ref, self.total_ref, self.special_ref = refs

    def lanes(self, pair, sub):
        if pair == self.total_ref.shape[0]:
            return slice(0, self.special_ref.shape[1])
        return slice(sub * self.rows, (sub + 1) * self.rows)

    def largest(self, pair):
        stop = self.special_ref.shape[1] if pair == self.total_ref.shape[0] else 2 * self.rows
        return self.largest_ref[pair : pair + 1, 0:stop]

    def weight(self, pair, sub):
        return self.weight_ref[pair : pair + 1, self.lanes(pair, sub)]

    def total(self, pair, sub):
        if pair == self.total_ref.shape[0]:
            return self.special_ref[...]
        return self.total_ref[pair, :, self.lanes(pair, sub)]

    def put(self, pair, sub, largest, total, weight):
        lanes = self.lanes(pair, sub)
        self.largest_ref[pair : pair + 1, lanes] = largest
        self.weight_ref[pair : pair + 1, lanes] = weight
        if pair == self.total_ref.shape[0]:
            self.special_ref[...] = total
        else:
            self.total_ref[pair, :, lanes] = total


def first_kernel(
    images, mask, own, other, special, other_special, weights, queries_out, special_out, *state_out
):
    patch_total = own.shape[0]
    columns = projector(
        jnp.concatenate([own[...], special[...]], axis=0),
        jnp.concatenate([other[...], other_special[...]], axis=0),
        weights,
    )
    pairs = queries_out.shape[0]
    zero = jnp.zeros((HEAD_DIM, patch_total), jnp.bfloat16)
    made = {}

    def patch_columns(which, quad):
        return columns(which, quad)[:patch_total]

    def columns_of(quad):
        if quad not in made:
            queries = columns(0, quad) * (HEAD_DIM ** (-0.5) * LOG2_E)
            made[quad] = queries[patch_total:]
            turned = jnp.transpose(queries[:patch_total]).astype(jnp.bfloat16)
            for i in range(2):
                first = i * PAIR
                upper = jnp.concatenate([turned[first : first + HEAD_DIM], zero], axis=1)
                lower = jnp.concatenate([zero, turned[first + HEAD_DIM : first + PAIR]], axis=1)
                queries_out[2 * quad + i] = jnp.concatenate([upper, lower], axis=0)
        return made[quad]

    def queries_of(pair):
        columns_of(pair // 2)
        return queries_out[pair]

    def special_queries():
        block = jnp.concatenate([columns_of(quad) for quad in range(pairs // 2)], axis=1)
        count = block.shape[0]
        block = jnp.concatenate([block] * (2 * pairs), axis=0)
        row = lax.broadcasted_iota(jnp.int32, block.shape, 0) // count
        lane = lax.broadcasted_iota(jnp.int32, block.shape, 1) // HEAD_DIM
        block = jnp.transpose(jnp.where(row == lane, block, 0.0)).astype(jnp.bfloat16)
        special_out[...] = block
        return block

    per_image = patch_total // images
    masks = [(per_image, mask[b : b + 1, :]) for b in range(images)]
    state = State(patch_total, state_out)
    for result in attend_all(
        patch_columns, masks, queries_of, special_queries, None, pairs, patch_total, 0
    ):
        state.put(*result)


def joined(stretches, mask, refs):
    count = len(stretches)
    own = jnp.concatenate([ref[...] for ref in refs[:count]], axis=0)
    other = jnp.concatenate([ref[...] for ref in refs[count : 2 * count]], axis=0)
    masks = [
        (rows, None if i is None else mask[i : i + 1, :]) for part in stretches for rows, i in part
    ]
    return own, other, masks, refs[2 * count :]


def later_kernel(stretches, special_real, mask, *refs):
    own, other, masks, refs = joined(stretches, mask, refs)
    weights, queries, special_queries = refs[:3]
    state_in, state_out = refs[3:7], refs[7:]
    pairs, rows = queries.shape[0], queries.shape[2] // 2
    state = State(rows, state_out)
    for result in attend_all(
        projector(own, other, weights), masks, lambda pair: queries[pair], lambda: special_queries[...],
        State(rows, state_in), pairs, rows, special_real,
    ):
        state.put(*result)


def last_kernel(stretches, special_real, mask, *refs):
    own, other, masks, refs = joined(stretches, mask, refs)
    weights, queries, special_queries = refs[:3]
    state_in = refs[3:7]
    w_out, kept_out, sent_out, w_here, copied = refs[7:]
    copy = pltpu.make_async_copy(w_out, w_here, copied)
    copy.start()
    pairs, rows = queries.shape[0], queries.shape[2] // 2
    columns, out, special = [], None, None
    for pair, sub, _, total, weight in attend_all(
        projector(own, other, weights), masks, lambda pair: queries[pair], lambda: special_queries[...],
        State(rows, state_in), pairs, rows, special_real,
    ):
        if pair == 0 and sub == 0:
            copy.wait()
        if pair == pairs:
            special = total / weight
            row = lax.broadcasted_iota(jnp.int32, special.shape, 0) // HEAD_DIM
            lane = lax.broadcasted_iota(jnp.int32, special.shape, 1) // TILE_ROWS
            special = jnp.transpose(jnp.where(row == lane, special, 0.0))
            special = sum(special[i * TILE_ROWS : (i + 1) * TILE_ROWS] for i in range(2 * pairs))
            special = product(special.astype(jnp.bfloat16), w_here[...])
            continue
        columns.append(total / weight)
        if pair % 2 == 1 and sub == 1:
            quad = jnp.transpose(jnp.concatenate(columns, axis=0)).astype(jnp.bfloat16)
            added = product(quad, w_here[(pair // 2) * QUAD : (pair // 2 + 1) * QUAD, :])
            out = added if out is None else out + added
            columns = []
    half = lax.axis_index("head")
    width = kept_out.shape[1]

    def put(place, values):
        left, right = values[:, :width], values[:, width:]
        kept_out[place, :] = jnp.where(half == 0, left, right)
        sent_out[place, :] = jnp.where(half == 0, right, left).astype(jnp.bfloat16)

    put(slice(0, rows), out)
    put(slice(rows, kept_out.shape[0]), special)


def end_kernel(images, kept, received, patch_out, special_out):
    patch_total = patch_out.shape[0]
    special_count = special_out.shape[0]
    patch_out[...] = (kept[:patch_total, :] + received[:patch_total, :].astype(jnp.float32)).astype(
        jnp.bfloat16
    )
    rest = kept[patch_total:, :] + received[patch_total:, :].astype(jnp.float32)
    rows = [rest[b * special_count : (b + 1) * special_count][:, None, :] for b in range(images)]
    special_out[...] = jnp.concatenate(rows, axis=1).astype(jnp.bfloat16)


def call(kernel, out_shape, operands, in_specs=None, out_specs=None, scratch=(), flops=0):
    if in_specs:
        operands = [
            pltpu.with_memory_space_constraint(operand, pltpu.HBM) if spec is HBM else operand
            for operand, spec in zip(operands, in_specs)
        ]
    return pl.pallas_call(
        kernel,
        out_shape=out_shape,
        in_specs=in_specs or [VMEM] * len(operands),
        out_specs=out_specs or [VMEM] * len(out_shape),
        scratch_shapes=scratch,
        compiler_params=pltpu.CompilerParams(vmem_limit_bytes=VMEM_BYTES),
        cost_estimate=pl.CostEstimate(flops=flops, transcendentals=0, bytes_accessed=0),
    )(*operands)


def stack_kernel(first, second, out):
    count = first.shape[0]
    out[:count, :] = first[...]
    out[count:, :] = second[...]


def gathered(block, axis, bits, flops=0):
    for bit in bits:
        shape = jax.ShapeDtypeStruct((2 * block.shape[0], block.shape[1]), block.dtype)
        (block,) = call(stack_kernel, [shape], (block, swapped(block, axis, bit)), flops=flops)
    return block


def after(array, *others):
    return lax.optimization_barrier((array, *others))[0]


def per_device(
    patch_rows, special_rows, role_first, role_rest, frame_order, covisible, w_qkv, w_out
):
    images, per_image, width = patch_rows.shape
    special_count = special_rows.shape[1]
    real_rows = images * special_count
    special_block = real_rows + -real_rows % TILE_ROWS
    owner_count = lax.axis_size("blk")
    reach = max(1, owner_count // 64)
    patch_total = images * per_image
    rows = patch_total + special_block
    heads = width // HEAD_DIM
    pairs = heads // 2
    paired = reach == 1 and owner_count % 2 == 0

    if paired:
        offsets = [0, (1, -1), (-1, 1)]
    else:
        offsets = [0] + [sign * d for d in range(1, reach + 1) for sign in (-1, 1)]
    mask_rows = -(-len(offsets) * images // 8) * 8
    bf16 = lambda *shape: jax.ShapeDtypeStruct(shape, jnp.bfloat16)
    f32 = lambda *shape: jax.ShapeDtypeStruct(shape, jnp.float32)
    state_shape = [
        f32(8, 2 * patch_total),
        f32(8, 2 * patch_total),
        f32(pairs, HEAD_DIM, 2 * patch_total),
        f32(width, heads * special_block),
    ]

    both = lambda part: (part, swapped(part, "head", 1))
    patches = patch_rows.reshape(patch_total, width)
    turned = jnp.transpose(special_rows, (1, 0, 2))
    power = owner_count & (owner_count - 1) == 0
    (specials,) = call(
        special_kernel,
        [bf16(special_block, width)],
        (frame_order, turned, role_first, role_rest),
        in_specs=[HBM] * 4,
        scratch=[
            pltpu.SMEM(frame_order.shape, jnp.int32),
            pltpu.VMEM(turned.shape, jnp.bfloat16),
            pltpu.VMEM(role_first.shape, jnp.bfloat16),
            pltpu.VMEM(role_rest.shape, jnp.bfloat16),
            pltpu.SemaphoreType.DMA((4,)),
        ],
    )
    bits = [1 << i for i in range(owner_count.bit_length() - 1)] if power else []
    everywhere = gathered(gathered(specials, "blk", bits[:1], FIRST), "blk", bits[1:2])
    own, mask, weights = call(
        functools.partial(start_kernel, offsets, special_count, special_block),
        [
            bf16(patch_total, width),
            f32(mask_rows, patch_total + heads * special_block),
            bf16(*w_qkv.shape),
        ],
        (covisible, patch_rows, w_qkv),
        in_specs=[HBM] * 3,
        scratch=[pltpu.SMEM(covisible.shape, jnp.int32), pltpu.SemaphoreType.DMA((1 + images + 3,))],
    )
    if paired:
        near = [swapped(patches, "blk", 1), crossed(after(patches, everywhere, mask), "blk")]
    else:
        near = [shifted(patches, "blk", -offset) for offset in offsets[1:]]
    queries, special_queries, *state = call(
        functools.partial(first_kernel, images),
        [bf16(pairs, PAIR, 2 * patch_total), bf16(width, heads * special_block), *state_shape],
        (mask, own, swapped(patches, "head", 1), *both(specials), weights),
    )
    fixed = (weights, queries, special_queries)

    def later(stretches, parts, state):
        return call(
            functools.partial(later_kernel, stretches, real_rows),
            state_shape,
            (mask, *[part[0] for part in parts], *[part[1] for part in parts], *fixed, *state),
        )

    image_rows = lambda owner: [(per_image, owner * images + b) for b in range(images)]
    for i, part in enumerate(near):
        part = after(part, state[0])
        if i == 0:
            if power:
                everywhere = gathered(after(everywhere, part), "blk", bits[2:])
            else:
                everywhere = lax.all_gather(specials, "blk", axis=0, tiled=True)
        stretches = [[image] for image in image_rows(i + 1)]
        parts = [both(part[b * per_image : (b + 1) * per_image]) for b in range(images)]
        if i < len(near) - 1:
            state = later(stretches, parts, state)
    stretches.append([(everywhere.shape[0], None)])
    parts.append(both(after(everywhere, state[0])))
    kept, sent = call(
        functools.partial(last_kernel, stretches, real_rows),
        [f32(rows, width), bf16(rows, width)],
        (
            mask, *[part[0] for part in parts], *[part[1] for part in parts], *fixed, *state, w_out,
        ),
        in_specs=[VMEM] * (1 + 2 * len(parts) + len(fixed) + len(state)) + [HBM],
        scratch=[pltpu.VMEM(w_out.shape, jnp.bfloat16), pltpu.SemaphoreType.DMA],
    )
    received = swapped(sent, "head", 1)
    patch_out, special_out = call(
        functools.partial(end_kernel, images),
        [bf16(patch_total, width), bf16(special_count, images, width)],
        (kept, received),
        out_specs=[pl.BlockSpec(), pl.BlockSpec()],
    )
    return patch_out.reshape(patch_rows.shape), jnp.transpose(special_out, (1, 0, 2))


def solution(mesh):
    in_specs = (
        P(("scene", "blk"), None, "head"),
        P(("scene", "blk"), None, "head"),
        P(),
        P(),
        P(("scene", "blk")),
        P(("scene", "blk"), None),
        P(None, None, "head"),
        P("head", None),
    )
    out_specs = (P(("scene", "blk"), None, "head"), P(("scene", "blk"), None, "head"))
    return jax.shard_map(
        per_device, mesh=mesh, in_specs=in_specs, out_specs=out_specs, check_vma=False
    )
```

```python
import functools

import jax
import jax.numpy as jnp
from jax import lax
from jax.experimental import pallas as pl
from jax.experimental.pallas import tpu as pltpu
from jax.sharding import PartitionSpec as P

HEAD_DIM = 64
PAIR = 2 * HEAD_DIM
QUAD = 2 * PAIR
TILE_ROWS = 16
LOG2_E = 1.4426950408889634
FIRST = 20_000_000_000
VMEM_BYTES = 32 * 1024 * 1024
SMEM = pl.BlockSpec(memory_space=pltpu.SMEM)
VMEM = pl.BlockSpec(memory_space=pltpu.VMEM)
HBM = pl.BlockSpec(memory_space=pltpu.HBM)


def shifted(block, axis, distance):
    count = lax.axis_size(axis)
    route = [((i - distance) % count, i) for i in range(count)]
    return lax.ppermute(block, axis, route)


def swapped(block, axis, bit):
    count = lax.axis_size(axis)
    return lax.ppermute(block, axis, [(i ^ bit, i) for i in range(count)])


def crossed(block, axis):
    count = lax.axis_size(axis)
    return lax.ppermute(block, axis, [(i, (i + (-1 if i % 2 == 0 else 1)) % count) for i in range(count)])


def halves(width):
    half = lax.axis_index("head")
    mine = pl.ds(pl.multiple_of(half * width, width), width)
    theirs = pl.ds(pl.multiple_of((1 - half) * width, width), width)
    return mine, theirs


def product(left, right):
    return jnp.dot(left, right, preferred_element_type=jnp.float32)


def owner_at(offset):
    count = lax.axis_size("blk")
    here = lax.axis_index("blk")
    if isinstance(offset, tuple):
        offset = jnp.where(lax.rem(here, 2) == 0, offset[0], offset[1])
    return lax.rem(here + offset + count, count)


def rows_kernel(
    frame_order, specials, role_first, role_rest, patches,
    special_out, patches_out, order, here, first_rows, rest_rows, copied,
):
    special_count, images, width = specials.shape
    moves = [(specials, here), (role_first, first_rows), (role_rest, rest_rows), (frame_order, order)]
    moves.append((patches, patches_out))
    copies = [
        pltpu.make_async_copy(source, target, copied.at[i]) for i, (source, target) in enumerate(moves)
    ]
    for copy in copies:
        copy.start()
    for copy in copies[:-1]:
        copy.wait()
    mine, _ = halves(width)
    first = first_rows[:, mine].astype(jnp.float32)
    rest = rest_rows[:, mine].astype(jnp.float32)
    summed = [
        here[:, b, :].astype(jnp.float32) + jnp.where(order[b] == 0, first, rest) for b in range(images)
    ]
    summed.append(jnp.zeros((special_out.shape[0] - images * special_count, width), jnp.float32))
    special_out[...] = jnp.concatenate(summed, axis=0).astype(jnp.bfloat16)
    copies[-1].wait()


def start_kernel(
    offsets, per_image, special_count, special_total, covisible, w_qkv, mask_out, weights_out, seen, copied
):
    images = covisible.shape[0]
    patch_total = images * per_image
    moves = [(covisible, seen)]
    moves += [(w_qkv.at[i], weights_out.at[i]) for i in range(3)]
    copies = [
        pltpu.make_async_copy(source, target, copied.at[i]) for i, (source, target) in enumerate(moves)
    ]
    for copy in copies:
        copy.start()
    copies[0].wait()
    lane = lax.broadcasted_iota(jnp.int32, (1, mask_out.shape[1]), 1)
    special_lane = lax.rem(lane - patch_total, special_total)
    image = jnp.where(
        lane < patch_total, lane // per_image, jnp.minimum(special_lane // special_count, images - 1)
    )
    for i, offset in enumerate(offsets):
        for b in range(images):
            row = jnp.zeros(lane.shape, jnp.float32)
            for a in range(images):
                hidden = seen[a, owner_at(offset) * images + b] <= 0
                row = jnp.where((image == a) & hidden, -jnp.inf, row)
            mask_out[i * images + b : i * images + b + 1, :] = row
    for copy in copies[1:]:
        copy.wait()


def projector(own, other, weights):
    mine, theirs = halves(own.shape[1])

    def columns(which, quad):
        lanes = slice(quad * QUAD, (quad + 1) * QUAD)
        return product(own, weights[which, mine, lanes]) + product(other, weights[which, theirs, lanes])

    return columns


def attend(scores, masks, state):
    largest = state
    start = 0
    for count, mask in masks:
        part = jnp.max(scores[start : start + count], axis=0, keepdims=True)
        part = part if mask is None else part + mask
        largest = part if largest is None else jnp.maximum(largest, part)
        start += count
    weights, start = [], 0
    for count, mask in masks:
        level = largest if mask is None else largest - mask
        weights.append(jnp.exp2((scores[start : start + count] - level).astype(jnp.bfloat16)))
        start += count
    factor = None if state is None else jnp.exp2(state - largest)
    return largest, factor, jnp.concatenate(weights, axis=0)


def attend_all(columns, masks, queries_of, special_queries, state, pairs, rows, special_real):
    keys, values = {}, {}
    quads = pairs // 2

    def keys_of(quad):
        if quad not in keys:
            keys[quad] = columns(1, quad).astype(jnp.bfloat16)
        return keys[quad]

    def values_of(quad):
        if quad not in values:
            values[quad] = jnp.transpose(columns(2, quad)).astype(jnp.bfloat16)
        return values[quad]

    def prepared(pair):
        if pair == pairs:
            scores = product(
                jnp.concatenate([keys_of(quad) for quad in range(quads)], axis=1), special_queries()
            )
        else:
            lanes = slice((pair % 2) * PAIR, (pair % 2 + 1) * PAIR)
            scores = product(keys_of(pair // 2)[:, lanes], queries_of(pair))
        if all(mask is not None for _, mask in masks):
            return scores
        parts, start = [], 0
        for count, mask in masks:
            part = scores[start : start + count]
            if mask is None:
                key_row = lax.broadcasted_iota(jnp.int32, (count, 1), 0)
                part = jnp.where(lax.rem(key_row, TILE_ROWS) < special_real, part, -jnp.inf)
            parts.append(part)
            start += count
        return jnp.concatenate(parts, axis=0)

    ones = jnp.ones((TILE_ROWS, sum(count for count, _ in masks)), jnp.bfloat16)
    both = [
        (count, None if mask is None else jnp.concatenate([mask[:, :rows]] * 2, axis=1))
        for count, mask in masks
    ]
    only = [(count, None if mask is None else mask[:, rows:]) for count, mask in masks]
    order = list(range(pairs))
    order.insert(pairs - 2, pairs)
    scores = prepared(order[0])
    for step, pair in enumerate(order):
        if pair < pairs:
            left = [
                values_of(pair // 2)[first : first + HEAD_DIM]
                for first in ((pair % 2) * PAIR, (pair % 2) * PAIR + HEAD_DIM)
            ]
        else:
            left = [jnp.concatenate([values_of(quad) for quad in range(quads)], axis=0)]
        following = prepared(order[step + 1]) if step < pairs else None
        largest, factor, weights = attend(
            scores, both if pair < pairs else only, state and state.largest(pair)
        )
        width = scores.shape[1] // len(left)
        for sub, part in enumerate(left):
            lanes = slice(sub * width, (sub + 1) * width)
            added = product(jnp.concatenate([part, ones], axis=0), weights[:, lanes])
            total, weight = added[: part.shape[0]], added[part.shape[0] : part.shape[0] + 1]
            if state is not None:
                total = total + state.total(pair, sub) * factor[:, lanes]
                weight = weight + state.weight(pair, sub) * factor[:, lanes]
            yield pair, sub, largest[:, lanes], total, weight
        scores = following


class State:
    def __init__(self, rows, refs):
        self.rows = rows
        self.largest_ref, self.weight_ref, self.total_ref, self.special_ref = refs

    def lanes(self, pair, sub):
        if pair == self.total_ref.shape[0]:
            return slice(0, self.special_ref.shape[1])
        return slice(sub * self.rows, (sub + 1) * self.rows)

    def largest(self, pair):
        stop = self.special_ref.shape[1] if pair == self.total_ref.shape[0] else 2 * self.rows
        return self.largest_ref[pair : pair + 1, 0:stop]

    def weight(self, pair, sub):
        return self.weight_ref[pair : pair + 1, self.lanes(pair, sub)]

    def total(self, pair, sub):
        if pair == self.total_ref.shape[0]:
            return self.special_ref[...]
        return self.total_ref[pair, :, self.lanes(pair, sub)]

    def put(self, pair, sub, largest, total, weight):
        lanes = self.lanes(pair, sub)
        self.largest_ref[pair : pair + 1, lanes] = largest
        self.weight_ref[pair : pair + 1, lanes] = weight
        if pair == self.total_ref.shape[0]:
            self.special_ref[...] = total
        else:
            self.total_ref[pair, :, lanes] = total


def first_kernel(
    images, mask, own, other, special, other_special, weights, queries_out, special_out, *state_out
):
    patch_total = own.shape[0]
    columns = projector(
        jnp.concatenate([own[...], special[...]], axis=0),
        jnp.concatenate([other[...], other_special[...]], axis=0),
        weights,
    )
    pairs = queries_out.shape[0]
    zero = jnp.zeros((HEAD_DIM, patch_total), jnp.bfloat16)
    made = {}

    def patch_columns(which, quad):
        return columns(which, quad)[:patch_total]

    def columns_of(quad):
        if quad not in made:
            queries = columns(0, quad) * (HEAD_DIM ** (-0.5) * LOG2_E)
            made[quad] = queries[patch_total:]
            turned = jnp.transpose(queries[:patch_total]).astype(jnp.bfloat16)
            for i in range(2):
                first = i * PAIR
                upper = jnp.concatenate([turned[first : first + HEAD_DIM], zero], axis=1)
                lower = jnp.concatenate([zero, turned[first + HEAD_DIM : first + PAIR]], axis=1)
                queries_out[2 * quad + i] = jnp.concatenate([upper, lower], axis=0)
        return made[quad]

    def queries_of(pair):
        columns_of(pair // 2)
        return queries_out[pair]

    def special_queries():
        block = jnp.concatenate([columns_of(quad) for quad in range(pairs // 2)], axis=1)
        count = block.shape[0]
        block = jnp.concatenate([block] * (2 * pairs), axis=0)
        row = lax.broadcasted_iota(jnp.int32, block.shape, 0) // count
        lane = lax.broadcasted_iota(jnp.int32, block.shape, 1) // HEAD_DIM
        block = jnp.transpose(jnp.where(row == lane, block, 0.0)).astype(jnp.bfloat16)
        special_out[...] = block
        return block

    per_image = patch_total // images
    masks = [(per_image, mask[b : b + 1, :]) for b in range(images)]
    state = State(patch_total, state_out)
    for result in attend_all(
        patch_columns, masks, queries_of, special_queries, None, pairs, patch_total, 0
    ):
        state.put(*result)


def joined(stretches, mask, refs):
    count = len(stretches)
    own = jnp.concatenate([ref[...] for ref in refs[:count]], axis=0)
    other = jnp.concatenate([ref[...] for ref in refs[count : 2 * count]], axis=0)
    masks = [
        (rows, None if i is None else mask[i : i + 1, :]) for part in stretches for rows, i in part
    ]
    return own, other, masks, refs[2 * count :]


def later_kernel(stretches, special_real, mask, *refs):
    own, other, masks, refs = joined(stretches, mask, refs)
    weights, queries, special_queries = refs[:3]
    state_in, state_out = refs[3:7], refs[7:]
    pairs, rows = queries.shape[0], queries.shape[2] // 2
    state = State(rows, state_out)
    for result in attend_all(
        projector(own, other, weights), masks, lambda pair: queries[pair], lambda: special_queries[...],
        State(rows, state_in), pairs, rows, special_real,
    ):
        state.put(*result)


def last_kernel(stretches, special_real, mask, *refs):
    own, other, masks, refs = joined(stretches, mask, refs)
    weights, queries, special_queries = refs[:3]
    state_in = refs[3:7]
    w_out, kept_out, sent_out, w_here, copied = refs[7:]
    copy = pltpu.make_async_copy(w_out, w_here, copied)
    copy.start()
    pairs, rows = queries.shape[0], queries.shape[2] // 2
    columns, out, special = [], None, None
    sides = halves(kept_out.shape[1])
    for pair, sub, _, total, weight in attend_all(
        projector(own, other, weights), masks, lambda pair: queries[pair], lambda: special_queries[...],
        State(rows, state_in), pairs, rows, special_real,
    ):
        if pair == 0 and sub == 0:
            copy.wait()
        share = total * (1.0 / weight)
        if pair == pairs:
            row = lax.broadcasted_iota(jnp.int32, share.shape, 0) // HEAD_DIM
            lane = lax.broadcasted_iota(jnp.int32, share.shape, 1) // TILE_ROWS
            share = jnp.transpose(jnp.where(row == lane, share, 0.0))
            share = sum(share[i * TILE_ROWS : (i + 1) * TILE_ROWS] for i in range(2 * pairs))
            special = [product(share.astype(jnp.bfloat16), w_here[:, side]) for side in sides]
            continue
        columns.append(share)
        if pair % 2 == 1 and sub == 1:
            quad = jnp.transpose(jnp.concatenate(columns, axis=0)).astype(jnp.bfloat16)
            features = slice((pair // 2) * QUAD, (pair // 2 + 1) * QUAD)
            added = [product(quad, w_here[features, side]) for side in sides]
            out = added if out is None else [before + more for before, more in zip(out, added)]
            columns = []
    for place, values in ((slice(0, rows), out), (slice(rows, kept_out.shape[0]), special)):
        sent_out[place, :] = values[1].astype(jnp.bfloat16)
        kept_out[place, :] = values[0]


def end_kernel(images, kept, received, patch_out, special_out):
    patch_total = patch_out.shape[0]
    special_count = special_out.shape[0]
    patch_out[...] = (kept[:patch_total, :] + received[:patch_total, :].astype(jnp.float32)).astype(
        jnp.bfloat16
    )
    rest = kept[patch_total:, :] + received[patch_total:, :].astype(jnp.float32)
    rows = [rest[b * special_count : (b + 1) * special_count][:, None, :] for b in range(images)]
    special_out[...] = jnp.concatenate(rows, axis=1).astype(jnp.bfloat16)


def call(kernel, out_shape, operands, in_specs=None, out_specs=None, scratch=(), flops=0):
    if in_specs:
        operands = [
            pltpu.with_memory_space_constraint(operand, pltpu.HBM) if spec is HBM else operand
            for operand, spec in zip(operands, in_specs)
        ]
    return pl.pallas_call(
        kernel,
        out_shape=out_shape,
        in_specs=in_specs or [VMEM] * len(operands),
        out_specs=out_specs or [VMEM] * len(out_shape),
        scratch_shapes=scratch,
        compiler_params=pltpu.CompilerParams(vmem_limit_bytes=VMEM_BYTES),
        cost_estimate=pl.CostEstimate(flops=flops, transcendentals=0, bytes_accessed=0),
    )(*operands)


def stack_kernel(first, second, out):
    count = first.shape[0]
    out[:count, :] = first[...]
    out[count:, :] = second[...]


def gathered(block, axis, bits, flops=0):
    for bit in bits:
        shape = jax.ShapeDtypeStruct((2 * block.shape[0], block.shape[1]), block.dtype)
        (block,) = call(stack_kernel, [shape], (block, swapped(block, axis, bit)), flops=flops)
    return block


def after(array, *others):
    return lax.optimization_barrier((array, *others))[0]


def per_device(
    patch_rows, special_rows, role_first, role_rest, frame_order, covisible, w_qkv, w_out
):
    images, per_image, width = patch_rows.shape
    special_count = special_rows.shape[1]
    real_rows = images * special_count
    special_block = real_rows + -real_rows % TILE_ROWS
    owner_count = lax.axis_size("blk")
    reach = max(1, owner_count // 64)
    patch_total = images * per_image
    rows = patch_total + special_block
    heads = width // HEAD_DIM
    pairs = heads // 2
    paired = reach == 1 and owner_count % 2 == 0

    if paired:
        offsets = [0, (1, -1), (-1, 1)]
    else:
        offsets = [0] + [sign * d for d in range(1, reach + 1) for sign in (-1, 1)]
    mask_rows = -(-len(offsets) * images // 8) * 8
    bf16 = lambda *shape: jax.ShapeDtypeStruct(shape, jnp.bfloat16)
    f32 = lambda *shape: jax.ShapeDtypeStruct(shape, jnp.float32)
    state_shape = [
        f32(8, 2 * patch_total),
        f32(8, 2 * patch_total),
        f32(pairs, HEAD_DIM, 2 * patch_total),
        f32(width, heads * special_block),
    ]

    both = lambda part: (part, swapped(part, "head", 1))
    patches = patch_rows.reshape(patch_total, width)
    turned = jnp.transpose(special_rows, (1, 0, 2))
    power = owner_count & (owner_count - 1) == 0
    specials, own = call(
        rows_kernel,
        [bf16(special_block, width), bf16(patch_total, width)],
        (frame_order, turned, role_first, role_rest, patches),
        in_specs=[HBM] * 5,
        scratch=[
            pltpu.SMEM(frame_order.shape, jnp.int32),
            pltpu.VMEM(turned.shape, jnp.bfloat16),
            pltpu.VMEM(role_first.shape, jnp.bfloat16),
            pltpu.VMEM(role_rest.shape, jnp.bfloat16),
            pltpu.SemaphoreType.DMA((5,)),
        ],
    )
    bits = [1 << i for i in range(owner_count.bit_length() - 1)] if power else []
    everywhere = gathered(gathered(specials, "blk", bits[:1], FIRST), "blk", bits[1:2])
    mask, weights = call(
        functools.partial(start_kernel, offsets, per_image, special_count, special_block),
        [
            f32(mask_rows, patch_total + heads * special_block),
            bf16(*w_qkv.shape),
        ],
        (covisible, w_qkv),
        in_specs=[HBM] * 2,
        scratch=[pltpu.SMEM(covisible.shape, jnp.int32), pltpu.SemaphoreType.DMA((1 + 3,))],
    )
    if paired:
        near = [swapped(own, "blk", 1), crossed(after(own, everywhere, mask), "blk")]
    else:
        near = [shifted(own, "blk", -offset) for offset in offsets[1:]]
    queries, special_queries, *state = call(
        functools.partial(first_kernel, images),
        [bf16(pairs, PAIR, 2 * patch_total), bf16(width, heads * special_block), *state_shape],
        (mask, *both(own), *both(specials), weights),
    )
    fixed = (weights, queries, special_queries)

    def later(stretches, parts, state):
        return call(
            functools.partial(later_kernel, stretches, real_rows),
            state_shape,
            (mask, *[part[0] for part in parts], *[part[1] for part in parts], *fixed, *state),
        )

    image_rows = lambda owner: [(per_image, owner * images + b) for b in range(images)]
    for i, part in enumerate(near):
        part = after(part, state[0])
        if i == 0:
            if power:
                everywhere = gathered(after(everywhere, part), "blk", bits[2:])
            else:
                everywhere = lax.all_gather(specials, "blk", axis=0, tiled=True)
        stretches = [[image] for image in image_rows(i + 1)]
        parts = [both(part[b * per_image : (b + 1) * per_image]) for b in range(images)]
        if i < len(near) - 1:
            state = later(stretches, parts, state)
    stretches.append([(everywhere.shape[0], None)])
    parts.append(both(after(everywhere, state[0])))
    kept, sent = call(
        functools.partial(last_kernel, stretches, real_rows),
        [f32(rows, width), bf16(rows, width)],
        (
            mask, *[part[0] for part in parts], *[part[1] for part in parts], *fixed, *state, w_out,
        ),
        in_specs=[VMEM] * (1 + 2 * len(parts) + len(fixed) + len(state)) + [HBM],
        scratch=[pltpu.VMEM(w_out.shape, jnp.bfloat16), pltpu.SemaphoreType.DMA],
    )
    received = swapped(sent, "head", 1)
    patch_out, special_out = call(
        functools.partial(end_kernel, images),
        [bf16(patch_total, width), bf16(special_count, images, width)],
        (kept, received),
        out_specs=[pl.BlockSpec(), pl.BlockSpec()],
    )
    return patch_out.reshape(patch_rows.shape), jnp.transpose(special_out, (1, 0, 2))


def solution(mesh):
    in_specs = (
        P(("scene", "blk"), None, "head"),
        P(("scene", "blk"), None, "head"),
        P(),
        P(),
        P(("scene", "blk")),
        P(("scene", "blk"), None),
        P(None, None, "head"),
        P("head", None),
    )
    out_specs = (P(("scene", "blk"), None, "head"), P(("scene", "blk"), None, "head"))
    return jax.shard_map(
        per_device, mesh=mesh, in_specs=in_specs, out_specs=out_specs, check_vma=False
    )
```

```python
import functools

import jax
import jax.numpy as jnp
from jax import lax
from jax.experimental import pallas as pl
from jax.experimental.pallas import tpu as pltpu
from jax.sharding import PartitionSpec as P

HEAD_DIM = 64
PAIR = 2 * HEAD_DIM
QUAD = 2 * PAIR
TILE_ROWS = 16
LOG2_E = 1.4426950408889634
FIRST = 20_000_000_000
VMEM_BYTES = 32 * 1024 * 1024
SMEM = pl.BlockSpec(memory_space=pltpu.SMEM)
VMEM = pl.BlockSpec(memory_space=pltpu.VMEM)
HBM = pl.BlockSpec(memory_space=pltpu.HBM)


def shifted(block, axis, distance):
    count = lax.axis_size(axis)
    route = [((i - distance) % count, i) for i in range(count)]
    return lax.ppermute(block, axis, route)


def swapped(block, axis, bit):
    count = lax.axis_size(axis)
    return lax.ppermute(block, axis, [(i ^ bit, i) for i in range(count)])


def crossed(block, axis):
    count = lax.axis_size(axis)
    return lax.ppermute(block, axis, [(i, (i + (-1 if i % 2 == 0 else 1)) % count) for i in range(count)])


def halves(width):
    half = lax.axis_index("head")
    mine = pl.ds(pl.multiple_of(half * width, width), width)
    theirs = pl.ds(pl.multiple_of((1 - half) * width, width), width)
    return mine, theirs


def product(left, right):
    return jnp.dot(left, right, preferred_element_type=jnp.float32)


def owner_at(offset):
    count = lax.axis_size("blk")
    here = lax.axis_index("blk")
    if isinstance(offset, tuple):
        offset = jnp.where(lax.rem(here, 2) == 0, offset[0], offset[1])
    return lax.rem(here + offset + count, count)


def rows_kernel(
    frame_order, specials, role_first, role_rest, patches,
    special_out, patches_out, order, here, first_rows, rest_rows, copied,
):
    special_count, images, width = specials.shape
    moves = [(specials, here), (role_first, first_rows), (role_rest, rest_rows), (frame_order, order)]
    moves.append((patches, patches_out))
    copies = [
        pltpu.make_async_copy(source, target, copied.at[i]) for i, (source, target) in enumerate(moves)
    ]
    for copy in copies:
        copy.start()
    for copy in copies[:-1]:
        copy.wait()
    mine, _ = halves(width)
    first = first_rows[:, mine].astype(jnp.float32)
    rest = rest_rows[:, mine].astype(jnp.float32)
    summed = [
        here[:, b, :].astype(jnp.float32) + jnp.where(order[b] == 0, first, rest) for b in range(images)
    ]
    summed.append(jnp.zeros((special_out.shape[0] - images * special_count, width), jnp.float32))
    special_out[...] = jnp.concatenate(summed, axis=0).astype(jnp.bfloat16)
    copies[-1].wait()


def start_kernel(
    offsets, per_image, special_count, special_total, covisible, w_qkv, mask_out, weights_out, seen, copied
):
    images = covisible.shape[0]
    patch_total = images * per_image
    moves = [(covisible, seen)]
    moves += [(w_qkv.at[i], weights_out.at[i]) for i in range(3)]
    copies = [
        pltpu.make_async_copy(source, target, copied.at[i]) for i, (source, target) in enumerate(moves)
    ]
    for copy in copies:
        copy.start()
    copies[0].wait()
    lane = lax.broadcasted_iota(jnp.int32, (1, mask_out.shape[1]), 1)
    special_lane = lax.rem(lane - patch_total, special_total)
    image = jnp.where(
        lane < patch_total, lane // per_image, jnp.minimum(special_lane // special_count, images - 1)
    )
    for i, offset in enumerate(offsets):
        for b in range(images):
            row = jnp.zeros(lane.shape, jnp.float32)
            for a in range(images):
                hidden = seen[a, owner_at(offset) * images + b] <= 0
                row = jnp.where((image == a) & hidden, -jnp.inf, row)
            mask_out[i * images + b : i * images + b + 1, :] = row
    for copy in copies[1:]:
        copy.wait()


def projector(own, other, weights):
    mine, theirs = halves(own.shape[1])

    def columns(which, quad):
        lanes = slice(quad * QUAD, (quad + 1) * QUAD)
        return product(own, weights[which, mine, lanes]) + product(other, weights[which, theirs, lanes])

    return columns


def attend(scores, masks, state):
    largest = state
    start = 0
    for count, mask in masks:
        part = jnp.max(scores[start : start + count], axis=0, keepdims=True)
        part = part if mask is None else part + mask
        largest = part if largest is None else jnp.maximum(largest, part)
        start += count
    weights, start = [], 0
    for count, mask in masks:
        level = largest if mask is None else largest - mask
        weights.append(jnp.exp2((scores[start : start + count] - level).astype(jnp.bfloat16)))
        start += count
    factor = None if state is None else jnp.exp2(state - largest)
    return largest, factor, jnp.concatenate(weights, axis=0)


def attend_all(columns, masks, queries_of, special_queries, state, pairs, rows, special_real):
    keys, values = {}, {}
    quads = pairs // 2

    def keys_of(quad):
        if quad not in keys:
            keys[quad] = columns(1, quad).astype(jnp.bfloat16)
        return keys[quad]

    def values_of(quad):
        if quad not in values:
            values[quad] = jnp.transpose(columns(2, quad)).astype(jnp.bfloat16)
        return values[quad]

    def prepared(pair):
        if pair == pairs:
            scores = product(
                jnp.concatenate([keys_of(quad) for quad in range(quads)], axis=1), special_queries()
            )
        else:
            lanes = slice((pair % 2) * PAIR, (pair % 2 + 1) * PAIR)
            scores = product(keys_of(pair // 2)[:, lanes], queries_of(pair))
        if all(mask is not None for _, mask in masks):
            return scores
        parts, start = [], 0
        for count, mask in masks:
            part = scores[start : start + count]
            if mask is None:
                key_row = lax.broadcasted_iota(jnp.int32, (count, 1), 0)
                part = jnp.where(lax.rem(key_row, TILE_ROWS) < special_real, part, -jnp.inf)
            parts.append(part)
            start += count
        return jnp.concatenate(parts, axis=0)

    ones = jnp.ones((TILE_ROWS, sum(count for count, _ in masks)), jnp.bfloat16)
    both = [
        (count, None if mask is None else jnp.concatenate([mask[:, :rows]] * 2, axis=1))
        for count, mask in masks
    ]
    only = [(count, None if mask is None else mask[:, rows:]) for count, mask in masks]
    order = list(range(pairs))
    order.insert(pairs - 2, pairs)
    scores = prepared(order[0])
    for step, pair in enumerate(order):
        if pair < pairs:
            left = [
                values_of(pair // 2)[first : first + HEAD_DIM]
                for first in ((pair % 2) * PAIR, (pair % 2) * PAIR + HEAD_DIM)
            ]
        else:
            left = [jnp.concatenate([values_of(quad) for quad in range(quads)], axis=0)]
        following = prepared(order[step + 1]) if step < pairs else None
        largest, factor, weights = attend(
            scores, both if pair < pairs else only, state and state.largest(pair)
        )
        width = scores.shape[1] // len(left)
        for sub, part in enumerate(left):
            lanes = slice(sub * width, (sub + 1) * width)
            added = product(jnp.concatenate([part, ones], axis=0), weights[:, lanes])
            total, weight = added[: part.shape[0]], added[part.shape[0] : part.shape[0] + 1]
            if state is not None:
                total = total + state.total(pair, sub) * factor[:, lanes]
                weight = weight + state.weight(pair, sub) * factor[:, lanes]
            yield pair, sub, largest[:, lanes], total, weight
        scores = following


class State:
    def __init__(self, rows, refs):
        self.rows = rows
        self.largest_ref, self.weight_ref, self.total_ref, self.special_ref = refs

    def lanes(self, pair, sub):
        if pair == self.total_ref.shape[0]:
            return slice(0, self.special_ref.shape[1])
        return slice(sub * self.rows, (sub + 1) * self.rows)

    def largest(self, pair):
        stop = self.special_ref.shape[1] if pair == self.total_ref.shape[0] else 2 * self.rows
        return self.largest_ref[pair : pair + 1, 0:stop]

    def weight(self, pair, sub):
        return self.weight_ref[pair : pair + 1, self.lanes(pair, sub)]

    def total(self, pair, sub):
        if pair == self.total_ref.shape[0]:
            return self.special_ref[...]
        return self.total_ref[pair, :, self.lanes(pair, sub)]

    def put(self, pair, sub, largest, total, weight):
        lanes = self.lanes(pair, sub)
        self.largest_ref[pair : pair + 1, lanes] = largest
        self.weight_ref[pair : pair + 1, lanes] = weight
        if pair == self.total_ref.shape[0]:
            self.special_ref[...] = total
        else:
            self.total_ref[pair, :, lanes] = total


def first_kernel(
    images, mask, own, other, special, other_special, weights, queries_out, special_out, *state_out
):
    patch_total = own.shape[0]
    columns = projector(
        jnp.concatenate([own[...], special[...]], axis=0),
        jnp.concatenate([other[...], other_special[...]], axis=0),
        weights,
    )
    pairs = queries_out.shape[0]
    zero = jnp.zeros((HEAD_DIM, patch_total), jnp.bfloat16)
    made = {}

    def patch_columns(which, quad):
        return columns(which, quad)[:patch_total]

    def columns_of(quad):
        if quad not in made:
            queries = columns(0, quad) * (HEAD_DIM ** (-0.5) * LOG2_E)
            made[quad] = queries[patch_total:]
            turned = jnp.transpose(queries[:patch_total]).astype(jnp.bfloat16)
            for i in range(2):
                first = i * PAIR
                upper = jnp.concatenate([turned[first : first + HEAD_DIM], zero], axis=1)
                lower = jnp.concatenate([zero, turned[first + HEAD_DIM : first + PAIR]], axis=1)
                queries_out[2 * quad + i] = jnp.concatenate([upper, lower], axis=0)
        return made[quad]

    def queries_of(pair):
        columns_of(pair // 2)
        return queries_out[pair]

    def special_queries():
        block = jnp.concatenate([columns_of(quad) for quad in range(pairs // 2)], axis=1)
        count = block.shape[0]
        block = jnp.concatenate([block] * (2 * pairs), axis=0)
        row = lax.broadcasted_iota(jnp.int32, block.shape, 0) // count
        lane = lax.broadcasted_iota(jnp.int32, block.shape, 1) // HEAD_DIM
        block = jnp.transpose(jnp.where(row == lane, block, 0.0)).astype(jnp.bfloat16)
        special_out[...] = block
        return block

    per_image = patch_total // images
    masks = [(per_image, mask[b : b + 1, :]) for b in range(images)]
    state = State(patch_total, state_out)
    for result in attend_all(
        patch_columns, masks, queries_of, special_queries, None, pairs, patch_total, 0
    ):
        state.put(*result)


def joined(stretches, mask, refs):
    count = len(stretches)
    own = jnp.concatenate([ref[...] for ref in refs[:count]], axis=0)
    other = jnp.concatenate([ref[...] for ref in refs[count : 2 * count]], axis=0)
    masks = [
        (rows, None if i is None else mask[i : i + 1, :]) for part in stretches for rows, i in part
    ]
    return own, other, masks, refs[2 * count :]


def later_kernel(stretches, special_real, mask, *refs):
    own, other, masks, refs = joined(stretches, mask, refs)
    weights, queries, special_queries = refs[:3]
    state_in, state_out = refs[3:7], refs[7:]
    pairs, rows = queries.shape[0], queries.shape[2] // 2
    state = State(rows, state_out)
    for result in attend_all(
        projector(own, other, weights), masks, lambda pair: queries[pair], lambda: special_queries[...],
        State(rows, state_in), pairs, rows, special_real,
    ):
        state.put(*result)


def last_kernel(stretches, special_real, mask, *refs):
    own, other, masks, refs = joined(stretches, mask, refs)
    weights, queries, special_queries = refs[:3]
    state_in = refs[3:7]
    w_out, kept_out, sent_out, w_here, copied = refs[7:]
    copy = pltpu.make_async_copy(w_out, w_here, copied)
    copy.start()
    pairs, rows = queries.shape[0], queries.shape[2] // 2
    columns, out, special = [], None, None
    sides = halves(kept_out.shape[1])
    for pair, sub, _, total, weight in attend_all(
        projector(own, other, weights), masks, lambda pair: queries[pair], lambda: special_queries[...],
        State(rows, state_in), pairs, rows, special_real,
    ):
        if pair == 0 and sub == 0:
            copy.wait()
        share = total * (1.0 / weight)
        if pair == pairs:
            row = lax.broadcasted_iota(jnp.int32, share.shape, 0) // HEAD_DIM
            lane = lax.broadcasted_iota(jnp.int32, share.shape, 1) // TILE_ROWS
            share = jnp.transpose(jnp.where(row == lane, share, 0.0))
            share = sum(share[i * TILE_ROWS : (i + 1) * TILE_ROWS] for i in range(2 * pairs))
            special = [product(share.astype(jnp.bfloat16), w_here[:, side]) for side in sides]
            continue
        columns.append(share)
        if pair % 2 == 1 and sub == 1:
            quad = jnp.transpose(jnp.concatenate(columns, axis=0)).astype(jnp.bfloat16)
            features = slice((pair // 2) * QUAD, (pair // 2 + 1) * QUAD)
            added = [product(quad, w_here[features, side]) for side in sides]
            out = added if out is None else [before + more for before, more in zip(out, added)]
            columns = []
    for place, values in ((slice(0, rows), out), (slice(rows, kept_out.shape[0]), special)):
        sent_out[place, :] = values[1].astype(jnp.bfloat16)
        kept_out[place, :] = values[0]


def end_kernel(images, kept, received, patch_out, special_out):
    patch_total = patch_out.shape[0]
    special_count = special_out.shape[0]
    patch_out[...] = (kept[:patch_total, :] + received[:patch_total, :].astype(jnp.float32)).astype(
        jnp.bfloat16
    )
    rest = kept[patch_total:, :] + received[patch_total:, :].astype(jnp.float32)
    rows = [rest[b * special_count : (b + 1) * special_count][:, None, :] for b in range(images)]
    special_out[...] = jnp.concatenate(rows, axis=1).astype(jnp.bfloat16)


def call(kernel, out_shape, operands, in_specs=None, out_specs=None, scratch=(), flops=0):
    if in_specs:
        operands = [
            pltpu.with_memory_space_constraint(operand, pltpu.HBM) if spec is HBM else operand
            for operand, spec in zip(operands, in_specs)
        ]
    return pl.pallas_call(
        kernel,
        out_shape=out_shape,
        in_specs=in_specs or [VMEM] * len(operands),
        out_specs=out_specs or [VMEM] * len(out_shape),
        scratch_shapes=scratch,
        compiler_params=pltpu.CompilerParams(vmem_limit_bytes=VMEM_BYTES),
        cost_estimate=pl.CostEstimate(flops=flops, transcendentals=0, bytes_accessed=0),
    )(*operands)


def stack_kernel(first, second, out):
    count = first.shape[0]
    out[:count, :] = first[...]
    out[count:, :] = second[...]


def stacked(first, second, flops=0):
    shape = jax.ShapeDtypeStruct((2 * first.shape[0], first.shape[1]), first.dtype)
    return call(stack_kernel, [shape], (first, second), flops=flops)[0]


def after(array, *others):
    return lax.optimization_barrier((array, *others))[0]


def per_device(
    patch_rows, special_rows, role_first, role_rest, frame_order, covisible, w_qkv, w_out
):
    images, per_image, width = patch_rows.shape
    special_count = special_rows.shape[1]
    real_rows = images * special_count
    special_block = real_rows + -real_rows % TILE_ROWS
    owner_count = lax.axis_size("blk")
    reach = max(1, owner_count // 64)
    patch_total = images * per_image
    rows = patch_total + special_block
    heads = width // HEAD_DIM
    pairs = heads // 2
    paired = reach == 1 and owner_count % 2 == 0

    if paired:
        offsets = [0, (-1, 1), (1, -1)]
    else:
        offsets = [0] + [sign * d for d in range(1, reach + 1) for sign in (-1, 1)]
    mask_rows = -(-len(offsets) * images // 8) * 8
    bf16 = lambda *shape: jax.ShapeDtypeStruct(shape, jnp.bfloat16)
    f32 = lambda *shape: jax.ShapeDtypeStruct(shape, jnp.float32)
    state_shape = [
        f32(8, 2 * patch_total),
        f32(8, 2 * patch_total),
        f32(pairs, HEAD_DIM, 2 * patch_total),
        f32(width, heads * special_block),
    ]

    both = lambda part: (part, swapped(part, "head", 1))
    patches = patch_rows.reshape(patch_total, width)
    turned = jnp.transpose(special_rows, (1, 0, 2))
    power = owner_count >= 8 and owner_count & (owner_count - 1) == 0
    specials, own = call(
        rows_kernel,
        [bf16(special_block, width), bf16(patch_total, width)],
        (frame_order, turned, role_first, role_rest, patches),
        in_specs=[HBM] * 5,
        scratch=[
            pltpu.SMEM(frame_order.shape, jnp.int32),
            pltpu.VMEM(turned.shape, jnp.bfloat16),
            pltpu.VMEM(role_first.shape, jnp.bfloat16),
            pltpu.VMEM(role_rest.shape, jnp.bfloat16),
            pltpu.SemaphoreType.DMA((5,)),
        ],
    )
    bits = [1 << i for i in range(1, owner_count.bit_length() - 1)] + [1] if power else []
    everywhere = specials
    if power:
        everywhere = stacked(specials, swapped(specials, "blk", bits[0]), FIRST)
    mask, weights = call(
        functools.partial(start_kernel, offsets, per_image, special_count, special_block),
        [
            f32(mask_rows, patch_total + heads * special_block),
            bf16(*w_qkv.shape),
        ],
        (covisible, w_qkv),
        in_specs=[HBM] * 2,
        scratch=[pltpu.SMEM(covisible.shape, jnp.int32), pltpu.SemaphoreType.DMA((1 + 3,))],
    )
    if paired:
        near = [crossed(own, "blk"), swapped(own, "blk", 1)]
    else:
        near = [shifted(own, "blk", -offset) for offset in offsets[1:]]
    queries, special_queries, *state = call(
        functools.partial(first_kernel, images),
        [bf16(pairs, PAIR, 2 * patch_total), bf16(width, heads * special_block), *state_shape],
        (after(mask, everywhere), *both(own), *both(specials), weights),
    )
    fixed = (weights, queries, special_queries)

    def later(stretches, parts, state):
        return call(
            functools.partial(later_kernel, stretches, real_rows),
            state_shape,
            (mask, *[part[0] for part in parts], *[part[1] for part in parts], *fixed, *state),
        )

    image_rows = lambda owner: [(per_image, owner * images + b) for b in range(images)]
    for i, part in enumerate(near):
        part = after(part, state[0])
        parts = [both(part[b * per_image : (b + 1) * per_image]) for b in range(images)]
        if i == 0 and power:
            everywhere = after(everywhere, part)
            for bit in bits[1:-2]:
                everywhere = stacked(everywhere, swapped(everywhere, "blk", bit))
            arrived = swapped(everywhere, "blk", bits[-2])
        state = later([[image] for image in image_rows(i + 1)], parts, state)
        if i == 0 and power:
            everywhere = stacked(after(everywhere, state[0]), arrived)
            everywhere = stacked(everywhere, swapped(everywhere, "blk", bits[-1]))
    if not power:
        everywhere = lax.all_gather(specials, "blk", axis=0, tiled=True)
    stretches, parts = [[(everywhere.shape[0], None)]], [both(everywhere)]
    kept, sent = call(
        functools.partial(last_kernel, stretches, real_rows),
        [f32(rows, width), bf16(rows, width)],
        (
            mask, *[part[0] for part in parts], *[part[1] for part in parts], *fixed, *state, w_out,
        ),
        in_specs=[VMEM] * (1 + 2 * len(parts) + len(fixed) + len(state)) + [HBM],
        scratch=[pltpu.VMEM(w_out.shape, jnp.bfloat16), pltpu.SemaphoreType.DMA],
    )
    received = swapped(sent, "head", 1)
    patch_out, special_out = call(
        functools.partial(end_kernel, images),
        [bf16(patch_total, width), bf16(special_count, images, width)],
        (kept, received),
        out_specs=[pl.BlockSpec(), pl.BlockSpec()],
    )
    return patch_out.reshape(patch_rows.shape), jnp.transpose(special_out, (1, 0, 2))


def solution(mesh):
    in_specs = (
        P(("scene", "blk"), None, "head"),
        P(("scene", "blk"), None, "head"),
        P(),
        P(),
        P(("scene", "blk")),
        P(("scene", "blk"), None),
        P(None, None, "head"),
        P("head", None),
    )
    out_specs = (P(("scene", "blk"), None, "head"), P(("scene", "blk"), None, "head"))
    return jax.shard_map(
        per_device, mesh=mesh, in_specs=in_specs, out_specs=out_specs, check_vma=False
    )
```

```python
import functools

import jax
import jax.numpy as jnp
from jax import lax
from jax.experimental import pallas as pl
from jax.experimental.pallas import tpu as pltpu
from jax.sharding import PartitionSpec as P

HEAD_DIM = 64
PAIR = 2 * HEAD_DIM
QUAD = 2 * PAIR
TILE_ROWS = 16
LOG2_E = 1.4426950408889634
FIRST = 20_000_000_000
VMEM_BYTES = 32 * 1024 * 1024
SMEM = pl.BlockSpec(memory_space=pltpu.SMEM)
VMEM = pl.BlockSpec(memory_space=pltpu.VMEM)
HBM = pl.BlockSpec(memory_space=pltpu.HBM)


def shifted(block, axis, distance):
    count = lax.axis_size(axis)
    route = [((i - distance) % count, i) for i in range(count)]
    return lax.ppermute(block, axis, route)


def swapped(block, axis, bit):
    count = lax.axis_size(axis)
    return lax.ppermute(block, axis, [(i ^ bit, i) for i in range(count)])


def crossed(block, axis):
    count = lax.axis_size(axis)
    return lax.ppermute(block, axis, [(i, (i + (-1 if i % 2 == 0 else 1)) % count) for i in range(count)])


def halves(width):
    half = lax.axis_index("head")
    mine = pl.ds(pl.multiple_of(half * width, width), width)
    theirs = pl.ds(pl.multiple_of((1 - half) * width, width), width)
    return mine, theirs


def product(left, right):
    return jnp.dot(left, right, preferred_element_type=jnp.float32)


def owner_at(offset):
    count = lax.axis_size("blk")
    here = lax.axis_index("blk")
    if isinstance(offset, tuple):
        offset = jnp.where(lax.rem(here, 2) == 0, offset[0], offset[1])
    return lax.rem(here + offset + count, count)


def rows_kernel(
    frame_order, specials, role_first, role_rest, patches,
    special_out, patches_out, order, here, first_rows, rest_rows, copied,
):
    special_count, images, width = specials.shape
    moves = [(specials, here), (role_first, first_rows), (role_rest, rest_rows), (frame_order, order)]
    moves.append((patches, patches_out))
    copies = [
        pltpu.make_async_copy(source, target, copied.at[i]) for i, (source, target) in enumerate(moves)
    ]
    for copy in copies:
        copy.start()
    for copy in copies[:-1]:
        copy.wait()
    mine, _ = halves(width)
    first = first_rows[:, mine].astype(jnp.float32)
    rest = rest_rows[:, mine].astype(jnp.float32)
    summed = [
        here[:, b, :].astype(jnp.float32) + jnp.where(order[b] == 0, first, rest) for b in range(images)
    ]
    summed.append(jnp.zeros((special_out.shape[0] - images * special_count, width), jnp.float32))
    special_out[...] = jnp.concatenate(summed, axis=0).astype(jnp.bfloat16)
    copies[-1].wait()


def start_kernel(
    offsets, per_image, special_count, special_total, covisible, w_qkv, mask_out, weights_out, seen, copied
):
    images = covisible.shape[0]
    patch_total = images * per_image
    moves = [(covisible, seen)]
    moves += [(w_qkv.at[i], weights_out.at[i]) for i in range(3)]
    copies = [
        pltpu.make_async_copy(source, target, copied.at[i]) for i, (source, target) in enumerate(moves)
    ]
    for copy in copies:
        copy.start()
    copies[0].wait()
    lane = lax.broadcasted_iota(jnp.int32, (1, mask_out.shape[1]), 1)
    special_lane = lax.rem(lane - patch_total, special_total)
    image = jnp.where(
        lane < patch_total, lane // per_image, jnp.minimum(special_lane // special_count, images - 1)
    )
    for i, offset in enumerate(offsets):
        for b in range(images):
            row = jnp.zeros(lane.shape, jnp.float32)
            for a in range(images):
                hidden = seen[a, owner_at(offset) * images + b] <= 0
                row = jnp.where((image == a) & hidden, -jnp.inf, row)
            mask_out[i * images + b : i * images + b + 1, :] = row
    for copy in copies[1:]:
        copy.wait()


def projector(own, other, weights):
    mine, theirs = halves(own.shape[1])

    def columns(which, quad):
        lanes = slice(quad * QUAD, (quad + 1) * QUAD)
        return product(own, weights[which, mine, lanes]) + product(other, weights[which, theirs, lanes])

    return columns


def attend(scores, masks, state):
    largest = state
    start = 0
    for count, mask in masks:
        part = jnp.max(scores[start : start + count], axis=0, keepdims=True)
        part = part if mask is None else part + mask
        largest = part if largest is None else jnp.maximum(largest, part)
        start += count
    weights, start = [], 0
    for count, mask in masks:
        level = largest if mask is None else largest - mask
        weights.append(jnp.exp2((scores[start : start + count] - level).astype(jnp.bfloat16)))
        start += count
    factor = None if state is None else jnp.exp2(state - largest)
    return largest, factor, jnp.concatenate(weights, axis=0)


def attend_all(columns, masks, queries_of, special_queries, state, pairs, rows, special_real):
    keys, values = {}, {}
    quads = pairs // 2

    def keys_of(quad):
        if quad not in keys:
            keys[quad] = columns(1, quad).astype(jnp.bfloat16)
        return keys[quad]

    def values_of(quad):
        if quad not in values:
            values[quad] = jnp.transpose(columns(2, quad)).astype(jnp.bfloat16)
        return values[quad]

    def prepared(pair):
        if pair == pairs:
            scores = product(
                jnp.concatenate([keys_of(quad) for quad in range(quads)], axis=1), special_queries()
            )
        else:
            lanes = slice((pair % 2) * PAIR, (pair % 2 + 1) * PAIR)
            scores = product(keys_of(pair // 2)[:, lanes], queries_of(pair))
        if all(mask is not None for _, mask in masks):
            return scores
        parts, start = [], 0
        for count, mask in masks:
            part = scores[start : start + count]
            if mask is None:
                key_row = lax.broadcasted_iota(jnp.int32, (count, 1), 0)
                part = jnp.where(lax.rem(key_row, TILE_ROWS) < special_real, part, -jnp.inf)
            parts.append(part)
            start += count
        return jnp.concatenate(parts, axis=0)

    ones = jnp.ones((TILE_ROWS, sum(count for count, _ in masks)), jnp.bfloat16)
    both = [
        (count, None if mask is None else jnp.concatenate([mask[:, :rows]] * 2, axis=1))
        for count, mask in masks
    ]
    only = [(count, None if mask is None else mask[:, rows:]) for count, mask in masks]
    order = list(range(pairs))
    order.insert(pairs - 2, pairs)
    scores = prepared(order[0])
    for step, pair in enumerate(order):
        if pair < pairs:
            left = [
                values_of(pair // 2)[first : first + HEAD_DIM]
                for first in ((pair % 2) * PAIR, (pair % 2) * PAIR + HEAD_DIM)
            ]
        else:
            left = [jnp.concatenate([values_of(quad) for quad in range(quads)], axis=0)]
        following = prepared(order[step + 1]) if step < pairs else None
        largest, factor, weights = attend(
            scores, both if pair < pairs else only, state and state.largest(pair)
        )
        width = scores.shape[1] // len(left)
        for sub, part in enumerate(left):
            lanes = slice(sub * width, (sub + 1) * width)
            added = product(jnp.concatenate([part, ones], axis=0), weights[:, lanes])
            total, weight = added[: part.shape[0]], added[part.shape[0] : part.shape[0] + 1]
            if state is not None:
                total = total + state.total(pair, sub) * factor[:, lanes]
                weight = weight + state.weight(pair, sub) * factor[:, lanes]
            yield pair, sub, largest[:, lanes], total, weight
        scores = following


class State:
    def __init__(self, rows, refs):
        self.rows = rows
        self.largest_ref, self.weight_ref, self.total_ref, self.special_ref = refs

    def lanes(self, pair, sub):
        if pair == self.total_ref.shape[0]:
            return slice(0, self.special_ref.shape[1])
        return slice(sub * self.rows, (sub + 1) * self.rows)

    def largest(self, pair):
        stop = self.special_ref.shape[1] if pair == self.total_ref.shape[0] else 2 * self.rows
        return self.largest_ref[pair : pair + 1, 0:stop]

    def weight(self, pair, sub):
        return self.weight_ref[pair : pair + 1, self.lanes(pair, sub)]

    def total(self, pair, sub):
        if pair == self.total_ref.shape[0]:
            return self.special_ref[...]
        return self.total_ref[pair, :, self.lanes(pair, sub)]

    def put(self, pair, sub, largest, total, weight):
        lanes = self.lanes(pair, sub)
        self.largest_ref[pair : pair + 1, lanes] = largest
        self.weight_ref[pair : pair + 1, lanes] = weight
        if pair == self.total_ref.shape[0]:
            self.special_ref[...] = total
        else:
            self.total_ref[pair, :, lanes] = total


def first_kernel(
    images, mask, own, other, special, other_special, weights, queries_out, special_out, *state_out
):
    patch_total = own.shape[0]
    columns = projector(
        jnp.concatenate([own[...], special[...]], axis=0),
        jnp.concatenate([other[...], other_special[...]], axis=0),
        weights,
    )
    pairs = queries_out.shape[0]
    zero = jnp.zeros((HEAD_DIM, patch_total), jnp.bfloat16)
    made = {}

    def patch_columns(which, quad):
        return columns(which, quad)[:patch_total]

    def columns_of(quad):
        if quad not in made:
            queries = columns(0, quad) * (HEAD_DIM ** (-0.5) * LOG2_E)
            made[quad] = queries[patch_total:]
            turned = jnp.transpose(queries[:patch_total]).astype(jnp.bfloat16)
            for i in range(2):
                first = i * PAIR
                upper = jnp.concatenate([turned[first : first + HEAD_DIM], zero], axis=1)
                lower = jnp.concatenate([zero, turned[first + HEAD_DIM : first + PAIR]], axis=1)
                queries_out[2 * quad + i] = jnp.concatenate([upper, lower], axis=0)
        return made[quad]

    def queries_of(pair):
        columns_of(pair // 2)
        return queries_out[pair]

    def special_queries():
        block = jnp.concatenate([columns_of(quad) for quad in range(pairs // 2)], axis=1)
        count = block.shape[0]
        block = jnp.concatenate([block] * (2 * pairs), axis=0)
        row = lax.broadcasted_iota(jnp.int32, block.shape, 0) // count
        lane = lax.broadcasted_iota(jnp.int32, block.shape, 1) // HEAD_DIM
        block = jnp.transpose(jnp.where(row == lane, block, 0.0)).astype(jnp.bfloat16)
        special_out[...] = block
        return block

    per_image = patch_total // images
    masks = [(per_image, mask[b : b + 1, :]) for b in range(images)]
    state = State(patch_total, state_out)
    for result in attend_all(
        patch_columns, masks, queries_of, special_queries, None, pairs, patch_total, 0
    ):
        state.put(*result)


def joined(stretches, mask, refs):
    count = len(stretches)
    own = jnp.concatenate([ref[...] for ref in refs[:count]], axis=0)
    other = jnp.concatenate([ref[...] for ref in refs[count : 2 * count]], axis=0)
    masks = [
        (rows, None if i is None else mask[i : i + 1, :]) for part in stretches for rows, i in part
    ]
    return own, other, masks, refs[2 * count :]


def later_kernel(stretches, special_real, mask, *refs):
    own, other, masks, refs = joined(stretches, mask, refs)
    weights, queries, special_queries = refs[:3]
    state_in, state_out = refs[3:7], refs[7:]
    pairs, rows = queries.shape[0], queries.shape[2] // 2
    state = State(rows, state_out)
    for result in attend_all(
        projector(own, other, weights), masks, lambda pair: queries[pair], lambda: special_queries[...],
        State(rows, state_in), pairs, rows, special_real,
    ):
        state.put(*result)


def last_kernel(stretches, special_real, mask, *refs):
    own, other, masks, refs = joined(stretches, mask, refs)
    weights, queries, special_queries = refs[:3]
    state_in = refs[3:7]
    w_out, kept_out, sent_out, w_here, copied = refs[7:]
    copy = pltpu.make_async_copy(w_out, w_here, copied)
    copy.start()
    pairs, rows = queries.shape[0], queries.shape[2] // 2
    columns, out, special = [], None, None
    sides = halves(kept_out.shape[1])
    for pair, sub, _, total, weight in attend_all(
        projector(own, other, weights), masks, lambda pair: queries[pair], lambda: special_queries[...],
        State(rows, state_in), pairs, rows, special_real,
    ):
        if pair == 0 and sub == 0:
            copy.wait()
        share = total * (1.0 / weight)
        if pair == pairs:
            row = lax.broadcasted_iota(jnp.int32, share.shape, 0) // HEAD_DIM
            lane = lax.broadcasted_iota(jnp.int32, share.shape, 1) // TILE_ROWS
            share = jnp.transpose(jnp.where(row == lane, share, 0.0))
            share = sum(share[i * TILE_ROWS : (i + 1) * TILE_ROWS] for i in range(2 * pairs))
            special = [product(share.astype(jnp.bfloat16), w_here[:, side]) for side in sides]
            continue
        columns.append(share)
        if pair % 2 == 1 and sub == 1:
            quad = jnp.transpose(jnp.concatenate(columns, axis=0)).astype(jnp.bfloat16)
            features = slice((pair // 2) * QUAD, (pair // 2 + 1) * QUAD)
            added = [product(quad, w_here[features, side]) for side in sides]
            out = added if out is None else [before + more for before, more in zip(out, added)]
            columns = []
    for place, values in ((slice(0, rows), out), (slice(rows, kept_out.shape[0]), special)):
        sent_out[place, :] = values[1].astype(jnp.bfloat16)
        kept_out[place, :] = values[0]


def end_kernel(images, kept, received, patch_out, special_out):
    patch_total = patch_out.shape[0]
    special_count = special_out.shape[0]
    patch_out[...] = (kept[:patch_total, :] + received[:patch_total, :].astype(jnp.float32)).astype(
        jnp.bfloat16
    )
    rest = kept[patch_total:, :] + received[patch_total:, :].astype(jnp.float32)
    rows = [rest[b * special_count : (b + 1) * special_count][:, None, :] for b in range(images)]
    special_out[...] = jnp.concatenate(rows, axis=1).astype(jnp.bfloat16)


def call(kernel, out_shape, operands, in_specs=None, out_specs=None, scratch=(), flops=0):
    if in_specs:
        operands = [
            pltpu.with_memory_space_constraint(operand, pltpu.HBM) if spec is HBM else operand
            for operand, spec in zip(operands, in_specs)
        ]
    return pl.pallas_call(
        kernel,
        out_shape=out_shape,
        in_specs=in_specs or [VMEM] * len(operands),
        out_specs=out_specs or [VMEM] * len(out_shape),
        scratch_shapes=scratch,
        compiler_params=pltpu.CompilerParams(vmem_limit_bytes=VMEM_BYTES),
        cost_estimate=pl.CostEstimate(flops=flops, transcendentals=0, bytes_accessed=0),
    )(*operands)


def stack_kernel(first, second, out):
    count = first.shape[0]
    out[:count, :] = first[...]
    out[count:, :] = second[...]


def stacked(first, second, flops=0):
    shape = jax.ShapeDtypeStruct((2 * first.shape[0], first.shape[1]), first.dtype)
    return call(stack_kernel, [shape], (first, second), flops=flops)[0]


def after(array, *others):
    return lax.optimization_barrier((array, *others))[0]


def per_device(
    patch_rows, special_rows, role_first, role_rest, frame_order, covisible, w_qkv, w_out
):
    images, per_image, width = patch_rows.shape
    special_count = special_rows.shape[1]
    real_rows = images * special_count
    special_block = real_rows + -real_rows % TILE_ROWS
    owner_count = lax.axis_size("blk")
    reach = max(1, owner_count // 64)
    patch_total = images * per_image
    rows = patch_total + special_block
    heads = width // HEAD_DIM
    pairs = heads // 2
    paired = reach == 1 and owner_count % 2 == 0

    if paired:
        offsets = [0, (-1, 1), (1, -1)]
    else:
        offsets = [0] + [sign * d for d in range(1, reach + 1) for sign in (-1, 1)]
    mask_rows = -(-len(offsets) * images // 8) * 8
    bf16 = lambda *shape: jax.ShapeDtypeStruct(shape, jnp.bfloat16)
    f32 = lambda *shape: jax.ShapeDtypeStruct(shape, jnp.float32)
    state_shape = [
        f32(8, 2 * patch_total),
        f32(8, 2 * patch_total),
        f32(pairs, HEAD_DIM, 2 * patch_total),
        f32(width, heads * special_block),
    ]

    both = lambda part: (part, swapped(part, "head", 1))
    patches = patch_rows.reshape(patch_total, width)
    turned = jnp.transpose(special_rows, (1, 0, 2))
    power = owner_count >= 8 and owner_count & (owner_count - 1) == 0
    specials, own = call(
        rows_kernel,
        [bf16(special_block, width), bf16(patch_total, width)],
        (frame_order, turned, role_first, role_rest, patches),
        in_specs=[HBM] * 5,
        scratch=[
            pltpu.SMEM(frame_order.shape, jnp.int32),
            pltpu.VMEM(turned.shape, jnp.bfloat16),
            pltpu.VMEM(role_first.shape, jnp.bfloat16),
            pltpu.VMEM(role_rest.shape, jnp.bfloat16),
            pltpu.SemaphoreType.DMA((5,)),
        ],
    )
    bits = [1 << i for i in range(1, owner_count.bit_length() - 1)] + [1] if power else []
    everywhere = specials
    if power:
        everywhere = stacked(specials, swapped(specials, "blk", bits[0]), FIRST)
    mask, weights = call(
        functools.partial(start_kernel, offsets, per_image, special_count, special_block),
        [
            f32(mask_rows, patch_total + heads * special_block),
            bf16(*w_qkv.shape),
        ],
        (covisible, w_qkv),
        in_specs=[HBM] * 2,
        scratch=[pltpu.SMEM(covisible.shape, jnp.int32), pltpu.SemaphoreType.DMA((1 + 3,))],
    )
    if paired:
        near = [crossed(patches, "blk"), swapped(patches, "blk", 1)]
    else:
        near = [shifted(patches, "blk", -offset) for offset in offsets[1:]]
    queries, special_queries, *state = call(
        functools.partial(first_kernel, images),
        [bf16(pairs, PAIR, 2 * patch_total), bf16(width, heads * special_block), *state_shape],
        (mask, own, swapped(patches, "head", 1), *both(specials), weights),
    )
    fixed = (weights, queries, special_queries)

    def later(stretches, parts, state):
        return call(
            functools.partial(later_kernel, stretches, real_rows),
            state_shape,
            (mask, *[part[0] for part in parts], *[part[1] for part in parts], *fixed, *state),
        )

    image_rows = lambda owner: [(per_image, owner * images + b) for b in range(images)]
    for i, part in enumerate(near):
        part = after(part, state[0])
        parts = [both(part[b * per_image : (b + 1) * per_image]) for b in range(images)]
        if i == 0 and power:
            everywhere = after(everywhere, part)
            for bit in bits[1:-2]:
                everywhere = stacked(everywhere, swapped(everywhere, "blk", bit))
            arrived = swapped(everywhere, "blk", bits[-2])
        state = later([[image] for image in image_rows(i + 1)], parts, state)
        if i == 0 and power:
            everywhere = stacked(after(everywhere, state[0]), arrived)
            everywhere = stacked(everywhere, swapped(everywhere, "blk", bits[-1]), FIRST)
    if not power:
        everywhere = lax.all_gather(specials, "blk", axis=0, tiled=True)
    stretches, parts = [[(everywhere.shape[0], None)]], [both(everywhere)]
    kept, sent = call(
        functools.partial(last_kernel, stretches, real_rows),
        [f32(rows, width), bf16(rows, width)],
        (
            mask, *[part[0] for part in parts], *[part[1] for part in parts], *fixed, *state, w_out,
        ),
        in_specs=[VMEM] * (1 + 2 * len(parts) + len(fixed) + len(state)) + [HBM],
        scratch=[pltpu.VMEM(w_out.shape, jnp.bfloat16), pltpu.SemaphoreType.DMA],
    )
    received = swapped(sent, "head", 1)
    patch_out, special_out = call(
        functools.partial(end_kernel, images),
        [bf16(patch_total, width), bf16(special_count, images, width)],
        (kept, received),
        out_specs=[pl.BlockSpec(), pl.BlockSpec()],
    )
    return patch_out.reshape(patch_rows.shape), jnp.transpose(special_out, (1, 0, 2))


def solution(mesh):
    in_specs = (
        P(("scene", "blk"), None, "head"),
        P(("scene", "blk"), None, "head"),
        P(),
        P(),
        P(("scene", "blk")),
        P(("scene", "blk"), None),
        P(None, None, "head"),
        P("head", None),
    )
    out_specs = (P(("scene", "blk"), None, "head"), P(("scene", "blk"), None, "head"))
    return jax.shard_map(
        per_device, mesh=mesh, in_specs=in_specs, out_specs=out_specs, check_vma=False
    )
```

```python
import functools

import jax
import jax.numpy as jnp
from jax import lax
from jax.experimental import pallas as pl
from jax.experimental.pallas import tpu as pltpu
from jax.sharding import PartitionSpec as P

HEAD_DIM = 64
PAIR = 2 * HEAD_DIM
QUAD = 2 * PAIR
TILE_ROWS = 16
LOG2_E = 1.4426950408889634
FIRST = 20_000_000_000
LAST = FIRST
VMEM_BYTES = 32 * 1024 * 1024
SMEM = pl.BlockSpec(memory_space=pltpu.SMEM)
VMEM = pl.BlockSpec(memory_space=pltpu.VMEM)
HBM = pl.BlockSpec(memory_space=pltpu.HBM)


def shifted(block, axis, distance):
    count = lax.axis_size(axis)
    route = [((i - distance) % count, i) for i in range(count)]
    return lax.ppermute(block, axis, route)


def swapped(block, axis, bit):
    count = lax.axis_size(axis)
    return lax.ppermute(block, axis, [(i ^ bit, i) for i in range(count)])


def crossed(block, axis):
    count = lax.axis_size(axis)
    return lax.ppermute(block, axis, [(i, (i + (-1 if i % 2 == 0 else 1)) % count) for i in range(count)])


def halves(width):
    half = lax.axis_index("head")
    mine = pl.ds(pl.multiple_of(half * width, width), width)
    theirs = pl.ds(pl.multiple_of((1 - half) * width, width), width)
    return mine, theirs


def product(left, right):
    return jnp.dot(left, right, preferred_element_type=jnp.float32)


def owner_at(offset):
    count = lax.axis_size("blk")
    here = lax.axis_index("blk")
    if isinstance(offset, tuple):
        offset = jnp.where(lax.rem(here, 2) == 0, offset[0], offset[1])
    return lax.rem(here + offset + count, count)


def rows_kernel(
    frame_order, specials, role_first, role_rest, patches,
    special_out, patches_out, early_out, late_out, order, here, first_rows, rest_rows, copied,
):
    cut = early_out.shape[0]
    special_count, images, width = specials.shape
    moves = [(specials, here), (role_first, first_rows), (role_rest, rest_rows), (frame_order, order)]
    moves.append((patches.at[pl.ds(0, cut)], early_out))
    moves.append((patches, patches_out))
    moves.append((patches.at[pl.ds(cut, late_out.shape[0])], late_out))
    copies = [
        pltpu.make_async_copy(source, target, copied.at[i]) for i, (source, target) in enumerate(moves)
    ]
    for copy in copies:
        copy.start()
    for copy in copies[:4]:
        copy.wait()
    mine, _ = halves(width)
    first = first_rows[:, mine].astype(jnp.float32)
    rest = rest_rows[:, mine].astype(jnp.float32)
    summed = [
        here[:, b, :].astype(jnp.float32) + jnp.where(order[b] == 0, first, rest) for b in range(images)
    ]
    summed.append(jnp.zeros((special_out.shape[0] - images * special_count, width), jnp.float32))
    special_out[...] = jnp.concatenate(summed, axis=0).astype(jnp.bfloat16)
    for copy in copies[4:]:
        copy.wait()


def start_kernel(
    offsets, per_image, special_count, special_total, covisible, w_qkv, mask_out, weights_out, seen, copied
):
    images = covisible.shape[0]
    patch_total = images * per_image
    moves = [(covisible, seen)]
    moves += [(w_qkv.at[i], weights_out.at[i]) for i in range(3)]
    copies = [
        pltpu.make_async_copy(source, target, copied.at[i]) for i, (source, target) in enumerate(moves)
    ]
    for copy in copies:
        copy.start()
    copies[0].wait()
    lane = lax.broadcasted_iota(jnp.int32, (1, mask_out.shape[1]), 1)
    special_lane = lax.rem(lane - patch_total, special_total)
    image = jnp.where(
        lane < patch_total, lane // per_image, jnp.minimum(special_lane // special_count, images - 1)
    )
    for i, offset in enumerate(offsets):
        for b in range(images):
            row = jnp.zeros(lane.shape, jnp.float32)
            for a in range(images):
                hidden = seen[a, owner_at(offset) * images + b] <= 0
                row = jnp.where((image == a) & hidden, -jnp.inf, row)
            mask_out[i * images + b : i * images + b + 1, :] = row
    for copy in copies[1:]:
        copy.wait()


def projector(own, other, weights):
    mine, theirs = halves(own.shape[1])

    def columns(which, quad):
        lanes = slice(quad * QUAD, (quad + 1) * QUAD)
        return product(own, weights[which, mine, lanes]) + product(other, weights[which, theirs, lanes])

    return columns


def attend(scores, masks, state):
    largest = state
    start = 0
    for count, mask in masks:
        part = jnp.max(scores[start : start + count], axis=0, keepdims=True)
        part = part if mask is None else part + mask
        largest = part if largest is None else jnp.maximum(largest, part)
        start += count
    weights, start = [], 0
    for count, mask in masks:
        level = largest if mask is None else largest - mask
        weights.append(jnp.exp2((scores[start : start + count] - level).astype(jnp.bfloat16)))
        start += count
    factor = None if state is None else jnp.exp2(state - largest)
    return largest, factor, jnp.concatenate(weights, axis=0)


def attend_all(columns, masks, queries_of, special_queries, state, pairs, rows, special_real):
    keys, values = {}, {}
    quads = pairs // 2

    def keys_of(quad):
        if quad not in keys:
            keys[quad] = columns(1, quad).astype(jnp.bfloat16)
        return keys[quad]

    def values_of(quad):
        if quad not in values:
            values[quad] = jnp.transpose(columns(2, quad)).astype(jnp.bfloat16)
        return values[quad]

    def prepared(pair):
        if pair == pairs:
            scores = product(
                jnp.concatenate([keys_of(quad) for quad in range(quads)], axis=1), special_queries()
            )
        else:
            lanes = slice((pair % 2) * PAIR, (pair % 2 + 1) * PAIR)
            scores = product(keys_of(pair // 2)[:, lanes], queries_of(pair))
        if all(mask is not None for _, mask in masks):
            return scores
        parts, start = [], 0
        for count, mask in masks:
            part = scores[start : start + count]
            if mask is None:
                key_row = lax.broadcasted_iota(jnp.int32, (count, 1), 0)
                part = jnp.where(lax.rem(key_row, TILE_ROWS) < special_real, part, -jnp.inf)
            parts.append(part)
            start += count
        return jnp.concatenate(parts, axis=0)

    ones = jnp.ones((TILE_ROWS, sum(count for count, _ in masks)), jnp.bfloat16)
    both = [
        (count, None if mask is None else jnp.concatenate([mask[:, :rows]] * 2, axis=1))
        for count, mask in masks
    ]
    only = [(count, None if mask is None else mask[:, rows:]) for count, mask in masks]
    order = list(range(pairs))
    order.insert(pairs - 2, pairs)
    scores = prepared(order[0])
    for step, pair in enumerate(order):
        if pair < pairs:
            left = values_of(pair // 2)[(pair % 2) * PAIR : (pair % 2 + 1) * PAIR]
        else:
            left = jnp.concatenate([values_of(quad) for quad in range(quads)], axis=0)
        following = prepared(order[step + 1]) if step < pairs else None
        largest, factor, weights = attend(
            scores, both if pair < pairs else only, state and state.largest(pair)
        )
        added = product(jnp.concatenate([left, ones], axis=0), weights)
        height, subs = (HEAD_DIM, 2) if pair < pairs else (left.shape[0], 1)
        width = scores.shape[1] // subs
        for sub in range(subs):
            lanes = slice(sub * width, (sub + 1) * width)
            total = added[sub * height : (sub + 1) * height, lanes]
            weight = added[left.shape[0] : left.shape[0] + 1, lanes]
            if state is not None:
                total = total + state.total(pair, sub) * factor[:, lanes]
                weight = weight + state.weight(pair, sub) * factor[:, lanes]
            yield pair, sub, largest[:, lanes], total, weight
        scores = following


class State:
    def __init__(self, rows, refs):
        self.rows = rows
        self.largest_ref, self.weight_ref, self.total_ref, self.special_ref = refs

    def lanes(self, pair, sub):
        if pair == self.total_ref.shape[0]:
            return slice(0, self.special_ref.shape[1])
        return slice(sub * self.rows, (sub + 1) * self.rows)

    def largest(self, pair):
        stop = self.special_ref.shape[1] if pair == self.total_ref.shape[0] else 2 * self.rows
        return self.largest_ref[pair : pair + 1, 0:stop]

    def weight(self, pair, sub):
        return self.weight_ref[pair : pair + 1, self.lanes(pair, sub)]

    def total(self, pair, sub):
        if pair == self.total_ref.shape[0]:
            return self.special_ref[...]
        return self.total_ref[pair, :, self.lanes(pair, sub)]

    def put(self, pair, sub, largest, total, weight):
        lanes = self.lanes(pair, sub)
        self.largest_ref[pair : pair + 1, lanes] = largest
        self.weight_ref[pair : pair + 1, lanes] = weight
        if pair == self.total_ref.shape[0]:
            self.special_ref[...] = total
        else:
            self.total_ref[pair, :, lanes] = total


def first_kernel(
    images, mask, own, other, special, weights, queries_out, special_out, *state_out
):
    patch_total = own.shape[0]
    columns = projector(
        jnp.concatenate([own[...], special[0]], axis=0),
        jnp.concatenate([other[...], special[1]], axis=0),
        weights,
    )
    pairs = queries_out.shape[0]
    zero = jnp.zeros((HEAD_DIM, patch_total), jnp.bfloat16)
    made = {}

    def patch_columns(which, quad):
        return columns(which, quad)[:patch_total]

    def columns_of(quad):
        if quad not in made:
            queries = columns(0, quad) * (HEAD_DIM ** (-0.5) * LOG2_E)
            made[quad] = queries[patch_total:]
            turned = jnp.transpose(queries[:patch_total]).astype(jnp.bfloat16)
            for i in range(2):
                first = i * PAIR
                upper = jnp.concatenate([turned[first : first + HEAD_DIM], zero], axis=1)
                lower = jnp.concatenate([zero, turned[first + HEAD_DIM : first + PAIR]], axis=1)
                queries_out[2 * quad + i] = jnp.concatenate([upper, lower], axis=0)
        return made[quad]

    def queries_of(pair):
        columns_of(pair // 2)
        return queries_out[pair]

    def special_queries():
        block = jnp.concatenate([columns_of(quad) for quad in range(pairs // 2)], axis=1)
        count = block.shape[0]
        block = jnp.concatenate([block] * (2 * pairs), axis=0)
        row = lax.broadcasted_iota(jnp.int32, block.shape, 0) // count
        lane = lax.broadcasted_iota(jnp.int32, block.shape, 1) // HEAD_DIM
        block = jnp.transpose(jnp.where(row == lane, block, 0.0)).astype(jnp.bfloat16)
        special_out[...] = block
        return block

    per_image = patch_total // images
    masks = [(per_image, mask[b : b + 1, :]) for b in range(images)]
    state = State(patch_total, state_out)
    for result in attend_all(
        patch_columns, masks, queries_of, special_queries, None, pairs, patch_total, 0
    ):
        state.put(*result)


def joined(stretches, mask, refs):
    count = len(stretches)
    flat = lambda ref, i: ref[i] if len(ref.shape) == 3 else ref[...]
    own = jnp.concatenate([flat(ref, 0) for ref in refs[:count]], axis=0)
    other = jnp.concatenate([flat(ref, 1) for ref in refs[count : 2 * count]], axis=0)
    masks = [
        (rows, None if i is None else mask[i : i + 1, :]) for part in stretches for rows, i in part
    ]
    return own, other, masks, refs[2 * count :]


def later_kernel(stretches, special_real, mask, *refs):
    own, other, masks, refs = joined(stretches, mask, refs)
    weights, queries, special_queries = refs[:3]
    state_in, state_out = refs[3:7], refs[7:]
    pairs, rows = queries.shape[0], queries.shape[2] // 2
    state = State(rows, state_out)
    for result in attend_all(
        projector(own, other, weights), masks, lambda pair: queries[pair], lambda: special_queries[...],
        State(rows, state_in), pairs, rows, special_real,
    ):
        state.put(*result)


def last_kernel(stretches, special_real, mask, *refs):
    own, other, masks, refs = joined(stretches, mask, refs)
    weights, queries, special_queries = refs[:3]
    state_in = refs[3:7]
    w_out, kept_out, sent_out, w_here, copied = refs[7:]
    copy = pltpu.make_async_copy(w_out, w_here, copied)
    copy.start()
    pairs, rows = queries.shape[0], queries.shape[2] // 2
    columns, out, special = [], None, None
    sides = halves(kept_out.shape[1])
    for pair, sub, _, total, weight in attend_all(
        projector(own, other, weights), masks, lambda pair: queries[pair], lambda: special_queries[...],
        State(rows, state_in), pairs, rows, special_real,
    ):
        if pair == 0 and sub == 0:
            copy.wait()
        share = total * (1.0 / weight)
        if pair == pairs:
            row = lax.broadcasted_iota(jnp.int32, share.shape, 0) // HEAD_DIM
            lane = lax.broadcasted_iota(jnp.int32, share.shape, 1) // TILE_ROWS
            share = jnp.transpose(jnp.where(row == lane, share, 0.0))
            share = sum(share[i * TILE_ROWS : (i + 1) * TILE_ROWS] for i in range(2 * pairs))
            special = [product(share.astype(jnp.bfloat16), w_here[:, side]) for side in sides]
            continue
        columns.append(share)
        if pair % 2 == 1 and sub == 1:
            quad = jnp.transpose(jnp.concatenate(columns, axis=0)).astype(jnp.bfloat16)
            features = slice((pair // 2) * QUAD, (pair // 2 + 1) * QUAD)
            added = [product(quad, w_here[features, side]) for side in sides]
            out = added if out is None else [before + more for before, more in zip(out, added)]
            columns = []
    for place, values in ((slice(0, rows), out), (slice(rows, kept_out.shape[0]), special)):
        sent_out[place, :] = values[1].astype(jnp.bfloat16)
        kept_out[place, :] = values[0]


def end_kernel(images, kept, received, patch_out, special_out):
    patch_total = patch_out.shape[0]
    special_count = special_out.shape[0]
    patch_out[...] = (kept[:patch_total, :] + received[:patch_total, :].astype(jnp.float32)).astype(
        jnp.bfloat16
    )
    rest = kept[patch_total:, :] + received[patch_total:, :].astype(jnp.float32)
    rows = [rest[b * special_count : (b + 1) * special_count][:, None, :] for b in range(images)]
    special_out[...] = jnp.concatenate(rows, axis=1).astype(jnp.bfloat16)


def call(kernel, out_shape, operands, in_specs=None, out_specs=None, scratch=(), flops=0):
    if in_specs:
        operands = [
            pltpu.with_memory_space_constraint(operand, pltpu.HBM) if spec is HBM else operand
            for operand, spec in zip(operands, in_specs)
        ]
    return pl.pallas_call(
        kernel,
        out_shape=out_shape,
        in_specs=in_specs or [VMEM] * len(operands),
        out_specs=out_specs or [VMEM] * len(out_shape),
        scratch_shapes=scratch,
        compiler_params=pltpu.CompilerParams(vmem_limit_bytes=VMEM_BYTES),
        cost_estimate=pl.CostEstimate(flops=flops, transcendentals=0, bytes_accessed=0),
    )(*operands)


def pair_kernel(first, second, out):
    out[0] = first[...]
    out[1] = second[...]


def stack_kernel(first, second, out):
    count = first.shape[1]
    out[:, :count, :] = first[...]
    out[:, count:, :] = second[...]


def stacked(first, second, flops=0):
    shape = jax.ShapeDtypeStruct((2, 2 * first.shape[1], first.shape[2]), first.dtype)
    return call(stack_kernel, [shape], (first, second), flops=flops)[0]


def after(array, *others):
    return lax.optimization_barrier((array, *others))[0]


def per_device(
    patch_rows, special_rows, role_first, role_rest, frame_order, covisible, w_qkv, w_out
):
    images, per_image, width = patch_rows.shape
    special_count = special_rows.shape[1]
    real_rows = images * special_count
    special_block = real_rows + -real_rows % TILE_ROWS
    owner_count = lax.axis_size("blk")
    reach = max(1, owner_count // 64)
    patch_total = images * per_image
    rows = patch_total + special_block
    cut = per_image * max(1, images // 2)
    heads = width // HEAD_DIM
    pairs = heads // 2
    paired = reach == 1 and owner_count % 2 == 0

    if paired:
        offsets = [0, (-1, 1), (1, -1)]
    else:
        offsets = [0] + [sign * d for d in range(1, reach + 1) for sign in (-1, 1)]
    mask_rows = -(-len(offsets) * images // 8) * 8
    bf16 = lambda *shape: jax.ShapeDtypeStruct(shape, jnp.bfloat16)
    f32 = lambda *shape: jax.ShapeDtypeStruct(shape, jnp.float32)
    state_shape = [
        f32(8, 2 * patch_total),
        f32(8, 2 * patch_total),
        f32(pairs, HEAD_DIM, 2 * patch_total),
        f32(width, heads * special_block),
    ]

    both = lambda part: (part, swapped(part, "head", 1))
    patches = patch_rows.reshape(patch_total, width)
    turned = jnp.transpose(special_rows, (1, 0, 2))
    power = owner_count >= 8 and owner_count & (owner_count - 1) == 0
    specials, own, *pieces = call(
        rows_kernel,
        [
            bf16(special_block, width),
            bf16(patch_total, width),
            bf16(cut, width),
            bf16(patch_total - cut, width),
        ],
        (frame_order, turned, role_first, role_rest, patches),
        in_specs=[HBM] * 5,
        scratch=[
            pltpu.SMEM(frame_order.shape, jnp.int32),
            pltpu.VMEM(turned.shape, jnp.bfloat16),
            pltpu.VMEM(role_first.shape, jnp.bfloat16),
            pltpu.VMEM(role_rest.shape, jnp.bfloat16),
            pltpu.SemaphoreType.DMA((7,)),
        ],
    )
    bits = [1 << i for i in range(1, owner_count.bit_length() - 1)] + [1] if power else []
    (specials,) = call(pair_kernel, [bf16(2, special_block, width)], both(specials))
    everywhere = specials
    if paired and power:
        everywhere = stacked(specials, swapped(specials, "blk", bits[0]), FIRST)
    mask, weights = call(
        functools.partial(start_kernel, offsets, per_image, special_count, special_block),
        [
            f32(mask_rows, patch_total + heads * special_block),
            bf16(*w_qkv.shape),
        ],
        (covisible, w_qkv),
        in_specs=[HBM] * 2,
        scratch=[pltpu.SMEM(covisible.shape, jnp.int32), pltpu.SemaphoreType.DMA((1 + 3,))],
    )
    queries, special_queries, *state = call(
        functools.partial(first_kernel, images),
        [bf16(pairs, PAIR, 2 * patch_total), bf16(width, heads * special_block), *state_shape],
        (mask, own, swapped(patches, "head", 1), specials, weights),
    )
    fixed = (weights, queries, special_queries)

    def later(stretches, parts, state):
        return call(
            functools.partial(later_kernel, stretches, real_rows),
            state_shape,
            (mask, *[part[0] for part in parts], *[part[1] for part in parts], *fixed, *state),
        )

    image_rows = lambda owner: [(per_image, owner * images + b) for b in range(images)]
    def halved(part, gate):
        part = after(part, gate)
        starts = range(0, part.shape[0], per_image)
        return [both(part[start : start + per_image]) for start in starts]

    stretches = lambda owner, first, last: [[image] for image in image_rows(owner)[first:last]]
    if paired:
        far = after(crossed(patches, "blk"), state[0])
        near = [swapped(pieces[0], "blk", 1), swapped(after(pieces[1], far), "blk", 1)]
        if power:
            everywhere = after(everywhere, far)
            for bit in bits[1:-2]:
                everywhere = stacked(everywhere, swapped(everywhere, "blk", bit))
            arrived = swapped(everywhere, "blk", bits[-2])
        state = later(stretches(1, 0, images), halved(far, state[0]), state)
        if power:
            everywhere = stacked(after(everywhere, state[0]), arrived, FIRST)
            arrived = swapped(everywhere, "blk", bits[-1])
        near = [halved(part, state[0]) for part in near]
        count = len(near[0])
        state = later(stretches(2, 0, count), near[0], state)
        if power:
            everywhere = stacked(after(everywhere, state[0]), arrived, LAST)
        last_stretches, parts = stretches(2, count, images), near[1]
    else:
        for i, offset in enumerate(offsets[1:]):
            parts = halved(shifted(patches, "blk", -offset), state[0])
            last_stretches = stretches(i + 1, 0, images)
            if i < len(offsets) - 2:
                state = later(last_stretches, parts, state)
    if not (paired and power):
        everywhere = lax.all_gather(specials, "blk", axis=1, tiled=True)
    stretches = last_stretches + [[(everywhere.shape[1], None)]]
    parts = parts + [(everywhere, everywhere)]
    kept, sent = call(
        functools.partial(last_kernel, stretches, real_rows),
        [f32(rows, width), bf16(rows, width)],
        (
            mask, *[part[0] for part in parts], *[part[1] for part in parts], *fixed, *state, w_out,
        ),
        in_specs=[VMEM] * (1 + 2 * len(parts) + len(fixed) + len(state)) + [HBM],
        scratch=[pltpu.VMEM(w_out.shape, jnp.bfloat16), pltpu.SemaphoreType.DMA],
    )
    received = swapped(sent, "head", 1)
    patch_out, special_out = call(
        functools.partial(end_kernel, images),
        [bf16(patch_total, width), bf16(special_count, images, width)],
        (kept, received),
        out_specs=[pl.BlockSpec(), pl.BlockSpec()],
    )
    return patch_out.reshape(patch_rows.shape), jnp.transpose(special_out, (1, 0, 2))


def solution(mesh):
    in_specs = (
        P(("scene", "blk"), None, "head"),
        P(("scene", "blk"), None, "head"),
        P(),
        P(),
        P(("scene", "blk")),
        P(("scene", "blk"), None),
        P(None, None, "head"),
        P("head", None),
    )
    out_specs = (P(("scene", "blk"), None, "head"), P(("scene", "blk"), None, "head"))
    return jax.shard_map(
        per_device, mesh=mesh, in_specs=in_specs, out_specs=out_specs, check_vma=False
    )
```

```python
import functools

import jax
import jax.numpy as jnp
from jax import lax
from jax.experimental import pallas as pl
from jax.experimental.pallas import tpu as pltpu
from jax.sharding import PartitionSpec as P

HEAD_DIM = 64
PAIR = 2 * HEAD_DIM
QUAD = 2 * PAIR
TILE_ROWS = 16
LOG2_E = 1.4426950408889634
FIRST = 20_000_000_000
VMEM_BYTES = 32 * 1024 * 1024
SMEM = pl.BlockSpec(memory_space=pltpu.SMEM)
VMEM = pl.BlockSpec(memory_space=pltpu.VMEM)
HBM = pl.BlockSpec(memory_space=pltpu.HBM)


def shifted(block, axis, distance):
    count = lax.axis_size(axis)
    route = [((i - distance) % count, i) for i in range(count)]
    return lax.ppermute(block, axis, route)


def swapped(block, axis, bit):
    count = lax.axis_size(axis)
    return lax.ppermute(block, axis, [(i ^ bit, i) for i in range(count)])


def crossed(block, axis):
    count = lax.axis_size(axis)
    return lax.ppermute(block, axis, [(i, (i + (-1 if i % 2 == 0 else 1)) % count) for i in range(count)])


def halves(width):
    half = lax.axis_index("head")
    mine = pl.ds(pl.multiple_of(half * width, width), width)
    theirs = pl.ds(pl.multiple_of((1 - half) * width, width), width)
    return mine, theirs


def product(left, right):
    return jnp.dot(left, right, preferred_element_type=jnp.float32)


def owner_at(offset):
    count = lax.axis_size("blk")
    here = lax.axis_index("blk")
    if isinstance(offset, tuple):
        offset = jnp.where(lax.rem(here, 2) == 0, offset[0], offset[1])
    return lax.rem(here + offset + count, count)


def rows_kernel(
    frame_order, specials, role_first, role_rest, patches,
    special_out, patches_out, order, here, first_rows, rest_rows, copied,
):
    special_count, images, width = specials.shape
    moves = [(specials, here), (role_first, first_rows), (role_rest, rest_rows), (frame_order, order)]
    moves.append((patches, patches_out))
    copies = [
        pltpu.make_async_copy(source, target, copied.at[i]) for i, (source, target) in enumerate(moves)
    ]
    for copy in copies:
        copy.start()
    for copy in copies[:4]:
        copy.wait()
    mine, _ = halves(width)
    first = first_rows[:, mine].astype(jnp.float32)
    rest = rest_rows[:, mine].astype(jnp.float32)
    summed = [
        here[:, b, :].astype(jnp.float32) + jnp.where(order[b] == 0, first, rest) for b in range(images)
    ]
    summed.append(jnp.zeros((special_out.shape[0] - images * special_count, width), jnp.float32))
    special_out[...] = jnp.concatenate(summed, axis=0).astype(jnp.bfloat16)
    for copy in copies[4:]:
        copy.wait()


def start_kernel(
    offsets, per_image, special_count, special_total, covisible, w_qkv, mask_out, weights_out, seen, copied
):
    images = covisible.shape[0]
    patch_total = images * per_image
    moves = [(covisible, seen)]
    depth = w_qkv.shape[1] // 2
    for i in range(3):
        for j, rows in enumerate(halves(depth)):
            moves.append((w_qkv.at[i, rows], weights_out.at[i, pl.ds(j * depth, depth)]))
    copies = [
        pltpu.make_async_copy(source, target, copied.at[i]) for i, (source, target) in enumerate(moves)
    ]
    for copy in copies:
        copy.start()
    copies[0].wait()
    lane = lax.broadcasted_iota(jnp.int32, (1, mask_out.shape[1]), 1)
    special_lane = lax.rem(lane - patch_total, special_total)
    image = jnp.where(
        lane < patch_total, lane // per_image, jnp.minimum(special_lane // special_count, images - 1)
    )
    for i, offset in enumerate(offsets):
        for b in range(images):
            row = jnp.zeros(lane.shape, jnp.float32)
            for a in range(images):
                hidden = seen[a, owner_at(offset) * images + b] <= 0
                row = jnp.where((image == a) & hidden, -jnp.inf, row)
            mask_out[i * images + b : i * images + b + 1, :] = row
    for copy in copies[1:]:
        copy.wait()


def projector(own, other, weights):
    rows = jnp.concatenate([own, other], axis=1)

    def columns(which, quad):
        return product(rows, weights[which, :, quad * QUAD : (quad + 1) * QUAD])

    return columns


def attend(scores, masks, state):
    largest = state
    start = 0
    for count, mask in masks:
        part = jnp.max(scores[start : start + count], axis=0, keepdims=True)
        part = part if mask is None else part + mask
        largest = part if largest is None else jnp.maximum(largest, part)
        start += count
    weights, start = [], 0
    for count, mask in masks:
        level = largest if mask is None else largest - mask
        weights.append(jnp.exp2((scores[start : start + count] - level).astype(jnp.bfloat16)))
        start += count
    factor = None if state is None else jnp.exp2(state - largest)
    return largest, factor, jnp.concatenate(weights, axis=0)


def attend_all(columns, masks, queries_of, special_queries, state, pairs, rows, special_real):
    keys, values = {}, {}
    quads = pairs // 2

    def keys_of(quad):
        if quad not in keys:
            keys[quad] = columns(1, quad).astype(jnp.bfloat16)
        return keys[quad]

    def values_of(quad):
        if quad not in values:
            values[quad] = jnp.transpose(columns(2, quad).astype(jnp.bfloat16))
        return values[quad]

    def prepared(pair):
        if pair == pairs:
            scores = product(
                jnp.concatenate([keys_of(quad) for quad in range(quads)], axis=1), special_queries()
            )
        else:
            lanes = slice((pair % 2) * PAIR, (pair % 2 + 1) * PAIR)
            scores = product(keys_of(pair // 2)[:, lanes], queries_of(pair))
        if all(mask is not None for _, mask in masks):
            return scores
        parts, start = [], 0
        for count, mask in masks:
            part = scores[start : start + count]
            if mask is None:
                key_row = lax.broadcasted_iota(jnp.int32, (count, 1), 0)
                part = jnp.where(lax.rem(key_row, TILE_ROWS) < special_real, part, -jnp.inf)
            parts.append(part)
            start += count
        return jnp.concatenate(parts, axis=0)

    ones = jnp.ones((TILE_ROWS, sum(count for count, _ in masks)), jnp.bfloat16)
    both = [
        (count, None if mask is None else jnp.concatenate([mask[:, :rows]] * 2, axis=1))
        for count, mask in masks
    ]
    only = [(count, None if mask is None else mask[:, rows:]) for count, mask in masks]
    order = list(range(pairs))
    order.insert(pairs - 2, pairs)
    scores = prepared(order[0])
    for step, pair in enumerate(order):
        if pair < pairs:
            left = values_of(pair // 2)[(pair % 2) * PAIR : (pair % 2 + 1) * PAIR]
        else:
            left = jnp.concatenate([values_of(quad) for quad in range(quads)], axis=0)
        following = prepared(order[step + 1]) if step < pairs else None
        largest, factor, weights = attend(
            scores, both if pair < pairs else only, state and state.largest(pair)
        )
        added = product(jnp.concatenate([left, ones], axis=0), weights)
        height, subs = (HEAD_DIM, 2) if pair < pairs else (left.shape[0], 1)
        width = scores.shape[1] // subs
        for sub in range(subs):
            lanes = slice(sub * width, (sub + 1) * width)
            total = added[sub * height : (sub + 1) * height, lanes]
            weight = added[left.shape[0] : left.shape[0] + 1, lanes]
            if state is not None:
                total = total + state.total(pair, sub) * factor[:, lanes]
                weight = weight + state.weight(pair, sub) * factor[:, lanes]
            yield pair, sub, largest[:, lanes], total, weight
        scores = following


class State:
    def __init__(self, rows, refs):
        self.rows = rows
        self.largest_ref, self.weight_ref, self.total_ref, self.special_ref = refs

    def lanes(self, pair, sub):
        if pair == self.total_ref.shape[0]:
            return slice(0, self.special_ref.shape[1])
        return slice(sub * self.rows, (sub + 1) * self.rows)

    def largest(self, pair):
        stop = self.special_ref.shape[1] if pair == self.total_ref.shape[0] else 2 * self.rows
        return self.largest_ref[pair : pair + 1, 0:stop]

    def weight(self, pair, sub):
        return self.weight_ref[pair : pair + 1, self.lanes(pair, sub)]

    def total(self, pair, sub):
        if pair == self.total_ref.shape[0]:
            return self.special_ref[...]
        return self.total_ref[pair, :, self.lanes(pair, sub)]

    def put(self, pair, sub, largest, total, weight):
        lanes = self.lanes(pair, sub)
        self.largest_ref[pair : pair + 1, lanes] = largest
        self.weight_ref[pair : pair + 1, lanes] = weight
        if pair == self.total_ref.shape[0]:
            self.special_ref[...] = total
        else:
            self.total_ref[pair, :, lanes] = total


def first_kernel(
    images, mask, own, other, special, weights, queries_out, special_out, *state_out
):
    patch_total = own.shape[0]
    columns = projector(
        jnp.concatenate([own[...], special[0]], axis=0),
        jnp.concatenate([other[...], special[1]], axis=0),
        weights,
    )
    pairs = queries_out.shape[0]
    zero = jnp.zeros((HEAD_DIM, patch_total), jnp.bfloat16)
    made = {}

    def patch_columns(which, quad):
        return columns(which, quad)[:patch_total]

    def columns_of(quad):
        if quad not in made:
            queries = columns(0, quad) * (HEAD_DIM ** (-0.5) * LOG2_E)
            made[quad] = queries[patch_total:]
            turned = jnp.transpose(queries[:patch_total].astype(jnp.bfloat16))
            for i in range(2):
                first = i * PAIR
                upper = jnp.concatenate([turned[first : first + HEAD_DIM], zero], axis=1)
                lower = jnp.concatenate([zero, turned[first + HEAD_DIM : first + PAIR]], axis=1)
                queries_out[2 * quad + i] = jnp.concatenate([upper, lower], axis=0)
        return made[quad]

    def queries_of(pair):
        columns_of(pair // 2)
        return queries_out[pair]

    def special_queries():
        block = jnp.concatenate([columns_of(quad) for quad in range(pairs // 2)], axis=1)
        count = block.shape[0]
        block = jnp.concatenate([block] * (2 * pairs), axis=0)
        row = lax.broadcasted_iota(jnp.int32, block.shape, 0) // count
        lane = lax.broadcasted_iota(jnp.int32, block.shape, 1) // HEAD_DIM
        block = jnp.transpose(jnp.where(row == lane, block, 0.0).astype(jnp.bfloat16))
        special_out[...] = block
        return block

    per_image = patch_total // images
    masks = [(per_image, mask[b : b + 1, :]) for b in range(images)]
    state = State(patch_total, state_out)
    for result in attend_all(
        patch_columns, masks, queries_of, special_queries, None, pairs, patch_total, 0
    ):
        state.put(*result)


def joined(stretches, mask, refs):
    count = len(stretches)
    flat = lambda ref, i: ref[i] if len(ref.shape) == 3 else ref[...]
    own = jnp.concatenate([flat(ref, 0) for ref in refs[:count]], axis=0)
    other = jnp.concatenate([flat(ref, 1) for ref in refs[count : 2 * count]], axis=0)
    masks = [
        (rows, None if i is None else mask[i : i + 1, :]) for part in stretches for rows, i in part
    ]
    return own, other, masks, refs[2 * count :]


def later_kernel(stretches, special_real, mask, *refs):
    own, other, masks, refs = joined(stretches, mask, refs)
    weights, queries, special_queries = refs[:3]
    state_in, state_out = refs[3:7], refs[7:]
    pairs, rows = queries.shape[0], queries.shape[2] // 2
    state = State(rows, state_out)
    for result in attend_all(
        projector(own, other, weights), masks, lambda pair: queries[pair], lambda: special_queries[...],
        State(rows, state_in), pairs, rows, special_real,
    ):
        state.put(*result)


def last_kernel(stretches, special_real, mask, *refs):
    own, other, masks, refs = joined(stretches, mask, refs)
    weights, queries, special_queries = refs[:3]
    state_in = refs[3:7]
    w_out, kept_out, sent_out, w_here, copied = refs[7:]
    copy = pltpu.make_async_copy(w_out, w_here, copied)
    copy.start()
    pairs, rows = queries.shape[0], queries.shape[2] // 2
    columns, out, special = [], None, None
    sides = halves(kept_out.shape[1])
    for pair, sub, _, total, weight in attend_all(
        projector(own, other, weights), masks, lambda pair: queries[pair], lambda: special_queries[...],
        State(rows, state_in), pairs, rows, special_real,
    ):
        if pair == 0 and sub == 0:
            copy.wait()
        share = total * (1.0 / weight)
        if pair == pairs:
            row = lax.broadcasted_iota(jnp.int32, share.shape, 0) // HEAD_DIM
            lane = lax.broadcasted_iota(jnp.int32, share.shape, 1) // TILE_ROWS
            share = jnp.transpose(jnp.where(row == lane, share, 0.0))
            share = sum(share[i * TILE_ROWS : (i + 1) * TILE_ROWS] for i in range(2 * pairs))
            special = [product(share.astype(jnp.bfloat16), w_here[:, side]) for side in sides]
            continue
        columns.append(share)
        if pair % 2 == 1 and sub == 1:
            quad = jnp.transpose(jnp.concatenate(columns, axis=0).astype(jnp.bfloat16))
            features = slice((pair // 2) * QUAD, (pair // 2 + 1) * QUAD)
            added = [product(quad, w_here[features, side]) for side in sides]
            out = added if out is None else [before + more for before, more in zip(out, added)]
            columns = []
    for place, values in ((slice(0, rows), out), (slice(rows, kept_out.shape[0]), special)):
        sent_out[place, :] = values[1].astype(jnp.bfloat16)
        kept_out[place, :] = values[0]


def end_kernel(images, kept, received, patch_out, special_out):
    patch_total = patch_out.shape[0]
    special_count = special_out.shape[0]
    patch_out[...] = (kept[:patch_total, :] + received[:patch_total, :].astype(jnp.float32)).astype(
        jnp.bfloat16
    )
    rest = kept[patch_total:, :] + received[patch_total:, :].astype(jnp.float32)
    rows = [rest[b * special_count : (b + 1) * special_count][:, None, :] for b in range(images)]
    special_out[...] = jnp.concatenate(rows, axis=1).astype(jnp.bfloat16)


def call(kernel, out_shape, operands, in_specs=None, out_specs=None, scratch=(), flops=0):
    if in_specs:
        operands = [
            pltpu.with_memory_space_constraint(operand, pltpu.HBM) if spec is HBM else operand
            for operand, spec in zip(operands, in_specs)
        ]
    return pl.pallas_call(
        kernel,
        out_shape=out_shape,
        in_specs=in_specs or [VMEM] * len(operands),
        out_specs=out_specs or [VMEM] * len(out_shape),
        scratch_shapes=scratch,
        compiler_params=pltpu.CompilerParams(vmem_limit_bytes=VMEM_BYTES),
        cost_estimate=pl.CostEstimate(flops=flops, transcendentals=0, bytes_accessed=0),
    )(*operands)


def pair_kernel(first, second, out):
    out[0] = first[...]
    out[1] = second[...]


def stack_kernel(first, second, out):
    count = first.shape[1]
    out[:, :count, :] = first[...]
    out[:, count:, :] = second[...]


def stacked(first, second, flops=0):
    shape = jax.ShapeDtypeStruct((2, 2 * first.shape[1], first.shape[2]), first.dtype)
    return call(stack_kernel, [shape], (first, second), flops=flops)[0]


def after(array, *others):
    return lax.optimization_barrier((array, *others))[0]


def per_device(
    patch_rows, special_rows, role_first, role_rest, frame_order, covisible, w_qkv, w_out
):
    images, per_image, width = patch_rows.shape
    special_count = special_rows.shape[1]
    real_rows = images * special_count
    special_block = real_rows + -real_rows % TILE_ROWS
    owner_count = lax.axis_size("blk")
    reach = max(1, owner_count // 64)
    patch_total = images * per_image
    rows = patch_total + special_block
    heads = width // HEAD_DIM
    pairs = heads // 2
    paired = reach == 1 and owner_count % 2 == 0

    if paired:
        offsets = [0, (-1, 1), (1, -1)]
    else:
        offsets = [0] + [sign * d for d in range(1, reach + 1) for sign in (-1, 1)]
    mask_rows = -(-len(offsets) * images // 8) * 8
    bf16 = lambda *shape: jax.ShapeDtypeStruct(shape, jnp.bfloat16)
    f32 = lambda *shape: jax.ShapeDtypeStruct(shape, jnp.float32)
    state_shape = [
        f32(8, 2 * patch_total),
        f32(8, 2 * patch_total),
        f32(pairs, HEAD_DIM, 2 * patch_total),
        f32(width, heads * special_block),
    ]

    both = lambda part: (part, swapped(part, "head", 1))
    patches = patch_rows.reshape(patch_total, width)
    turned = jnp.transpose(special_rows, (1, 0, 2))
    power = owner_count >= 8 and owner_count & (owner_count - 1) == 0
    specials, own = call(
        rows_kernel,
        [
            bf16(special_block, width),
            bf16(patch_total, width),
        ],
        (frame_order, turned, role_first, role_rest, patches),
        in_specs=[HBM] * 5,
        scratch=[
            pltpu.SMEM(frame_order.shape, jnp.int32),
            pltpu.VMEM(turned.shape, jnp.bfloat16),
            pltpu.VMEM(role_first.shape, jnp.bfloat16),
            pltpu.VMEM(role_rest.shape, jnp.bfloat16),
            pltpu.SemaphoreType.DMA((5,)),
        ],
    )
    bits = [1 << i for i in range(1, owner_count.bit_length() - 1)] + [1] if power else []
    (specials,) = call(pair_kernel, [bf16(2, special_block, width)], both(specials))
    everywhere = specials
    if paired and power:
        everywhere = stacked(specials, swapped(specials, "blk", bits[0]), FIRST)
    mask, weights = call(
        functools.partial(start_kernel, offsets, per_image, special_count, special_block),
        [
            f32(mask_rows, patch_total + heads * special_block),
            bf16(*w_qkv.shape),
        ],
        (covisible, w_qkv),
        in_specs=[HBM] * 2,
        scratch=[pltpu.SMEM(covisible.shape, jnp.int32), pltpu.SemaphoreType.DMA((1 + 6,))],
    )
    queries, special_queries, *state = call(
        functools.partial(first_kernel, images),
        [bf16(pairs, PAIR, 2 * patch_total), bf16(width, heads * special_block), *state_shape],
        (mask, own, swapped(patches, "head", 1), specials, weights),
    )
    fixed = (weights, queries, special_queries)

    def later(stretches, parts, state):
        return call(
            functools.partial(later_kernel, stretches, real_rows),
            state_shape,
            (mask, *[part[0] for part in parts], *[part[1] for part in parts], *fixed, *state),
        )

    image_rows = lambda owner: [(per_image, owner * images + b) for b in range(images)]
    def halved(part, gate):
        part = after(part, gate)
        starts = range(0, part.shape[0], per_image)
        return [both(part[start : start + per_image]) for start in starts]

    stretches = lambda owner: [[image] for image in image_rows(owner)]
    if paired:
        far = after(crossed(patches, "blk"), state[0])
        near = swapped(patches, "blk", 1)
        if power:
            everywhere = after(everywhere, far)
            for bit in bits[1:-2]:
                everywhere = stacked(everywhere, swapped(everywhere, "blk", bit))
            arrived = swapped(everywhere, "blk", bits[-2])
        state = later(stretches(1), halved(far, state[0]), state)
        if power:
            everywhere = stacked(after(everywhere, state[0]), arrived, FIRST)
            arrived = swapped(everywhere, "blk", bits[-1])
        state = later(stretches(2), halved(near, state[0]), state)
        if power:
            everywhere = stacked(after(everywhere, state[0]), arrived)
    else:
        for i, offset in enumerate(offsets[1:]):
            state = later(stretches(i + 1), halved(shifted(patches, "blk", -offset), state[0]), state)
    if not (paired and power):
        everywhere = lax.all_gather(specials, "blk", axis=1, tiled=True)
    stretches, parts = [[(everywhere.shape[1], None)]], [(everywhere, everywhere)]
    kept, sent = call(
        functools.partial(last_kernel, stretches, real_rows),
        [f32(rows, width), bf16(rows, width)],
        (
            mask, *[part[0] for part in parts], *[part[1] for part in parts], *fixed, *state, w_out,
        ),
        in_specs=[VMEM] * (1 + 2 * len(parts) + len(fixed) + len(state)) + [HBM],
        scratch=[pltpu.VMEM(w_out.shape, jnp.bfloat16), pltpu.SemaphoreType.DMA],
    )
    received = swapped(sent, "head", 1)
    patch_out, special_out = call(
        functools.partial(end_kernel, images),
        [bf16(patch_total, width), bf16(special_count, images, width)],
        (kept, received),
        out_specs=[pl.BlockSpec(), pl.BlockSpec()],
    )
    return patch_out.reshape(patch_rows.shape), jnp.transpose(special_out, (1, 0, 2))


def solution(mesh):
    in_specs = (
        P(("scene", "blk"), None, "head"),
        P(("scene", "blk"), None, "head"),
        P(),
        P(),
        P(("scene", "blk")),
        P(("scene", "blk"), None),
        P(None, None, "head"),
        P("head", None),
    )
    out_specs = (P(("scene", "blk"), None, "head"), P(("scene", "blk"), None, "head"))
    return jax.shard_map(
        per_device, mesh=mesh, in_specs=in_specs, out_specs=out_specs, check_vma=False
    )
```

```python
import functools

import jax
import jax.numpy as jnp
from jax import lax
from jax.experimental import pallas as pl
from jax.experimental.pallas import tpu as pltpu
from jax.sharding import PartitionSpec as P

HEAD_DIM = 64
PAIR = 2 * HEAD_DIM
QUAD = 2 * PAIR
TILE_ROWS = 16
LOG2_E = 1.4426950408889634
FIRST = 20_000_000_000
VMEM_BYTES = 32 * 1024 * 1024
SMEM = pl.BlockSpec(memory_space=pltpu.SMEM)
VMEM = pl.BlockSpec(memory_space=pltpu.VMEM)
HBM = pl.BlockSpec(memory_space=pltpu.HBM)


def shifted(block, axis, distance):
    count = lax.axis_size(axis)
    route = [((i - distance) % count, i) for i in range(count)]
    return lax.ppermute(block, axis, route)


def swapped(block, axis, bit):
    count = lax.axis_size(axis)
    return lax.ppermute(block, axis, [(i ^ bit, i) for i in range(count)])


def crossed(block, axis):
    count = lax.axis_size(axis)
    return lax.ppermute(block, axis, [(i, (i + (-1 if i % 2 == 0 else 1)) % count) for i in range(count)])


def halves(width):
    half = lax.axis_index("head")
    mine = pl.ds(pl.multiple_of(half * width, width), width)
    theirs = pl.ds(pl.multiple_of((1 - half) * width, width), width)
    return mine, theirs


def product(left, right):
    return jnp.dot(left, right, preferred_element_type=jnp.float32)


def owner_at(offset):
    count = lax.axis_size("blk")
    here = lax.axis_index("blk")
    if isinstance(offset, tuple):
        offset = jnp.where(lax.rem(here, 2) == 0, offset[0], offset[1])
    return lax.rem(here + offset + count, count)


def rows_kernel(
    frame_order, specials, role_first, role_rest, patches,
    special_out, patches_out, early_out, late_out, order, here, first_rows, rest_rows, copied,
):
    cut = early_out.shape[0]
    special_count, images, width = specials.shape
    moves = [(specials, here), (role_first, first_rows), (role_rest, rest_rows), (frame_order, order)]
    moves.append((patches.at[pl.ds(0, cut)], early_out))
    moves.append((patches, patches_out))
    moves.append((patches.at[pl.ds(cut, late_out.shape[0])], late_out))
    copies = [
        pltpu.make_async_copy(source, target, copied.at[i]) for i, (source, target) in enumerate(moves)
    ]
    for copy in copies:
        copy.start()
    for copy in copies[:4]:
        copy.wait()
    mine, _ = halves(width)
    first = first_rows[:, mine].astype(jnp.float32)
    rest = rest_rows[:, mine].astype(jnp.float32)
    summed = [
        here[:, b, :].astype(jnp.float32) + jnp.where(order[b] == 0, first, rest) for b in range(images)
    ]
    summed.append(jnp.zeros((special_out.shape[0] - images * special_count, width), jnp.float32))
    special_out[...] = jnp.concatenate(summed, axis=0).astype(jnp.bfloat16)
    for copy in copies[4:]:
        copy.wait()


def start_kernel(
    offsets, per_image, special_count, special_total, covisible, w_qkv, mask_out, weights_out, seen, copied
):
    images = covisible.shape[0]
    patch_total = images * per_image
    moves = [(covisible, seen)]
    depth = w_qkv.shape[1] // 2
    for i in range(3):
        for j, rows in enumerate(halves(depth)):
            moves.append((w_qkv.at[i, rows], weights_out.at[i, pl.ds(j * depth, depth)]))
    copies = [
        pltpu.make_async_copy(source, target, copied.at[i]) for i, (source, target) in enumerate(moves)
    ]
    for copy in copies:
        copy.start()
    copies[0].wait()
    lane = lax.broadcasted_iota(jnp.int32, (1, mask_out.shape[1]), 1)
    special_lane = lax.rem(lane - patch_total, special_total)
    image = jnp.where(
        lane < patch_total, lane // per_image, jnp.minimum(special_lane // special_count, images - 1)
    )
    for i, offset in enumerate(offsets):
        for b in range(images):
            row = jnp.zeros(lane.shape, jnp.float32)
            for a in range(images):
                hidden = seen[a, owner_at(offset) * images + b] <= 0
                row = jnp.where((image == a) & hidden, -jnp.inf, row)
            mask_out[i * images + b : i * images + b + 1, :] = row
    for copy in copies[1:]:
        copy.wait()


def projector(own, other, weights):
    rows = jnp.concatenate([own, other], axis=1)

    def columns(which, quad):
        return product(rows, weights[which, :, quad * QUAD : (quad + 1) * QUAD])

    return columns


def attend(scores, masks, state):
    largest = state
    start = 0
    for count, mask in masks:
        part = jnp.max(scores[start : start + count], axis=0, keepdims=True)
        part = part if mask is None else part + mask
        largest = part if largest is None else jnp.maximum(largest, part)
        start += count
    weights, start = [], 0
    for count, mask in masks:
        level = largest if mask is None else largest - mask
        weights.append(jnp.exp2((scores[start : start + count] - level).astype(jnp.bfloat16)))
        start += count
    factor = None if state is None else jnp.exp2(state - largest)
    return largest, factor, jnp.concatenate(weights, axis=0)


def attend_all(columns, masks, queries_of, special_queries, state, pairs, rows, special_real):
    keys, values = {}, {}
    quads = pairs // 2

    def keys_of(quad):
        if quad not in keys:
            keys[quad] = columns(1, quad).astype(jnp.bfloat16)
        return keys[quad]

    def values_of(quad):
        if quad not in values:
            values[quad] = jnp.transpose(columns(2, quad).astype(jnp.bfloat16))
        return values[quad]

    def prepared(pair):
        if pair == pairs:
            scores = product(
                jnp.concatenate([keys_of(quad) for quad in range(quads)], axis=1), special_queries()
            )
        else:
            lanes = slice((pair % 2) * PAIR, (pair % 2 + 1) * PAIR)
            scores = product(keys_of(pair // 2)[:, lanes], queries_of(pair))
        if all(mask is not None for _, mask in masks):
            return scores
        parts, start = [], 0
        for count, mask in masks:
            part = scores[start : start + count]
            if mask is None:
                key_row = lax.broadcasted_iota(jnp.int32, (count, 1), 0)
                part = jnp.where(lax.rem(key_row, TILE_ROWS) < special_real, part, -jnp.inf)
            parts.append(part)
            start += count
        return jnp.concatenate(parts, axis=0)

    ones = jnp.ones((TILE_ROWS, sum(count for count, _ in masks)), jnp.bfloat16)
    both = [
        (count, None if mask is None else jnp.concatenate([mask[:, :rows]] * 2, axis=1))
        for count, mask in masks
    ]
    only = [(count, None if mask is None else mask[:, rows:]) for count, mask in masks]
    order = list(range(pairs))
    order.insert(pairs - 2, pairs)
    scores = prepared(order[0])
    for step, pair in enumerate(order):
        if pair < pairs:
            left = values_of(pair // 2)[(pair % 2) * PAIR : (pair % 2 + 1) * PAIR]
        else:
            left = jnp.concatenate([values_of(quad) for quad in range(quads)], axis=0)
        following = prepared(order[step + 1]) if step < pairs else None
        largest, factor, weights = attend(
            scores, both if pair < pairs else only, state and state.largest(pair)
        )
        added = product(jnp.concatenate([left, ones], axis=0), weights)
        height, subs = (HEAD_DIM, 2) if pair < pairs else (left.shape[0], 1)
        width = scores.shape[1] // subs
        for sub in range(subs):
            lanes = slice(sub * width, (sub + 1) * width)
            total = added[sub * height : (sub + 1) * height, lanes]
            weight = added[left.shape[0] : left.shape[0] + 1, lanes]
            if state is not None:
                total = total + state.total(pair, sub) * factor[:, lanes]
                weight = weight + state.weight(pair, sub) * factor[:, lanes]
            yield pair, sub, largest[:, lanes], total, weight
        scores = following


class State:
    def __init__(self, rows, refs):
        self.rows = rows
        self.largest_ref, self.weight_ref, self.total_ref, self.special_ref = refs

    def lanes(self, pair, sub):
        if pair == self.total_ref.shape[0]:
            return slice(0, self.special_ref.shape[1])
        return slice(sub * self.rows, (sub + 1) * self.rows)

    def largest(self, pair):
        stop = self.special_ref.shape[1] if pair == self.total_ref.shape[0] else 2 * self.rows
        return self.largest_ref[pair : pair + 1, 0:stop]

    def weight(self, pair, sub):
        return self.weight_ref[pair : pair + 1, self.lanes(pair, sub)]

    def total(self, pair, sub):
        if pair == self.total_ref.shape[0]:
            return self.special_ref[...]
        return self.total_ref[pair, :, self.lanes(pair, sub)]

    def put(self, pair, sub, largest, total, weight):
        lanes = self.lanes(pair, sub)
        self.largest_ref[pair : pair + 1, lanes] = largest
        self.weight_ref[pair : pair + 1, lanes] = weight
        if pair == self.total_ref.shape[0]:
            self.special_ref[...] = total
        else:
            self.total_ref[pair, :, lanes] = total


def first_kernel(
    images, special_block, mask, own, other, special, weights, queries_out, special_out, *state_out
):
    patch_total = own.shape[0]
    columns = projector(
        jnp.concatenate([own[...], special[0, :special_block, :]], axis=0),
        jnp.concatenate([other[...], special[1, :special_block, :]], axis=0),
        weights,
    )
    pairs = queries_out.shape[0]
    zero = jnp.zeros((HEAD_DIM, patch_total), jnp.bfloat16)
    made = {}

    def patch_columns(which, quad):
        return columns(which, quad)[:patch_total]

    def columns_of(quad):
        if quad not in made:
            queries = columns(0, quad) * (HEAD_DIM ** (-0.5) * LOG2_E)
            made[quad] = queries[patch_total:]
            turned = jnp.transpose(queries[:patch_total].astype(jnp.bfloat16))
            for i in range(2):
                first = i * PAIR
                upper = jnp.concatenate([turned[first : first + HEAD_DIM], zero], axis=1)
                lower = jnp.concatenate([zero, turned[first + HEAD_DIM : first + PAIR]], axis=1)
                queries_out[2 * quad + i] = jnp.concatenate([upper, lower], axis=0)
        return made[quad]

    def queries_of(pair):
        columns_of(pair // 2)
        return queries_out[pair]

    def special_queries():
        block = jnp.concatenate([columns_of(quad) for quad in range(pairs // 2)], axis=1)
        count = block.shape[0]
        block = jnp.concatenate([block] * (2 * pairs), axis=0)
        row = lax.broadcasted_iota(jnp.int32, block.shape, 0) // count
        lane = lax.broadcasted_iota(jnp.int32, block.shape, 1) // HEAD_DIM
        block = jnp.transpose(jnp.where(row == lane, block, 0.0).astype(jnp.bfloat16))
        special_out[...] = block
        return block

    per_image = patch_total // images
    masks = [(per_image, mask[b : b + 1, :]) for b in range(images)]
    state = State(patch_total, state_out)
    for result in attend_all(
        patch_columns, masks, queries_of, special_queries, None, pairs, patch_total, 0
    ):
        state.put(*result)


def joined(stretches, mask, refs):
    count = len(stretches)
    flat = lambda ref, i: ref[i] if len(ref.shape) == 3 else ref[...]
    own = jnp.concatenate([flat(ref, 0) for ref in refs[:count]], axis=0)
    other = jnp.concatenate([flat(ref, 1) for ref in refs[count : 2 * count]], axis=0)
    masks = [
        (rows, None if i is None else mask[i : i + 1, :]) for part in stretches for rows, i in part
    ]
    return own, other, masks, refs[2 * count :]


def later_kernel(stretches, special_real, mask, *refs):
    own, other, masks, refs = joined(stretches, mask, refs)
    weights, queries, special_queries = refs[:3]
    state_in, state_out = refs[3:7], refs[7:]
    pairs, rows = queries.shape[0], queries.shape[2] // 2
    state = State(rows, state_out)
    for result in attend_all(
        projector(own, other, weights), masks, lambda pair: queries[pair], lambda: special_queries[...],
        State(rows, state_in), pairs, rows, special_real,
    ):
        state.put(*result)


def last_kernel(stretches, special_real, mask, *refs):
    own, other, masks, refs = joined(stretches, mask, refs)
    weights, queries, special_queries = refs[:3]
    state_in = refs[3:7]
    w_out, kept_out, sent_out, w_here, copied = refs[7:]
    copy = pltpu.make_async_copy(w_out, w_here, copied)
    copy.start()
    pairs, rows = queries.shape[0], queries.shape[2] // 2
    columns, out, special = [], None, None
    sides = halves(kept_out.shape[1])
    for pair, sub, _, total, weight in attend_all(
        projector(own, other, weights), masks, lambda pair: queries[pair], lambda: special_queries[...],
        State(rows, state_in), pairs, rows, special_real,
    ):
        if pair == 0 and sub == 0:
            copy.wait()
        share = total * (1.0 / weight)
        if pair == pairs:
            row = lax.broadcasted_iota(jnp.int32, share.shape, 0) // HEAD_DIM
            lane = lax.broadcasted_iota(jnp.int32, share.shape, 1) // TILE_ROWS
            share = jnp.transpose(jnp.where(row == lane, share, 0.0))
            share = sum(share[i * TILE_ROWS : (i + 1) * TILE_ROWS] for i in range(2 * pairs))
            special = [product(share.astype(jnp.bfloat16), w_here[:, side]) for side in sides]
            continue
        columns.append(share)
        if pair % 2 == 1 and sub == 1:
            quad = jnp.transpose(jnp.concatenate(columns, axis=0).astype(jnp.bfloat16))
            features = slice((pair // 2) * QUAD, (pair // 2 + 1) * QUAD)
            added = [product(quad, w_here[features, side]) for side in sides]
            out = added if out is None else [before + more for before, more in zip(out, added)]
            columns = []
    for place, values in ((slice(0, rows), out), (slice(rows, kept_out.shape[0]), special)):
        sent_out[place, :] = values[1].astype(jnp.bfloat16)
        kept_out[place, :] = values[0]


def end_kernel(images, kept, received, patch_out, special_out):
    patch_total = patch_out.shape[0]
    special_count = special_out.shape[0]
    patch_out[...] = (kept[:patch_total, :] + received[:patch_total, :].astype(jnp.float32)).astype(
        jnp.bfloat16
    )
    rest = kept[patch_total:, :] + received[patch_total:, :].astype(jnp.float32)
    rows = [rest[b * special_count : (b + 1) * special_count][:, None, :] for b in range(images)]
    special_out[...] = jnp.concatenate(rows, axis=1).astype(jnp.bfloat16)


def call(kernel, out_shape, operands, in_specs=None, out_specs=None, scratch=(), flops=0):
    if in_specs:
        operands = [
            pltpu.with_memory_space_constraint(operand, pltpu.HBM) if spec is HBM else operand
            for operand, spec in zip(operands, in_specs)
        ]
    return pl.pallas_call(
        kernel,
        out_shape=out_shape,
        in_specs=in_specs or [VMEM] * len(operands),
        out_specs=out_specs or [VMEM] * len(out_shape),
        scratch_shapes=scratch,
        compiler_params=pltpu.CompilerParams(vmem_limit_bytes=VMEM_BYTES),
        cost_estimate=pl.CostEstimate(flops=flops, transcendentals=0, bytes_accessed=0),
    )(*operands)


def pair_kernel(first, second, out):
    out[0] = first[...]
    out[1] = second[...]


def stack_kernel(first, second, out):
    count = first.shape[-2]
    out[..., :count, :] = first[...]
    out[..., count:, :] = second[...]


def stacked(first, second, flops=0):
    shape = jax.ShapeDtypeStruct((*first.shape[:-2], 2 * first.shape[-2], first.shape[-1]), first.dtype)
    return call(stack_kernel, [shape], (first, second), flops=flops)[0]


def after(array, *others):
    return lax.optimization_barrier((array, *others))[0]


def per_device(
    patch_rows, special_rows, role_first, role_rest, frame_order, covisible, w_qkv, w_out
):
    images, per_image, width = patch_rows.shape
    special_count = special_rows.shape[1]
    real_rows = images * special_count
    special_block = real_rows + -real_rows % TILE_ROWS
    owner_count = lax.axis_size("blk")
    reach = max(1, owner_count // 64)
    patch_total = images * per_image
    rows = patch_total + special_block
    cut = per_image * max(1, images // 2)
    heads = width // HEAD_DIM
    pairs = heads // 2
    paired = reach == 1 and owner_count % 2 == 0

    if paired:
        offsets = [0, (-1, 1), (1, -1)]
    else:
        offsets = [0] + [sign * d for d in range(1, reach + 1) for sign in (-1, 1)]
    mask_rows = -(-len(offsets) * images // 8) * 8
    bf16 = lambda *shape: jax.ShapeDtypeStruct(shape, jnp.bfloat16)
    f32 = lambda *shape: jax.ShapeDtypeStruct(shape, jnp.float32)
    state_shape = [
        f32(8, 2 * patch_total),
        f32(8, 2 * patch_total),
        f32(pairs, HEAD_DIM, 2 * patch_total),
        f32(width, heads * special_block),
    ]

    both = lambda part: (part, swapped(part, "head", 1))
    patches = patch_rows.reshape(patch_total, width)
    turned = jnp.transpose(special_rows, (1, 0, 2))
    power = owner_count >= 8 and owner_count & (owner_count - 1) == 0
    specials, own, early, late = call(
        rows_kernel,
        [
            bf16(special_block, width),
            bf16(patch_total, width),
            bf16(cut, width),
            bf16(patch_total - cut, width),
        ],
        (frame_order, turned, role_first, role_rest, patches),
        in_specs=[HBM] * 5,
        scratch=[
            pltpu.SMEM(frame_order.shape, jnp.int32),
            pltpu.VMEM(turned.shape, jnp.bfloat16),
            pltpu.VMEM(role_first.shape, jnp.bfloat16),
            pltpu.VMEM(role_rest.shape, jnp.bfloat16),
            pltpu.SemaphoreType.DMA((7,)),
        ],
    )
    everywhere = specials
    if paired and power:
        everywhere = stacked(specials, swapped(specials, "blk", 2), FIRST)
    (everywhere,) = call(pair_kernel, [bf16(2, *everywhere.shape)], both(everywhere))
    specials = everywhere
    mask, weights = call(
        functools.partial(start_kernel, offsets, per_image, special_count, special_block),
        [
            f32(mask_rows, patch_total + heads * special_block),
            bf16(*w_qkv.shape),
        ],
        (covisible, w_qkv),
        in_specs=[HBM] * 2,
        scratch=[pltpu.SMEM(covisible.shape, jnp.int32), pltpu.SemaphoreType.DMA((1 + 6,))],
    )
    queries, special_queries, *state = call(
        functools.partial(first_kernel, images, special_block),
        [bf16(pairs, PAIR, 2 * patch_total), bf16(width, heads * special_block), *state_shape],
        (mask, own, swapped(patches, "head", 1), specials, weights),
    )
    fixed = (weights, queries, special_queries)

    def later(stretches, parts, state):
        return call(
            functools.partial(later_kernel, stretches, real_rows),
            state_shape,
            (mask, *[part[0] for part in parts], *[part[1] for part in parts], *fixed, *state),
        )

    image_rows = lambda owner: [(per_image, owner * images + b) for b in range(images)]
    def halved(part, gate, step=per_image):
        part = after(part, gate)
        return [both(part[start : start + step]) for start in range(0, part.shape[0], step)]

    stretches = lambda owner: [[image] for image in image_rows(owner)]
    if paired:
        if power:
            bit = 4
            while bit < owner_count:
                everywhere = stacked(everywhere, swapped(everywhere, "blk", bit), FIRST)
                bit *= 2
        far = halved(crossed(patches, "blk"), state[0])
        early = swapped(early, "blk", 1)
        late = swapped(after(late,mask), "blk", 1)
        count = early.shape[0] // per_image
        state[0] = after(state[0], everywhere)
        state = later(stretches(1), far, state)
        if power:
            everywhere = after(everywhere, state[0])
            arrived = swapped(everywhere, "blk", 1)
        step = per_image // 2
        stretches_early = [[(step, image)] for (_, image), in stretches(2)[:count] for _ in range(2)]
        state = later(stretches_early, halved(early, state[0], step), state)
        if power:
            everywhere = stacked(after(everywhere, state[0]), arrived, FIRST)
        stretches, parts = stretches(2)[count:], halved(late, state[0])
    else:
        for i, offset in enumerate(offsets[1:]):
            parts = halved(shifted(patches, "blk", -offset), state[0])
            if i < len(offsets) - 2:
                state = later(stretches(i + 1), parts, state)
        stretches = stretches(len(offsets) - 1)
    if not (paired and power):
        everywhere = lax.all_gather(specials, "blk", axis=1, tiled=True)
    stretches, parts = stretches + [[(everywhere.shape[1], None)]], parts + [(everywhere, everywhere)]
    kept, sent = call(
        functools.partial(last_kernel, stretches, real_rows),
        [f32(rows, width), bf16(rows, width)],
        (
            mask, *[part[0] for part in parts], *[part[1] for part in parts], *fixed, *state, w_out,
        ),
        in_specs=[VMEM] * (1 + 2 * len(parts) + len(fixed) + len(state)) + [HBM],
        scratch=[pltpu.VMEM(w_out.shape, jnp.bfloat16), pltpu.SemaphoreType.DMA],
    )
    received = swapped(sent, "head", 1)
    patch_out, special_out = call(
        functools.partial(end_kernel, images),
        [bf16(patch_total, width), bf16(special_count, images, width)],
        (kept, received),
        out_specs=[pl.BlockSpec(), pl.BlockSpec()],
    )
    return patch_out.reshape(patch_rows.shape), jnp.transpose(special_out, (1, 0, 2))


def solution(mesh):
    in_specs = (
        P(("scene", "blk"), None, "head"),
        P(("scene", "blk"), None, "head"),
        P(),
        P(),
        P(("scene", "blk")),
        P(("scene", "blk"), None),
        P(None, None, "head"),
        P("head", None),
    )
    out_specs = (P(("scene", "blk"), None, "head"), P(("scene", "blk"), None, "head"))
    return jax.shard_map(
        per_device, mesh=mesh, in_specs=in_specs, out_specs=out_specs, check_vma=False
    )
```

```python
import functools

import jax
import jax.numpy as jnp
from jax import lax
from jax.experimental import pallas as pl
from jax.experimental.pallas import tpu as pltpu
from jax.sharding import PartitionSpec as P

HEAD_DIM = 64
PAIR = 2 * HEAD_DIM
QUAD = 2 * PAIR
TILE_ROWS = 16
LOG2_E = 1.4426950408889634
FIRST = 20_000_000_000
VMEM_BYTES = 32 * 1024 * 1024
SMEM = pl.BlockSpec(memory_space=pltpu.SMEM)
VMEM = pl.BlockSpec(memory_space=pltpu.VMEM)
HBM = pl.BlockSpec(memory_space=pltpu.HBM)


def shifted(block, axis, distance):
    count = lax.axis_size(axis)
    route = [((i - distance) % count, i) for i in range(count)]
    return lax.ppermute(block, axis, route)


def swapped(block, axis, bit):
    count = lax.axis_size(axis)
    return lax.ppermute(block, axis, [(i ^ bit, i) for i in range(count)])


def crossed(block, axis):
    count = lax.axis_size(axis)
    return lax.ppermute(block, axis, [(i, (i + (-1 if i % 2 == 0 else 1)) % count) for i in range(count)])


def halves(width):
    half = lax.axis_index("head")
    mine = pl.ds(pl.multiple_of(half * width, width), width)
    theirs = pl.ds(pl.multiple_of((1 - half) * width, width), width)
    return mine, theirs


def product(left, right):
    return jnp.dot(left, right, preferred_element_type=jnp.float32)


def owner_at(offset):
    count = lax.axis_size("blk")
    here = lax.axis_index("blk")
    if isinstance(offset, tuple):
        offset = jnp.where(lax.rem(here, 2) == 0, offset[0], offset[1])
    return lax.rem(here + offset + count, count)


def rows_kernel(
    frame_order, specials, role_first, role_rest, patches,
    special_out, patches_out, order, here, first_rows, rest_rows, copied,
):
    special_count, images, width = specials.shape
    moves = [(specials, here), (role_first, first_rows), (role_rest, rest_rows), (frame_order, order)]
    moves.append((patches, patches_out))
    copies = [
        pltpu.make_async_copy(source, target, copied.at[i]) for i, (source, target) in enumerate(moves)
    ]
    for copy in copies:
        copy.start()
    for copy in copies[:4]:
        copy.wait()
    mine, _ = halves(width)
    first = first_rows[:, mine].astype(jnp.float32)
    rest = rest_rows[:, mine].astype(jnp.float32)
    summed = [
        here[:, b, :].astype(jnp.float32) + jnp.where(order[b] == 0, first, rest) for b in range(images)
    ]
    summed.append(jnp.zeros((special_out.shape[0] - images * special_count, width), jnp.float32))
    special_out[...] = jnp.concatenate(summed, axis=0).astype(jnp.bfloat16)
    for copy in copies[4:]:
        copy.wait()


def start_kernel(
    offsets, per_image, special_count, special_total, covisible, w_qkv, mask_out, weights_out, seen, copied
):
    images = covisible.shape[0]
    patch_total = images * per_image
    moves = [(covisible, seen)]
    depth = w_qkv.shape[1] // 2
    for i in range(3):
        for j, rows in enumerate(halves(depth)):
            moves.append((w_qkv.at[i, rows], weights_out.at[i, pl.ds(j * depth, depth)]))
    copies = [
        pltpu.make_async_copy(source, target, copied.at[i]) for i, (source, target) in enumerate(moves)
    ]
    for copy in copies:
        copy.start()
    copies[0].wait()
    lane = lax.broadcasted_iota(jnp.int32, (1, mask_out.shape[1]), 1)
    special_lane = lax.rem(lane - patch_total, special_total)
    image = jnp.where(
        lane < patch_total, lane // per_image, jnp.minimum(special_lane // special_count, images - 1)
    )
    for i, offset in enumerate(offsets):
        for b in range(images):
            row = jnp.zeros(lane.shape, jnp.float32)
            for a in range(images):
                hidden = seen[a, owner_at(offset) * images + b] <= 0
                row = jnp.where((image == a) & hidden, -jnp.inf, row)
            mask_out[i * images + b : i * images + b + 1, :] = row
    for copy in copies[1:]:
        copy.wait()


def projector(own, other, weights):
    rows = jnp.concatenate([own, other], axis=1)

    def columns(which, quad):
        return product(rows, weights[which, :, quad * QUAD : (quad + 1) * QUAD])

    return columns


def attend(scores, masks, state):
    largest = state
    start = 0
    for count, mask in masks:
        part = jnp.max(scores[start : start + count], axis=0, keepdims=True)
        part = part if mask is None else part + mask
        largest = part if largest is None else jnp.maximum(largest, part)
        start += count
    weights, start = [], 0
    for count, mask in masks:
        level = largest if mask is None else largest - mask
        weights.append(jnp.exp2((scores[start : start + count] - level).astype(jnp.bfloat16)))
        start += count
    factor = None if state is None else jnp.exp2(state - largest)
    return largest, factor, jnp.concatenate(weights, axis=0)


def attend_all(columns, masks, queries_of, special_queries, state, pairs, rows, special_real):
    keys, values = {}, {}
    quads = pairs // 2

    def keys_of(quad):
        if quad not in keys:
            keys[quad] = columns(1, quad).astype(jnp.bfloat16)
        return keys[quad]

    def values_of(quad):
        if quad not in values:
            values[quad] = jnp.transpose(columns(2, quad).astype(jnp.bfloat16))
        return values[quad]

    def prepared(pair):
        if pair == pairs:
            scores = product(
                jnp.concatenate([keys_of(quad) for quad in range(quads)], axis=1), special_queries()
            )
        else:
            lanes = slice((pair % 2) * PAIR, (pair % 2 + 1) * PAIR)
            scores = product(keys_of(pair // 2)[:, lanes], queries_of(pair))
        if all(mask is not None for _, mask in masks):
            return scores
        parts, start = [], 0
        for count, mask in masks:
            part = scores[start : start + count]
            if mask is None:
                key_row = lax.broadcasted_iota(jnp.int32, (count, 1), 0)
                part = jnp.where(lax.rem(key_row, TILE_ROWS) < special_real, part, -jnp.inf)
            parts.append(part)
            start += count
        return jnp.concatenate(parts, axis=0)

    ones = jnp.ones((TILE_ROWS, sum(count for count, _ in masks)), jnp.bfloat16)
    both = [
        (count, None if mask is None else jnp.concatenate([mask[:, :rows]] * 2, axis=1))
        for count, mask in masks
    ]
    only = [(count, None if mask is None else mask[:, rows:]) for count, mask in masks]
    order = list(range(pairs))
    order.insert(pairs - 2, pairs)
    scores = prepared(order[0])
    for step, pair in enumerate(order):
        if pair < pairs:
            left = values_of(pair // 2)[(pair % 2) * PAIR : (pair % 2 + 1) * PAIR]
        else:
            left = jnp.concatenate([values_of(quad) for quad in range(quads)], axis=0)
        following = prepared(order[step + 1]) if step < pairs else None
        largest, factor, weights = attend(
            scores, both if pair < pairs else only, state and state.largest(pair)
        )
        added = product(jnp.concatenate([left, ones], axis=0), weights)
        height, subs = (HEAD_DIM, 2) if pair < pairs else (left.shape[0], 1)
        width = scores.shape[1] // subs
        for sub in range(subs):
            lanes = slice(sub * width, (sub + 1) * width)
            total = added[sub * height : (sub + 1) * height, lanes]
            weight = added[left.shape[0] : left.shape[0] + 1, lanes]
            if state is not None:
                total = total + state.total(pair, sub) * factor[:, lanes]
                weight = weight + state.weight(pair, sub) * factor[:, lanes]
            yield pair, sub, largest[:, lanes], total, weight
        scores = following


class State:
    def __init__(self, rows, refs):
        self.rows = rows
        self.largest_ref, self.weight_ref, self.total_ref, self.special_ref = refs

    def lanes(self, pair, sub):
        if pair == self.total_ref.shape[0]:
            return slice(0, self.special_ref.shape[1])
        return slice(sub * self.rows, (sub + 1) * self.rows)

    def largest(self, pair):
        stop = self.special_ref.shape[1] if pair == self.total_ref.shape[0] else 2 * self.rows
        return self.largest_ref[pair : pair + 1, 0:stop]

    def weight(self, pair, sub):
        return self.weight_ref[pair : pair + 1, self.lanes(pair, sub)]

    def total(self, pair, sub):
        if pair == self.total_ref.shape[0]:
            return self.special_ref[...]
        return self.total_ref[pair, :, self.lanes(pair, sub)]

    def put(self, pair, sub, largest, total, weight):
        lanes = self.lanes(pair, sub)
        self.largest_ref[pair : pair + 1, lanes] = largest
        self.weight_ref[pair : pair + 1, lanes] = weight
        if pair == self.total_ref.shape[0]:
            self.special_ref[...] = total
        else:
            self.total_ref[pair, :, lanes] = total


def first_kernel(
    images, mask, own, other, special, weights, queries_out, special_out, *state_out
):
    patch_total = own.shape[0]
    columns = projector(
        jnp.concatenate([own[...], special[0]], axis=0),
        jnp.concatenate([other[...], special[1]], axis=0),
        weights,
    )
    pairs = queries_out.shape[0]
    zero = jnp.zeros((HEAD_DIM, patch_total), jnp.bfloat16)
    made = {}

    def patch_columns(which, quad):
        return columns(which, quad)[:patch_total]

    def columns_of(quad):
        if quad not in made:
            queries = columns(0, quad) * (HEAD_DIM ** (-0.5) * LOG2_E)
            made[quad] = queries[patch_total:]
            turned = jnp.transpose(queries[:patch_total].astype(jnp.bfloat16))
            for i in range(2):
                first = i * PAIR
                upper = jnp.concatenate([turned[first : first + HEAD_DIM], zero], axis=1)
                lower = jnp.concatenate([zero, turned[first + HEAD_DIM : first + PAIR]], axis=1)
                queries_out[2 * quad + i] = jnp.concatenate([upper, lower], axis=0)
        return made[quad]

    def queries_of(pair):
        columns_of(pair // 2)
        return queries_out[pair]

    def special_queries():
        block = jnp.concatenate([columns_of(quad) for quad in range(pairs // 2)], axis=1)
        count = block.shape[0]
        block = jnp.concatenate([block] * (2 * pairs), axis=0)
        row = lax.broadcasted_iota(jnp.int32, block.shape, 0) // count
        lane = lax.broadcasted_iota(jnp.int32, block.shape, 1) // HEAD_DIM
        block = jnp.transpose(jnp.where(row == lane, block, 0.0).astype(jnp.bfloat16))
        special_out[...] = block
        return block

    per_image = patch_total // images
    masks = [(per_image, mask[b : b + 1, :]) for b in range(images)]
    state = State(patch_total, state_out)
    for result in attend_all(
        patch_columns, masks, queries_of, special_queries, None, pairs, patch_total, 0
    ):
        state.put(*result)


def joined(stretches, mask, refs):
    count = len(stretches)
    flat = lambda ref, i: ref[i] if len(ref.shape) == 3 else ref[...]
    own = jnp.concatenate([flat(ref, 0) for ref in refs[:count]], axis=0)
    other = jnp.concatenate([flat(ref, 1) for ref in refs[count : 2 * count]], axis=0)
    masks = [
        (rows, None if i is None else mask[i : i + 1, :]) for part in stretches for rows, i in part
    ]
    return own, other, masks, refs[2 * count :]


def later_kernel(stretches, special_real, mask, *refs):
    own, other, masks, refs = joined(stretches, mask, refs)
    weights, queries, special_queries = refs[:3]
    state_in, state_out = refs[3:7], refs[7:]
    pairs, rows = queries.shape[0], queries.shape[2] // 2
    state = State(rows, state_out)
    for result in attend_all(
        projector(own, other, weights), masks, lambda pair: queries[pair], lambda: special_queries[...],
        State(rows, state_in), pairs, rows, special_real,
    ):
        state.put(*result)


def last_kernel(stretches, special_real, mask, *refs):
    own, other, masks, refs = joined(stretches, mask, refs)
    weights, queries, special_queries = refs[:3]
    state_in = refs[3:7]
    w_out, kept_out, sent_out, w_here, copied = refs[7:]
    copy = pltpu.make_async_copy(w_out, w_here, copied)
    copy.start()
    pairs, rows = queries.shape[0], queries.shape[2] // 2
    columns, out, special = [], None, None
    sides = halves(kept_out.shape[1])
    for pair, sub, _, total, weight in attend_all(
        projector(own, other, weights), masks, lambda pair: queries[pair], lambda: special_queries[...],
        State(rows, state_in), pairs, rows, special_real,
    ):
        if pair == 0 and sub == 0:
            copy.wait()
        share = total * (1.0 / weight)
        if pair == pairs:
            row = lax.broadcasted_iota(jnp.int32, share.shape, 0) // HEAD_DIM
            lane = lax.broadcasted_iota(jnp.int32, share.shape, 1) // TILE_ROWS
            share = jnp.transpose(jnp.where(row == lane, share, 0.0))
            share = sum(share[i * TILE_ROWS : (i + 1) * TILE_ROWS] for i in range(2 * pairs))
            special = [product(share.astype(jnp.bfloat16), w_here[:, side]) for side in sides]
            continue
        columns.append(share)
        if pair % 2 == 1 and sub == 1:
            quad = jnp.transpose(jnp.concatenate(columns, axis=0).astype(jnp.bfloat16))
            features = slice((pair // 2) * QUAD, (pair // 2 + 1) * QUAD)
            added = [product(quad, w_here[features, side]) for side in sides]
            out = added if out is None else [before + more for before, more in zip(out, added)]
            columns = []
    for place, values in ((slice(0, rows), out), (slice(rows, kept_out.shape[0]), special)):
        sent_out[place, :] = values[1].astype(jnp.bfloat16)
        kept_out[place, :] = values[0]


def end_kernel(images, kept, received, patch_out, special_out):
    patch_total = patch_out.shape[0]
    special_count = special_out.shape[0]
    patch_out[...] = (kept[:patch_total, :] + received[:patch_total, :].astype(jnp.float32)).astype(
        jnp.bfloat16
    )
    rest = kept[patch_total:, :] + received[patch_total:, :].astype(jnp.float32)
    rows = [rest[b * special_count : (b + 1) * special_count][:, None, :] for b in range(images)]
    special_out[...] = jnp.concatenate(rows, axis=1).astype(jnp.bfloat16)


def call(kernel, out_shape, operands, in_specs=None, out_specs=None, scratch=(), flops=0):
    if in_specs:
        operands = [
            pltpu.with_memory_space_constraint(operand, pltpu.HBM) if spec is HBM else operand
            for operand, spec in zip(operands, in_specs)
        ]
    return pl.pallas_call(
        kernel,
        out_shape=out_shape,
        in_specs=in_specs or [VMEM] * len(operands),
        out_specs=out_specs or [VMEM] * len(out_shape),
        scratch_shapes=scratch,
        compiler_params=pltpu.CompilerParams(vmem_limit_bytes=VMEM_BYTES),
        cost_estimate=pl.CostEstimate(flops=flops, transcendentals=0, bytes_accessed=0),
    )(*operands)


def pair_kernel(first, second, out):
    out[0] = first[...]
    out[1] = second[...]


def stack_kernel(first, second, out):
    count = first.shape[1]
    out[:, :count, :] = first[...]
    out[:, count:, :] = second[...]


def stacked(first, second, flops=0):
    shape = jax.ShapeDtypeStruct((2, 2 * first.shape[1], first.shape[2]), first.dtype)
    return call(stack_kernel, [shape], (first, second), flops=flops)[0]


def after(array, *others):
    return lax.optimization_barrier((array, *others))[0]


def per_device(
    patch_rows, special_rows, role_first, role_rest, frame_order, covisible, w_qkv, w_out
):
    images, per_image, width = patch_rows.shape
    special_count = special_rows.shape[1]
    real_rows = images * special_count
    special_block = real_rows + -real_rows % TILE_ROWS
    owner_count = lax.axis_size("blk")
    reach = max(1, owner_count // 64)
    patch_total = images * per_image
    rows = patch_total + special_block
    heads = width // HEAD_DIM
    pairs = heads // 2
    paired = reach == 1 and owner_count % 2 == 0

    if paired:
        offsets = [0, (-1, 1), (1, -1)]
    else:
        offsets = [0] + [sign * d for d in range(1, reach + 1) for sign in (-1, 1)]
    mask_rows = -(-len(offsets) * images // 8) * 8
    bf16 = lambda *shape: jax.ShapeDtypeStruct(shape, jnp.bfloat16)
    f32 = lambda *shape: jax.ShapeDtypeStruct(shape, jnp.float32)
    state_shape = [
        f32(8, 2 * patch_total),
        f32(8, 2 * patch_total),
        f32(pairs, HEAD_DIM, 2 * patch_total),
        f32(width, heads * special_block),
    ]

    both = lambda part: (part, swapped(part, "head", 1))
    patches = patch_rows.reshape(patch_total, width)
    turned = jnp.transpose(special_rows, (1, 0, 2))
    power = owner_count >= 8 and owner_count & (owner_count - 1) == 0
    specials, own = call(
        rows_kernel,
        [
            bf16(special_block, width),
            bf16(patch_total, width),
        ],
        (frame_order, turned, role_first, role_rest, patches),
        in_specs=[HBM] * 5,
        scratch=[
            pltpu.SMEM(frame_order.shape, jnp.int32),
            pltpu.VMEM(turned.shape, jnp.bfloat16),
            pltpu.VMEM(role_first.shape, jnp.bfloat16),
            pltpu.VMEM(role_rest.shape, jnp.bfloat16),
            pltpu.SemaphoreType.DMA((5,)),
        ],
    )
    bits = [1 << i for i in range(1, owner_count.bit_length() - 1)] + [1] if power else []
    (specials,) = call(pair_kernel, [bf16(2, special_block, width)], both(specials))
    everywhere = specials
    if paired and power:
        everywhere = stacked(specials, swapped(specials, "blk", bits[0]), FIRST)
    mask, weights = call(
        functools.partial(start_kernel, offsets, per_image, special_count, special_block),
        [
            f32(mask_rows, patch_total + heads * special_block),
            bf16(*w_qkv.shape),
        ],
        (covisible, w_qkv),
        in_specs=[HBM] * 2,
        scratch=[pltpu.SMEM(covisible.shape, jnp.int32), pltpu.SemaphoreType.DMA((1 + 6,))],
    )
    queries, special_queries, *state = call(
        functools.partial(first_kernel, images),
        [bf16(pairs, PAIR, 2 * patch_total), bf16(width, heads * special_block), *state_shape],
        (mask, own, swapped(patches, "head", 1), specials, weights),
    )
    fixed = (weights, queries, special_queries)

    def later(stretches, parts, state):
        return call(
            functools.partial(later_kernel, stretches, real_rows),
            state_shape,
            (mask, *[part[0] for part in parts], *[part[1] for part in parts], *fixed, *state),
        )

    image_rows = lambda owner: [(per_image, owner * images + b) for b in range(images)]
    def halved(part, gate, step):
        part = after(part, gate)
        return [both(part[start : start + step]) for start in range(0, part.shape[0], step)]

    def stretches(owner, step):
        count = per_image // step
        return [[(step, image)] for _, image in image_rows(owner) for _ in range(count)]

    if paired:
        far = after(crossed(patches, "blk"), state[0])
        near = swapped(patches, "blk", 1)
        if power:
            everywhere = after(everywhere, far)
            for bit in bits[1:-2]:
                everywhere = stacked(everywhere, swapped(everywhere, "blk", bit))
            arrived = swapped(everywhere, "blk", bits[-2])
        far = halved(far, state[0], per_image)
        state = later(stretches(1, per_image)[:1], far[:1], state)
        if power:
            everywhere = stacked(after(everywhere, state[0]), arrived)
            arrived = swapped(everywhere, "blk", bits[-1])
        state = later(stretches(1, per_image)[1:], far[1:], state)
        step = per_image // 2
        stretches, parts = stretches(2, step), halved(near, state[0], step)
        if power:
            everywhere = stacked(everywhere, arrived)
    else:
        for i, offset in enumerate(offsets[1:]):
            parts = halved(shifted(patches, "blk", -offset), state[0], per_image)
            if i < len(offsets) - 2:
                state = later(stretches(i + 1, per_image), parts, state)
        stretches = stretches(len(offsets) - 1, per_image)
    if not (paired and power):
        everywhere = lax.all_gather(specials, "blk", axis=1, tiled=True)
    stretches, parts = stretches + [[(everywhere.shape[1], None)]], parts + [(everywhere, everywhere)]
    kept, sent = call(
        functools.partial(last_kernel, stretches, real_rows),
        [f32(rows, width), bf16(rows, width)],
        (
            mask, *[part[0] for part in parts], *[part[1] for part in parts], *fixed, *state, w_out,
        ),
        in_specs=[VMEM] * (1 + 2 * len(parts) + len(fixed) + len(state)) + [HBM],
        scratch=[pltpu.VMEM(w_out.shape, jnp.bfloat16), pltpu.SemaphoreType.DMA],
    )
    received = swapped(sent, "head", 1)
    patch_out, special_out = call(
        functools.partial(end_kernel, images),
        [bf16(patch_total, width), bf16(special_count, images, width)],
        (kept, received),
        out_specs=[pl.BlockSpec(), pl.BlockSpec()],
    )
    return patch_out.reshape(patch_rows.shape), jnp.transpose(special_out, (1, 0, 2))


def solution(mesh):
    in_specs = (
        P(("scene", "blk"), None, "head"),
        P(("scene", "blk"), None, "head"),
        P(),
        P(),
        P(("scene", "blk")),
        P(("scene", "blk"), None),
        P(None, None, "head"),
        P("head", None),
    )
    out_specs = (P(("scene", "blk"), None, "head"), P(("scene", "blk"), None, "head"))
    return jax.shard_map(
        per_device, mesh=mesh, in_specs=in_specs, out_specs=out_specs, check_vma=False
    )
```

```python
import functools

import jax
import jax.numpy as jnp
from jax import lax
from jax.experimental import pallas as pl
from jax.experimental.pallas import tpu as pltpu
from jax.sharding import PartitionSpec as P

HEAD_DIM = 64
PAIR = 2 * HEAD_DIM
QUAD = 2 * PAIR
TILE_ROWS = 16
LOG2_E = 1.4426950408889634
FIRST = 20_000_000_000
VMEM_BYTES = 32 * 1024 * 1024
SMEM = pl.BlockSpec(memory_space=pltpu.SMEM)
VMEM = pl.BlockSpec(memory_space=pltpu.VMEM)
HBM = pl.BlockSpec(memory_space=pltpu.HBM)


def shifted(block, axis, distance):
    count = lax.axis_size(axis)
    route = [((i - distance) % count, i) for i in range(count)]
    return lax.ppermute(block, axis, route)


def swapped(block, axis, bit):
    count = lax.axis_size(axis)
    return lax.ppermute(block, axis, [(i ^ bit, i) for i in range(count)])


def crossed(block, axis):
    count = lax.axis_size(axis)
    return lax.ppermute(block, axis, [(i, (i + (-1 if i % 2 == 0 else 1)) % count) for i in range(count)])


def halves(width):
    half = lax.axis_index("head")
    mine = pl.ds(pl.multiple_of(half * width, width), width)
    theirs = pl.ds(pl.multiple_of((1 - half) * width, width), width)
    return mine, theirs


def product(left, right):
    return jnp.dot(left, right, preferred_element_type=jnp.float32)


def owner_at(offset):
    count = lax.axis_size("blk")
    here = lax.axis_index("blk")
    if isinstance(offset, tuple):
        offset = jnp.where(lax.rem(here, 2) == 0, offset[0], offset[1])
    return lax.rem(here + offset + count, count)


def rows_kernel(
    frame_order, specials, role_first, role_rest, patches,
    special_out, patches_out, order, here, first_rows, rest_rows, copied,
):
    special_count, images, width = specials.shape
    moves = [(specials, here), (role_first, first_rows), (role_rest, rest_rows), (frame_order, order)]
    moves.append((patches, patches_out))
    copies = [
        pltpu.make_async_copy(source, target, copied.at[i]) for i, (source, target) in enumerate(moves)
    ]
    for copy in copies:
        copy.start()
    for copy in copies[:4]:
        copy.wait()
    mine, _ = halves(width)
    first = first_rows[:, mine].astype(jnp.float32)
    rest = rest_rows[:, mine].astype(jnp.float32)
    summed = [
        here[:, b, :].astype(jnp.float32) + jnp.where(order[b] == 0, first, rest) for b in range(images)
    ]
    summed.append(jnp.zeros((special_out.shape[0] - images * special_count, width), jnp.float32))
    special_out[...] = jnp.concatenate(summed, axis=0).astype(jnp.bfloat16)
    for copy in copies[4:]:
        copy.wait()


def start_kernel(
    offsets, per_image, special_count, special_total, covisible, w_qkv, mask_out, weights_out, seen, copied
):
    images = covisible.shape[0]
    patch_total = images * per_image
    moves = [(covisible, seen)]
    depth = w_qkv.shape[1] // 2
    for i in range(3):
        for j, rows in enumerate(halves(depth)):
            moves.append((w_qkv.at[i, rows], weights_out.at[i, pl.ds(j * depth, depth)]))
    copies = [
        pltpu.make_async_copy(source, target, copied.at[i]) for i, (source, target) in enumerate(moves)
    ]
    for copy in copies:
        copy.start()
    copies[0].wait()
    lane = lax.broadcasted_iota(jnp.int32, (1, mask_out.shape[1]), 1)
    special_lane = lax.rem(lane - patch_total, special_total)
    image = jnp.where(
        lane < patch_total, lane // per_image, jnp.minimum(special_lane // special_count, images - 1)
    )
    for i, offset in enumerate(offsets):
        for b in range(images):
            row = jnp.zeros(lane.shape, jnp.float32)
            for a in range(images):
                hidden = seen[a, owner_at(offset) * images + b] <= 0
                row = jnp.where((image == a) & hidden, -jnp.inf, row)
            mask_out[i * images + b : i * images + b + 1, :] = row
    for copy in copies[1:]:
        copy.wait()


def projector(own, other, weights):
    rows = jnp.concatenate([own, other], axis=1)

    def columns(which, quad):
        return product(rows, weights[which, :, quad * QUAD : (quad + 1) * QUAD])

    return columns


def attend(scores, masks, state):
    largest = state
    start = 0
    for count, mask in masks:
        part = jnp.max(scores[start : start + count], axis=0, keepdims=True)
        part = part if mask is None else part + mask
        largest = part if largest is None else jnp.maximum(largest, part)
        start += count
    weights, start = [], 0
    for count, mask in masks:
        level = largest if mask is None else largest - mask
        weights.append(jnp.exp2((scores[start : start + count] - level).astype(jnp.bfloat16)))
        start += count
    factor = None if state is None else jnp.exp2(state - largest)
    return largest, factor, jnp.concatenate(weights, axis=0)


def attend_all(columns, masks, queries_of, special_queries, state, pairs, rows, special_real):
    keys, values = {}, {}
    quads = pairs // 2

    def keys_of(quad):
        if quad not in keys:
            keys[quad] = columns(1, quad).astype(jnp.bfloat16)
        return keys[quad]

    def values_of(quad):
        if quad not in values:
            values[quad] = jnp.transpose(columns(2, quad).astype(jnp.bfloat16))
        return values[quad]

    def prepared(pair):
        if pair == pairs:
            scores = product(
                jnp.concatenate([keys_of(quad) for quad in range(quads)], axis=1), special_queries()
            )
        else:
            lanes = slice((pair % 2) * PAIR, (pair % 2 + 1) * PAIR)
            scores = product(keys_of(pair // 2)[:, lanes], queries_of(pair))
        if all(mask is not None for _, mask in masks):
            return scores
        parts, start = [], 0
        for count, mask in masks:
            part = scores[start : start + count]
            if mask is None:
                key_row = lax.broadcasted_iota(jnp.int32, (count, 1), 0)
                part = jnp.where(lax.rem(key_row, TILE_ROWS) < special_real, part, -jnp.inf)
            parts.append(part)
            start += count
        return jnp.concatenate(parts, axis=0)

    ones = jnp.ones((TILE_ROWS, sum(count for count, _ in masks)), jnp.bfloat16)
    both = [
        (count, None if mask is None else jnp.concatenate([mask[:, :rows]] * 2, axis=1))
        for count, mask in masks
    ]
    only = [(count, None if mask is None else mask[:, rows:]) for count, mask in masks]
    order = list(range(pairs))
    order.insert(pairs - 2, pairs)
    scores = prepared(order[0])
    for step, pair in enumerate(order):
        if pair < pairs:
            left = values_of(pair // 2)[(pair % 2) * PAIR : (pair % 2 + 1) * PAIR]
        else:
            left = jnp.concatenate([values_of(quad) for quad in range(quads)], axis=0)
        following = prepared(order[step + 1]) if step < pairs else None
        largest, factor, weights = attend(
            scores, both if pair < pairs else only, state and state.largest(pair)
        )
        added = product(jnp.concatenate([left, ones], axis=0), weights)
        height, subs = (HEAD_DIM, 2) if pair < pairs else (left.shape[0], 1)
        width = scores.shape[1] // subs
        for sub in range(subs):
            lanes = slice(sub * width, (sub + 1) * width)
            total = added[sub * height : (sub + 1) * height, lanes]
            weight = added[left.shape[0] : left.shape[0] + 1, lanes]
            if state is not None:
                total = total + state.total(pair, sub) * factor[:, lanes]
                weight = weight + state.weight(pair, sub) * factor[:, lanes]
            yield pair, sub, largest[:, lanes], total, weight
        scores = following


class State:
    def __init__(self, rows, refs):
        self.rows = rows
        self.largest_ref, self.weight_ref, self.total_ref, self.special_ref = refs

    def lanes(self, pair, sub):
        if pair == self.total_ref.shape[0]:
            return slice(0, self.special_ref.shape[1])
        return slice(sub * self.rows, (sub + 1) * self.rows)

    def largest(self, pair):
        stop = self.special_ref.shape[1] if pair == self.total_ref.shape[0] else 2 * self.rows
        return self.largest_ref[pair : pair + 1, 0:stop]

    def weight(self, pair, sub):
        return self.weight_ref[pair : pair + 1, self.lanes(pair, sub)]

    def total(self, pair, sub):
        if pair == self.total_ref.shape[0]:
            return self.special_ref[...]
        return self.total_ref[pair, :, self.lanes(pair, sub)]

    def put(self, pair, sub, largest, total, weight):
        lanes = self.lanes(pair, sub)
        self.largest_ref[pair : pair + 1, lanes] = largest
        self.weight_ref[pair : pair + 1, lanes] = weight
        if pair == self.total_ref.shape[0]:
            self.special_ref[...] = total
        else:
            self.total_ref[pair, :, lanes] = total


def first_kernel(
    images, mask, own, other, special, weights, queries_out, special_out, *state_out
):
    patch_total = own.shape[0]
    columns = projector(
        jnp.concatenate([own[...], special[0]], axis=0),
        jnp.concatenate([other[...], special[1]], axis=0),
        weights,
    )
    pairs = queries_out.shape[0]
    zero = jnp.zeros((HEAD_DIM, patch_total), jnp.bfloat16)
    made = {}

    def patch_columns(which, quad):
        return columns(which, quad)[:patch_total]

    def columns_of(quad):
        if quad not in made:
            queries = columns(0, quad) * (HEAD_DIM ** (-0.5) * LOG2_E)
            made[quad] = queries[patch_total:]
            turned = jnp.transpose(queries[:patch_total].astype(jnp.bfloat16))
            for i in range(2):
                first = i * PAIR
                upper = jnp.concatenate([turned[first : first + HEAD_DIM], zero], axis=1)
                lower = jnp.concatenate([zero, turned[first + HEAD_DIM : first + PAIR]], axis=1)
                queries_out[2 * quad + i] = jnp.concatenate([upper, lower], axis=0)
        return made[quad]

    def queries_of(pair):
        columns_of(pair // 2)
        return queries_out[pair]

    def special_queries():
        block = jnp.concatenate([columns_of(quad) for quad in range(pairs // 2)], axis=1)
        count = block.shape[0]
        block = jnp.concatenate([block] * (2 * pairs), axis=0)
        row = lax.broadcasted_iota(jnp.int32, block.shape, 0) // count
        lane = lax.broadcasted_iota(jnp.int32, block.shape, 1) // HEAD_DIM
        block = jnp.transpose(jnp.where(row == lane, block, 0.0).astype(jnp.bfloat16))
        special_out[...] = block
        return block

    per_image = patch_total // images
    masks = [(per_image, mask[b : b + 1, :]) for b in range(images)]
    state = State(patch_total, state_out)
    for result in attend_all(
        patch_columns, masks, queries_of, special_queries, None, pairs, patch_total, 0
    ):
        state.put(*result)


def joined(stretches, mask, refs):
    count = len(stretches)
    flat = lambda ref, i: ref[i] if len(ref.shape) == 3 else ref[...]
    own = jnp.concatenate([flat(ref, 0) for ref in refs[:count]], axis=0)
    other = jnp.concatenate([flat(ref, 1) for ref in refs[count : 2 * count]], axis=0)
    masks = [
        (rows, None if i is None else mask[i : i + 1, :]) for part in stretches for rows, i in part
    ]
    return own, other, masks, refs[2 * count :]


def later_kernel(stretches, special_real, mask, *refs):
    own, other, masks, refs = joined(stretches, mask, refs)
    weights, queries, special_queries = refs[:3]
    state_in, state_out = refs[3:7], refs[7:]
    pairs, rows = queries.shape[0], queries.shape[2] // 2
    state = State(rows, state_out)
    for result in attend_all(
        projector(own, other, weights), masks, lambda pair: queries[pair], lambda: special_queries[...],
        State(rows, state_in), pairs, rows, special_real,
    ):
        state.put(*result)


def last_kernel(stretches, special_real, mask, *refs):
    own, other, masks, refs = joined(stretches, mask, refs)
    weights, queries, special_queries = refs[:3]
    state_in = refs[3:7]
    w_out, kept_out, sent_out, w_here, copied = refs[7:]
    copy = pltpu.make_async_copy(w_out, w_here, copied)
    copy.start()
    pairs, rows = queries.shape[0], queries.shape[2] // 2
    columns, out, special = [], None, None
    sides = halves(kept_out.shape[1])
    for pair, sub, _, total, weight in attend_all(
        projector(own, other, weights), masks, lambda pair: queries[pair], lambda: special_queries[...],
        State(rows, state_in), pairs, rows, special_real,
    ):
        if pair == 0 and sub == 0:
            copy.wait()
        share = total * (1.0 / weight)
        if pair == pairs:
            row = lax.broadcasted_iota(jnp.int32, share.shape, 0) // HEAD_DIM
            lane = lax.broadcasted_iota(jnp.int32, share.shape, 1) // TILE_ROWS
            share = jnp.transpose(jnp.where(row == lane, share, 0.0))
            share = sum(share[i * TILE_ROWS : (i + 1) * TILE_ROWS] for i in range(2 * pairs))
            special = [product(share.astype(jnp.bfloat16), w_here[:, side]) for side in sides]
            continue
        columns.append(share)
        if pair % 2 == 1 and sub == 1:
            quad = jnp.transpose(jnp.concatenate(columns, axis=0).astype(jnp.bfloat16))
            features = slice((pair // 2) * QUAD, (pair // 2 + 1) * QUAD)
            added = [product(quad, w_here[features, side]) for side in sides]
            out = added if out is None else [before + more for before, more in zip(out, added)]
            columns = []
    for place, values in ((slice(0, rows), out), (slice(rows, kept_out.shape[0]), special)):
        sent_out[place, :] = values[1].astype(jnp.bfloat16)
        kept_out[place, :] = values[0]


def end_kernel(images, kept, received, patch_out, special_out):
    patch_total = patch_out.shape[0]
    special_count = special_out.shape[0]
    patch_out[...] = (kept[:patch_total, :] + received[:patch_total, :].astype(jnp.float32)).astype(
        jnp.bfloat16
    )
    rest = kept[patch_total:, :] + received[patch_total:, :].astype(jnp.float32)
    rows = [rest[b * special_count : (b + 1) * special_count][:, None, :] for b in range(images)]
    special_out[...] = jnp.concatenate(rows, axis=1).astype(jnp.bfloat16)


def call(kernel, out_shape, operands, in_specs=None, out_specs=None, scratch=(), flops=0):
    if in_specs:
        operands = [
            pltpu.with_memory_space_constraint(operand, pltpu.HBM) if spec is HBM else operand
            for operand, spec in zip(operands, in_specs)
        ]
    return pl.pallas_call(
        kernel,
        out_shape=out_shape,
        in_specs=in_specs or [VMEM] * len(operands),
        out_specs=out_specs or [VMEM] * len(out_shape),
        scratch_shapes=scratch,
        compiler_params=pltpu.CompilerParams(vmem_limit_bytes=VMEM_BYTES),
        cost_estimate=pl.CostEstimate(flops=flops, transcendentals=0, bytes_accessed=0),
    )(*operands)


def pair_kernel(first, second, out):
    out[0] = first[...]
    out[1] = second[...]


def stack_kernel(first, second, out):
    count = first.shape[0]
    out[:count, :] = first[...]
    out[count:, :] = second[...]


def stacked(first, second, flops=0):
    shape = jax.ShapeDtypeStruct((2 * first.shape[0], first.shape[1]), first.dtype)
    return call(stack_kernel, [shape], (first, second), flops=flops)[0]


def after(array, *others):
    return lax.optimization_barrier((array, *others))[0]


def per_device(
    patch_rows, special_rows, role_first, role_rest, frame_order, covisible, w_qkv, w_out
):
    images, per_image, width = patch_rows.shape
    special_count = special_rows.shape[1]
    real_rows = images * special_count
    special_block = real_rows + -real_rows % TILE_ROWS
    owner_count = lax.axis_size("blk")
    reach = max(1, owner_count // 64)
    patch_total = images * per_image
    rows = patch_total + special_block
    heads = width // HEAD_DIM
    pairs = heads // 2
    paired = reach == 1 and owner_count % 2 == 0

    if paired:
        offsets = [0, (-1, 1), (1, -1)]
    else:
        offsets = [0] + [sign * d for d in range(1, reach + 1) for sign in (-1, 1)]
    mask_rows = -(-len(offsets) * images // 8) * 8
    bf16 = lambda *shape: jax.ShapeDtypeStruct(shape, jnp.bfloat16)
    f32 = lambda *shape: jax.ShapeDtypeStruct(shape, jnp.float32)
    state_shape = [
        f32(8, 2 * patch_total),
        f32(8, 2 * patch_total),
        f32(pairs, HEAD_DIM, 2 * patch_total),
        f32(width, heads * special_block),
    ]

    both = lambda part: (part, swapped(part, "head", 1))
    patches = patch_rows.reshape(patch_total, width)
    turned = jnp.transpose(special_rows, (1, 0, 2))
    power = owner_count >= 8 and owner_count & (owner_count - 1) == 0
    specials, own = call(
        rows_kernel,
        [
            bf16(special_block, width),
            bf16(patch_total, width),
        ],
        (frame_order, turned, role_first, role_rest, patches),
        in_specs=[HBM] * 5,
        scratch=[
            pltpu.SMEM(frame_order.shape, jnp.int32),
            pltpu.VMEM(turned.shape, jnp.bfloat16),
            pltpu.VMEM(role_first.shape, jnp.bfloat16),
            pltpu.VMEM(role_rest.shape, jnp.bfloat16),
            pltpu.SemaphoreType.DMA((5,)),
        ],
    )
    everywhere = specials
    (specials,) = call(pair_kernel, [bf16(2, special_block, width)], both(specials))
    if paired and power:
        everywhere = stacked(everywhere, swapped(everywhere, "blk", 1), FIRST)
    mask, weights = call(
        functools.partial(start_kernel, offsets, per_image, special_count, special_block),
        [
            f32(mask_rows, patch_total + heads * special_block),
            bf16(*w_qkv.shape),
        ],
        (covisible, w_qkv),
        in_specs=[HBM] * 2,
        scratch=[pltpu.SMEM(covisible.shape, jnp.int32), pltpu.SemaphoreType.DMA((1 + 6,))],
    )
    queries, special_queries, *state = call(
        functools.partial(first_kernel, images),
        [bf16(pairs, PAIR, 2 * patch_total), bf16(width, heads * special_block), *state_shape],
        (mask, own, swapped(patches, "head", 1), specials, weights),
    )
    fixed = (weights, queries, special_queries)

    def later(stretches, parts, state):
        return call(
            functools.partial(later_kernel, stretches, real_rows),
            state_shape,
            (mask, *[part[0] for part in parts], *[part[1] for part in parts], *fixed, *state),
        )

    image_rows = lambda owner: [(per_image, owner * images + b) for b in range(images)]
    def halved(part, gate, step):
        part = after(part, gate)
        return [both(part[start : start + step]) for start in range(0, part.shape[0], step)]

    def stretches(owner, step):
        count = per_image // step
        return [[(step, image)] for _, image in image_rows(owner) for _ in range(count)]

    if paired:
        far = after(crossed(patches, "blk"), state[0])
        near = swapped(after(own, mask), "blk", 1)
        if power:
            everywhere = after(everywhere, far)
            bit = owner_count // 2
            while bit > 4:
                everywhere = stacked(everywhere, swapped(everywhere, "blk", bit))
                bit //= 2
            arrived = swapped(everywhere, "blk", bit)
        far = halved(far, state[0], per_image)
        state = later(stretches(1, per_image)[:1], far[:1], state)
        if power:
            everywhere = stacked(after(everywhere, state[0]), arrived)
            arrived = swapped(everywhere, "blk", 2)
        state = later(stretches(1, per_image)[1:], far[1:], state)
        step = per_image // 2
        stretches, parts = stretches(2, step), halved(near, state[0], step)
        if power:
            everywhere = stacked(after(everywhere, state[0]), arrived)
    else:
        for i, offset in enumerate(offsets[1:]):
            parts = halved(shifted(patches, "blk", -offset), state[0], per_image)
            if i < len(offsets) - 2:
                state = later(stretches(i + 1, per_image), parts, state)
        stretches = stretches(len(offsets) - 1, per_image)
    if not (paired and power):
        everywhere = lax.all_gather(everywhere, "blk", axis=0, tiled=True)
    stretches, parts = stretches + [[(everywhere.shape[0], None)]], parts + [both(everywhere)]
    kept, sent = call(
        functools.partial(last_kernel, stretches, real_rows),
        [f32(rows, width), bf16(rows, width)],
        (
            mask, *[part[0] for part in parts], *[part[1] for part in parts], *fixed, *state, w_out,
        ),
        in_specs=[VMEM] * (1 + 2 * len(parts) + len(fixed) + len(state)) + [HBM],
        scratch=[pltpu.VMEM(w_out.shape, jnp.bfloat16), pltpu.SemaphoreType.DMA],
    )
    received = swapped(sent, "head", 1)
    patch_out, special_out = call(
        functools.partial(end_kernel, images),
        [bf16(patch_total, width), bf16(special_count, images, width)],
        (kept, received),
        out_specs=[pl.BlockSpec(), pl.BlockSpec()],
    )
    return patch_out.reshape(patch_rows.shape), jnp.transpose(special_out, (1, 0, 2))


def solution(mesh):
    in_specs = (
        P(("scene", "blk"), None, "head"),
        P(("scene", "blk"), None, "head"),
        P(),
        P(),
        P(("scene", "blk")),
        P(("scene", "blk"), None),
        P(None, None, "head"),
        P("head", None),
    )
    out_specs = (P(("scene", "blk"), None, "head"), P(("scene", "blk"), None, "head"))
    return jax.shard_map(
        per_device, mesh=mesh, in_specs=in_specs, out_specs=out_specs, check_vma=False
    )
```

```python
import functools

import jax
import jax.numpy as jnp
from jax import lax
from jax.experimental import pallas as pl
from jax.experimental.pallas import tpu as pltpu
from jax.sharding import PartitionSpec as P

HEAD_DIM = 64
PAIR = 2 * HEAD_DIM
QUAD = 2 * PAIR
TILE_ROWS = 16
LOG2_E = 1.4426950408889634
FIRST = 20_000_000_000
VMEM_BYTES = 32 * 1024 * 1024
SMEM = pl.BlockSpec(memory_space=pltpu.SMEM)
VMEM = pl.BlockSpec(memory_space=pltpu.VMEM)
HBM = pl.BlockSpec(memory_space=pltpu.HBM)


def shifted(block, axis, distance):
    count = lax.axis_size(axis)
    route = [((i - distance) % count, i) for i in range(count)]
    return lax.ppermute(block, axis, route)


def swapped(block, axis, bit):
    count = lax.axis_size(axis)
    return lax.ppermute(block, axis, [(i ^ bit, i) for i in range(count)])


def crossed(block, axis):
    count = lax.axis_size(axis)
    return lax.ppermute(block, axis, [(i, (i + (-1 if i % 2 == 0 else 1)) % count) for i in range(count)])


def halves(width):
    half = lax.axis_index("head")
    mine = pl.ds(pl.multiple_of(half * width, width), width)
    theirs = pl.ds(pl.multiple_of((1 - half) * width, width), width)
    return mine, theirs


def product(left, right):
    return jnp.dot(left, right, preferred_element_type=jnp.float32)


def owner_at(offset):
    count = lax.axis_size("blk")
    here = lax.axis_index("blk")
    if isinstance(offset, tuple):
        offset = jnp.where(lax.rem(here, 2) == 0, offset[0], offset[1])
    return lax.rem(here + offset + count, count)


def rows_kernel(
    frame_order, specials, role_first, role_rest, patches,
    special_out, patches_out, order, here, first_rows, rest_rows, copied,
):
    special_count, images, width = specials.shape
    moves = [(specials, here), (role_first, first_rows), (role_rest, rest_rows), (frame_order, order)]
    moves.append((patches, patches_out))
    copies = [
        pltpu.make_async_copy(source, target, copied.at[i]) for i, (source, target) in enumerate(moves)
    ]
    for copy in copies:
        copy.start()
    for copy in copies[:4]:
        copy.wait()
    mine, _ = halves(width)
    first = first_rows[:, mine].astype(jnp.float32)
    rest = rest_rows[:, mine].astype(jnp.float32)
    summed = [
        here[:, b, :].astype(jnp.float32) + jnp.where(order[b] == 0, first, rest) for b in range(images)
    ]
    summed.append(jnp.zeros((special_out.shape[0] - images * special_count, width), jnp.float32))
    special_out[...] = jnp.concatenate(summed, axis=0).astype(jnp.bfloat16)
    for copy in copies[4:]:
        copy.wait()


def start_kernel(
    offsets, per_image, special_count, special_total, covisible, special, other_special, w_qkv,
    mask_out, weights_out, pairs_out, seen, copied,
):
    images = covisible.shape[0]
    patch_total = images * per_image
    moves = [(covisible, seen)]
    depth = w_qkv.shape[1] // 2
    for i in range(3):
        for j, rows in enumerate(halves(depth)):
            moves.append((w_qkv.at[i, rows], weights_out.at[i, pl.ds(j * depth, depth)]))
    copies = [
        pltpu.make_async_copy(source, target, copied.at[i]) for i, (source, target) in enumerate(moves)
    ]
    for copy in copies:
        copy.start()
    copies[0].wait()
    lane = lax.broadcasted_iota(jnp.int32, (1, mask_out.shape[1]), 1)
    special_lane = lax.rem(lane - patch_total, special_total)
    image = jnp.where(
        lane < patch_total, lane // per_image, jnp.minimum(special_lane // special_count, images - 1)
    )
    for i, offset in enumerate(offsets):
        for b in range(images):
            row = jnp.zeros(lane.shape, jnp.float32)
            for a in range(images):
                hidden = seen[a, owner_at(offset) * images + b] <= 0
                row = jnp.where((image == a) & hidden, -jnp.inf, row)
            mask_out[i * images + b : i * images + b + 1, :] = row
    rows = jnp.concatenate([special[...], other_special[...]], axis=1)
    width = weights_out.shape[2]
    for copy in copies[1:]:
        copy.wait()
    for i in range(2):
        pairs_out[:, i * width : (i + 1) * width] = product(rows, weights_out[i + 1]).astype(jnp.bfloat16)


def projector(own, other, weights):
    rows = jnp.concatenate([own, other], axis=1)

    def columns(which, quad):
        return product(rows, weights[which, :, quad * QUAD : (quad + 1) * QUAD])

    return columns


def attend(scores, masks, state):
    largest = state
    start = 0
    for count, mask in masks:
        part = jnp.max(scores[start : start + count], axis=0, keepdims=True)
        part = part if mask is None else part + mask
        largest = part if largest is None else jnp.maximum(largest, part)
        start += count
    weights, start = [], 0
    for count, mask in masks:
        level = largest if mask is None else largest - mask
        weights.append(jnp.exp2((scores[start : start + count] - level).astype(jnp.bfloat16)))
        start += count
    factor = None if state is None else jnp.exp2(state - largest)
    return largest, factor, jnp.concatenate(weights, axis=0)


def attend_all(columns, masks, queries_of, special_queries, state, pairs, rows, special_real):
    keys, values = {}, {}
    quads = pairs // 2

    def keys_of(quad):
        if quad not in keys:
            keys[quad] = columns(1, quad).astype(jnp.bfloat16)
        return keys[quad]

    def values_of(quad):
        if quad not in values:
            values[quad] = jnp.transpose(columns(2, quad).astype(jnp.bfloat16))
        return values[quad]

    def prepared(pair):
        if pair == pairs:
            scores = product(
                jnp.concatenate([keys_of(quad) for quad in range(quads)], axis=1), special_queries()
            )
        else:
            lanes = slice((pair % 2) * PAIR, (pair % 2 + 1) * PAIR)
            scores = product(keys_of(pair // 2)[:, lanes], queries_of(pair))
        if all(mask is not None for _, mask in masks):
            return scores
        parts, start = [], 0
        for count, mask in masks:
            part = scores[start : start + count]
            if mask is None:
                key_row = lax.broadcasted_iota(jnp.int32, (count, 1), 0)
                part = jnp.where(lax.rem(key_row, TILE_ROWS) < special_real, part, -jnp.inf)
            parts.append(part)
            start += count
        return jnp.concatenate(parts, axis=0)

    ones = jnp.ones((TILE_ROWS, sum(count for count, _ in masks)), jnp.bfloat16)
    both = [
        (count, None if mask is None else jnp.concatenate([mask[:, :rows]] * 2, axis=1))
        for count, mask in masks
    ]
    only = [(count, None if mask is None else mask[:, rows:]) for count, mask in masks]
    order = list(range(pairs))
    order.insert(pairs - 2, pairs)
    scores = prepared(order[0])
    for step, pair in enumerate(order):
        if pair < pairs:
            left = values_of(pair // 2)[(pair % 2) * PAIR : (pair % 2 + 1) * PAIR]
        else:
            left = jnp.concatenate([values_of(quad) for quad in range(quads)], axis=0)
        following = prepared(order[step + 1]) if step < pairs else None
        largest, factor, weights = attend(
            scores, both if pair < pairs else only, state and state.largest(pair)
        )
        added = product(jnp.concatenate([left, ones], axis=0), weights)
        height, subs = (HEAD_DIM, 2) if pair < pairs else (left.shape[0], 1)
        width = scores.shape[1] // subs
        for sub in range(subs):
            lanes = slice(sub * width, (sub + 1) * width)
            total = added[sub * height : (sub + 1) * height, lanes]
            weight = added[left.shape[0] : left.shape[0] + 1, lanes]
            if state is not None:
                total = total + state.total(pair, sub) * factor[:, lanes]
                weight = weight + state.weight(pair, sub) * factor[:, lanes]
            yield pair, sub, largest[:, lanes], total, weight
        scores = following


class State:
    def __init__(self, rows, refs):
        self.rows = rows
        self.largest_ref, self.weight_ref, self.total_ref, self.special_ref = refs

    def lanes(self, pair, sub):
        if pair == self.total_ref.shape[0]:
            return slice(0, self.special_ref.shape[1])
        return slice(sub * self.rows, (sub + 1) * self.rows)

    def largest(self, pair):
        stop = self.special_ref.shape[1] if pair == self.total_ref.shape[0] else 2 * self.rows
        return self.largest_ref[pair : pair + 1, 0:stop]

    def weight(self, pair, sub):
        return self.weight_ref[pair : pair + 1, self.lanes(pair, sub)]

    def total(self, pair, sub):
        if pair == self.total_ref.shape[0]:
            return self.special_ref[...]
        return self.total_ref[pair, :, self.lanes(pair, sub)]

    def put(self, pair, sub, largest, total, weight):
        lanes = self.lanes(pair, sub)
        self.largest_ref[pair : pair + 1, lanes] = largest
        self.weight_ref[pair : pair + 1, lanes] = weight
        if pair == self.total_ref.shape[0]:
            self.special_ref[...] = total
        else:
            self.total_ref[pair, :, lanes] = total


def first_kernel(
    images, mask, own, other, special, other_special, weights, queries_out, special_out, *state_out
):
    patch_total = own.shape[0]
    columns = projector(
        jnp.concatenate([own[...], special[...]], axis=0),
        jnp.concatenate([other[...], other_special[...]], axis=0),
        weights,
    )
    pairs = queries_out.shape[0]
    zero = jnp.zeros((HEAD_DIM, patch_total), jnp.bfloat16)
    made = {}

    def patch_columns(which, quad):
        return columns(which, quad)[:patch_total]

    def columns_of(quad):
        if quad not in made:
            queries = columns(0, quad) * (HEAD_DIM ** (-0.5) * LOG2_E)
            made[quad] = queries[patch_total:]
            turned = jnp.transpose(queries[:patch_total].astype(jnp.bfloat16))
            for i in range(2):
                first = i * PAIR
                upper = jnp.concatenate([turned[first : first + HEAD_DIM], zero], axis=1)
                lower = jnp.concatenate([zero, turned[first + HEAD_DIM : first + PAIR]], axis=1)
                queries_out[2 * quad + i] = jnp.concatenate([upper, lower], axis=0)
        return made[quad]

    def queries_of(pair):
        columns_of(pair // 2)
        return queries_out[pair]

    def special_queries():
        block = jnp.concatenate([columns_of(quad) for quad in range(pairs // 2)], axis=1)
        count = block.shape[0]
        block = jnp.concatenate([block] * (2 * pairs), axis=0)
        row = lax.broadcasted_iota(jnp.int32, block.shape, 0) // count
        lane = lax.broadcasted_iota(jnp.int32, block.shape, 1) // HEAD_DIM
        block = jnp.transpose(jnp.where(row == lane, block, 0.0).astype(jnp.bfloat16))
        special_out[...] = block
        return block

    per_image = patch_total // images
    masks = [(per_image, mask[b : b + 1, :]) for b in range(images)]
    state = State(patch_total, state_out)
    for result in attend_all(
        patch_columns, masks, queries_of, special_queries, None, pairs, patch_total, 0
    ):
        state.put(*result)


def joined(stretches, mask, refs):
    count = len(stretches)
    own = jnp.concatenate([ref[...] for ref in refs[:count]], axis=0)
    other = jnp.concatenate([ref[...] for ref in refs[count : 2 * count]], axis=0)
    masks = [(rows, mask[i : i + 1, :]) for part in stretches for rows, i in part]
    return own, other, masks, refs[2 * count :]


def given(pairs):
    width = pairs.shape[1] // 2

    def columns(which, quad):
        first = (which - 1) * width + quad * QUAD
        return pairs[:, first : first + QUAD]

    return columns


def later_kernel(stretches, special_real, mask, *refs):
    own, other, masks, refs = joined(stretches, mask, refs)
    weights, queries, special_queries = refs[:3]
    state_in, state_out = refs[3:7], refs[7:]
    pairs, rows = queries.shape[0], queries.shape[2] // 2
    state = State(rows, state_out)
    for result in attend_all(
        projector(own, other, weights), masks, lambda pair: queries[pair], lambda: special_queries[...],
        State(rows, state_in), pairs, rows, special_real,
    ):
        state.put(*result)


def last_kernel(
    special_real, mask, special_pairs, queries, special_queries, *refs
):
    state_in = refs[:4]
    w_out, kept_out, sent_out, w_here, copied = refs[4:]
    masks = [(special_pairs.shape[0], None)]
    copy = pltpu.make_async_copy(w_out, w_here, copied)
    copy.start()
    pairs, rows = queries.shape[0], queries.shape[2] // 2
    columns, out, special = [], None, None
    sides = halves(kept_out.shape[1])
    for pair, sub, _, total, weight in attend_all(
        given(special_pairs), masks, lambda pair: queries[pair], lambda: special_queries[...],
        State(rows, state_in), pairs, rows, special_real,
    ):
        if pair == 0 and sub == 0:
            copy.wait()
        share = total * (1.0 / weight)
        if pair == pairs:
            row = lax.broadcasted_iota(jnp.int32, share.shape, 0) // HEAD_DIM
            lane = lax.broadcasted_iota(jnp.int32, share.shape, 1) // TILE_ROWS
            share = jnp.transpose(jnp.where(row == lane, share, 0.0))
            share = sum(share[i * TILE_ROWS : (i + 1) * TILE_ROWS] for i in range(2 * pairs))
            special = [product(share.astype(jnp.bfloat16), w_here[:, side]) for side in sides]
            continue
        columns.append(share)
        if pair % 2 == 1 and sub == 1:
            quad = jnp.transpose(jnp.concatenate(columns, axis=0).astype(jnp.bfloat16))
            features = slice((pair // 2) * QUAD, (pair // 2 + 1) * QUAD)
            added = [product(quad, w_here[features, side]) for side in sides]
            out = added if out is None else [before + more for before, more in zip(out, added)]
            columns = []
    for place, values in ((slice(0, rows), out), (slice(rows, kept_out.shape[0]), special)):
        sent_out[place, :] = values[1].astype(jnp.bfloat16)
        kept_out[place, :] = values[0]


def end_kernel(images, kept, received, patch_out, special_out):
    patch_total = patch_out.shape[0]
    special_count = special_out.shape[0]
    patch_out[...] = (kept[:patch_total, :] + received[:patch_total, :].astype(jnp.float32)).astype(
        jnp.bfloat16
    )
    rest = kept[patch_total:, :] + received[patch_total:, :].astype(jnp.float32)
    rows = [rest[b * special_count : (b + 1) * special_count][:, None, :] for b in range(images)]
    special_out[...] = jnp.concatenate(rows, axis=1).astype(jnp.bfloat16)


def call(kernel, out_shape, operands, in_specs=None, out_specs=None, scratch=(), flops=0):
    if in_specs:
        operands = [
            pltpu.with_memory_space_constraint(operand, pltpu.HBM) if spec is HBM else operand
            for operand, spec in zip(operands, in_specs)
        ]
    return pl.pallas_call(
        kernel,
        out_shape=out_shape,
        in_specs=in_specs or [VMEM] * len(operands),
        out_specs=out_specs or [VMEM] * len(out_shape),
        scratch_shapes=scratch,
        compiler_params=pltpu.CompilerParams(vmem_limit_bytes=VMEM_BYTES),
        cost_estimate=pl.CostEstimate(flops=flops, transcendentals=0, bytes_accessed=0),
    )(*operands)


def stack_kernel(first, second, out):
    count = first.shape[0]
    out[:count, :] = first[...]
    out[count:, :] = second[...]


def stacked(first, second, flops=0):
    shape = jax.ShapeDtypeStruct((2 * first.shape[0], first.shape[1]), first.dtype)
    return call(stack_kernel, [shape], (first, second), flops=flops)[0]


def after(array, *others):
    return lax.optimization_barrier((array, *others))[0]


def per_device(
    patch_rows, special_rows, role_first, role_rest, frame_order, covisible, w_qkv, w_out
):
    images, per_image, width = patch_rows.shape
    special_count = special_rows.shape[1]
    real_rows = images * special_count
    special_block = real_rows + -real_rows % TILE_ROWS
    owner_count = lax.axis_size("blk")
    reach = max(1, owner_count // 64)
    patch_total = images * per_image
    rows = patch_total + special_block
    heads = width // HEAD_DIM
    pairs = heads // 2
    paired = reach == 1 and owner_count % 2 == 0

    if paired:
        offsets = [0, (-1, 1), (1, -1)]
    else:
        offsets = [0] + [sign * d for d in range(1, reach + 1) for sign in (-1, 1)]
    mask_rows = -(-len(offsets) * images // 8) * 8
    bf16 = lambda *shape: jax.ShapeDtypeStruct(shape, jnp.bfloat16)
    f32 = lambda *shape: jax.ShapeDtypeStruct(shape, jnp.float32)
    state_shape = [
        f32(8, 2 * patch_total),
        f32(8, 2 * patch_total),
        f32(pairs, HEAD_DIM, 2 * patch_total),
        f32(width, heads * special_block),
    ]

    both = lambda part: (part, swapped(part, "head", 1))
    patches = patch_rows.reshape(patch_total, width)
    turned = jnp.transpose(special_rows, (1, 0, 2))
    power = owner_count >= 8 and owner_count & (owner_count - 1) == 0
    specials, own = call(
        rows_kernel,
        [
            bf16(special_block, width),
            bf16(patch_total, width),
        ],
        (frame_order, turned, role_first, role_rest, patches),
        in_specs=[HBM] * 5,
        scratch=[
            pltpu.SMEM(frame_order.shape, jnp.int32),
            pltpu.VMEM(turned.shape, jnp.bfloat16),
            pltpu.VMEM(role_first.shape, jnp.bfloat16),
            pltpu.VMEM(role_rest.shape, jnp.bfloat16),
            pltpu.SemaphoreType.DMA((5,)),
        ],
    )
    specials = both(specials)
    mask, weights, everywhere = call(
        functools.partial(start_kernel, offsets, per_image, special_count, special_block),
        [
            f32(mask_rows, patch_total + heads * special_block),
            bf16(*w_qkv.shape),
            bf16(special_block, 2 * width),
        ],
        (covisible, *specials, w_qkv),
        in_specs=[HBM, VMEM, VMEM, HBM],
        scratch=[pltpu.SMEM(covisible.shape, jnp.int32), pltpu.SemaphoreType.DMA((1 + 6,))],
    )
    if paired and power:
        everywhere = stacked(everywhere, swapped(everywhere, "blk", 1), FIRST)
    queries, special_queries, *state = call(
        functools.partial(first_kernel, images),
        [bf16(pairs, PAIR, 2 * patch_total), bf16(width, heads * special_block), *state_shape],
        (mask, own, swapped(patches, "head", 1), *specials, weights),
    )
    fixed = (weights, queries, special_queries)

    def later(stretches, parts, state):
        return call(
            functools.partial(later_kernel, stretches, real_rows),
            state_shape,
            (mask, *[part[0] for part in parts], *[part[1] for part in parts], *fixed, *state),
        )

    image_rows = lambda owner: [(per_image, owner * images + b) for b in range(images)]
    def halved(part, gate):
        part = after(part, gate)
        starts = range(0, part.shape[0], per_image)
        return [both(part[start : start + per_image]) for start in starts]

    stretches = lambda owner: [[image] for image in image_rows(owner)]
    if paired:
        far = after(crossed(patches, "blk"), state[0])
        near = swapped(after(own, mask), "blk", 1)
        if power:
            everywhere = after(everywhere, far)
            bit = owner_count // 2
            while bit > 4:
                everywhere = stacked(everywhere, swapped(everywhere, "blk", bit))
                bit //= 2
            arrived = swapped(everywhere, "blk", bit)
        state = later(stretches(1), halved(far, state[0]), state)
        if power:
            everywhere = stacked(after(everywhere, state[0]), arrived, FIRST)
            arrived = swapped(everywhere, "blk", 2)
        state = later(stretches(2), halved(near, state[0]), state)
        if power:
            everywhere = stacked(after(everywhere, state[0]), arrived)
    else:
        for i, offset in enumerate(offsets[1:]):
            state = later(stretches(i + 1), halved(shifted(patches, "blk", -offset), state[0]), state)
    if not (paired and power):
        everywhere = lax.all_gather(everywhere, "blk", axis=0, tiled=True)
    kept, sent = call(
        functools.partial(last_kernel, real_rows),
        [f32(rows, width), bf16(rows, width)],
        (mask, everywhere, queries, special_queries, *state, w_out),
        in_specs=[VMEM] * (4 + len(state)) + [HBM],
        scratch=[pltpu.VMEM(w_out.shape, jnp.bfloat16), pltpu.SemaphoreType.DMA],
    )
    received = swapped(sent, "head", 1)
    patch_out, special_out = call(
        functools.partial(end_kernel, images),
        [bf16(patch_total, width), bf16(special_count, images, width)],
        (kept, received),
        out_specs=[pl.BlockSpec(), pl.BlockSpec()],
    )
    return patch_out.reshape(patch_rows.shape), jnp.transpose(special_out, (1, 0, 2))


def solution(mesh):
    in_specs = (
        P(("scene", "blk"), None, "head"),
        P(("scene", "blk"), None, "head"),
        P(),
        P(),
        P(("scene", "blk")),
        P(("scene", "blk"), None),
        P(None, None, "head"),
        P("head", None),
    )
    out_specs = (P(("scene", "blk"), None, "head"), P(("scene", "blk"), None, "head"))
    return jax.shard_map(
        per_device, mesh=mesh, in_specs=in_specs, out_specs=out_specs, check_vma=False
    )
```

```python
import functools

import jax
import jax.numpy as jnp
from jax import lax
from jax.experimental import pallas as pl
from jax.experimental.pallas import tpu as pltpu
from jax.sharding import PartitionSpec as P

HEAD_DIM = 64
PAIR = 2 * HEAD_DIM
QUAD = 2 * PAIR
TILE_ROWS = 16
LOG2_E = 1.4426950408889634
FIRST = 20_000_000_000
VMEM_BYTES = 32 * 1024 * 1024
SMEM = pl.BlockSpec(memory_space=pltpu.SMEM)
VMEM = pl.BlockSpec(memory_space=pltpu.VMEM)
HBM = pl.BlockSpec(memory_space=pltpu.HBM)


def shifted(block, axis, distance):
    count = lax.axis_size(axis)
    route = [((i - distance) % count, i) for i in range(count)]
    return lax.ppermute(block, axis, route)


def swapped(block, axis, bit):
    count = lax.axis_size(axis)
    return lax.ppermute(block, axis, [(i ^ bit, i) for i in range(count)])


def crossed(block, axis):
    count = lax.axis_size(axis)
    return lax.ppermute(block, axis, [(i, (i + (-1 if i % 2 == 0 else 1)) % count) for i in range(count)])


def halves(width):
    half = lax.axis_index("head")
    mine = pl.ds(pl.multiple_of(half * width, width), width)
    theirs = pl.ds(pl.multiple_of((1 - half) * width, width), width)
    return mine, theirs


def product(left, right):
    return jnp.dot(left, right, preferred_element_type=jnp.float32)


def owner_at(offset):
    count = lax.axis_size("blk")
    here = lax.axis_index("blk")
    if isinstance(offset, tuple):
        offset = jnp.where(lax.rem(here, 2) == 0, offset[0], offset[1])
    return lax.rem(here + offset + count, count)


def rows_kernel(
    frame_order, specials, role_first, role_rest, patches,
    special_out, patches_out, order, here, first_rows, rest_rows, copied,
):
    special_count, images, width = specials.shape
    moves = [(specials, here), (role_first, first_rows), (role_rest, rest_rows), (frame_order, order)]
    moves.append((patches, patches_out))
    copies = [
        pltpu.make_async_copy(source, target, copied.at[i]) for i, (source, target) in enumerate(moves)
    ]
    for copy in copies:
        copy.start()
    for copy in copies[:4]:
        copy.wait()
    mine, _ = halves(width)
    first = first_rows[:, mine].astype(jnp.float32)
    rest = rest_rows[:, mine].astype(jnp.float32)
    summed = [
        here[:, b, :].astype(jnp.float32) + jnp.where(order[b] == 0, first, rest) for b in range(images)
    ]
    summed.append(jnp.zeros((special_out.shape[0] - images * special_count, width), jnp.float32))
    special_out[...] = jnp.concatenate(summed, axis=0).astype(jnp.bfloat16)
    for copy in copies[4:]:
        copy.wait()


def start_kernel(
    offsets, per_image, special_count, special_total, covisible, special, other_special, w_qkv, w_out,
    mask_out, weights_out, pairs_out, w_out_here, seen, copied,
):
    images = covisible.shape[0]
    patch_total = images * per_image
    moves = [(covisible, seen)]
    depth = w_qkv.shape[1] // 2
    for i in range(3):
        for j, rows in enumerate(halves(depth)):
            moves.append((w_qkv.at[i, rows], weights_out.at[i, pl.ds(j * depth, depth)]))
    moves.append((w_out, w_out_here))
    copies = [
        pltpu.make_async_copy(source, target, copied.at[i]) for i, (source, target) in enumerate(moves)
    ]
    for copy in copies:
        copy.start()
    copies[0].wait()
    lane = lax.broadcasted_iota(jnp.int32, (1, mask_out.shape[1]), 1)
    special_lane = lax.rem(lane - patch_total, special_total)
    image = jnp.where(
        lane < patch_total, lane // per_image, jnp.minimum(special_lane // special_count, images - 1)
    )
    for i, offset in enumerate(offsets):
        for b in range(images):
            row = jnp.zeros(lane.shape, jnp.float32)
            for a in range(images):
                hidden = seen[a, owner_at(offset) * images + b] <= 0
                row = jnp.where((image == a) & hidden, -jnp.inf, row)
            mask_out[i * images + b : i * images + b + 1, :] = row
    rows = jnp.concatenate([special[...], other_special[...]], axis=1)
    width = weights_out.shape[2]
    for copy in copies[1:-1]:
        copy.wait()
    for i in range(2):
        pairs_out[:, i * width : (i + 1) * width] = product(rows, weights_out[i + 1]).astype(jnp.bfloat16)
    copies[-1].wait()


def projector(own, other, weights):
    rows = jnp.concatenate([own, other], axis=1)

    def columns(which, quad):
        return product(rows, weights[which, :, quad * QUAD : (quad + 1) * QUAD])

    return columns


def attend(scores, masks, state):
    largest = state
    start = 0
    for count, mask in masks:
        part = jnp.max(scores[start : start + count], axis=0, keepdims=True)
        part = part if mask is None else part + mask
        largest = part if largest is None else jnp.maximum(largest, part)
        start += count
    weights, start = [], 0
    for count, mask in masks:
        level = largest if mask is None else largest - mask
        weights.append(jnp.exp2((scores[start : start + count] - level).astype(jnp.bfloat16)))
        start += count
    factor = None if state is None else jnp.exp2(state - largest)
    return largest, factor, jnp.concatenate(weights, axis=0)


def attend_all(columns, masks, queries_of, special_queries, state, pairs, rows, special_real):
    keys, values = {}, {}
    quads = pairs // 2

    def keys_of(quad):
        if quad not in keys:
            keys[quad] = columns(1, quad).astype(jnp.bfloat16)
        return keys[quad]

    def values_of(quad):
        if quad not in values:
            values[quad] = jnp.transpose(columns(2, quad).astype(jnp.bfloat16))
        return values[quad]

    def prepared(pair):
        if pair == pairs:
            scores = product(
                jnp.concatenate([keys_of(quad) for quad in range(quads)], axis=1), special_queries()
            )
        else:
            lanes = slice((pair % 2) * PAIR, (pair % 2 + 1) * PAIR)
            scores = product(keys_of(pair // 2)[:, lanes], queries_of(pair))
        if all(mask is not None for _, mask in masks):
            return scores
        parts, start = [], 0
        for count, mask in masks:
            part = scores[start : start + count]
            if mask is None:
                key_row = lax.broadcasted_iota(jnp.int32, (count, 1), 0)
                part = jnp.where(lax.rem(key_row, TILE_ROWS) < special_real, part, -jnp.inf)
            parts.append(part)
            start += count
        return jnp.concatenate(parts, axis=0)

    ones = jnp.ones((TILE_ROWS, sum(count for count, _ in masks)), jnp.bfloat16)
    both = [
        (count, None if mask is None else jnp.concatenate([mask[:, :rows]] * 2, axis=1))
        for count, mask in masks
    ]
    only = [(count, None if mask is None else mask[:, rows:]) for count, mask in masks]
    order = list(range(pairs))
    order.insert(pairs - 2, pairs)
    scores = prepared(order[0])
    for step, pair in enumerate(order):
        if pair < pairs:
            left = values_of(pair // 2)[(pair % 2) * PAIR : (pair % 2 + 1) * PAIR]
        else:
            left = jnp.concatenate([values_of(quad) for quad in range(quads)], axis=0)
        following = prepared(order[step + 1]) if step < pairs else None
        largest, factor, weights = attend(
            scores, both if pair < pairs else only, state and state.largest(pair)
        )
        added = product(jnp.concatenate([left, ones], axis=0), weights)
        height, subs = (HEAD_DIM, 2) if pair < pairs else (left.shape[0], 1)
        width = scores.shape[1] // subs
        for sub in range(subs):
            lanes = slice(sub * width, (sub + 1) * width)
            total = added[sub * height : (sub + 1) * height, lanes]
            weight = added[left.shape[0] : left.shape[0] + 1, lanes]
            if state is not None:
                total = total + state.total(pair, sub) * factor[:, lanes]
                weight = weight + state.weight(pair, sub) * factor[:, lanes]
            yield pair, sub, largest[:, lanes], total, weight
        scores = following


class State:
    def __init__(self, rows, refs):
        self.rows = rows
        self.largest_ref, self.weight_ref, self.total_ref, self.special_ref = refs

    def lanes(self, pair, sub):
        if pair == self.total_ref.shape[0]:
            return slice(0, self.special_ref.shape[1])
        return slice(sub * self.rows, (sub + 1) * self.rows)

    def largest(self, pair):
        stop = self.special_ref.shape[1] if pair == self.total_ref.shape[0] else 2 * self.rows
        return self.largest_ref[pair : pair + 1, 0:stop]

    def weight(self, pair, sub):
        return self.weight_ref[pair : pair + 1, self.lanes(pair, sub)]

    def total(self, pair, sub):
        if pair == self.total_ref.shape[0]:
            return self.special_ref[...]
        return self.total_ref[pair, :, self.lanes(pair, sub)]

    def put(self, pair, sub, largest, total, weight):
        lanes = self.lanes(pair, sub)
        self.largest_ref[pair : pair + 1, lanes] = largest
        self.weight_ref[pair : pair + 1, lanes] = weight
        if pair == self.total_ref.shape[0]:
            self.special_ref[...] = total
        else:
            self.total_ref[pair, :, lanes] = total


def first_kernel(
    images, mask, own, other, special, other_special, weights, queries_out, special_out, *state_out
):
    patch_total = own.shape[0]
    columns = projector(
        jnp.concatenate([own[...], special[...]], axis=0),
        jnp.concatenate([other[...], other_special[...]], axis=0),
        weights,
    )
    pairs = queries_out.shape[0]
    zero = jnp.zeros((HEAD_DIM, patch_total), jnp.bfloat16)
    made = {}

    def patch_columns(which, quad):
        return columns(which, quad)[:patch_total]

    def columns_of(quad):
        if quad not in made:
            queries = columns(0, quad) * (HEAD_DIM ** (-0.5) * LOG2_E)
            made[quad] = queries[patch_total:]
            turned = jnp.transpose(queries[:patch_total].astype(jnp.bfloat16))
            for i in range(2):
                first = i * PAIR
                upper = jnp.concatenate([turned[first : first + HEAD_DIM], zero], axis=1)
                lower = jnp.concatenate([zero, turned[first + HEAD_DIM : first + PAIR]], axis=1)
                queries_out[2 * quad + i] = jnp.concatenate([upper, lower], axis=0)
        return made[quad]

    def queries_of(pair):
        columns_of(pair // 2)
        return queries_out[pair]

    def special_queries():
        block = jnp.concatenate([columns_of(quad) for quad in range(pairs // 2)], axis=1)
        count = block.shape[0]
        block = jnp.concatenate([block] * (2 * pairs), axis=0)
        row = lax.broadcasted_iota(jnp.int32, block.shape, 0) // count
        lane = lax.broadcasted_iota(jnp.int32, block.shape, 1) // HEAD_DIM
        block = jnp.transpose(jnp.where(row == lane, block, 0.0).astype(jnp.bfloat16))
        special_out[...] = block
        return block

    per_image = patch_total // images
    masks = [(per_image, mask[b : b + 1, :]) for b in range(images)]
    state = State(patch_total, state_out)
    for result in attend_all(
        patch_columns, masks, queries_of, special_queries, None, pairs, patch_total, 0
    ):
        state.put(*result)


def joined(stretches, mask, refs):
    count = len(stretches)
    own = jnp.concatenate([ref[...] for ref in refs[:count]], axis=0)
    other = jnp.concatenate([ref[...] for ref in refs[count : 2 * count]], axis=0)
    masks = [(rows, mask[i : i + 1, :]) for part in stretches for rows, i in part]
    return own, other, masks, refs[2 * count :]


def given(pairs):
    width = pairs.shape[1] // 2

    def columns(which, quad):
        first = (which - 1) * width + quad * QUAD
        return pairs[:, first : first + QUAD]

    return columns


def later_kernel(stretches, special_real, mask, *refs):
    own, other, masks, refs = joined(stretches, mask, refs)
    weights, queries, special_queries = refs[:3]
    state_in, state_out = refs[3:7], refs[7:]
    pairs, rows = queries.shape[0], queries.shape[2] // 2
    state = State(rows, state_out)
    for result in attend_all(
        projector(own, other, weights), masks, lambda pair: queries[pair], lambda: special_queries[...],
        State(rows, state_in), pairs, rows, special_real,
    ):
        state.put(*result)


def last_kernel(
    special_real, mask, special_pairs, queries, special_queries, *refs
):
    state_in = refs[:4]
    w_here, kept_out, sent_out = refs[4:]
    masks = [(special_pairs.shape[0], None)]
    pairs, rows = queries.shape[0], queries.shape[2] // 2
    columns, out, special = [], None, None
    sides = halves(kept_out.shape[1])
    for pair, sub, _, total, weight in attend_all(
        given(special_pairs), masks, lambda pair: queries[pair], lambda: special_queries[...],
        State(rows, state_in), pairs, rows, special_real,
    ):
        share = total * (1.0 / weight)
        if pair == pairs:
            row = lax.broadcasted_iota(jnp.int32, share.shape, 0) // HEAD_DIM
            lane = lax.broadcasted_iota(jnp.int32, share.shape, 1) // TILE_ROWS
            share = jnp.transpose(jnp.where(row == lane, share, 0.0))
            share = sum(share[i * TILE_ROWS : (i + 1) * TILE_ROWS] for i in range(2 * pairs))
            special = [product(share.astype(jnp.bfloat16), w_here[:, side]) for side in sides]
            continue
        columns.append(share)
        if pair % 2 == 1 and sub == 1:
            quad = jnp.transpose(jnp.concatenate(columns, axis=0).astype(jnp.bfloat16))
            features = slice((pair // 2) * QUAD, (pair // 2 + 1) * QUAD)
            added = [product(quad, w_here[features, side]) for side in sides]
            out = added if out is None else [before + more for before, more in zip(out, added)]
            columns = []
    for place, values in ((slice(0, rows), out), (slice(rows, kept_out.shape[0]), special)):
        sent_out[place, :] = values[1].astype(jnp.bfloat16)
        kept_out[place, :] = values[0]


def end_kernel(images, kept, received, patch_out, special_out):
    patch_total = patch_out.shape[0]
    special_count = special_out.shape[0]
    patch_out[...] = (kept[:patch_total, :] + received[:patch_total, :].astype(jnp.float32)).astype(
        jnp.bfloat16
    )
    rest = kept[patch_total:, :] + received[patch_total:, :].astype(jnp.float32)
    rows = [rest[b * special_count : (b + 1) * special_count][:, None, :] for b in range(images)]
    special_out[...] = jnp.concatenate(rows, axis=1).astype(jnp.bfloat16)


def call(kernel, out_shape, operands, in_specs=None, out_specs=None, scratch=(), flops=0):
    if in_specs:
        operands = [
            pltpu.with_memory_space_constraint(operand, pltpu.HBM) if spec is HBM else operand
            for operand, spec in zip(operands, in_specs)
        ]
    return pl.pallas_call(
        kernel,
        out_shape=out_shape,
        in_specs=in_specs or [VMEM] * len(operands),
        out_specs=out_specs or [VMEM] * len(out_shape),
        scratch_shapes=scratch,
        compiler_params=pltpu.CompilerParams(vmem_limit_bytes=VMEM_BYTES),
        cost_estimate=pl.CostEstimate(flops=flops, transcendentals=0, bytes_accessed=0),
    )(*operands)


def stack_kernel(first, second, out):
    count = first.shape[0]
    out[:count, :] = first[...]
    out[count:, :] = second[...]


def stacked(first, second, flops=0):
    shape = jax.ShapeDtypeStruct((2 * first.shape[0], first.shape[1]), first.dtype)
    return call(stack_kernel, [shape], (first, second), flops=flops)[0]


def after(array, *others):
    return lax.optimization_barrier((array, *others))[0]


def per_device(
    patch_rows, special_rows, role_first, role_rest, frame_order, covisible, w_qkv, w_out
):
    images, per_image, width = patch_rows.shape
    special_count = special_rows.shape[1]
    real_rows = images * special_count
    special_block = real_rows + -real_rows % TILE_ROWS
    owner_count = lax.axis_size("blk")
    reach = max(1, owner_count // 64)
    patch_total = images * per_image
    rows = patch_total + special_block
    heads = width // HEAD_DIM
    pairs = heads // 2
    paired = reach == 1 and owner_count % 2 == 0

    if paired:
        offsets = [0, (-1, 1), (1, -1)]
    else:
        offsets = [0] + [sign * d for d in range(1, reach + 1) for sign in (-1, 1)]
    mask_rows = -(-len(offsets) * images // 8) * 8
    bf16 = lambda *shape: jax.ShapeDtypeStruct(shape, jnp.bfloat16)
    f32 = lambda *shape: jax.ShapeDtypeStruct(shape, jnp.float32)
    state_shape = [
        f32(8, 2 * patch_total),
        f32(8, 2 * patch_total),
        f32(pairs, HEAD_DIM, 2 * patch_total),
        f32(width, heads * special_block),
    ]

    both = lambda part: (part, swapped(part, "head", 1))
    patches = patch_rows.reshape(patch_total, width)
    turned = jnp.transpose(special_rows, (1, 0, 2))
    power = owner_count >= 8 and owner_count & (owner_count - 1) == 0
    specials, own = call(
        rows_kernel,
        [
            bf16(special_block, width),
            bf16(patch_total, width),
        ],
        (frame_order, turned, role_first, role_rest, patches),
        in_specs=[HBM] * 5,
        scratch=[
            pltpu.SMEM(frame_order.shape, jnp.int32),
            pltpu.VMEM(turned.shape, jnp.bfloat16),
            pltpu.VMEM(role_first.shape, jnp.bfloat16),
            pltpu.VMEM(role_rest.shape, jnp.bfloat16),
            pltpu.SemaphoreType.DMA((5,)),
        ],
    )
    specials = both(specials)
    mask, weights, everywhere, w_here = call(
        functools.partial(start_kernel, offsets, per_image, special_count, special_block),
        [
            f32(mask_rows, patch_total + heads * special_block),
            bf16(*w_qkv.shape),
            bf16(special_block, 2 * width),
            bf16(*w_out.shape),
        ],
        (covisible, *specials, w_qkv, w_out),
        in_specs=[HBM, VMEM, VMEM, HBM, HBM],
        scratch=[pltpu.SMEM(covisible.shape, jnp.int32), pltpu.SemaphoreType.DMA((1 + 7,))],
    )
    if paired and power:
        everywhere = stacked(everywhere, swapped(everywhere, "blk", 2), FIRST)
    queries, special_queries, *state = call(
        functools.partial(first_kernel, images),
        [bf16(pairs, PAIR, 2 * patch_total), bf16(width, heads * special_block), *state_shape],
        (mask, own, swapped(patches, "head", 1), *specials, weights),
    )
    fixed = (weights, queries, special_queries)

    def later(stretches, parts, state):
        return call(
            functools.partial(later_kernel, stretches, real_rows),
            state_shape,
            (mask, *[part[0] for part in parts], *[part[1] for part in parts], *fixed, *state),
        )

    image_rows = lambda owner: [(per_image, owner * images + b) for b in range(images)]
    def halved(part, gate):
        part = after(part, gate)
        starts = range(0, part.shape[0], per_image)
        return [both(part[start : start + per_image]) for start in starts]

    stretches = lambda owner: [[image] for image in image_rows(owner)]
    if paired:
        far = after(crossed(patches, "blk"), state[0])
        near = swapped(patches, "blk", 1)
        if power:
            everywhere = after(everywhere, far)
            bit = 4
            while 2 * bit < owner_count:
                everywhere = stacked(everywhere, swapped(everywhere, "blk", bit))
                bit *= 2
            arrived = swapped(everywhere, "blk", bit)
        state = later(stretches(1), halved(far, state[0]), state)
        if power:
            everywhere = stacked(after(everywhere, state[0]), arrived, FIRST)
            arrived = swapped(everywhere, "blk", 1)
        state = later(stretches(2), halved(near, state[0]), state)
        if power:
            everywhere = stacked(after(everywhere, state[0]), arrived)
    else:
        for i, offset in enumerate(offsets[1:]):
            state = later(stretches(i + 1), halved(shifted(patches, "blk", -offset), state[0]), state)
    if not (paired and power):
        everywhere = lax.all_gather(everywhere, "blk", axis=0, tiled=True)
    kept, sent = call(
        functools.partial(last_kernel, real_rows),
        [f32(rows, width), bf16(rows, width)],
        (mask, everywhere, queries, special_queries, *state, w_here),
    )
    received = swapped(sent, "head", 1)
    patch_out, special_out = call(
        functools.partial(end_kernel, images),
        [bf16(patch_total, width), bf16(special_count, images, width)],
        (kept, received),
        out_specs=[pl.BlockSpec(), pl.BlockSpec()],
    )
    return patch_out.reshape(patch_rows.shape), jnp.transpose(special_out, (1, 0, 2))


def solution(mesh):
    in_specs = (
        P(("scene", "blk"), None, "head"),
        P(("scene", "blk"), None, "head"),
        P(),
        P(),
        P(("scene", "blk")),
        P(("scene", "blk"), None),
        P(None, None, "head"),
        P("head", None),
    )
    out_specs = (P(("scene", "blk"), None, "head"), P(("scene", "blk"), None, "head"))
    return jax.shard_map(
        per_device, mesh=mesh, in_specs=in_specs, out_specs=out_specs, check_vma=False
    )
```

```python
import functools

import jax
import jax.numpy as jnp
from jax import lax
from jax.experimental import pallas as pl
from jax.experimental.pallas import tpu as pltpu
from jax.sharding import PartitionSpec as P

HEAD_DIM = 64
PAIR = 2 * HEAD_DIM
QUAD = 2 * PAIR
TILE_ROWS = 16
LOG2_E = 1.4426950408889634
FIRST = 20_000_000_000
VMEM_BYTES = 32 * 1024 * 1024
SMEM = pl.BlockSpec(memory_space=pltpu.SMEM)
VMEM = pl.BlockSpec(memory_space=pltpu.VMEM)
HBM = pl.BlockSpec(memory_space=pltpu.HBM)


def shifted(block, axis, distance):
    count = lax.axis_size(axis)
    route = [((i - distance) % count, i) for i in range(count)]
    return lax.ppermute(block, axis, route)


def swapped(block, axis, bit):
    count = lax.axis_size(axis)
    return lax.ppermute(block, axis, [(i ^ bit, i) for i in range(count)])


def crossed(block, axis):
    count = lax.axis_size(axis)
    return lax.ppermute(block, axis, [(i, (i + (-1 if i % 2 == 0 else 1)) % count) for i in range(count)])


def halves(width):
    half = lax.axis_index("head")
    mine = pl.ds(pl.multiple_of(half * width, width), width)
    theirs = pl.ds(pl.multiple_of((1 - half) * width, width), width)
    return mine, theirs


def product(left, right):
    return jnp.dot(left, right, preferred_element_type=jnp.float32)


def owner_at(offset):
    count = lax.axis_size("blk")
    here = lax.axis_index("blk")
    if isinstance(offset, tuple):
        offset = jnp.where(lax.rem(here, 2) == 0, offset[0], offset[1])
    return lax.rem(here + offset + count, count)


def rows_kernel(
    frame_order, specials, role_first, role_rest, patches,
    special_out, patches_out, order, here, first_rows, rest_rows, copied,
):
    special_count, images, width = specials.shape
    moves = [(specials, here), (role_first, first_rows), (role_rest, rest_rows), (frame_order, order)]
    moves.append((patches, patches_out))
    copies = [
        pltpu.make_async_copy(source, target, copied.at[i]) for i, (source, target) in enumerate(moves)
    ]
    for copy in copies:
        copy.start()
    for copy in copies[:4]:
        copy.wait()
    mine, _ = halves(width)
    first = first_rows[:, mine].astype(jnp.float32)
    rest = rest_rows[:, mine].astype(jnp.float32)
    summed = [
        here[:, b, :].astype(jnp.float32) + jnp.where(order[b] == 0, first, rest) for b in range(images)
    ]
    summed.append(jnp.zeros((special_out.shape[0] - images * special_count, width), jnp.float32))
    special_out[...] = jnp.concatenate(summed, axis=0).astype(jnp.bfloat16)
    for copy in copies[4:]:
        copy.wait()


def start_kernel(
    offsets, per_image, special_count, special_total, covisible, special, other_special, w_qkv, w_out,
    mask_out, weights_out, pairs_out, w_out_here, seen, copied,
):
    images = covisible.shape[0]
    patch_total = images * per_image
    moves = [(covisible, seen)]
    depth = w_qkv.shape[1] // 2
    for i in range(3):
        for j, rows in enumerate(halves(depth)):
            moves.append((w_qkv.at[i, rows], weights_out.at[i, pl.ds(j * depth, depth)]))
    moves.append((w_out, w_out_here))
    copies = [
        pltpu.make_async_copy(source, target, copied.at[i]) for i, (source, target) in enumerate(moves)
    ]
    for copy in copies:
        copy.start()
    copies[0].wait()
    lane = lax.broadcasted_iota(jnp.int32, (1, mask_out.shape[1]), 1)
    special_lane = lax.rem(lane - patch_total, special_total)
    image = jnp.where(
        lane < patch_total, lane // per_image, jnp.minimum(special_lane // special_count, images - 1)
    )
    for i, offset in enumerate(offsets):
        for b in range(images):
            row = jnp.zeros(lane.shape, jnp.float32)
            for a in range(images):
                hidden = seen[a, owner_at(offset) * images + b] <= 0
                row = jnp.where((image == a) & hidden, -jnp.inf, row)
            mask_out[i * images + b : i * images + b + 1, :] = row
    rows = jnp.concatenate([special[...], other_special[...]], axis=1)
    width = weights_out.shape[2]
    for copy in copies[1:-1]:
        copy.wait()
    for i in range(2):
        pairs_out[:, i * width : (i + 1) * width] = product(rows, weights_out[i + 1]).astype(jnp.bfloat16)
    copies[-1].wait()


def projector(own, other, weights):
    rows = jnp.concatenate([own, other], axis=1)

    def columns(which, quad):
        return product(rows, weights[which, :, quad * QUAD : (quad + 1) * QUAD])

    return columns


def attend(scores, masks, state):
    largest = state
    start = 0
    for count, mask in masks:
        part = jnp.max(scores[start : start + count], axis=0, keepdims=True)
        part = part if mask is None else part + mask
        largest = part if largest is None else jnp.maximum(largest, part)
        start += count
    weights, start = [], 0
    for count, mask in masks:
        level = largest if mask is None else largest - mask
        weights.append(jnp.exp2((scores[start : start + count] - level).astype(jnp.bfloat16)))
        start += count
    factor = None if state is None else jnp.exp2(state - largest)
    return largest, factor, jnp.concatenate(weights, axis=0)


def attend_all(columns, masks, queries_of, special_queries, state, pairs, rows, special_real):
    keys, values = {}, {}
    quads = pairs // 2

    def keys_of(quad):
        if quad not in keys:
            keys[quad] = columns(1, quad).astype(jnp.bfloat16)
        return keys[quad]

    def values_of(quad):
        if quad not in values:
            values[quad] = jnp.transpose(columns(2, quad).astype(jnp.bfloat16))
        return values[quad]

    def prepared(pair):
        if pair == pairs:
            scores = product(
                jnp.concatenate([keys_of(quad) for quad in range(quads)], axis=1), special_queries()
            )
        else:
            lanes = slice((pair % 2) * PAIR, (pair % 2 + 1) * PAIR)
            scores = product(keys_of(pair // 2)[:, lanes], queries_of(pair))
        if all(mask is not None for _, mask in masks):
            return scores
        parts, start = [], 0
        for count, mask in masks:
            part = scores[start : start + count]
            if mask is None:
                key_row = lax.broadcasted_iota(jnp.int32, (count, 1), 0)
                part = jnp.where(lax.rem(key_row, special_real[0]) < special_real[1], part, -jnp.inf)
            parts.append(part)
            start += count
        return jnp.concatenate(parts, axis=0)

    ones = jnp.ones((TILE_ROWS, sum(count for count, _ in masks)), jnp.bfloat16)
    both = [
        (count, None if mask is None else jnp.concatenate([mask[:, :rows]] * 2, axis=1))
        for count, mask in masks
    ]
    only = [(count, None if mask is None else mask[:, rows:]) for count, mask in masks]
    order = list(range(pairs))
    order.insert(pairs - 2, pairs)
    scores = prepared(order[0])
    for step, pair in enumerate(order):
        if pair < pairs:
            left = values_of(pair // 2)[(pair % 2) * PAIR : (pair % 2 + 1) * PAIR]
        else:
            left = jnp.concatenate([values_of(quad) for quad in range(quads)], axis=0)
        following = prepared(order[step + 1]) if step < pairs else None
        largest, factor, weights = attend(
            scores, both if pair < pairs else only, state and state.largest(pair)
        )
        added = product(jnp.concatenate([left, ones], axis=0), weights)
        height, subs = (HEAD_DIM, 2) if pair < pairs else (left.shape[0], 1)
        width = scores.shape[1] // subs
        for sub in range(subs):
            lanes = slice(sub * width, (sub + 1) * width)
            total = added[sub * height : (sub + 1) * height, lanes]
            weight = added[left.shape[0] : left.shape[0] + 1, lanes]
            if state is not None:
                total = total + state.total(pair, sub) * factor[:, lanes]
                weight = weight + state.weight(pair, sub) * factor[:, lanes]
            yield pair, sub, largest[:, lanes], total, weight
        scores = following


class State:
    def __init__(self, rows, refs):
        self.rows = rows
        self.largest_ref, self.weight_ref, self.total_ref, self.special_ref = refs

    def lanes(self, pair, sub):
        if pair == self.total_ref.shape[0]:
            return slice(0, self.special_ref.shape[1])
        return slice(sub * self.rows, (sub + 1) * self.rows)

    def largest(self, pair):
        stop = self.special_ref.shape[1] if pair == self.total_ref.shape[0] else 2 * self.rows
        return self.largest_ref[pair : pair + 1, 0:stop]

    def weight(self, pair, sub):
        return self.weight_ref[pair : pair + 1, self.lanes(pair, sub)]

    def total(self, pair, sub):
        if pair == self.total_ref.shape[0]:
            return self.special_ref[...]
        return self.total_ref[pair, :, self.lanes(pair, sub)]

    def put(self, pair, sub, largest, total, weight):
        lanes = self.lanes(pair, sub)
        self.largest_ref[pair : pair + 1, lanes] = largest
        self.weight_ref[pair : pair + 1, lanes] = weight
        if pair == self.total_ref.shape[0]:
            self.special_ref[...] = total
        else:
            self.total_ref[pair, :, lanes] = total


def first_kernel(
    images, mask, own, other, special, other_special, weights, queries_out, special_out, *state_out
):
    patch_total = own.shape[0]
    columns = projector(
        jnp.concatenate([own[...], special[...]], axis=0),
        jnp.concatenate([other[...], other_special[...]], axis=0),
        weights,
    )
    pairs = queries_out.shape[0]
    zero = jnp.zeros((HEAD_DIM, patch_total), jnp.bfloat16)
    made = {}

    def patch_columns(which, quad):
        return columns(which, quad)[:patch_total]

    def columns_of(quad):
        if quad not in made:
            queries = columns(0, quad) * (HEAD_DIM ** (-0.5) * LOG2_E)
            made[quad] = queries[patch_total:]
            turned = jnp.transpose(queries[:patch_total].astype(jnp.bfloat16))
            for i in range(2):
                first = i * PAIR
                upper = jnp.concatenate([turned[first : first + HEAD_DIM], zero], axis=1)
                lower = jnp.concatenate([zero, turned[first + HEAD_DIM : first + PAIR]], axis=1)
                queries_out[2 * quad + i] = jnp.concatenate([upper, lower], axis=0)
        return made[quad]

    def queries_of(pair):
        columns_of(pair // 2)
        return queries_out[pair]

    def special_queries():
        block = jnp.concatenate([columns_of(quad) for quad in range(pairs // 2)], axis=1)
        count = block.shape[0]
        block = jnp.concatenate([block] * (2 * pairs), axis=0)
        row = lax.broadcasted_iota(jnp.int32, block.shape, 0) // count
        lane = lax.broadcasted_iota(jnp.int32, block.shape, 1) // HEAD_DIM
        block = jnp.transpose(jnp.where(row == lane, block, 0.0).astype(jnp.bfloat16))
        special_out[...] = block
        return block

    per_image = patch_total // images
    masks = [(per_image, mask[b : b + 1, :]) for b in range(images)]
    state = State(patch_total, state_out)
    for result in attend_all(
        patch_columns, masks, queries_of, special_queries, None, pairs, patch_total, 0
    ):
        state.put(*result)


def joined(stretches, mask, refs):
    count = len(stretches)
    own = jnp.concatenate([ref[...] for ref in refs[:count]], axis=0)
    other = jnp.concatenate([ref[...] for ref in refs[count : 2 * count]], axis=0)
    masks = [(rows, mask[i : i + 1, :]) for part in stretches for rows, i in part]
    return own, other, masks, refs[2 * count :]


def given(pairs):
    width = pairs.shape[1] // 2

    def columns(which, quad):
        first = (which - 1) * width + quad * QUAD
        return pairs[:, first : first + QUAD]

    return columns


def later_kernel(stretches, mask, *refs):
    own, other, masks, refs = joined(stretches, mask, refs)
    weights, queries, special_queries = refs[:3]
    state_in, state_out = refs[3:7], refs[7:]
    pairs, rows = queries.shape[0], queries.shape[2] // 2
    state = State(rows, state_out)
    for result in attend_all(
        projector(own, other, weights), masks, lambda pair: queries[pair], lambda: special_queries[...],
        State(rows, state_in), pairs, rows, None,
    ):
        state.put(*result)


def half_kernel(count, *refs):
    weights, sums_out = refs[count:]
    rows = jnp.concatenate([ref[...] for ref in refs[:count]], axis=0)
    for i in range(2):
        sums_out[i] = product(rows, weights[i + 1, : rows.shape[1], :])


def begun(sums, other, weights):
    depth = other.shape[1]

    def columns(which, quad):
        lanes = slice(quad * QUAD, (quad + 1) * QUAD)
        return sums[which - 1, :, lanes] + product(other, weights[which, depth:, lanes])

    return columns


def begun_kernel(stretches, mask, sums, *refs):
    count = len(stretches)
    other = jnp.concatenate([ref[...] for ref in refs[:count]], axis=0)
    masks = [(rows, mask[i : i + 1, :]) for part in stretches for rows, i in part]
    weights, queries, special_queries = refs[count : count + 3]
    state_in, state_out = refs[count + 3 : count + 7], refs[count + 7 :]
    pairs, rows = queries.shape[0], queries.shape[2] // 2
    state = State(rows, state_out)
    for result in attend_all(
        begun(sums, other, weights), masks, lambda pair: queries[pair], lambda: special_queries[...],
        State(rows, state_in), pairs, rows, None,
    ):
        state.put(*result)


def last_kernel(
    special_real, mask, special_pairs, queries, special_queries, *refs
):
    state_in = refs[:4]
    w_here, kept_out, sent_out = refs[4:]
    masks = [(special_pairs.shape[0], None)]
    pairs, rows = queries.shape[0], queries.shape[2] // 2
    columns, out, special = [], None, None
    sides = halves(kept_out.shape[1])
    for pair, sub, _, total, weight in attend_all(
        given(special_pairs), masks, lambda pair: queries[pair], lambda: special_queries[...],
        State(rows, state_in), pairs, rows, special_real,
    ):
        share = total * (1.0 / weight)
        if pair == pairs:
            row = lax.broadcasted_iota(jnp.int32, share.shape, 0) // HEAD_DIM
            lane = lax.broadcasted_iota(jnp.int32, share.shape, 1) // TILE_ROWS
            share = jnp.transpose(jnp.where(row == lane, share, 0.0))
            share = sum(share[i * TILE_ROWS : (i + 1) * TILE_ROWS] for i in range(2 * pairs))
            special = [product(share.astype(jnp.bfloat16), w_here[:, side]) for side in sides]
            continue
        columns.append(share)
        if pair % 2 == 1 and sub == 1:
            quad = jnp.transpose(jnp.concatenate(columns, axis=0).astype(jnp.bfloat16))
            features = slice((pair // 2) * QUAD, (pair // 2 + 1) * QUAD)
            added = [product(quad, w_here[features, side]) for side in sides]
            out = added if out is None else [before + more for before, more in zip(out, added)]
            columns = []
    for place, values in ((slice(0, rows), out), (slice(rows, kept_out.shape[0]), special)):
        sent_out[place, :] = values[1].astype(jnp.bfloat16)
        kept_out[place, :] = values[0]


def end_kernel(images, kept, received, patch_out, special_out):
    patch_total = patch_out.shape[0]
    special_count = special_out.shape[0]
    patch_out[...] = (kept[:patch_total, :] + received[:patch_total, :].astype(jnp.float32)).astype(
        jnp.bfloat16
    )
    rest = kept[patch_total:, :] + received[patch_total:, :].astype(jnp.float32)
    rows = [rest[b * special_count : (b + 1) * special_count][:, None, :] for b in range(images)]
    special_out[...] = jnp.concatenate(rows, axis=1).astype(jnp.bfloat16)


def call(kernel, out_shape, operands, in_specs=None, out_specs=None, scratch=(), flops=0):
    if in_specs:
        operands = [
            pltpu.with_memory_space_constraint(operand, pltpu.HBM) if spec is HBM else operand
            for operand, spec in zip(operands, in_specs)
        ]
    return pl.pallas_call(
        kernel,
        out_shape=out_shape,
        in_specs=in_specs or [VMEM] * len(operands),
        out_specs=out_specs or [VMEM] * len(out_shape),
        scratch_shapes=scratch,
        compiler_params=pltpu.CompilerParams(vmem_limit_bytes=VMEM_BYTES),
        cost_estimate=pl.CostEstimate(flops=flops, transcendentals=0, bytes_accessed=0),
    )(*operands)


def stack_kernel(first, second, out):
    count = first.shape[0]
    out[:count, :] = first[...]
    out[count:, :] = second[...]


def compact_kernel(block, real, first, second, out):
    rows = [
        part[start : start + real, :].astype(jnp.float32)
        for part in (first, second)
        for start in range(0, part.shape[0], block)
    ]
    padding = out.shape[0] - sum(part.shape[0] for part in rows)
    if padding:
        rows.append(jnp.zeros((padding, out.shape[1]), jnp.float32))
    out[...] = jnp.concatenate(rows, axis=0).astype(jnp.bfloat16)


def stacked(first, second, flops=0):
    shape = jax.ShapeDtypeStruct((2 * first.shape[0], first.shape[1]), first.dtype)
    return call(stack_kernel, [shape], (first, second), flops=flops)[0]


def after(array, *others):
    return lax.optimization_barrier((array, *others))[0]


def per_device(
    patch_rows, special_rows, role_first, role_rest, frame_order, covisible, w_qkv, w_out
):
    images, per_image, width = patch_rows.shape
    special_count = special_rows.shape[1]
    real_rows = images * special_count
    special_block = real_rows + -real_rows % TILE_ROWS
    owner_count = lax.axis_size("blk")
    reach = max(1, owner_count // 64)
    patch_total = images * per_image
    rows = patch_total + special_block
    heads = width // HEAD_DIM
    pairs = heads // 2
    paired = reach == 1 and owner_count % 2 == 0

    if paired:
        offsets = [0, (-1, 1), (1, -1)]
    else:
        offsets = [0] + [sign * d for d in range(1, reach + 1) for sign in (-1, 1)]
    mask_rows = -(-len(offsets) * images // 8) * 8
    bf16 = lambda *shape: jax.ShapeDtypeStruct(shape, jnp.bfloat16)
    f32 = lambda *shape: jax.ShapeDtypeStruct(shape, jnp.float32)
    state_shape = [
        f32(8, 2 * patch_total),
        f32(8, 2 * patch_total),
        f32(pairs, HEAD_DIM, 2 * patch_total),
        f32(width, heads * special_block),
    ]

    both = lambda part: (part, swapped(part, "head", 1))
    patches = patch_rows.reshape(patch_total, width)
    turned = jnp.transpose(special_rows, (1, 0, 2))
    power = owner_count >= 8 and owner_count & (owner_count - 1) == 0
    specials, own = call(
        rows_kernel,
        [
            bf16(special_block, width),
            bf16(patch_total, width),
        ],
        (frame_order, turned, role_first, role_rest, patches),
        in_specs=[HBM] * 5,
        scratch=[
            pltpu.SMEM(frame_order.shape, jnp.int32),
            pltpu.VMEM(turned.shape, jnp.bfloat16),
            pltpu.VMEM(role_first.shape, jnp.bfloat16),
            pltpu.VMEM(role_rest.shape, jnp.bfloat16),
            pltpu.SemaphoreType.DMA((5,)),
        ],
    )
    specials = both(specials)
    mask, weights, everywhere, w_here = call(
        functools.partial(start_kernel, offsets, per_image, special_count, special_block),
        [
            f32(mask_rows, patch_total + heads * special_block),
            bf16(*w_qkv.shape),
            bf16(special_block, 2 * width),
            bf16(*w_out.shape),
        ],
        (covisible, *specials, w_qkv, w_out),
        in_specs=[HBM, VMEM, VMEM, HBM, HBM],
        scratch=[pltpu.SMEM(covisible.shape, jnp.int32), pltpu.SemaphoreType.DMA((1 + 7,))],
    )
    if paired and power:
        everywhere = stacked(everywhere, swapped(everywhere, "blk", 2), FIRST)
    queries, special_queries, *state = call(
        functools.partial(first_kernel, images),
        [bf16(pairs, PAIR, 2 * patch_total), bf16(width, heads * special_block), *state_shape],
        (mask, own, swapped(patches, "head", 1), *specials, weights),
    )
    fixed = (weights, queries, special_queries)

    def later(stretches, parts, state):
        return call(
            functools.partial(later_kernel, stretches),
            state_shape,
            (mask, *[part[0] for part in parts], *[part[1] for part in parts], *fixed, *state),
        )

    image_rows = lambda owner: [(per_image, owner * images + b) for b in range(images)]
    def halved(part, gate):
        part = after(part, gate)
        starts = range(0, part.shape[0], per_image)
        return [both(part[start : start + per_image]) for start in starts]

    stretches = lambda owner: [[image] for image in image_rows(owner)]
    if paired:
        far = after(crossed(patches, "blk"), state[0])
        near = swapped(patches, "blk", 1)
        if power:
            everywhere = after(everywhere, far)
            bit = 4
            while 2 * bit < owner_count:
                everywhere = stacked(everywhere, swapped(everywhere, "blk", bit))
                bit *= 2
            arrived = swapped(everywhere, "blk", bit)
        state = later(stretches(1), halved(far, state[0]), state)
        if power:
            real = real_rows * owner_count // 2
            blocks = (real + -real % TILE_ROWS, real)
            (everywhere,) = call(
                functools.partial(compact_kernel, special_block, real_rows),
                [bf16(blocks[0], 2 * width)],
                (after(everywhere, state[0]), arrived),
                flops=FIRST,
            )
            arrived = swapped(everywhere, "blk", 1)
        parts = halved(near, state[0])
        (sums,) = call(
            functools.partial(half_kernel, len(parts)),
            [f32(2, patch_total, width)],
            (*[part[0] for part in parts], weights),
            flops=0,
        )
        state = call(
            functools.partial(begun_kernel, stretches(2)),
            state_shape,
            (mask, sums, *[part[1] for part in parts], *fixed, *state),
        )
        if power:
            everywhere = stacked(after(everywhere, state[0]), arrived)
    else:
        for i, offset in enumerate(offsets[1:]):
            state = later(stretches(i + 1), halved(shifted(patches, "blk", -offset), state[0]), state)
    if not (paired and power):
        blocks = (special_block, real_rows)
        everywhere = lax.all_gather(everywhere, "blk", axis=0, tiled=True)
    kept, sent = call(
        functools.partial(last_kernel, blocks),
        [f32(rows, width), bf16(rows, width)],
        (mask, everywhere, queries, special_queries, *state, w_here),
    )
    received = swapped(sent, "head", 1)
    patch_out, special_out = call(
        functools.partial(end_kernel, images),
        [bf16(patch_total, width), bf16(special_count, images, width)],
        (kept, received),
        out_specs=[pl.BlockSpec(), pl.BlockSpec()],
    )
    return patch_out.reshape(patch_rows.shape), jnp.transpose(special_out, (1, 0, 2))


def solution(mesh):
    in_specs = (
        P(("scene", "blk"), None, "head"),
        P(("scene", "blk"), None, "head"),
        P(),
        P(),
        P(("scene", "blk")),
        P(("scene", "blk"), None),
        P(None, None, "head"),
        P("head", None),
    )
    out_specs = (P(("scene", "blk"), None, "head"), P(("scene", "blk"), None, "head"))
    return jax.shard_map(
        per_device, mesh=mesh, in_specs=in_specs, out_specs=out_specs, check_vma=False
    )
```

```python
import functools

import jax
import jax.numpy as jnp
from jax import lax
from jax.experimental import pallas as pl
from jax.experimental.pallas import tpu as pltpu
from jax.sharding import PartitionSpec as P

HEAD_DIM = 64
PAIR = 2 * HEAD_DIM
QUAD = 2 * PAIR
TILE_ROWS = 16
LOG2_E = 1.4426950408889634
FIRST = 20_000_000_000
VMEM_BYTES = 32 * 1024 * 1024
SMEM = pl.BlockSpec(memory_space=pltpu.SMEM)
VMEM = pl.BlockSpec(memory_space=pltpu.VMEM)
HBM = pl.BlockSpec(memory_space=pltpu.HBM)


def shifted(block, axis, distance):
    count = lax.axis_size(axis)
    route = [((i - distance) % count, i) for i in range(count)]
    return lax.ppermute(block, axis, route)


def swapped(block, axis, bit):
    count = lax.axis_size(axis)
    return lax.ppermute(block, axis, [(i ^ bit, i) for i in range(count)])


def crossed(block, axis):
    count = lax.axis_size(axis)
    return lax.ppermute(block, axis, [(i, (i + (-1 if i % 2 == 0 else 1)) % count) for i in range(count)])


def halves(width):
    half = lax.axis_index("head")
    mine = pl.ds(pl.multiple_of(half * width, width), width)
    theirs = pl.ds(pl.multiple_of((1 - half) * width, width), width)
    return mine, theirs


def product(left, right):
    return jnp.dot(left, right, preferred_element_type=jnp.float32)


def owner_at(offset):
    count = lax.axis_size("blk")
    here = lax.axis_index("blk")
    if isinstance(offset, tuple):
        offset = jnp.where(lax.rem(here, 2) == 0, offset[0], offset[1])
    return lax.rem(here + offset + count, count)


def rows_kernel(
    frame_order, specials, role_first, role_rest, patches,
    special_out, patches_out, order, here, first_rows, rest_rows, copied,
):
    special_count, images, width = specials.shape
    moves = [(specials, here), (role_first, first_rows), (role_rest, rest_rows), (frame_order, order)]
    moves.append((patches, patches_out))
    copies = [
        pltpu.make_async_copy(source, target, copied.at[i]) for i, (source, target) in enumerate(moves)
    ]
    for copy in copies:
        copy.start()
    for copy in copies[:4]:
        copy.wait()
    mine, _ = halves(width)
    first = first_rows[:, mine].astype(jnp.float32)
    rest = rest_rows[:, mine].astype(jnp.float32)
    summed = [
        here[:, b, :].astype(jnp.float32) + jnp.where(order[b] == 0, first, rest) for b in range(images)
    ]
    summed.append(jnp.zeros((special_out.shape[0] - images * special_count, width), jnp.float32))
    special_out[...] = jnp.concatenate(summed, axis=0).astype(jnp.bfloat16)
    for copy in copies[4:]:
        copy.wait()


def start_kernel(
    offsets, per_image, special_count, special_total, covisible, special, other_special, w_qkv, w_out,
    mask_out, weights_out, pairs_out, w_out_here, seen, copied,
):
    images = covisible.shape[0]
    patch_total = images * per_image
    moves = [(covisible, seen)]
    depth = w_qkv.shape[1] // 2
    for i in range(3):
        for j, rows in enumerate(halves(depth)):
            moves.append((w_qkv.at[i, rows], weights_out.at[i, pl.ds(j * depth, depth)]))
    moves.append((w_out, w_out_here))
    copies = [
        pltpu.make_async_copy(source, target, copied.at[i]) for i, (source, target) in enumerate(moves)
    ]
    for copy in copies:
        copy.start()
    copies[0].wait()
    lane = lax.broadcasted_iota(jnp.int32, (1, mask_out.shape[1]), 1)
    special_lane = lax.rem(lane - patch_total, special_total)
    image = jnp.where(
        lane < patch_total, lane // per_image, jnp.minimum(special_lane // special_count, images - 1)
    )
    for i, offset in enumerate(offsets):
        for b in range(images):
            row = jnp.zeros(lane.shape, jnp.float32)
            for a in range(images):
                hidden = seen[a, owner_at(offset) * images + b] <= 0
                row = jnp.where((image == a) & hidden, -jnp.inf, row)
            mask_out[i * images + b : i * images + b + 1, :] = row
    rows = jnp.concatenate([special[...], other_special[...]], axis=1)
    width = weights_out.shape[2]
    for copy in copies[1:-1]:
        copy.wait()
    for i in range(2):
        pairs_out[:, i * width : (i + 1) * width] = product(rows, weights_out[i + 1]).astype(jnp.bfloat16)
    copies[-1].wait()


def projector(own, other, weights):
    rows = jnp.concatenate([own, other], axis=1)

    def columns(which, quad):
        return product(rows, weights[which, :, quad * QUAD : (quad + 1) * QUAD])

    return columns


def attend(scores, masks, state):
    largest = state
    start = 0
    for count, mask in masks:
        part = jnp.max(scores[start : start + count], axis=0, keepdims=True)
        part = part if mask is None else part + mask
        largest = part if largest is None else jnp.maximum(largest, part)
        start += count
    weights, start = [], 0
    for count, mask in masks:
        level = largest if mask is None else largest - mask
        weights.append(jnp.exp2((scores[start : start + count] - level).astype(jnp.bfloat16)))
        start += count
    factor = None if state is None else jnp.exp2(state - largest)
    return largest, factor, jnp.concatenate(weights, axis=0)


def attend_all(columns, masks, queries_of, special_queries, state, pairs, rows, special_real):
    keys, values = {}, {}
    quads = pairs // 2

    def keys_of(quad):
        if quad not in keys:
            keys[quad] = columns(1, quad).astype(jnp.bfloat16)
        return keys[quad]

    def values_of(quad):
        if quad not in values:
            values[quad] = jnp.transpose(columns(2, quad).astype(jnp.bfloat16))
        return values[quad]

    def prepared(pair):
        if pair == pairs:
            scores = product(
                jnp.concatenate([keys_of(quad) for quad in range(quads)], axis=1), special_queries()
            )
        else:
            lanes = slice((pair % 2) * PAIR, (pair % 2 + 1) * PAIR)
            scores = product(keys_of(pair // 2)[:, lanes], queries_of(pair))
        if all(mask is not None for _, mask in masks):
            return scores
        parts, start = [], 0
        for count, mask in masks:
            part = scores[start : start + count]
            if mask is None:
                key_row = lax.broadcasted_iota(jnp.int32, (count, 1), 0)
                part = jnp.where(lax.rem(key_row, special_real[0]) < special_real[1], part, -jnp.inf)
            parts.append(part)
            start += count
        return jnp.concatenate(parts, axis=0)

    ones = jnp.ones((TILE_ROWS, sum(count for count, _ in masks)), jnp.bfloat16)
    both = [
        (count, None if mask is None else jnp.concatenate([mask[:, :rows]] * 2, axis=1))
        for count, mask in masks
    ]
    only = [(count, None if mask is None else mask[:, rows:]) for count, mask in masks]
    order = list(range(pairs))
    order.insert(pairs - 2, pairs)
    scores = prepared(order[0])
    for step, pair in enumerate(order):
        if pair < pairs:
            left = values_of(pair // 2)[(pair % 2) * PAIR : (pair % 2 + 1) * PAIR]
        else:
            left = jnp.concatenate([values_of(quad) for quad in range(quads)], axis=0)
        following = prepared(order[step + 1]) if step < pairs else None
        largest, factor, weights = attend(
            scores, both if pair < pairs else only, state and state.largest(pair)
        )
        added = product(jnp.concatenate([left, ones], axis=0), weights)
        height, subs = (HEAD_DIM, 2) if pair < pairs else (left.shape[0], 1)
        width = scores.shape[1] // subs
        for sub in range(subs):
            lanes = slice(sub * width, (sub + 1) * width)
            total = added[sub * height : (sub + 1) * height, lanes]
            weight = added[left.shape[0] : left.shape[0] + 1, lanes]
            if state is not None:
                total = total + state.total(pair, sub) * factor[:, lanes]
                weight = weight + state.weight(pair, sub) * factor[:, lanes]
            yield pair, sub, largest[:, lanes], total, weight
        scores = following


class State:
    def __init__(self, rows, refs):
        self.rows = rows
        self.largest_ref, self.weight_ref, self.total_ref, self.special_ref = refs

    def lanes(self, pair, sub):
        if pair == self.total_ref.shape[0]:
            return slice(0, self.special_ref.shape[1])
        return slice(sub * self.rows, (sub + 1) * self.rows)

    def largest(self, pair):
        stop = self.special_ref.shape[1] if pair == self.total_ref.shape[0] else 2 * self.rows
        return self.largest_ref[pair : pair + 1, 0:stop]

    def weight(self, pair, sub):
        return self.weight_ref[pair : pair + 1, self.lanes(pair, sub)]

    def total(self, pair, sub):
        if pair == self.total_ref.shape[0]:
            return self.special_ref[...]
        return self.total_ref[pair, :, self.lanes(pair, sub)]

    def put(self, pair, sub, largest, total, weight):
        lanes = self.lanes(pair, sub)
        self.largest_ref[pair : pair + 1, lanes] = largest
        self.weight_ref[pair : pair + 1, lanes] = weight
        if pair == self.total_ref.shape[0]:
            self.special_ref[...] = total
        else:
            self.total_ref[pair, :, lanes] = total


def first_kernel(
    images, mask, own, other, special, other_special, weights, queries_out, special_out, *state_out
):
    patch_total = own.shape[0]
    columns = projector(
        jnp.concatenate([own[...], special[...]], axis=0),
        jnp.concatenate([other[...], other_special[...]], axis=0),
        weights,
    )
    pairs = queries_out.shape[0]
    zero = jnp.zeros((HEAD_DIM, patch_total), jnp.bfloat16)
    made = {}

    def patch_columns(which, quad):
        return columns(which, quad)[:patch_total]

    def columns_of(quad):
        if quad not in made:
            queries = columns(0, quad) * (HEAD_DIM ** (-0.5) * LOG2_E)
            made[quad] = queries[patch_total:]
            turned = jnp.transpose(queries[:patch_total].astype(jnp.bfloat16))
            for i in range(2):
                first = i * PAIR
                upper = jnp.concatenate([turned[first : first + HEAD_DIM], zero], axis=1)
                lower = jnp.concatenate([zero, turned[first + HEAD_DIM : first + PAIR]], axis=1)
                queries_out[2 * quad + i] = jnp.concatenate([upper, lower], axis=0)
        return made[quad]

    def queries_of(pair):
        columns_of(pair // 2)
        return queries_out[pair]

    def special_queries():
        block = jnp.concatenate([columns_of(quad) for quad in range(pairs // 2)], axis=1)
        count = block.shape[0]
        block = jnp.concatenate([block] * (2 * pairs), axis=0)
        row = lax.broadcasted_iota(jnp.int32, block.shape, 0) // count
        lane = lax.broadcasted_iota(jnp.int32, block.shape, 1) // HEAD_DIM
        block = jnp.transpose(jnp.where(row == lane, block, 0.0).astype(jnp.bfloat16))
        special_out[...] = block
        return block

    per_image = patch_total // images
    masks = [(per_image, mask[b : b + 1, :]) for b in range(images)]
    state = State(patch_total, state_out)
    for result in attend_all(
        patch_columns, masks, queries_of, special_queries, None, pairs, patch_total, 0
    ):
        state.put(*result)


def joined(stretches, mask, refs):
    count = len(stretches)
    own = jnp.concatenate([ref[...] for ref in refs[:count]], axis=0)
    other = jnp.concatenate([ref[...] for ref in refs[count : 2 * count]], axis=0)
    masks = [(rows, mask[i : i + 1, :]) for part in stretches for rows, i in part]
    return own, other, masks, refs[2 * count :]


def given(pairs):
    width = pairs.shape[1] // 2

    def columns(which, quad):
        first = (which - 1) * width + quad * QUAD
        return pairs[:, first : first + QUAD]

    return columns


def later_kernel(stretches, mask, *refs):
    own, other, masks, refs = joined(stretches, mask, refs)
    weights, queries, special_queries = refs[:3]
    state_in, state_out = refs[3:7], refs[7:]
    pairs, rows = queries.shape[0], queries.shape[2] // 2
    state = State(rows, state_out)
    for result in attend_all(
        projector(own, other, weights), masks, lambda pair: queries[pair], lambda: special_queries[...],
        State(rows, state_in), pairs, rows, None,
    ):
        state.put(*result)


def half_kernel(count, *refs):
    weights, sums_out = refs[count:]
    rows = jnp.concatenate([ref[...] for ref in refs[:count]], axis=0)
    for i in range(2):
        sums_out[i] = product(rows, weights[i + 1, : rows.shape[1], :])


def finish_kernel(count, sums, *refs):
    weights, pairs_out = refs[count:]
    rows = jnp.concatenate([ref[...] for ref in refs[:count]], axis=0)
    depth, width = rows.shape[1], weights.shape[2]
    for i in range(2):
        total = sums[i] + product(rows, weights[i + 1, depth:, :])
        pairs_out[:, i * width : (i + 1) * width] = total.astype(jnp.bfloat16)


def given_kernel(stretches, mask, key_pairs, queries, special_queries, *refs):
    masks = [(rows, mask[i : i + 1, :]) for part in stretches for rows, i in part]
    state_in, state_out = refs[:4], refs[4:]
    pairs, rows = queries.shape[0], queries.shape[2] // 2
    state = State(rows, state_out)
    for result in attend_all(
        given(key_pairs), masks, lambda pair: queries[pair], lambda: special_queries[...],
        State(rows, state_in), pairs, rows, None,
    ):
        state.put(*result)


def last_kernel(
    special_real, mask, special_pairs, queries, special_queries, *refs
):
    state_in = refs[:4]
    w_here, kept_out, sent_out = refs[4:]
    masks = [(special_pairs.shape[0], None)]
    pairs, rows = queries.shape[0], queries.shape[2] // 2
    columns, out, special = [], None, None
    sides = halves(kept_out.shape[1])
    for pair, sub, _, total, weight in attend_all(
        given(special_pairs), masks, lambda pair: queries[pair], lambda: special_queries[...],
        State(rows, state_in), pairs, rows, special_real,
    ):
        share = total * (1.0 / weight)
        if pair == pairs:
            row = lax.broadcasted_iota(jnp.int32, share.shape, 0) // HEAD_DIM
            lane = lax.broadcasted_iota(jnp.int32, share.shape, 1) // TILE_ROWS
            share = jnp.transpose(jnp.where(row == lane, share, 0.0))
            share = sum(share[i * TILE_ROWS : (i + 1) * TILE_ROWS] for i in range(2 * pairs))
            special = [product(share.astype(jnp.bfloat16), w_here[:, side]) for side in sides]
            continue
        columns.append(share)
        if pair % 2 == 1 and sub == 1:
            quad = jnp.transpose(jnp.concatenate(columns, axis=0).astype(jnp.bfloat16))
            features = slice((pair // 2) * QUAD, (pair // 2 + 1) * QUAD)
            added = [product(quad, w_here[features, side]) for side in sides]
            out = added if out is None else [before + more for before, more in zip(out, added)]
            columns = []
    for place, values in ((slice(0, rows), out), (slice(rows, kept_out.shape[0]), special)):
        sent_out[place, :] = values[1].astype(jnp.bfloat16)
        kept_out[place, :] = values[0]


def end_kernel(images, kept, received, patch_out, special_out):
    patch_total = patch_out.shape[0]
    special_count = special_out.shape[0]
    patch_out[...] = (kept[:patch_total, :] + received[:patch_total, :].astype(jnp.float32)).astype(
        jnp.bfloat16
    )
    rest = kept[patch_total:, :] + received[patch_total:, :].astype(jnp.float32)
    rows = [rest[b * special_count : (b + 1) * special_count][:, None, :] for b in range(images)]
    special_out[...] = jnp.concatenate(rows, axis=1).astype(jnp.bfloat16)


def call(kernel, out_shape, operands, in_specs=None, out_specs=None, scratch=(), flops=0):
    if in_specs:
        operands = [
            pltpu.with_memory_space_constraint(operand, pltpu.HBM) if spec is HBM else operand
            for operand, spec in zip(operands, in_specs)
        ]
    return pl.pallas_call(
        kernel,
        out_shape=out_shape,
        in_specs=in_specs or [VMEM] * len(operands),
        out_specs=out_specs or [VMEM] * len(out_shape),
        scratch_shapes=scratch,
        compiler_params=pltpu.CompilerParams(vmem_limit_bytes=VMEM_BYTES),
        cost_estimate=pl.CostEstimate(flops=flops, transcendentals=0, bytes_accessed=0),
    )(*operands)


def stack_kernel(first, second, out):
    count = first.shape[0]
    out[:count, :] = first[...]
    out[count:, :] = second[...]


def compact_kernel(block, real, first, second, out):
    rows = [
        part[start : start + real, :].astype(jnp.float32)
        for part in (first, second)
        for start in range(0, part.shape[0], block)
    ]
    padding = out.shape[0] - sum(part.shape[0] for part in rows)
    if padding:
        rows.append(jnp.zeros((padding, out.shape[1]), jnp.float32))
    out[...] = jnp.concatenate(rows, axis=0).astype(jnp.bfloat16)


def stacked(first, second, flops=0):
    shape = jax.ShapeDtypeStruct((2 * first.shape[0], first.shape[1]), first.dtype)
    return call(stack_kernel, [shape], (first, second), flops=flops)[0]


def after(array, *others):
    return lax.optimization_barrier((array, *others))[0]


def per_device(
    patch_rows, special_rows, role_first, role_rest, frame_order, covisible, w_qkv, w_out
):
    images, per_image, width = patch_rows.shape
    special_count = special_rows.shape[1]
    real_rows = images * special_count
    special_block = real_rows + -real_rows % TILE_ROWS
    owner_count = lax.axis_size("blk")
    reach = max(1, owner_count // 64)
    patch_total = images * per_image
    rows = patch_total + special_block
    heads = width // HEAD_DIM
    pairs = heads // 2
    paired = reach == 1 and owner_count % 2 == 0

    if paired:
        offsets = [0, (-1, 1), (1, -1)]
    else:
        offsets = [0] + [sign * d for d in range(1, reach + 1) for sign in (-1, 1)]
    mask_rows = -(-len(offsets) * images // 8) * 8
    bf16 = lambda *shape: jax.ShapeDtypeStruct(shape, jnp.bfloat16)
    f32 = lambda *shape: jax.ShapeDtypeStruct(shape, jnp.float32)
    state_shape = [
        f32(8, 2 * patch_total),
        f32(8, 2 * patch_total),
        f32(pairs, HEAD_DIM, 2 * patch_total),
        f32(width, heads * special_block),
    ]

    both = lambda part: (part, swapped(part, "head", 1))
    patches = patch_rows.reshape(patch_total, width)
    turned = jnp.transpose(special_rows, (1, 0, 2))
    power = owner_count >= 8 and owner_count & (owner_count - 1) == 0
    specials, own = call(
        rows_kernel,
        [
            bf16(special_block, width),
            bf16(patch_total, width),
        ],
        (frame_order, turned, role_first, role_rest, patches),
        in_specs=[HBM] * 5,
        scratch=[
            pltpu.SMEM(frame_order.shape, jnp.int32),
            pltpu.VMEM(turned.shape, jnp.bfloat16),
            pltpu.VMEM(role_first.shape, jnp.bfloat16),
            pltpu.VMEM(role_rest.shape, jnp.bfloat16),
            pltpu.SemaphoreType.DMA((5,)),
        ],
    )
    specials = both(specials)
    mask, weights, everywhere, w_here = call(
        functools.partial(start_kernel, offsets, per_image, special_count, special_block),
        [
            f32(mask_rows, patch_total + heads * special_block),
            bf16(*w_qkv.shape),
            bf16(special_block, 2 * width),
            bf16(*w_out.shape),
        ],
        (covisible, *specials, w_qkv, w_out),
        in_specs=[HBM, VMEM, VMEM, HBM, HBM],
        scratch=[pltpu.SMEM(covisible.shape, jnp.int32), pltpu.SemaphoreType.DMA((1 + 7,))],
    )
    if paired and power:
        everywhere = stacked(everywhere, swapped(everywhere, "blk", 2), FIRST)
    queries, special_queries, *state = call(
        functools.partial(first_kernel, images),
        [bf16(pairs, PAIR, 2 * patch_total), bf16(width, heads * special_block), *state_shape],
        (mask, own, swapped(patches, "head", 1), *specials, weights),
    )
    fixed = (weights, queries, special_queries)

    def later(stretches, parts, state):
        return call(
            functools.partial(later_kernel, stretches),
            state_shape,
            (mask, *[part[0] for part in parts], *[part[1] for part in parts], *fixed, *state),
        )

    image_rows = lambda owner: [(per_image, owner * images + b) for b in range(images)]
    def prepared(owner, parts, state):
        (sums,) = call(
            functools.partial(half_kernel, len(parts)),
            [f32(2, patch_total, width)],
            (*[part[0] for part in parts], weights),
        )
        (key_pairs,) = call(
            functools.partial(finish_kernel, len(parts)),
            [bf16(patch_total, 2 * width)],
            (sums, *[part[1] for part in parts], weights),
        )
        return call(
            functools.partial(given_kernel, stretches(owner)),
            state_shape,
            (mask, key_pairs, queries, special_queries, *state),
        )

    def halved(part, gate):
        part = after(part, gate)
        starts = range(0, part.shape[0], per_image)
        return [both(part[start : start + per_image]) for start in starts]

    stretches = lambda owner: [[image] for image in image_rows(owner)]
    if paired:
        far = after(crossed(patches, "blk"), state[0])
        near = swapped(patches, "blk", 1)
        if power:
            everywhere = after(everywhere, far)
            bit = 4
            while 2 * bit < owner_count:
                everywhere = stacked(everywhere, swapped(everywhere, "blk", bit))
                bit *= 2
            arrived = swapped(everywhere, "blk", bit)
        state = prepared(1, halved(far, state[0]), state)
        if power:
            real = real_rows * owner_count // 2
            blocks = (real + -real % TILE_ROWS, real)
            (everywhere,) = call(
                functools.partial(compact_kernel, special_block, real_rows),
                [bf16(blocks[0], 2 * width)],
                (after(everywhere, state[0]), arrived),
                flops=FIRST,
            )
            arrived = swapped(everywhere, "blk", 1)
        state = prepared(2, halved(near, state[0]), state)
        if power:
            everywhere = stacked(after(everywhere, state[0]), arrived)
    else:
        for i, offset in enumerate(offsets[1:]):
            state = later(stretches(i + 1), halved(shifted(patches, "blk", -offset), state[0]), state)
    if not (paired and power):
        blocks = (special_block, real_rows)
        everywhere = lax.all_gather(everywhere, "blk", axis=0, tiled=True)
    kept, sent = call(
        functools.partial(last_kernel, blocks),
        [f32(rows, width), bf16(rows, width)],
        (mask, everywhere, queries, special_queries, *state, w_here),
    )
    received = swapped(sent, "head", 1)
    patch_out, special_out = call(
        functools.partial(end_kernel, images),
        [bf16(patch_total, width), bf16(special_count, images, width)],
        (kept, received),
        out_specs=[pl.BlockSpec(), pl.BlockSpec()],
    )
    return patch_out.reshape(patch_rows.shape), jnp.transpose(special_out, (1, 0, 2))


def solution(mesh):
    in_specs = (
        P(("scene", "blk"), None, "head"),
        P(("scene", "blk"), None, "head"),
        P(),
        P(),
        P(("scene", "blk")),
        P(("scene", "blk"), None),
        P(None, None, "head"),
        P("head", None),
    )
    out_specs = (P(("scene", "blk"), None, "head"), P(("scene", "blk"), None, "head"))
    return jax.shard_map(
        per_device, mesh=mesh, in_specs=in_specs, out_specs=out_specs, check_vma=False
    )
```

```python
import functools

import jax
import jax.numpy as jnp
from jax import lax
from jax.experimental import pallas as pl
from jax.experimental.pallas import tpu as pltpu
from jax.sharding import PartitionSpec as P

HEAD_DIM = 64
PAIR = 2 * HEAD_DIM
QUAD = 2 * PAIR
TILE_ROWS = 16
LOG2_E = 1.4426950408889634
FIRST = 20_000_000_000
VMEM_BYTES = 32 * 1024 * 1024
SMEM = pl.BlockSpec(memory_space=pltpu.SMEM)
VMEM = pl.BlockSpec(memory_space=pltpu.VMEM)
HBM = pl.BlockSpec(memory_space=pltpu.HBM)


def shifted(block, axis, distance):
    count = lax.axis_size(axis)
    route = [((i - distance) % count, i) for i in range(count)]
    return lax.ppermute(block, axis, route)


def swapped(block, axis, bit):
    count = lax.axis_size(axis)
    return lax.ppermute(block, axis, [(i ^ bit, i) for i in range(count)])


def crossed(block, axis):
    count = lax.axis_size(axis)
    return lax.ppermute(block, axis, [(i, (i + (-1 if i % 2 == 0 else 1)) % count) for i in range(count)])


def halves(width):
    half = lax.axis_index("head")
    mine = pl.ds(pl.multiple_of(half * width, width), width)
    theirs = pl.ds(pl.multiple_of((1 - half) * width, width), width)
    return mine, theirs


def product(left, right):
    return jnp.dot(left, right, preferred_element_type=jnp.float32)


def owner_at(offset):
    count = lax.axis_size("blk")
    here = lax.axis_index("blk")
    if isinstance(offset, tuple):
        offset = jnp.where(lax.rem(here, 2) == 0, offset[0], offset[1])
    return lax.rem(here + offset + count, count)


def rows_kernel(
    frame_order, specials, role_first, role_rest, patches,
    special_out, patches_out, order, here, first_rows, rest_rows, copied,
):
    special_count, images, width = specials.shape
    moves = [(specials, here), (role_first, first_rows), (role_rest, rest_rows), (frame_order, order)]
    moves.append((patches, patches_out))
    copies = [
        pltpu.make_async_copy(source, target, copied.at[i]) for i, (source, target) in enumerate(moves)
    ]
    for copy in copies:
        copy.start()
    for copy in copies[:4]:
        copy.wait()
    mine, _ = halves(width)
    first = first_rows[:, mine].astype(jnp.float32)
    rest = rest_rows[:, mine].astype(jnp.float32)
    summed = [
        here[:, b, :].astype(jnp.float32) + jnp.where(order[b] == 0, first, rest) for b in range(images)
    ]
    summed.append(jnp.zeros((special_out.shape[0] - images * special_count, width), jnp.float32))
    special_out[...] = jnp.concatenate(summed, axis=0).astype(jnp.bfloat16)
    for copy in copies[4:]:
        copy.wait()


def start_kernel(
    offsets, per_image, special_count, special_total, covisible, special, other_special, w_qkv, w_out,
    mask_out, weights_out, pairs_out, w_out_here, seen, copied,
):
    images = covisible.shape[0]
    patch_total = images * per_image
    moves = [(covisible, seen)]
    depth = w_qkv.shape[1] // 2
    for i in range(3):
        for j, rows in enumerate(halves(depth)):
            moves.append((w_qkv.at[i, rows], weights_out.at[i, pl.ds(j * depth, depth)]))
    moves.append((w_out, w_out_here))
    copies = [
        pltpu.make_async_copy(source, target, copied.at[i]) for i, (source, target) in enumerate(moves)
    ]
    for copy in copies:
        copy.start()
    copies[0].wait()
    lane = lax.broadcasted_iota(jnp.int32, (1, mask_out.shape[1]), 1)
    special_lane = lax.rem(lane - patch_total, special_total)
    image = jnp.where(
        lane < patch_total, lane // per_image, jnp.minimum(special_lane // special_count, images - 1)
    )
    for i, offset in enumerate(offsets):
        for b in range(images):
            row = jnp.zeros(lane.shape, jnp.float32)
            for a in range(images):
                hidden = seen[a, owner_at(offset) * images + b] <= 0
                row = jnp.where((image == a) & hidden, -jnp.inf, row)
            mask_out[i * images + b : i * images + b + 1, :] = row
    rows = jnp.concatenate([special[...], other_special[...]], axis=1)
    width = weights_out.shape[2]
    for copy in copies[1:-1]:
        copy.wait()
    for i in range(2):
        pairs_out[:, i * width : (i + 1) * width] = product(rows, weights_out[i + 1]).astype(jnp.bfloat16)
    copies[-1].wait()


def projector(own, other, weights):
    rows = jnp.concatenate([own, other], axis=1)

    def columns(which, quad):
        return product(rows, weights[which, :, quad * QUAD : (quad + 1) * QUAD])

    return columns


def attend(scores, masks, state):
    largest = state
    start = 0
    for count, mask in masks:
        part = jnp.max(scores[start : start + count], axis=0, keepdims=True)
        part = part if mask is None else part + mask
        largest = part if largest is None else jnp.maximum(largest, part)
        start += count
    weights, start = [], 0
    for count, mask in masks:
        level = largest if mask is None else largest - mask
        weights.append(jnp.exp2((scores[start : start + count] - level).astype(jnp.bfloat16)))
        start += count
    factor = None if state is None else jnp.exp2(state - largest)
    return largest, factor, jnp.concatenate(weights, axis=0)


def attend_all(columns, masks, queries_of, special_queries, state, pairs, rows, special_real):
    keys, values = {}, {}
    quads = pairs // 2

    def keys_of(quad):
        if quad not in keys:
            keys[quad] = columns(1, quad).astype(jnp.bfloat16)
        return keys[quad]

    def values_of(quad):
        if quad not in values:
            values[quad] = jnp.transpose(columns(2, quad).astype(jnp.bfloat16))
        return values[quad]

    def prepared(pair):
        if pair == pairs:
            scores = product(
                jnp.concatenate([keys_of(quad) for quad in range(quads)], axis=1), special_queries()
            )
        else:
            lanes = slice((pair % 2) * PAIR, (pair % 2 + 1) * PAIR)
            scores = product(keys_of(pair // 2)[:, lanes], queries_of(pair))
        if all(mask is not None for _, mask in masks):
            return scores
        parts, start = [], 0
        for count, mask in masks:
            part = scores[start : start + count]
            if mask is None:
                key_row = lax.broadcasted_iota(jnp.int32, (count, 1), 0)
                part = jnp.where(lax.rem(key_row, special_real[0]) < special_real[1], part, -jnp.inf)
            parts.append(part)
            start += count
        return jnp.concatenate(parts, axis=0)

    ones = jnp.ones((TILE_ROWS, sum(count for count, _ in masks)), jnp.bfloat16)
    both = [
        (count, None if mask is None else jnp.concatenate([mask[:, :rows]] * 2, axis=1))
        for count, mask in masks
    ]
    only = [(count, None if mask is None else mask[:, rows:]) for count, mask in masks]
    order = list(range(pairs))
    order.insert(pairs - 2, pairs)
    scores = prepared(order[0])
    for step, pair in enumerate(order):
        if pair < pairs:
            left = values_of(pair // 2)[(pair % 2) * PAIR : (pair % 2 + 1) * PAIR]
        else:
            left = jnp.concatenate([values_of(quad) for quad in range(quads)], axis=0)
        following = prepared(order[step + 1]) if step < pairs else None
        largest, factor, weights = attend(
            scores, both if pair < pairs else only, state and state.largest(pair)
        )
        added = product(jnp.concatenate([left, ones], axis=0), weights)
        height, subs = (HEAD_DIM, 2) if pair < pairs else (left.shape[0], 1)
        width = scores.shape[1] // subs
        for sub in range(subs):
            lanes = slice(sub * width, (sub + 1) * width)
            total = added[sub * height : (sub + 1) * height, lanes]
            weight = added[left.shape[0] : left.shape[0] + 1, lanes]
            if state is not None:
                total = total + state.total(pair, sub) * factor[:, lanes]
                weight = weight + state.weight(pair, sub) * factor[:, lanes]
            yield pair, sub, largest[:, lanes], total, weight
        scores = following


class State:
    def __init__(self, rows, refs):
        self.rows = rows
        self.largest_ref, self.weight_ref, self.total_ref, self.special_ref = refs

    def lanes(self, pair, sub):
        if pair == self.total_ref.shape[0]:
            return slice(0, self.special_ref.shape[1])
        return slice(sub * self.rows, (sub + 1) * self.rows)

    def largest(self, pair):
        stop = self.special_ref.shape[1] if pair == self.total_ref.shape[0] else 2 * self.rows
        return self.largest_ref[pair : pair + 1, 0:stop]

    def weight(self, pair, sub):
        return self.weight_ref[pair : pair + 1, self.lanes(pair, sub)]

    def total(self, pair, sub):
        if pair == self.total_ref.shape[0]:
            return self.special_ref[...]
        return self.total_ref[pair, :, self.lanes(pair, sub)]

    def put(self, pair, sub, largest, total, weight):
        lanes = self.lanes(pair, sub)
        self.largest_ref[pair : pair + 1, lanes] = largest
        self.weight_ref[pair : pair + 1, lanes] = weight
        if pair == self.total_ref.shape[0]:
            self.special_ref[...] = total
        else:
            self.total_ref[pair, :, lanes] = total


def first_kernel(
    images, mask, own, other, special, other_special, weights, queries_out, special_out, *state_out
):
    patch_total = own.shape[0]
    columns = projector(
        jnp.concatenate([own[...], special[...]], axis=0),
        jnp.concatenate([other[...], other_special[...]], axis=0),
        weights,
    )
    pairs = queries_out.shape[0]
    zero = jnp.zeros((HEAD_DIM, patch_total), jnp.bfloat16)
    made = {}

    def patch_columns(which, quad):
        return columns(which, quad)[:patch_total]

    def columns_of(quad):
        if quad not in made:
            queries = columns(0, quad) * (HEAD_DIM ** (-0.5) * LOG2_E)
            made[quad] = queries[patch_total:]
            turned = jnp.transpose(queries[:patch_total].astype(jnp.bfloat16))
            for i in range(2):
                first = i * PAIR
                upper = jnp.concatenate([turned[first : first + HEAD_DIM], zero], axis=1)
                lower = jnp.concatenate([zero, turned[first + HEAD_DIM : first + PAIR]], axis=1)
                queries_out[2 * quad + i] = jnp.concatenate([upper, lower], axis=0)
        return made[quad]

    def queries_of(pair):
        columns_of(pair // 2)
        return queries_out[pair]

    def special_queries():
        block = jnp.concatenate([columns_of(quad) for quad in range(pairs // 2)], axis=1)
        count = block.shape[0]
        block = jnp.concatenate([block] * (2 * pairs), axis=0)
        row = lax.broadcasted_iota(jnp.int32, block.shape, 0) // count
        lane = lax.broadcasted_iota(jnp.int32, block.shape, 1) // HEAD_DIM
        block = jnp.transpose(jnp.where(row == lane, block, 0.0).astype(jnp.bfloat16))
        special_out[...] = block
        return block

    per_image = patch_total // images
    masks = [(per_image, mask[b : b + 1, :]) for b in range(images)]
    state = State(patch_total, state_out)
    for result in attend_all(
        patch_columns, masks, queries_of, special_queries, None, pairs, patch_total, 0
    ):
        state.put(*result)


def joined(stretches, mask, refs):
    count = len(stretches)
    own = jnp.concatenate([ref[...] for ref in refs[:count]], axis=0)
    other = jnp.concatenate([ref[...] for ref in refs[count : 2 * count]], axis=0)
    masks = [(rows, mask[i : i + 1, :]) for part in stretches for rows, i in part]
    return own, other, masks, refs[2 * count :]


def given(pairs):
    width = pairs.shape[1] // 2

    def columns(which, quad):
        first = (which - 1) * width + quad * QUAD
        return pairs[:, first : first + QUAD]

    return columns


def later_kernel(stretches, mask, *refs):
    own, other, masks, refs = joined(stretches, mask, refs)
    weights, queries, special_queries = refs[:3]
    state_in, state_out = refs[3:7], refs[7:]
    pairs, rows = queries.shape[0], queries.shape[2] // 2
    state = State(rows, state_out)
    for result in attend_all(
        projector(own, other, weights), masks, lambda pair: queries[pair], lambda: special_queries[...],
        State(rows, state_in), pairs, rows, None,
    ):
        state.put(*result)


def half_kernel(count, *refs):
    weights, sums_out = refs[count:]
    rows = jnp.concatenate([ref[...] for ref in refs[:count]], axis=0)
    for i in range(2):
        sums_out[i] = product(rows, weights[i + 1, : rows.shape[1], :])


def finish_kernel(count, sums, *refs):
    weights, pairs_out = refs[count:]
    rows = jnp.concatenate([ref[...] for ref in refs[:count]], axis=0)
    depth, width = rows.shape[1], weights.shape[2]
    for i in range(2):
        total = sums[i] + product(rows, weights[i + 1, depth:, :])
        pairs_out[:, i * width : (i + 1) * width] = total.astype(jnp.bfloat16)


def given_kernel(stretches, mask, key_pairs, queries, special_queries, *refs):
    masks = [(rows, mask[i : i + 1, :]) for part in stretches for rows, i in part]
    state_in, state_out = refs[:4], refs[4:]
    pairs, rows = queries.shape[0], queries.shape[2] // 2
    state = State(rows, state_out)
    for result in attend_all(
        given(key_pairs), masks, lambda pair: queries[pair], lambda: special_queries[...],
        State(rows, state_in), pairs, rows, None,
    ):
        state.put(*result)


def last_kernel(
    special_real, mask, special_pairs, queries, special_queries, *refs
):
    state_in = refs[:4]
    w_here, kept_out, sent_out = refs[4:]
    masks = [(special_pairs.shape[0], None)]
    pairs, rows = queries.shape[0], queries.shape[2] // 2
    columns, out, special = [], None, None
    sides = halves(kept_out.shape[1])
    for pair, sub, _, total, weight in attend_all(
        given(special_pairs), masks, lambda pair: queries[pair], lambda: special_queries[...],
        State(rows, state_in), pairs, rows, special_real,
    ):
        share = total * (1.0 / weight)
        if pair == pairs:
            row = lax.broadcasted_iota(jnp.int32, share.shape, 0) // HEAD_DIM
            lane = lax.broadcasted_iota(jnp.int32, share.shape, 1) // TILE_ROWS
            share = jnp.transpose(jnp.where(row == lane, share, 0.0))
            share = sum(share[i * TILE_ROWS : (i + 1) * TILE_ROWS] for i in range(2 * pairs))
            special = [product(share.astype(jnp.bfloat16), w_here[:, side]) for side in sides]
            continue
        columns.append(share)
        if pair % 2 == 1 and sub == 1:
            quad = jnp.transpose(jnp.concatenate(columns, axis=0).astype(jnp.bfloat16))
            features = slice((pair // 2) * QUAD, (pair // 2 + 1) * QUAD)
            added = [product(quad, w_here[features, side]) for side in sides]
            out = added if out is None else [before + more for before, more in zip(out, added)]
            columns = []
    for place, values in ((slice(0, rows), out), (slice(rows, kept_out.shape[0]), special)):
        sent_out[place, :] = values[1].astype(jnp.bfloat16)
        kept_out[place, :] = values[0]


def end_kernel(images, kept, received, patch_out, special_out):
    patch_total = patch_out.shape[0]
    special_count = special_out.shape[0]
    patch_out[...] = (kept[:patch_total, :] + received[:patch_total, :].astype(jnp.float32)).astype(
        jnp.bfloat16
    )
    rest = kept[patch_total:, :] + received[patch_total:, :].astype(jnp.float32)
    rows = [rest[b * special_count : (b + 1) * special_count][:, None, :] for b in range(images)]
    special_out[...] = jnp.concatenate(rows, axis=1).astype(jnp.bfloat16)


def call(kernel, out_shape, operands, in_specs=None, out_specs=None, scratch=(), flops=0):
    if in_specs:
        operands = [
            pltpu.with_memory_space_constraint(operand, pltpu.HBM) if spec is HBM else operand
            for operand, spec in zip(operands, in_specs)
        ]
    return pl.pallas_call(
        kernel,
        out_shape=out_shape,
        in_specs=in_specs or [VMEM] * len(operands),
        out_specs=out_specs or [VMEM] * len(out_shape),
        scratch_shapes=scratch,
        compiler_params=pltpu.CompilerParams(vmem_limit_bytes=VMEM_BYTES),
        cost_estimate=pl.CostEstimate(flops=flops, transcendentals=0, bytes_accessed=0),
    )(*operands)


def stack_kernel(first, second, out):
    count = first.shape[0]
    out[:count, :] = first[...]
    out[count:, :] = second[...]


def compact_kernel(block, real, first, second, out):
    rows = [
        part[start : start + real, :].astype(jnp.float32)
        for part in (first, second)
        for start in range(0, part.shape[0], block)
    ]
    padding = out.shape[0] - sum(part.shape[0] for part in rows)
    if padding:
        rows.append(jnp.zeros((padding, out.shape[1]), jnp.float32))
    out[...] = jnp.concatenate(rows, axis=0).astype(jnp.bfloat16)


def stacked(first, second, flops=0):
    shape = jax.ShapeDtypeStruct((2 * first.shape[0], first.shape[1]), first.dtype)
    return call(stack_kernel, [shape], (first, second), flops=flops)[0]


def after(array, *others):
    return lax.optimization_barrier((array, *others))[0]


def per_device(
    patch_rows, special_rows, role_first, role_rest, frame_order, covisible, w_qkv, w_out
):
    images, per_image, width = patch_rows.shape
    special_count = special_rows.shape[1]
    real_rows = images * special_count
    special_block = real_rows + -real_rows % TILE_ROWS
    owner_count = lax.axis_size("blk")
    reach = max(1, owner_count // 64)
    patch_total = images * per_image
    rows = patch_total + special_block
    heads = width // HEAD_DIM
    pairs = heads // 2
    paired = reach == 1 and owner_count % 2 == 0

    if paired:
        offsets = [0, (-1, 1), (1, -1)]
    else:
        offsets = [0] + [sign * d for d in range(1, reach + 1) for sign in (-1, 1)]
    mask_rows = -(-len(offsets) * images // 8) * 8
    bf16 = lambda *shape: jax.ShapeDtypeStruct(shape, jnp.bfloat16)
    f32 = lambda *shape: jax.ShapeDtypeStruct(shape, jnp.float32)
    state_shape = [
        f32(8, 2 * patch_total),
        f32(8, 2 * patch_total),
        f32(pairs, HEAD_DIM, 2 * patch_total),
        f32(width, heads * special_block),
    ]

    both = lambda part: (part, swapped(part, "head", 1))
    patches = patch_rows.reshape(patch_total, width)
    turned = jnp.transpose(special_rows, (1, 0, 2))
    power = owner_count >= 8 and owner_count & (owner_count - 1) == 0
    specials, own = call(
        rows_kernel,
        [
            bf16(special_block, width),
            bf16(patch_total, width),
        ],
        (frame_order, turned, role_first, role_rest, patches),
        in_specs=[HBM] * 5,
        scratch=[
            pltpu.SMEM(frame_order.shape, jnp.int32),
            pltpu.VMEM(turned.shape, jnp.bfloat16),
            pltpu.VMEM(role_first.shape, jnp.bfloat16),
            pltpu.VMEM(role_rest.shape, jnp.bfloat16),
            pltpu.SemaphoreType.DMA((5,)),
        ],
    )
    specials = both(specials)
    mask, weights, everywhere, w_here = call(
        functools.partial(start_kernel, offsets, per_image, special_count, special_block),
        [
            f32(mask_rows, patch_total + heads * special_block),
            bf16(*w_qkv.shape),
            bf16(special_block, 2 * width),
            bf16(*w_out.shape),
        ],
        (covisible, *specials, w_qkv, w_out),
        in_specs=[HBM, VMEM, VMEM, HBM, HBM],
        scratch=[pltpu.SMEM(covisible.shape, jnp.int32), pltpu.SemaphoreType.DMA((1 + 7,))],
    )
    if paired and power:
        everywhere = stacked(everywhere, swapped(everywhere, "blk", 2), FIRST // 10)
    queries, special_queries, *state = call(
        functools.partial(first_kernel, images),
        [bf16(pairs, PAIR, 2 * patch_total), bf16(width, heads * special_block), *state_shape],
        (mask, own, swapped(patches, "head", 1), *specials, weights),
    )
    fixed = (weights, queries, special_queries)

    def later(stretches, parts, state):
        return call(
            functools.partial(later_kernel, stretches),
            state_shape,
            (mask, *[part[0] for part in parts], *[part[1] for part in parts], *fixed, *state),
        )

    image_rows = lambda owner: [(per_image, owner * images + b) for b in range(images)]
    def prepared(owner, parts, state):
        (sums,) = call(
            functools.partial(half_kernel, len(parts)),
            [f32(2, patch_total, width)],
            (*[part[0] for part in parts], weights),
        )
        (key_pairs,) = call(
            functools.partial(finish_kernel, len(parts)),
            [bf16(patch_total, 2 * width)],
            (sums, *[part[1] for part in parts], weights),
        )
        return call(
            functools.partial(given_kernel, stretches(owner)),
            state_shape,
            (mask, key_pairs, queries, special_queries, *state),
        )

    def halved(part, gate, step=per_image):
        part = after(part, gate)
        return [both(part[start : start + step]) for start in range(0, part.shape[0], step)]

    stretches = lambda owner: [[image] for image in image_rows(owner)]
    if paired:
        piece = patch_total // 3
        far = [
            after(crossed(own[start : start + piece], "blk"), state[0])
            for start in range(0, patch_total, piece)
        ]
        near = swapped(patches, "blk", 1)
        if power:
            everywhere = after(everywhere, *far)
            bit = 4
            while 2 * bit < owner_count:
                everywhere = stacked(everywhere, swapped(everywhere, "blk", bit))
                bit *= 2
            arrived = swapped(everywhere, "blk", bit)
        parts = [half for part in far for half in halved(part, state[0], piece)]
        state = prepared(1, parts, state)
        if power:
            real = real_rows * owner_count // 2
            blocks = (real + -real % TILE_ROWS, real)
            (everywhere,) = call(
                functools.partial(compact_kernel, special_block, real_rows),
                [bf16(blocks[0], 2 * width)],
                (after(everywhere, state[0]), arrived),
                flops=FIRST,
            )
            arrived = swapped(everywhere, "blk", 1)
        state = prepared(2, halved(near, state[0]), state)
        if power:
            everywhere = stacked(after(everywhere, state[0]), arrived)
    else:
        for i, offset in enumerate(offsets[1:]):
            state = later(stretches(i + 1), halved(shifted(patches, "blk", -offset), state[0]), state)
    if not (paired and power):
        blocks = (special_block, real_rows)
        everywhere = lax.all_gather(everywhere, "blk", axis=0, tiled=True)
    kept, sent = call(
        functools.partial(last_kernel, blocks),
        [f32(rows, width), bf16(rows, width)],
        (mask, everywhere, queries, special_queries, *state, w_here),
    )
    received = swapped(sent, "head", 1)
    patch_out, special_out = call(
        functools.partial(end_kernel, images),
        [bf16(patch_total, width), bf16(special_count, images, width)],
        (kept, received),
        out_specs=[pl.BlockSpec(), pl.BlockSpec()],
    )
    return patch_out.reshape(patch_rows.shape), jnp.transpose(special_out, (1, 0, 2))


def solution(mesh):
    in_specs = (
        P(("scene", "blk"), None, "head"),
        P(("scene", "blk"), None, "head"),
        P(),
        P(),
        P(("scene", "blk")),
        P(("scene", "blk"), None),
        P(None, None, "head"),
        P("head", None),
    )
    out_specs = (P(("scene", "blk"), None, "head"), P(("scene", "blk"), None, "head"))
    return jax.shard_map(
        per_device, mesh=mesh, in_specs=in_specs, out_specs=out_specs, check_vma=False
    )
```

```python
import functools

import jax
import jax.numpy as jnp
from jax import lax
from jax.experimental import pallas as pl
from jax.experimental.pallas import tpu as pltpu
from jax.sharding import PartitionSpec as P

HEAD_DIM = 64
PAIR = 2 * HEAD_DIM
QUAD = 2 * PAIR
TILE_ROWS = 16
LOG2_E = 1.4426950408889634
FIRST = 20_000_000_000
VMEM_BYTES = 32 * 1024 * 1024
SMEM = pl.BlockSpec(memory_space=pltpu.SMEM)
VMEM = pl.BlockSpec(memory_space=pltpu.VMEM)
HBM = pl.BlockSpec(memory_space=pltpu.HBM)


def shifted(block, axis, distance):
    count = lax.axis_size(axis)
    route = [((i - distance) % count, i) for i in range(count)]
    return lax.ppermute(block, axis, route)


def swapped(block, axis, bit):
    count = lax.axis_size(axis)
    return lax.ppermute(block, axis, [(i ^ bit, i) for i in range(count)])


def crossed(block, axis):
    count = lax.axis_size(axis)
    return lax.ppermute(block, axis, [(i, (i + (-1 if i % 2 == 0 else 1)) % count) for i in range(count)])


def halves(width):
    half = lax.axis_index("head")
    mine = pl.ds(pl.multiple_of(half * width, width), width)
    theirs = pl.ds(pl.multiple_of((1 - half) * width, width), width)
    return mine, theirs


def product(left, right):
    return jnp.dot(left, right, preferred_element_type=jnp.float32)


def owner_at(offset):
    count = lax.axis_size("blk")
    here = lax.axis_index("blk")
    if isinstance(offset, tuple):
        offset = jnp.where(lax.rem(here, 2) == 0, offset[0], offset[1])
    return lax.rem(here + offset + count, count)


def rows_kernel(
    frame_order, specials, role_first, role_rest, patches,
    special_out, patches_out, order, here, first_rows, rest_rows, copied,
):
    special_count, images, width = specials.shape
    moves = [(specials, here), (role_first, first_rows), (role_rest, rest_rows), (frame_order, order)]
    moves.append((patches, patches_out))
    copies = [
        pltpu.make_async_copy(source, target, copied.at[i]) for i, (source, target) in enumerate(moves)
    ]
    for copy in copies:
        copy.start()
    for copy in copies[:4]:
        copy.wait()
    mine, _ = halves(width)
    first = first_rows[:, mine].astype(jnp.float32)
    rest = rest_rows[:, mine].astype(jnp.float32)
    summed = [
        here[:, b, :].astype(jnp.float32) + jnp.where(order[b] == 0, first, rest) for b in range(images)
    ]
    summed.append(jnp.zeros((special_out.shape[0] - images * special_count, width), jnp.float32))
    special_out[...] = jnp.concatenate(summed, axis=0).astype(jnp.bfloat16)
    for copy in copies[4:]:
        copy.wait()


def start_kernel(
    offsets, per_image, special_count, special_total, covisible, special, other_special, w_qkv, w_out,
    mask_out, weights_out, pairs_out, w_out_here, seen, copied,
):
    images = covisible.shape[0]
    patch_total = images * per_image
    moves = [(covisible, seen)]
    depth = w_qkv.shape[1] // 2
    for i in range(3):
        for j, rows in enumerate(halves(depth)):
            moves.append((w_qkv.at[i, rows], weights_out.at[i, pl.ds(j * depth, depth)]))
    moves.append((w_out, w_out_here))
    copies = [
        pltpu.make_async_copy(source, target, copied.at[i]) for i, (source, target) in enumerate(moves)
    ]
    for copy in copies:
        copy.start()
    copies[0].wait()
    lane = lax.broadcasted_iota(jnp.int32, (1, mask_out.shape[1]), 1)
    special_lane = lax.rem(lane - patch_total, special_total)
    image = jnp.where(
        lane < patch_total, lane // per_image, jnp.minimum(special_lane // special_count, images - 1)
    )
    for i, offset in enumerate(offsets):
        for b in range(images):
            row = jnp.zeros(lane.shape, jnp.float32)
            for a in range(images):
                hidden = seen[a, owner_at(offset) * images + b] <= 0
                row = jnp.where((image == a) & hidden, -jnp.inf, row)
            mask_out[i * images + b : i * images + b + 1, :] = row
    rows = jnp.concatenate([special[...], other_special[...]], axis=1)
    width = weights_out.shape[2]
    for copy in copies[1:-1]:
        copy.wait()
    for i in range(2):
        pairs_out[:, i * width : (i + 1) * width] = product(rows, weights_out[i + 1]).astype(jnp.bfloat16)
    copies[-1].wait()


def projector(own, other, weights):
    rows = jnp.concatenate([own, other], axis=1)

    def columns(which, quad):
        return product(rows, weights[which, :, quad * QUAD : (quad + 1) * QUAD])

    return columns


def attend(scores, masks, state):
    largest = state
    start = 0
    for count, mask in masks:
        part = jnp.max(scores[start : start + count], axis=0, keepdims=True)
        part = part if mask is None else part + mask
        largest = part if largest is None else jnp.maximum(largest, part)
        start += count
    weights, start = [], 0
    for count, mask in masks:
        level = largest if mask is None else largest - mask
        weights.append(jnp.exp2((scores[start : start + count] - level).astype(jnp.bfloat16)))
        start += count
    factor = None if state is None else jnp.exp2(state - largest)
    return largest, factor, jnp.concatenate(weights, axis=0)


def attend_all(columns, masks, queries_of, special_queries, state, pairs, rows, special_real):
    keys, values = {}, {}
    quads = pairs // 2

    def keys_of(quad):
        if quad not in keys:
            keys[quad] = columns(1, quad).astype(jnp.bfloat16)
        return keys[quad]

    def values_of(quad):
        if quad not in values:
            values[quad] = jnp.transpose(columns(2, quad).astype(jnp.bfloat16))
        return values[quad]

    def prepared(pair):
        if pair == pairs:
            scores = product(
                jnp.concatenate([keys_of(quad) for quad in range(quads)], axis=1), special_queries()
            )
        else:
            lanes = slice((pair % 2) * PAIR, (pair % 2 + 1) * PAIR)
            scores = product(keys_of(pair // 2)[:, lanes], queries_of(pair))
        if all(mask is not None for _, mask in masks):
            return scores
        parts, start = [], 0
        for count, mask in masks:
            part = scores[start : start + count]
            if mask is None:
                key_row = lax.broadcasted_iota(jnp.int32, (count, 1), 0)
                part = jnp.where(lax.rem(key_row, special_real[0]) < special_real[1], part, -jnp.inf)
            parts.append(part)
            start += count
        return jnp.concatenate(parts, axis=0)

    ones = jnp.ones((TILE_ROWS, sum(count for count, _ in masks)), jnp.bfloat16)
    both = [
        (count, None if mask is None else jnp.concatenate([mask[:, :rows]] * 2, axis=1))
        for count, mask in masks
    ]
    only = [(count, None if mask is None else mask[:, rows:]) for count, mask in masks]
    order = list(range(pairs))
    order.insert(pairs - 2, pairs)
    scores = prepared(order[0])
    for step, pair in enumerate(order):
        if pair < pairs:
            left = values_of(pair // 2)[(pair % 2) * PAIR : (pair % 2 + 1) * PAIR]
        else:
            left = jnp.concatenate([values_of(quad) for quad in range(quads)], axis=0)
        following = prepared(order[step + 1]) if step < pairs else None
        largest, factor, weights = attend(
            scores, both if pair < pairs else only, state and state.largest(pair)
        )
        added = product(jnp.concatenate([left, ones], axis=0), weights)
        height, subs = (HEAD_DIM, 2) if pair < pairs else (left.shape[0], 1)
        width = scores.shape[1] // subs
        for sub in range(subs):
            lanes = slice(sub * width, (sub + 1) * width)
            total = added[sub * height : (sub + 1) * height, lanes]
            weight = added[left.shape[0] : left.shape[0] + 1, lanes]
            if state is not None:
                total = total + state.total(pair, sub) * factor[:, lanes]
                weight = weight + state.weight(pair, sub) * factor[:, lanes]
            yield pair, sub, largest[:, lanes], total, weight
        scores = following


class State:
    def __init__(self, rows, refs):
        self.rows = rows
        self.largest_ref, self.weight_ref, self.total_ref, self.special_ref = refs

    def lanes(self, pair, sub):
        if pair == self.total_ref.shape[0]:
            return slice(0, self.special_ref.shape[1])
        return slice(sub * self.rows, (sub + 1) * self.rows)

    def largest(self, pair):
        stop = self.special_ref.shape[1] if pair == self.total_ref.shape[0] else 2 * self.rows
        return self.largest_ref[pair : pair + 1, 0:stop]

    def weight(self, pair, sub):
        return self.weight_ref[pair : pair + 1, self.lanes(pair, sub)]

    def total(self, pair, sub):
        if pair == self.total_ref.shape[0]:
            return self.special_ref[...]
        return self.total_ref[pair, :, self.lanes(pair, sub)]

    def put(self, pair, sub, largest, total, weight):
        lanes = self.lanes(pair, sub)
        self.largest_ref[pair : pair + 1, lanes] = largest
        self.weight_ref[pair : pair + 1, lanes] = weight
        if pair == self.total_ref.shape[0]:
            self.special_ref[...] = total
        else:
            self.total_ref[pair, :, lanes] = total


def first_kernel(
    images, mask, own, other, special, other_special, weights, queries_out, special_out, *state_out
):
    patch_total = own.shape[0]
    columns = projector(
        jnp.concatenate([own[...], special[...]], axis=0),
        jnp.concatenate([other[...], other_special[...]], axis=0),
        weights,
    )
    pairs = queries_out.shape[0]
    zero = jnp.zeros((HEAD_DIM, patch_total), jnp.bfloat16)
    made = {}

    def patch_columns(which, quad):
        return columns(which, quad)[:patch_total]

    def columns_of(quad):
        if quad not in made:
            queries = columns(0, quad) * (HEAD_DIM ** (-0.5) * LOG2_E)
            made[quad] = queries[patch_total:]
            turned = jnp.transpose(queries[:patch_total].astype(jnp.bfloat16))
            for i in range(2):
                first = i * PAIR
                upper = jnp.concatenate([turned[first : first + HEAD_DIM], zero], axis=1)
                lower = jnp.concatenate([zero, turned[first + HEAD_DIM : first + PAIR]], axis=1)
                queries_out[2 * quad + i] = jnp.concatenate([upper, lower], axis=0)
        return made[quad]

    def queries_of(pair):
        columns_of(pair // 2)
        return queries_out[pair]

    def special_queries():
        block = jnp.concatenate([columns_of(quad) for quad in range(pairs // 2)], axis=1)
        count = block.shape[0]
        block = jnp.concatenate([block] * (2 * pairs), axis=0)
        row = lax.broadcasted_iota(jnp.int32, block.shape, 0) // count
        lane = lax.broadcasted_iota(jnp.int32, block.shape, 1) // HEAD_DIM
        block = jnp.transpose(jnp.where(row == lane, block, 0.0).astype(jnp.bfloat16))
        special_out[...] = block
        return block

    per_image = patch_total // images
    masks = [(per_image, mask[b : b + 1, :]) for b in range(images)]
    state = State(patch_total, state_out)
    for result in attend_all(
        patch_columns, masks, queries_of, special_queries, None, pairs, patch_total, 0
    ):
        state.put(*result)


def joined(stretches, mask, refs):
    count = len(stretches)
    own = jnp.concatenate([ref[...] for ref in refs[:count]], axis=0)
    other = jnp.concatenate([ref[...] for ref in refs[count : 2 * count]], axis=0)
    masks = [(rows, mask[i : i + 1, :]) for part in stretches for rows, i in part]
    return own, other, masks, refs[2 * count :]


def given(pairs):
    width = pairs.shape[1] // 2

    def columns(which, quad):
        first = (which - 1) * width + quad * QUAD
        return pairs[:, first : first + QUAD]

    return columns


def later_kernel(stretches, mask, *refs):
    own, other, masks, refs = joined(stretches, mask, refs)
    weights, queries, special_queries = refs[:3]
    state_in, state_out = refs[3:7], refs[7:]
    pairs, rows = queries.shape[0], queries.shape[2] // 2
    state = State(rows, state_out)
    for result in attend_all(
        projector(own, other, weights), masks, lambda pair: queries[pair], lambda: special_queries[...],
        State(rows, state_in), pairs, rows, None,
    ):
        state.put(*result)


def half_kernel(count, *refs):
    weights, sums_out = refs[count:]
    rows = jnp.concatenate([ref[...] for ref in refs[:count]], axis=0)
    for i in range(2):
        sums_out[i] = product(rows, weights[i + 1, : rows.shape[1], :])


def begun(sums, other, weights):
    depth = other.shape[1]

    def columns(which, quad):
        lanes = slice(quad * QUAD, (quad + 1) * QUAD)
        return sums[which - 1, :, lanes] + product(other, weights[which, depth:, lanes])

    return columns


def begun_kernel(stretches, mask, sums, *refs):
    count = len(stretches)
    other = jnp.concatenate([ref[...] for ref in refs[:count]], axis=0)
    masks = [(rows, mask[i : i + 1, :]) for part in stretches for rows, i in part]
    weights, queries, special_queries = refs[count : count + 3]
    state_in, state_out = refs[count + 3 : count + 7], refs[count + 7 :]
    pairs, rows = queries.shape[0], queries.shape[2] // 2
    state = State(rows, state_out)
    for result in attend_all(
        begun(sums, other, weights), masks, lambda pair: queries[pair], lambda: special_queries[...],
        State(rows, state_in), pairs, rows, None,
    ):
        state.put(*result)


def last_kernel(
    special_real, mask, special_pairs, queries, special_queries, *refs
):
    state_in = refs[:4]
    w_here, kept_out, sent_out = refs[4:]
    masks = [(special_pairs.shape[0], None)]
    pairs, rows = queries.shape[0], queries.shape[2] // 2
    columns, waiting, out, special = [], [], None, None
    sides = halves(kept_out.shape[1])
    for pair, sub, _, total, weight in attend_all(
        given(special_pairs), masks, lambda pair: queries[pair], lambda: special_queries[...],
        State(rows, state_in), pairs, rows, special_real,
    ):
        share = total * (1.0 / weight)
        if pair == pairs:
            row = lax.broadcasted_iota(jnp.int32, share.shape, 0) // HEAD_DIM
            lane = lax.broadcasted_iota(jnp.int32, share.shape, 1) // TILE_ROWS
            share = jnp.transpose(jnp.where(row == lane, share, 0.0))
            share = sum(share[i * TILE_ROWS : (i + 1) * TILE_ROWS] for i in range(2 * pairs))
            special = share.astype(jnp.bfloat16)
        else:
            columns.append(share)
            if pair % 2 == 1 and sub == 1:
                quad = jnp.transpose(jnp.concatenate(columns, axis=0).astype(jnp.bfloat16))
                waiting.append((slice((pair // 2) * QUAD, (pair // 2 + 1) * QUAD), quad))
                columns = []
        if special is not None:
            for features, quad in waiting:
                quad = jnp.concatenate([quad, special[:, features]], axis=0)
                added = [product(quad, w_here[features, side]) for side in sides]
                out = added if out is None else [before + more for before, more in zip(out, added)]
            waiting = []
    sent_out[...] = out[1].astype(jnp.bfloat16)
    kept_out[...] = out[0]


def end_kernel(images, kept, received, patch_out, special_out):
    patch_total = patch_out.shape[0]
    special_count = special_out.shape[0]
    patch_out[...] = (kept[:patch_total, :] + received[:patch_total, :].astype(jnp.float32)).astype(
        jnp.bfloat16
    )
    rest = kept[patch_total:, :] + received[patch_total:, :].astype(jnp.float32)
    rows = [rest[b * special_count : (b + 1) * special_count][:, None, :] for b in range(images)]
    special_out[...] = jnp.concatenate(rows, axis=1).astype(jnp.bfloat16)


def call(kernel, out_shape, operands, in_specs=None, out_specs=None, scratch=(), flops=0):
    if in_specs:
        operands = [
            pltpu.with_memory_space_constraint(operand, pltpu.HBM) if spec is HBM else operand
            for operand, spec in zip(operands, in_specs)
        ]
    return pl.pallas_call(
        kernel,
        out_shape=out_shape,
        in_specs=in_specs or [VMEM] * len(operands),
        out_specs=out_specs or [VMEM] * len(out_shape),
        scratch_shapes=scratch,
        compiler_params=pltpu.CompilerParams(vmem_limit_bytes=VMEM_BYTES),
        cost_estimate=pl.CostEstimate(flops=flops, transcendentals=0, bytes_accessed=0),
    )(*operands)


def stack_kernel(first, second, out):
    count = first.shape[0]
    out[:count, :] = first[...]
    out[count:, :] = second[...]


def compact_kernel(block, real, first, second, out):
    rows = [
        part[start : start + real, :].astype(jnp.float32)
        for part in (first, second)
        for start in range(0, part.shape[0], block)
    ]
    padding = out.shape[0] - sum(part.shape[0] for part in rows)
    if padding:
        rows.append(jnp.zeros((padding, out.shape[1]), jnp.float32))
    out[...] = jnp.concatenate(rows, axis=0).astype(jnp.bfloat16)


def stacked(first, second, flops=0):
    shape = jax.ShapeDtypeStruct((2 * first.shape[0], first.shape[1]), first.dtype)
    return call(stack_kernel, [shape], (first, second), flops=flops)[0]


def after(array, *others):
    return lax.optimization_barrier((array, *others))[0]


def per_device(
    patch_rows, special_rows, role_first, role_rest, frame_order, covisible, w_qkv, w_out
):
    images, per_image, width = patch_rows.shape
    special_count = special_rows.shape[1]
    real_rows = images * special_count
    special_block = real_rows + -real_rows % TILE_ROWS
    owner_count = lax.axis_size("blk")
    reach = max(1, owner_count // 64)
    patch_total = images * per_image
    rows = patch_total + special_block
    heads = width // HEAD_DIM
    pairs = heads // 2
    paired = reach == 1 and owner_count % 2 == 0

    if paired:
        offsets = [0, (-1, 1), (1, -1)]
    else:
        offsets = [0] + [sign * d for d in range(1, reach + 1) for sign in (-1, 1)]
    mask_rows = -(-len(offsets) * images // 8) * 8
    bf16 = lambda *shape: jax.ShapeDtypeStruct(shape, jnp.bfloat16)
    f32 = lambda *shape: jax.ShapeDtypeStruct(shape, jnp.float32)
    state_shape = [
        f32(8, 2 * patch_total),
        f32(8, 2 * patch_total),
        f32(pairs, HEAD_DIM, 2 * patch_total),
        f32(width, heads * special_block),
    ]

    both = lambda part: (part, swapped(part, "head", 1))
    patches = patch_rows.reshape(patch_total, width)
    turned = jnp.transpose(special_rows, (1, 0, 2))
    power = owner_count >= 8 and owner_count & (owner_count - 1) == 0
    specials, own = call(
        rows_kernel,
        [
            bf16(special_block, width),
            bf16(patch_total, width),
        ],
        (frame_order, turned, role_first, role_rest, patches),
        in_specs=[HBM] * 5,
        scratch=[
            pltpu.SMEM(frame_order.shape, jnp.int32),
            pltpu.VMEM(turned.shape, jnp.bfloat16),
            pltpu.VMEM(role_first.shape, jnp.bfloat16),
            pltpu.VMEM(role_rest.shape, jnp.bfloat16),
            pltpu.SemaphoreType.DMA((5,)),
        ],
    )
    specials = both(specials)
    mask, weights, everywhere, w_here = call(
        functools.partial(start_kernel, offsets, per_image, special_count, special_block),
        [
            f32(mask_rows, patch_total + heads * special_block),
            bf16(*w_qkv.shape),
            bf16(special_block, 2 * width),
            bf16(*w_out.shape),
        ],
        (covisible, *specials, w_qkv, w_out),
        in_specs=[HBM, VMEM, VMEM, HBM, HBM],
        scratch=[pltpu.SMEM(covisible.shape, jnp.int32), pltpu.SemaphoreType.DMA((1 + 7,))],
    )
    if paired and power:
        everywhere = stacked(everywhere, swapped(everywhere, "blk", 2), FIRST)
    queries, special_queries, *state = call(
        functools.partial(first_kernel, images),
        [bf16(pairs, PAIR, 2 * patch_total), bf16(width, heads * special_block), *state_shape],
        (mask, own, swapped(patches, "head", 1), *specials, weights),
    )
    fixed = (weights, queries, special_queries)

    def later(stretches, parts, state):
        return call(
            functools.partial(later_kernel, stretches),
            state_shape,
            (mask, *[part[0] for part in parts], *[part[1] for part in parts], *fixed, *state),
        )

    image_rows = lambda owner: [(per_image, owner * images + b) for b in range(images)]
    def halved(part, gate):
        part = after(part, gate)
        starts = range(0, part.shape[0], per_image)
        return [both(part[start : start + per_image]) for start in starts]

    stretches = lambda owner: [[image] for image in image_rows(owner)]
    if paired:
        far = after(crossed(patches, "blk"), state[0])
        near = swapped(patches, "blk", 1)
        if power:
            everywhere = after(everywhere, far)
            bit = 4
            while 2 * bit < owner_count:
                everywhere = stacked(everywhere, swapped(everywhere, "blk", bit))
                bit *= 2
            arrived = swapped(everywhere, "blk", bit)
        state = later(stretches(1), halved(far, state[0]), state)
        if power:
            real = real_rows * owner_count // 2
            blocks = (real + -real % TILE_ROWS, real)
            (everywhere,) = call(
                functools.partial(compact_kernel, special_block, real_rows),
                [bf16(blocks[0], 2 * width)],
                (after(everywhere, state[0]), arrived),
                flops=FIRST,
            )
            arrived = swapped(everywhere, "blk", 1)
        parts = halved(near, state[0])
        (sums,) = call(
            functools.partial(half_kernel, len(parts)),
            [f32(2, patch_total, width)],
            (*[part[0] for part in parts], weights),
            flops=0,
        )
        state = call(
            functools.partial(begun_kernel, stretches(2)),
            state_shape,
            (mask, sums, *[part[1] for part in parts], *fixed, *state),
        )
        if power:
            everywhere = stacked(after(everywhere, state[0]), arrived)
    else:
        for i, offset in enumerate(offsets[1:]):
            state = later(stretches(i + 1), halved(shifted(patches, "blk", -offset), state[0]), state)
    if not (paired and power):
        blocks = (special_block, real_rows)
        everywhere = lax.all_gather(everywhere, "blk", axis=0, tiled=True)
    kept, sent = call(
        functools.partial(last_kernel, blocks),
        [f32(rows, width), bf16(rows, width)],
        (mask, everywhere, queries, special_queries, *state, w_here),
    )
    received = swapped(sent, "head", 1)
    patch_out, special_out = call(
        functools.partial(end_kernel, images),
        [bf16(patch_total, width), bf16(special_count, images, width)],
        (kept, received),
        out_specs=[pl.BlockSpec(), pl.BlockSpec()],
    )
    return patch_out.reshape(patch_rows.shape), jnp.transpose(special_out, (1, 0, 2))


def solution(mesh):
    in_specs = (
        P(("scene", "blk"), None, "head"),
        P(("scene", "blk"), None, "head"),
        P(),
        P(),
        P(("scene", "blk")),
        P(("scene", "blk"), None),
        P(None, None, "head"),
        P("head", None),
    )
    out_specs = (P(("scene", "blk"), None, "head"), P(("scene", "blk"), None, "head"))
    return jax.shard_map(
        per_device, mesh=mesh, in_specs=in_specs, out_specs=out_specs, check_vma=False
    )
```

```python
import functools

import jax
import jax.numpy as jnp
from jax import lax
from jax.experimental import pallas as pl
from jax.experimental.pallas import tpu as pltpu
from jax.sharding import PartitionSpec as P

HEAD_DIM = 64
PAIR = 2 * HEAD_DIM
QUAD = 2 * PAIR
TILE_ROWS = 16
LOG2_E = 1.4426950408889634
FIRST = 20_000_000_000
VMEM_BYTES = 32 * 1024 * 1024
SMEM = pl.BlockSpec(memory_space=pltpu.SMEM)
VMEM = pl.BlockSpec(memory_space=pltpu.VMEM)
HBM = pl.BlockSpec(memory_space=pltpu.HBM)


def shifted(block, axis, distance):
    count = lax.axis_size(axis)
    route = [((i - distance) % count, i) for i in range(count)]
    return lax.ppermute(block, axis, route)


def swapped(block, axis, bit):
    count = lax.axis_size(axis)
    return lax.ppermute(block, axis, [(i ^ bit, i) for i in range(count)])


def crossed(block, axis):
    count = lax.axis_size(axis)
    return lax.ppermute(block, axis, [(i, (i + (-1 if i % 2 == 0 else 1)) % count) for i in range(count)])


def halves(width):
    half = lax.axis_index("head")
    mine = pl.ds(pl.multiple_of(half * width, width), width)
    theirs = pl.ds(pl.multiple_of((1 - half) * width, width), width)
    return mine, theirs


def product(left, right):
    return jnp.dot(left, right, preferred_element_type=jnp.float32)


def owner_at(offset):
    count = lax.axis_size("blk")
    here = lax.axis_index("blk")
    if isinstance(offset, tuple):
        offset = jnp.where(lax.rem(here, 2) == 0, offset[0], offset[1])
    return lax.rem(here + offset + count, count)


def rows_kernel(
    frame_order, specials, role_first, role_rest, patches,
    special_out, patches_out, order, here, first_rows, rest_rows, copied,
):
    special_count, images, width = specials.shape
    moves = [(specials, here), (role_first, first_rows), (role_rest, rest_rows), (frame_order, order)]
    moves.append((patches, patches_out))
    copies = [
        pltpu.make_async_copy(source, target, copied.at[i]) for i, (source, target) in enumerate(moves)
    ]
    for copy in copies:
        copy.start()
    for copy in copies[:4]:
        copy.wait()
    mine, _ = halves(width)
    first = first_rows[:, mine].astype(jnp.float32)
    rest = rest_rows[:, mine].astype(jnp.float32)
    summed = [
        here[:, b, :].astype(jnp.float32) + jnp.where(order[b] == 0, first, rest) for b in range(images)
    ]
    summed.append(jnp.zeros((special_out.shape[0] - images * special_count, width), jnp.float32))
    special_out[...] = jnp.concatenate(summed, axis=0).astype(jnp.bfloat16)
    for copy in copies[4:]:
        copy.wait()


def start_kernel(
    offsets, per_image, special_count, special_total, covisible, special, other_special, w_qkv, w_out,
    mask_out, weights_out, pairs_out, w_out_here, seen, copied,
):
    images = covisible.shape[0]
    patch_total = images * per_image
    moves = [(covisible, seen)]
    depth = w_qkv.shape[1] // 2
    for i in range(3):
        for j, rows in enumerate(halves(depth)):
            moves.append((w_qkv.at[i, rows], weights_out.at[i, pl.ds(j * depth, depth)]))
    moves.append((w_out, w_out_here))
    copies = [
        pltpu.make_async_copy(source, target, copied.at[i]) for i, (source, target) in enumerate(moves)
    ]
    for copy in copies:
        copy.start()
    copies[0].wait()
    lane = lax.broadcasted_iota(jnp.int32, (1, mask_out.shape[1]), 1)
    special_lane = lax.rem(lane - patch_total, special_total)
    image = jnp.where(
        lane < patch_total, lane // per_image, jnp.minimum(special_lane // special_count, images - 1)
    )
    for i, offset in enumerate(offsets):
        for b in range(images):
            row = jnp.zeros(lane.shape, jnp.float32)
            for a in range(images):
                hidden = seen[a, owner_at(offset) * images + b] <= 0
                row = jnp.where((image == a) & hidden, -jnp.inf, row)
            mask_out[i * images + b : i * images + b + 1, :] = row
    rows = jnp.concatenate([special[...], other_special[...]], axis=1)
    width = weights_out.shape[2]
    for copy in copies[1:-1]:
        copy.wait()
    for i in range(2):
        pairs_out[:, i * width : (i + 1) * width] = product(rows, weights_out[i + 1]).astype(jnp.bfloat16)
    copies[-1].wait()


def projector(own, other, weights):
    rows = jnp.concatenate([own, other], axis=1)

    def columns(which, quad):
        return product(rows, weights[which, :, quad * QUAD : (quad + 1) * QUAD])

    return columns


def attend(scores, masks, state):
    largest = state
    start = 0
    for count, mask in masks:
        part = jnp.max(scores[start : start + count], axis=0, keepdims=True)
        part = part if mask is None else part + mask
        largest = part if largest is None else jnp.maximum(largest, part)
        start += count
    weights, start = [], 0
    for count, mask in masks:
        level = largest if mask is None else largest - mask
        weights.append(jnp.exp2((scores[start : start + count] - level).astype(jnp.bfloat16)))
        start += count
    factor = None if state is None else jnp.exp2(state - largest)
    return largest, factor, jnp.concatenate(weights, axis=0)


def attend_all(columns, masks, queries_of, special_queries, state, pairs, rows, special_real):
    keys, values = {}, {}
    quads = pairs // 2

    def keys_of(quad):
        if quad not in keys:
            keys[quad] = columns(1, quad).astype(jnp.bfloat16)
        return keys[quad]

    def values_of(quad):
        if quad not in values:
            values[quad] = jnp.transpose(columns(2, quad).astype(jnp.bfloat16))
        return values[quad]

    def prepared(pair):
        if pair == pairs:
            scores = product(
                jnp.concatenate([keys_of(quad) for quad in range(quads)], axis=1), special_queries()
            )
        else:
            lanes = slice((pair % 2) * PAIR, (pair % 2 + 1) * PAIR)
            scores = product(keys_of(pair // 2)[:, lanes], queries_of(pair))
        if all(mask is not None for _, mask in masks):
            return scores
        parts, start = [], 0
        for count, mask in masks:
            part = scores[start : start + count]
            if mask is None:
                key_row = lax.broadcasted_iota(jnp.int32, (count, 1), 0)
                part = jnp.where(lax.rem(key_row, special_real[0]) < special_real[1], part, -jnp.inf)
            parts.append(part)
            start += count
        return jnp.concatenate(parts, axis=0)

    ones = jnp.ones((TILE_ROWS, sum(count for count, _ in masks)), jnp.bfloat16)
    both = [
        (count, None if mask is None else jnp.concatenate([mask[:, :rows]] * 2, axis=1))
        for count, mask in masks
    ]
    only = [(count, None if mask is None else mask[:, rows:]) for count, mask in masks]
    order = list(range(pairs))
    order.insert(pairs - 2, pairs)
    scores = prepared(order[0])
    for step, pair in enumerate(order):
        if pair < pairs:
            left = values_of(pair // 2)[(pair % 2) * PAIR : (pair % 2 + 1) * PAIR]
        else:
            left = jnp.concatenate([values_of(quad) for quad in range(quads)], axis=0)
        following = prepared(order[step + 1]) if step < pairs else None
        largest, factor, weights = attend(
            scores, both if pair < pairs else only, state and state.largest(pair)
        )
        added = product(jnp.concatenate([left, ones], axis=0), weights)
        height, subs = (HEAD_DIM, 2) if pair < pairs else (left.shape[0], 1)
        width = scores.shape[1] // subs
        for sub in range(subs):
            lanes = slice(sub * width, (sub + 1) * width)
            total = added[sub * height : (sub + 1) * height, lanes]
            weight = added[left.shape[0] : left.shape[0] + 1, lanes]
            if state is not None:
                total = total + state.total(pair, sub) * factor[:, lanes]
                weight = weight + state.weight(pair, sub) * factor[:, lanes]
            yield pair, sub, largest[:, lanes], total, weight
        scores = following


class State:
    def __init__(self, rows, refs):
        self.rows = rows
        self.largest_ref, self.weight_ref, self.total_ref, self.special_ref = refs

    def lanes(self, pair, sub):
        if pair == self.total_ref.shape[0]:
            return slice(0, self.special_ref.shape[1])
        return slice(sub * self.rows, (sub + 1) * self.rows)

    def largest(self, pair):
        stop = self.special_ref.shape[1] if pair == self.total_ref.shape[0] else 2 * self.rows
        return self.largest_ref[pair : pair + 1, 0:stop]

    def weight(self, pair, sub):
        return self.weight_ref[pair : pair + 1, self.lanes(pair, sub)]

    def total(self, pair, sub):
        if pair == self.total_ref.shape[0]:
            return self.special_ref[...]
        return self.total_ref[pair, :, self.lanes(pair, sub)]

    def put(self, pair, sub, largest, total, weight):
        lanes = self.lanes(pair, sub)
        self.largest_ref[pair : pair + 1, lanes] = largest
        self.weight_ref[pair : pair + 1, lanes] = weight
        if pair == self.total_ref.shape[0]:
            self.special_ref[...] = total
        else:
            self.total_ref[pair, :, lanes] = total


def first_kernel(
    images, mask, own, other, special, other_special, weights, queries_out, special_out, *state_out
):
    patch_total = own.shape[0]
    columns = projector(
        jnp.concatenate([own[...], special[...]], axis=0),
        jnp.concatenate([other[...], other_special[...]], axis=0),
        weights,
    )
    pairs = queries_out.shape[0]
    zero = jnp.zeros((HEAD_DIM, patch_total), jnp.bfloat16)
    made = {}

    def patch_columns(which, quad):
        return columns(which, quad)[:patch_total]

    def columns_of(quad):
        if quad not in made:
            queries = columns(0, quad) * (HEAD_DIM ** (-0.5) * LOG2_E)
            made[quad] = queries[patch_total:]
            turned = jnp.transpose(queries[:patch_total].astype(jnp.bfloat16))
            for i in range(2):
                first = i * PAIR
                upper = jnp.concatenate([turned[first : first + HEAD_DIM], zero], axis=1)
                lower = jnp.concatenate([zero, turned[first + HEAD_DIM : first + PAIR]], axis=1)
                queries_out[2 * quad + i] = jnp.concatenate([upper, lower], axis=0)
        return made[quad]

    def queries_of(pair):
        columns_of(pair // 2)
        return queries_out[pair]

    def special_queries():
        block = jnp.concatenate([columns_of(quad) for quad in range(pairs // 2)], axis=1)
        count = block.shape[0]
        block = jnp.concatenate([block] * (2 * pairs), axis=0)
        row = lax.broadcasted_iota(jnp.int32, block.shape, 0) // count
        lane = lax.broadcasted_iota(jnp.int32, block.shape, 1) // HEAD_DIM
        block = jnp.transpose(jnp.where(row == lane, block, 0.0).astype(jnp.bfloat16))
        special_out[...] = block
        return block

    per_image = patch_total // images
    masks = [(per_image, mask[b : b + 1, :]) for b in range(images)]
    state = State(patch_total, state_out)
    for result in attend_all(
        patch_columns, masks, queries_of, special_queries, None, pairs, patch_total, 0
    ):
        state.put(*result)


def joined(stretches, mask, refs):
    count = len(stretches)
    own = jnp.concatenate([ref[...] for ref in refs[:count]], axis=0)
    other = jnp.concatenate([ref[...] for ref in refs[count : 2 * count]], axis=0)
    masks = [(rows, mask[i : i + 1, :]) for part in stretches for rows, i in part]
    return own, other, masks, refs[2 * count :]


def given(pairs):
    width = pairs.shape[1] // 2

    def columns(which, quad):
        first = (which - 1) * width + quad * QUAD
        return pairs[:, first : first + QUAD]

    return columns


def later_kernel(stretches, mask, *refs):
    own, other, masks, refs = joined(stretches, mask, refs)
    weights, queries, special_queries = refs[:3]
    state_in, state_out = refs[3:7], refs[7:]
    pairs, rows = queries.shape[0], queries.shape[2] // 2
    state = State(rows, state_out)
    for result in attend_all(
        projector(own, other, weights), masks, lambda pair: queries[pair], lambda: special_queries[...],
        State(rows, state_in), pairs, rows, None,
    ):
        state.put(*result)


def half_kernel(count, *refs):
    weights, sums_out = refs[count:]
    rows = jnp.concatenate([ref[...] for ref in refs[:count]], axis=0)
    for i in range(2):
        sums_out[i] = product(rows, weights[i + 1, : rows.shape[1], :])


def begun(sums, other, weights):
    depth = other.shape[1]

    def columns(which, quad):
        lanes = slice(quad * QUAD, (quad + 1) * QUAD)
        return sums[which - 1, :, lanes] + product(other, weights[which, depth:, lanes])

    return columns


def begun_kernel(stretches, special_real, mask, sums, *refs):
    count = len(stretches)
    other = jnp.concatenate([ref[...] for ref in refs[:count]], axis=0)
    masks = [(rows, mask[i : i + 1, :]) for part in stretches for rows, i in part]
    weights, queries, special_queries, special_pairs = refs[count : count + 4]
    state_in, state_out = refs[count + 4 : count + 8], refs[count + 8 :]
    sources = [begun(sums, other, weights)]
    if special_real is not None:
        sources.append(given(special_pairs))
        masks.append((special_pairs.shape[0], None))
    pairs, rows = queries.shape[0], queries.shape[2] // 2

    def joint(which, quad):
        parts = [source(which, quad).astype(jnp.bfloat16) for source in sources]
        return jnp.concatenate(parts, axis=0)

    state = State(rows, state_out)
    for result in attend_all(
        joint, masks, lambda pair: queries[pair], lambda: special_queries[...],
        State(rows, state_in), pairs, rows, special_real,
    ):
        state.put(*result)


def last_kernel(
    special_real, mask, special_pairs, queries, special_queries, *refs
):
    state_in = refs[:4]
    w_here, kept_out, sent_out = refs[4:]
    masks = [(special_pairs.shape[0], None)]
    pairs, rows = queries.shape[0], queries.shape[2] // 2
    columns, waiting, out, special = [], [], None, None
    sides = halves(kept_out.shape[1])
    for pair, sub, _, total, weight in attend_all(
        given(special_pairs), masks, lambda pair: queries[pair], lambda: special_queries[...],
        State(rows, state_in), pairs, rows, special_real,
    ):
        share = total * (1.0 / weight)
        if pair == pairs:
            row = lax.broadcasted_iota(jnp.int32, share.shape, 0) // HEAD_DIM
            lane = lax.broadcasted_iota(jnp.int32, share.shape, 1) // TILE_ROWS
            share = jnp.transpose(jnp.where(row == lane, share, 0.0))
            share = sum(share[i * TILE_ROWS : (i + 1) * TILE_ROWS] for i in range(2 * pairs))
            special = share.astype(jnp.bfloat16)
        else:
            columns.append(share)
            if pair % 2 == 1 and sub == 1:
                quad = jnp.transpose(jnp.concatenate(columns, axis=0).astype(jnp.bfloat16))
                waiting.append((slice((pair // 2) * QUAD, (pair // 2 + 1) * QUAD), quad))
                columns = []
        if special is not None:
            for features, quad in waiting:
                quad = jnp.concatenate([quad, special[:, features]], axis=0)
                added = [product(quad, w_here[features, side]) for side in sides]
                out = added if out is None else [before + more for before, more in zip(out, added)]
            waiting = []
    sent_out[...] = out[1].astype(jnp.bfloat16)
    kept_out[...] = out[0]


def end_kernel(images, kept, received, patch_out, special_out):
    patch_total = patch_out.shape[0]
    special_count = special_out.shape[0]
    patch_out[...] = (kept[:patch_total, :] + received[:patch_total, :].astype(jnp.float32)).astype(
        jnp.bfloat16
    )
    rest = kept[patch_total:, :] + received[patch_total:, :].astype(jnp.float32)
    rows = [rest[b * special_count : (b + 1) * special_count][:, None, :] for b in range(images)]
    special_out[...] = jnp.concatenate(rows, axis=1).astype(jnp.bfloat16)


def call(kernel, out_shape, operands, in_specs=None, out_specs=None, scratch=(), flops=0):
    if in_specs:
        operands = [
            pltpu.with_memory_space_constraint(operand, pltpu.HBM) if spec is HBM else operand
            for operand, spec in zip(operands, in_specs)
        ]
    return pl.pallas_call(
        kernel,
        out_shape=out_shape,
        in_specs=in_specs or [VMEM] * len(operands),
        out_specs=out_specs or [VMEM] * len(out_shape),
        scratch_shapes=scratch,
        compiler_params=pltpu.CompilerParams(vmem_limit_bytes=VMEM_BYTES),
        cost_estimate=pl.CostEstimate(flops=flops, transcendentals=0, bytes_accessed=0),
    )(*operands)


def stack_kernel(first, second, out):
    count = first.shape[0]
    out[:count, :] = first[...]
    out[count:, :] = second[...]


def compact_kernel(block, real, first, second, out):
    rows = [
        part[start : start + real, :].astype(jnp.float32)
        for part in (first, second)
        for start in range(0, part.shape[0], block)
    ]
    padding = out.shape[0] - sum(part.shape[0] for part in rows)
    if padding:
        rows.append(jnp.zeros((padding, out.shape[1]), jnp.float32))
    out[...] = jnp.concatenate(rows, axis=0).astype(jnp.bfloat16)


def stacked(first, second, flops=0):
    shape = jax.ShapeDtypeStruct((2 * first.shape[0], first.shape[1]), first.dtype)
    return call(stack_kernel, [shape], (first, second), flops=flops)[0]


def after(array, *others):
    return lax.optimization_barrier((array, *others))[0]


def per_device(
    patch_rows, special_rows, role_first, role_rest, frame_order, covisible, w_qkv, w_out
):
    images, per_image, width = patch_rows.shape
    special_count = special_rows.shape[1]
    real_rows = images * special_count
    special_block = real_rows + -real_rows % TILE_ROWS
    owner_count = lax.axis_size("blk")
    reach = max(1, owner_count // 64)
    patch_total = images * per_image
    rows = patch_total + special_block
    heads = width // HEAD_DIM
    pairs = heads // 2
    paired = reach == 1 and owner_count % 2 == 0

    if paired:
        offsets = [0, (-1, 1), (1, -1)]
    else:
        offsets = [0] + [sign * d for d in range(1, reach + 1) for sign in (-1, 1)]
    mask_rows = -(-len(offsets) * images // 8) * 8
    bf16 = lambda *shape: jax.ShapeDtypeStruct(shape, jnp.bfloat16)
    f32 = lambda *shape: jax.ShapeDtypeStruct(shape, jnp.float32)
    state_shape = [
        f32(8, 2 * patch_total),
        f32(8, 2 * patch_total),
        f32(pairs, HEAD_DIM, 2 * patch_total),
        f32(width, heads * special_block),
    ]

    both = lambda part: (part, swapped(part, "head", 1))
    patches = patch_rows.reshape(patch_total, width)
    turned = jnp.transpose(special_rows, (1, 0, 2))
    power = owner_count >= 8 and owner_count & (owner_count - 1) == 0
    specials, own = call(
        rows_kernel,
        [
            bf16(special_block, width),
            bf16(patch_total, width),
        ],
        (frame_order, turned, role_first, role_rest, patches),
        in_specs=[HBM] * 5,
        scratch=[
            pltpu.SMEM(frame_order.shape, jnp.int32),
            pltpu.VMEM(turned.shape, jnp.bfloat16),
            pltpu.VMEM(role_first.shape, jnp.bfloat16),
            pltpu.VMEM(role_rest.shape, jnp.bfloat16),
            pltpu.SemaphoreType.DMA((5,)),
        ],
    )
    specials = both(specials)
    mask, weights, everywhere, w_here = call(
        functools.partial(start_kernel, offsets, per_image, special_count, special_block),
        [
            f32(mask_rows, patch_total + heads * special_block),
            bf16(*w_qkv.shape),
            bf16(special_block, 2 * width),
            bf16(*w_out.shape),
        ],
        (covisible, *specials, w_qkv, w_out),
        in_specs=[HBM, VMEM, VMEM, HBM, HBM],
        scratch=[pltpu.SMEM(covisible.shape, jnp.int32), pltpu.SemaphoreType.DMA((1 + 7,))],
    )
    if paired and power:
        everywhere = stacked(everywhere, swapped(everywhere, "blk", 2), FIRST)
    queries, special_queries, *state = call(
        functools.partial(first_kernel, images),
        [bf16(pairs, PAIR, 2 * patch_total), bf16(width, heads * special_block), *state_shape],
        (mask, own, swapped(patches, "head", 1), *specials, weights),
    )
    fixed = (weights, queries, special_queries)

    def later(stretches, parts, state):
        return call(
            functools.partial(later_kernel, stretches),
            state_shape,
            (mask, *[part[0] for part in parts], *[part[1] for part in parts], *fixed, *state),
        )

    image_rows = lambda owner: [(per_image, owner * images + b) for b in range(images)]
    def halved(part, gate):
        part = after(part, gate)
        starts = range(0, part.shape[0], per_image)
        return [both(part[start : start + per_image]) for start in starts]

    stretches = lambda owner: [[image] for image in image_rows(owner)]
    if paired:
        far = after(crossed(patches, "blk"), state[0])
        near = swapped(patches, "blk", 1)
        if power:
            everywhere = after(everywhere, far)
            bit = 4
            while 2 * bit < owner_count:
                everywhere = stacked(everywhere, swapped(everywhere, "blk", bit))
                bit *= 2
            arrived = swapped(everywhere, "blk", bit)
        state = later(stretches(1), halved(far, state[0]), state)
        if power:
            real = real_rows * owner_count // 2
            blocks = (real + -real % TILE_ROWS, real)
            (everywhere,) = call(
                functools.partial(compact_kernel, special_block, real_rows),
                [bf16(blocks[0], 2 * width)],
                (after(everywhere, state[0]), arrived),
                flops=FIRST,
            )
            arrived = swapped(everywhere, "blk", 1)
        parts = halved(near, state[0])
        (sums,) = call(
            functools.partial(half_kernel, len(parts)),
            [f32(2, patch_total, width)],
            (*[part[0] for part in parts], weights),
            flops=0,
        )
        state = call(
            functools.partial(begun_kernel, stretches(2), blocks if power else None),
            state_shape,
            (mask, sums, *[part[1] for part in parts], *fixed, everywhere, *state),
        )
        if power:
            everywhere = arrived
    else:
        for i, offset in enumerate(offsets[1:]):
            state = later(stretches(i + 1), halved(shifted(patches, "blk", -offset), state[0]), state)
    if not (paired and power):
        blocks = (special_block, real_rows)
        everywhere = lax.all_gather(everywhere, "blk", axis=0, tiled=True)
    kept, sent = call(
        functools.partial(last_kernel, blocks),
        [f32(rows, width), bf16(rows, width)],
        (mask, everywhere, queries, special_queries, *state, w_here),
    )
    received = swapped(sent, "head", 1)
    patch_out, special_out = call(
        functools.partial(end_kernel, images),
        [bf16(patch_total, width), bf16(special_count, images, width)],
        (kept, received),
        out_specs=[pl.BlockSpec(), pl.BlockSpec()],
    )
    return patch_out.reshape(patch_rows.shape), jnp.transpose(special_out, (1, 0, 2))


def solution(mesh):
    in_specs = (
        P(("scene", "blk"), None, "head"),
        P(("scene", "blk"), None, "head"),
        P(),
        P(),
        P(("scene", "blk")),
        P(("scene", "blk"), None),
        P(None, None, "head"),
        P("head", None),
    )
    out_specs = (P(("scene", "blk"), None, "head"), P(("scene", "blk"), None, "head"))
    return jax.shard_map(
        per_device, mesh=mesh, in_specs=in_specs, out_specs=out_specs, check_vma=False
    )
```

```python
import functools

import jax
import jax.numpy as jnp
from jax import lax
from jax.experimental import pallas as pl
from jax.experimental.pallas import tpu as pltpu
from jax.sharding import PartitionSpec as P

HEAD_DIM = 64
PAIR = 2 * HEAD_DIM
QUAD = 2 * PAIR
TILE_ROWS = 16
LOG2_E = 1.4426950408889634
FIRST = 20_000_000_000
VMEM_BYTES = 32 * 1024 * 1024
SMEM = pl.BlockSpec(memory_space=pltpu.SMEM)
VMEM = pl.BlockSpec(memory_space=pltpu.VMEM)
HBM = pl.BlockSpec(memory_space=pltpu.HBM)


def shifted(block, axis, distance):
    count = lax.axis_size(axis)
    route = [((i - distance) % count, i) for i in range(count)]
    return lax.ppermute(block, axis, route)


def swapped(block, axis, bit):
    count = lax.axis_size(axis)
    return lax.ppermute(block, axis, [(i ^ bit, i) for i in range(count)])


def crossed(block, axis):
    count = lax.axis_size(axis)
    return lax.ppermute(block, axis, [(i, (i + (-1 if i % 2 == 0 else 1)) % count) for i in range(count)])


def halves(width):
    half = lax.axis_index("head")
    mine = pl.ds(pl.multiple_of(half * width, width), width)
    theirs = pl.ds(pl.multiple_of((1 - half) * width, width), width)
    return mine, theirs


def product(left, right):
    return jnp.dot(left, right, preferred_element_type=jnp.float32)


def owner_at(offset):
    count = lax.axis_size("blk")
    here = lax.axis_index("blk")
    if isinstance(offset, tuple):
        offset = jnp.where(lax.rem(here, 2) == 0, offset[0], offset[1])
    return lax.rem(here + offset + count, count)


def rows_kernel(
    frame_order, specials, role_first, role_rest, patches,
    special_out, patches_out, order, here, first_rows, rest_rows, copied,
):
    special_count, images, width = specials.shape
    moves = [(specials, here), (role_first, first_rows), (role_rest, rest_rows), (frame_order, order)]
    moves.append((patches, patches_out))
    copies = [
        pltpu.make_async_copy(source, target, copied.at[i]) for i, (source, target) in enumerate(moves)
    ]
    for copy in copies:
        copy.start()
    for copy in copies[:4]:
        copy.wait()
    mine, _ = halves(width)
    first = first_rows[:, mine].astype(jnp.float32)
    rest = rest_rows[:, mine].astype(jnp.float32)
    summed = [
        here[:, b, :].astype(jnp.float32) + jnp.where(order[b] == 0, first, rest) for b in range(images)
    ]
    summed.append(jnp.zeros((special_out.shape[0] - images * special_count, width), jnp.float32))
    special_out[...] = jnp.concatenate(summed, axis=0).astype(jnp.bfloat16)
    for copy in copies[4:]:
        copy.wait()


def start_kernel(
    offsets, per_image, special_count, special_total, covisible, special, other_special, w_qkv, w_out,
    mask_out, weights_out, pairs_out, w_out_here, seen, copied,
):
    images = covisible.shape[0]
    patch_total = images * per_image
    moves = [(covisible, seen)]
    depth = w_qkv.shape[1] // 2
    for i in range(3):
        for j, rows in enumerate(halves(depth)):
            moves.append((w_qkv.at[i, rows], weights_out.at[i, pl.ds(j * depth, depth)]))
    moves.append((w_out, w_out_here))
    copies = [
        pltpu.make_async_copy(source, target, copied.at[i]) for i, (source, target) in enumerate(moves)
    ]
    for copy in copies:
        copy.start()
    copies[0].wait()
    lane = lax.broadcasted_iota(jnp.int32, (1, mask_out.shape[1]), 1)
    special_lane = lax.rem(lane - patch_total, special_total)
    image = jnp.where(
        lane < patch_total, lane // per_image, jnp.minimum(special_lane // special_count, images - 1)
    )
    for i, offset in enumerate(offsets):
        for b in range(images):
            row = jnp.zeros(lane.shape, jnp.float32)
            for a in range(images):
                hidden = seen[a, owner_at(offset) * images + b] <= 0
                row = jnp.where((image == a) & hidden, -jnp.inf, row)
            mask_out[i * images + b : i * images + b + 1, :] = row
    rows = jnp.concatenate([special[...], other_special[...]], axis=1)
    width = weights_out.shape[2]
    for copy in copies[1:-1]:
        copy.wait()
    for i in range(2):
        pairs_out[:, i * width : (i + 1) * width] = product(rows, weights_out[i + 1]).astype(jnp.bfloat16)
    copies[-1].wait()


def projector(own, other, weights):
    rows = jnp.concatenate([own, other], axis=1)

    def columns(which, quad):
        return product(rows, weights[which, :, quad * QUAD : (quad + 1) * QUAD])

    return columns


def attend(scores, masks, state):
    largest = state
    start = 0
    for count, mask in masks:
        part = jnp.max(scores[start : start + count], axis=0, keepdims=True)
        part = part if mask is None else part + mask
        largest = part if largest is None else jnp.maximum(largest, part)
        start += count
    weights, start = [], 0
    for count, mask in masks:
        level = largest if mask is None else largest - mask
        weights.append(jnp.exp2((scores[start : start + count] - level).astype(jnp.bfloat16)))
        start += count
    factor = None if state is None else jnp.exp2(state - largest)
    return largest, factor, jnp.concatenate(weights, axis=0)


def attend_all(columns, masks, queries_of, special_queries, state, pairs, rows, special_real):
    keys, values = {}, {}
    quads = pairs // 2

    def keys_of(quad):
        if quad not in keys:
            keys[quad] = columns(1, quad).astype(jnp.bfloat16)
        return keys[quad]

    def values_of(quad):
        if quad not in values:
            values[quad] = jnp.transpose(columns(2, quad).astype(jnp.bfloat16))
        return values[quad]

    def prepared(pair):
        if pair == pairs:
            scores = product(
                jnp.concatenate([keys_of(quad) for quad in range(quads)], axis=1), special_queries()
            )
        else:
            lanes = slice((pair % 2) * PAIR, (pair % 2 + 1) * PAIR)
            scores = product(keys_of(pair // 2)[:, lanes], queries_of(pair))
        if all(mask is not None for _, mask in masks):
            return scores
        parts, start = [], 0
        for count, mask in masks:
            part = scores[start : start + count]
            if mask is None:
                key_row = lax.broadcasted_iota(jnp.int32, (count, 1), 0)
                part = jnp.where(lax.rem(key_row, special_real[0]) < special_real[1], part, -jnp.inf)
            parts.append(part)
            start += count
        return jnp.concatenate(parts, axis=0)

    ones = jnp.ones((TILE_ROWS, sum(count for count, _ in masks)), jnp.bfloat16)
    both = [
        (count, None if mask is None else jnp.concatenate([mask[:, :rows]] * 2, axis=1))
        for count, mask in masks
    ]
    only = [(count, None if mask is None else mask[:, rows:]) for count, mask in masks]
    order = list(range(pairs))
    order.insert(pairs - 2, pairs)
    scores = prepared(order[0])
    for step, pair in enumerate(order):
        if pair < pairs:
            left = values_of(pair // 2)[(pair % 2) * PAIR : (pair % 2 + 1) * PAIR]
        else:
            left = jnp.concatenate([values_of(quad) for quad in range(quads)], axis=0)
        following = prepared(order[step + 1]) if step < pairs else None
        largest, factor, weights = attend(
            scores, both if pair < pairs else only, state and state.largest(pair)
        )
        added = product(jnp.concatenate([left, ones], axis=0), weights)
        height, subs = (HEAD_DIM, 2) if pair < pairs else (left.shape[0], 1)
        width = scores.shape[1] // subs
        for sub in range(subs):
            lanes = slice(sub * width, (sub + 1) * width)
            total = added[sub * height : (sub + 1) * height, lanes]
            weight = added[left.shape[0] : left.shape[0] + 1, lanes]
            if state is not None:
                total = total + state.total(pair, sub) * factor[:, lanes]
                weight = weight + state.weight(pair, sub) * factor[:, lanes]
            yield pair, sub, largest[:, lanes], total, weight
        scores = following


class State:
    def __init__(self, rows, refs):
        self.rows = rows
        self.largest_ref, self.weight_ref, self.total_ref, self.special_ref = refs

    def lanes(self, pair, sub):
        if pair == self.total_ref.shape[0]:
            return slice(0, self.special_ref.shape[1])
        return slice(sub * self.rows, (sub + 1) * self.rows)

    def largest(self, pair):
        stop = self.special_ref.shape[1] if pair == self.total_ref.shape[0] else 2 * self.rows
        return self.largest_ref[pair : pair + 1, 0:stop]

    def weight(self, pair, sub):
        return self.weight_ref[pair : pair + 1, self.lanes(pair, sub)]

    def total(self, pair, sub):
        if pair == self.total_ref.shape[0]:
            return self.special_ref[...]
        return self.total_ref[pair, :, self.lanes(pair, sub)]

    def put(self, pair, sub, largest, total, weight):
        lanes = self.lanes(pair, sub)
        self.largest_ref[pair : pair + 1, lanes] = largest
        self.weight_ref[pair : pair + 1, lanes] = weight
        if pair == self.total_ref.shape[0]:
            self.special_ref[...] = total
        else:
            self.total_ref[pair, :, lanes] = total


def first_kernel(
    images, mask, own, other, special, other_special, weights, queries_out, special_out, *state_out
):
    patch_total = own.shape[0]
    columns = projector(
        jnp.concatenate([own[...], special[...]], axis=0),
        jnp.concatenate([other[...], other_special[...]], axis=0),
        weights,
    )
    pairs = queries_out.shape[0]
    zero = jnp.zeros((HEAD_DIM, patch_total), jnp.bfloat16)
    made = {}

    def patch_columns(which, quad):
        return columns(which, quad)[:patch_total]

    def columns_of(quad):
        if quad not in made:
            queries = columns(0, quad) * (HEAD_DIM ** (-0.5) * LOG2_E)
            made[quad] = queries[patch_total:]
            turned = jnp.transpose(queries[:patch_total].astype(jnp.bfloat16))
            for i in range(2):
                first = i * PAIR
                upper = jnp.concatenate([turned[first : first + HEAD_DIM], zero], axis=1)
                lower = jnp.concatenate([zero, turned[first + HEAD_DIM : first + PAIR]], axis=1)
                queries_out[2 * quad + i] = jnp.concatenate([upper, lower], axis=0)
        return made[quad]

    def queries_of(pair):
        columns_of(pair // 2)
        return queries_out[pair]

    def special_queries():
        block = jnp.concatenate([columns_of(quad) for quad in range(pairs // 2)], axis=1)
        count = block.shape[0]
        block = jnp.concatenate([block] * (2 * pairs), axis=0)
        row = lax.broadcasted_iota(jnp.int32, block.shape, 0) // count
        lane = lax.broadcasted_iota(jnp.int32, block.shape, 1) // HEAD_DIM
        block = jnp.transpose(jnp.where(row == lane, block, 0.0).astype(jnp.bfloat16))
        special_out[...] = block
        return block

    per_image = patch_total // images
    masks = [(per_image, mask[b : b + 1, :]) for b in range(images)]
    state = State(patch_total, state_out)
    for result in attend_all(
        patch_columns, masks, queries_of, special_queries, None, pairs, patch_total, 0
    ):
        state.put(*result)


def joined(stretches, mask, refs):
    count = len(stretches)
    own = jnp.concatenate([ref[...] for ref in refs[:count]], axis=0)
    other = jnp.concatenate([ref[...] for ref in refs[count : 2 * count]], axis=0)
    masks = [(rows, mask[i : i + 1, :]) for part in stretches for rows, i in part]
    return own, other, masks, refs[2 * count :]


def given(pairs):
    width = pairs.shape[1] // 2

    def columns(which, quad):
        first = (which - 1) * width + quad * QUAD
        return pairs[:, first : first + QUAD]

    return columns


def later_kernel(stretches, mask, *refs):
    own, other, masks, refs = joined(stretches, mask, refs)
    weights, queries, special_queries = refs[:3]
    state_in, state_out = refs[3:7], refs[7:]
    pairs, rows = queries.shape[0], queries.shape[2] // 2
    state = State(rows, state_out)
    for result in attend_all(
        projector(own, other, weights), masks, lambda pair: queries[pair], lambda: special_queries[...],
        State(rows, state_in), pairs, rows, None,
    ):
        state.put(*result)


def half_kernel(count, *refs):
    weights, sums_out = refs[count:]
    rows = jnp.concatenate([ref[...] for ref in refs[:count]], axis=0)
    for i in range(2):
        sums_out[i] = product(rows, weights[i + 1, : rows.shape[1], :])


def begun(sums, other, weights):
    depth = other.shape[1]

    def columns(which, quad):
        lanes = slice(quad * QUAD, (quad + 1) * QUAD)
        return sums[which - 1, :, lanes] + product(other, weights[which, depth:, lanes])

    return columns


def begun_kernel(stretches, special_real, mask, sums, *refs):
    count = len(stretches)
    other = jnp.concatenate([ref[...] for ref in refs[:count]], axis=0)
    masks = [(rows, mask[i : i + 1, :]) for part in stretches for rows, i in part]
    weights, queries, special_queries, special_pairs = refs[count : count + 4]
    state_in, state_out = refs[count + 4 : count + 8], refs[count + 8 :]
    sources = [begun(sums, other, weights)]
    if special_real is not None:
        sources.append(given(special_pairs))
        masks.append((special_pairs.shape[0], None))
    pairs, rows = queries.shape[0], queries.shape[2] // 2

    def joint(which, quad):
        parts = [source(which, quad).astype(jnp.bfloat16) for source in sources]
        return jnp.concatenate(parts, axis=0)

    state = State(rows, state_out)
    for result in attend_all(
        joint, masks, lambda pair: queries[pair], lambda: special_queries[...],
        State(rows, state_in), pairs, rows, special_real,
    ):
        state.put(*result)


def last_kernel(
    special_real, mask, special_pairs, queries, special_queries, *refs
):
    state_in = refs[:4]
    w_here, kept_out, sent_out = refs[4:]
    masks = [(special_pairs.shape[0], None)]
    pairs, rows = queries.shape[0], queries.shape[2] // 2
    columns, waiting, out, special = [], [], None, None
    sides = halves(kept_out.shape[1])
    for pair, sub, _, total, weight in attend_all(
        given(special_pairs), masks, lambda pair: queries[pair], lambda: special_queries[...],
        State(rows, state_in), pairs, rows, special_real,
    ):
        share = total * (1.0 / weight)
        if pair == pairs:
            row = lax.broadcasted_iota(jnp.int32, share.shape, 0) // HEAD_DIM
            lane = lax.broadcasted_iota(jnp.int32, share.shape, 1) // TILE_ROWS
            share = jnp.transpose(jnp.where(row == lane, share, 0.0))
            share = sum(share[i * TILE_ROWS : (i + 1) * TILE_ROWS] for i in range(2 * pairs))
            special = share.astype(jnp.bfloat16)
        else:
            columns.append(share)
            if pair % 2 == 1 and sub == 1:
                quad = jnp.transpose(jnp.concatenate(columns, axis=0).astype(jnp.bfloat16))
                waiting.append((slice((pair // 2) * QUAD, (pair // 2 + 1) * QUAD), quad))
                columns = []
        if special is not None:
            for features, quad in waiting:
                quad = jnp.concatenate([quad, special[:, features]], axis=0)
                added = [product(quad, w_here[features, side]) for side in sides]
                out = added if out is None else [before + more for before, more in zip(out, added)]
            waiting = []
    sent_out[...] = out[1].astype(jnp.bfloat16)
    kept_out[...] = out[0]


def end_kernel(images, kept, received, patch_out, special_out):
    patch_total = patch_out.shape[0]
    special_count = special_out.shape[0]
    patch_out[...] = (kept[:patch_total, :] + received[:patch_total, :].astype(jnp.float32)).astype(
        jnp.bfloat16
    )
    rest = kept[patch_total:, :] + received[patch_total:, :].astype(jnp.float32)
    rows = [rest[b * special_count : (b + 1) * special_count][:, None, :] for b in range(images)]
    special_out[...] = jnp.concatenate(rows, axis=1).astype(jnp.bfloat16)


def call(kernel, out_shape, operands, in_specs=None, out_specs=None, scratch=(), flops=0):
    if in_specs:
        operands = [
            pltpu.with_memory_space_constraint(operand, pltpu.HBM) if spec is HBM else operand
            for operand, spec in zip(operands, in_specs)
        ]
    return pl.pallas_call(
        kernel,
        out_shape=out_shape,
        in_specs=in_specs or [VMEM] * len(operands),
        out_specs=out_specs or [VMEM] * len(out_shape),
        scratch_shapes=scratch,
        compiler_params=pltpu.CompilerParams(vmem_limit_bytes=VMEM_BYTES),
        cost_estimate=pl.CostEstimate(flops=flops, transcendentals=0, bytes_accessed=0),
    )(*operands)


def stack_kernel(first, second, out):
    count = first.shape[0]
    out[:count, :] = first[...]
    out[count:, :] = second[...]


def compact_kernel(block, real, first, second, out):
    rows = [
        part[start : start + real, :].astype(jnp.float32)
        for part in (first, second)
        for start in range(0, part.shape[0], block)
    ]
    padding = out.shape[0] - sum(part.shape[0] for part in rows)
    if padding:
        rows.append(jnp.zeros((padding, out.shape[1]), jnp.float32))
    out[...] = jnp.concatenate(rows, axis=0).astype(jnp.bfloat16)


def stacked(first, second, flops=0):
    shape = jax.ShapeDtypeStruct((2 * first.shape[0], first.shape[1]), first.dtype)
    return call(stack_kernel, [shape], (first, second), flops=flops)[0]


def after(array, *others):
    return lax.optimization_barrier((array, *others))[0]


def per_device(
    patch_rows, special_rows, role_first, role_rest, frame_order, covisible, w_qkv, w_out
):
    images, per_image, width = patch_rows.shape
    special_count = special_rows.shape[1]
    real_rows = images * special_count
    special_block = real_rows + -real_rows % TILE_ROWS
    owner_count = lax.axis_size("blk")
    reach = max(1, owner_count // 64)
    patch_total = images * per_image
    rows = patch_total + special_block
    heads = width // HEAD_DIM
    pairs = heads // 2
    paired = reach == 1 and owner_count % 2 == 0

    if paired:
        offsets = [0, (-1, 1), (1, -1)]
    else:
        offsets = [0] + [sign * d for d in range(1, reach + 1) for sign in (-1, 1)]
    mask_rows = -(-len(offsets) * images // 8) * 8
    bf16 = lambda *shape: jax.ShapeDtypeStruct(shape, jnp.bfloat16)
    f32 = lambda *shape: jax.ShapeDtypeStruct(shape, jnp.float32)
    state_shape = [
        f32(8, 2 * patch_total),
        f32(8, 2 * patch_total),
        f32(pairs, HEAD_DIM, 2 * patch_total),
        f32(width, heads * special_block),
    ]

    both = lambda part: (part, swapped(part, "head", 1))
    patches = patch_rows.reshape(patch_total, width)
    turned = jnp.transpose(special_rows, (1, 0, 2))
    power = owner_count >= 8 and owner_count & (owner_count - 1) == 0
    specials, own = call(
        rows_kernel,
        [
            bf16(special_block, width),
            bf16(patch_total, width),
        ],
        (frame_order, turned, role_first, role_rest, patches),
        in_specs=[HBM] * 5,
        scratch=[
            pltpu.SMEM(frame_order.shape, jnp.int32),
            pltpu.VMEM(turned.shape, jnp.bfloat16),
            pltpu.VMEM(role_first.shape, jnp.bfloat16),
            pltpu.VMEM(role_rest.shape, jnp.bfloat16),
            pltpu.SemaphoreType.DMA((5,)),
        ],
    )
    specials = both(specials)
    mask, weights, everywhere, w_here = call(
        functools.partial(start_kernel, offsets, per_image, special_count, special_block),
        [
            f32(mask_rows, patch_total + heads * special_block),
            bf16(*w_qkv.shape),
            bf16(special_block, 2 * width),
            bf16(*w_out.shape),
        ],
        (covisible, *specials, w_qkv, w_out),
        in_specs=[HBM, VMEM, VMEM, HBM, HBM],
        scratch=[pltpu.SMEM(covisible.shape, jnp.int32), pltpu.SemaphoreType.DMA((1 + 7,))],
    )
    if paired and power:
        everywhere = stacked(everywhere, swapped(everywhere, "blk", 2), FIRST)
    queries, special_queries, *state = call(
        functools.partial(first_kernel, images),
        [bf16(pairs, PAIR, 2 * patch_total), bf16(width, heads * special_block), *state_shape],
        (mask, own, swapped(patches, "head", 1), *specials, weights),
    )
    fixed = (weights, queries, special_queries)

    def later(stretches, parts, state):
        return call(
            functools.partial(later_kernel, stretches),
            state_shape,
            (mask, *[part[0] for part in parts], *[part[1] for part in parts], *fixed, *state),
        )

    image_rows = lambda owner: [(per_image, owner * images + b) for b in range(images)]
    def halved(part, gate):
        part = after(part, gate)
        starts = range(0, part.shape[0], per_image)
        return [both(part[start : start + per_image]) for start in starts]

    stretches = lambda owner: [[image] for image in image_rows(owner)]
    if paired:
        far = after(crossed(patches, "blk"), state[0])
        near = swapped(patches, "blk", 1)
        if power:
            everywhere = after(everywhere, far)
            bit = 4
            while 2 * bit < owner_count:
                everywhere = stacked(everywhere, swapped(everywhere, "blk", bit))
                bit *= 2
            arrived = swapped(everywhere, "blk", bit)
        state = later(stretches(1), halved(far, state[0]), state)
        if power:
            real = real_rows * owner_count // 2
            blocks = (real + -real % TILE_ROWS, real)
            (everywhere,) = call(
                functools.partial(compact_kernel, special_block, real_rows),
                [bf16(blocks[0], 2 * width)],
                (after(everywhere, state[0]), arrived),
                flops=FIRST,
            )
            arrived = swapped(everywhere, "blk", 1)
        parts = [both(after(near, state[0]))]
        (sums,) = call(
            functools.partial(half_kernel, len(parts)),
            [f32(2, patch_total, width)],
            (*[part[0] for part in parts], weights),
            flops=0,
        )
        state = call(
            functools.partial(begun_kernel, [image_rows(2)], blocks if power else None),
            state_shape,
            (mask, sums, *[part[1] for part in parts], *fixed, everywhere, *state),
        )
        if power:
            everywhere = arrived
    else:
        for i, offset in enumerate(offsets[1:]):
            state = later(stretches(i + 1), halved(shifted(patches, "blk", -offset), state[0]), state)
    if not (paired and power):
        blocks = (special_block, real_rows)
        everywhere = lax.all_gather(everywhere, "blk", axis=0, tiled=True)
    kept, sent = call(
        functools.partial(last_kernel, blocks),
        [f32(rows, width), bf16(rows, width)],
        (mask, everywhere, queries, special_queries, *state, w_here),
    )
    received = swapped(sent, "head", 1)
    patch_out, special_out = call(
        functools.partial(end_kernel, images),
        [bf16(patch_total, width), bf16(special_count, images, width)],
        (kept, received),
        out_specs=[pl.BlockSpec(), pl.BlockSpec()],
    )
    return patch_out.reshape(patch_rows.shape), jnp.transpose(special_out, (1, 0, 2))


def solution(mesh):
    in_specs = (
        P(("scene", "blk"), None, "head"),
        P(("scene", "blk"), None, "head"),
        P(),
        P(),
        P(("scene", "blk")),
        P(("scene", "blk"), None),
        P(None, None, "head"),
        P("head", None),
    )
    out_specs = (P(("scene", "blk"), None, "head"), P(("scene", "blk"), None, "head"))
    return jax.shard_map(
        per_device, mesh=mesh, in_specs=in_specs, out_specs=out_specs, check_vma=False
    )
```

```python
import functools

import jax
import jax.numpy as jnp
from jax import lax
from jax.experimental import pallas as pl
from jax.experimental.pallas import tpu as pltpu
from jax.sharding import PartitionSpec as P

HEAD_DIM = 64
PAIR = 2 * HEAD_DIM
QUAD = 2 * PAIR
TILE_ROWS = 16
LOG2_E = 1.4426950408889634
FIRST = 20_000_000_000
VMEM_BYTES = 32 * 1024 * 1024
SMEM = pl.BlockSpec(memory_space=pltpu.SMEM)
VMEM = pl.BlockSpec(memory_space=pltpu.VMEM)
HBM = pl.BlockSpec(memory_space=pltpu.HBM)


def shifted(block, axis, distance):
    count = lax.axis_size(axis)
    route = [((i - distance) % count, i) for i in range(count)]
    return lax.ppermute(block, axis, route)


def swapped(block, axis, bit):
    count = lax.axis_size(axis)
    return lax.ppermute(block, axis, [(i ^ bit, i) for i in range(count)])


def crossed(block, axis):
    count = lax.axis_size(axis)
    return lax.ppermute(block, axis, [(i, (i + (-1 if i % 2 == 0 else 1)) % count) for i in range(count)])


def halves(width):
    half = lax.axis_index("head")
    mine = pl.ds(pl.multiple_of(half * width, width), width)
    theirs = pl.ds(pl.multiple_of((1 - half) * width, width), width)
    return mine, theirs


def product(left, right):
    return jnp.dot(left, right, preferred_element_type=jnp.float32)


def owner_at(offset):
    count = lax.axis_size("blk")
    here = lax.axis_index("blk")
    if isinstance(offset, tuple):
        offset = jnp.where(lax.rem(here, 2) == 0, offset[0], offset[1])
    return lax.rem(here + offset + count, count)


def rows_kernel(
    frame_order, specials, role_first, role_rest, patches,
    special_out, patches_out, order, here, first_rows, rest_rows, copied,
):
    special_count, images, width = specials.shape
    moves = [(specials, here), (role_first, first_rows), (role_rest, rest_rows), (frame_order, order)]
    moves.append((patches, patches_out))
    copies = [
        pltpu.make_async_copy(source, target, copied.at[i]) for i, (source, target) in enumerate(moves)
    ]
    for copy in copies:
        copy.start()
    for copy in copies[:4]:
        copy.wait()
    mine, _ = halves(width)
    first = first_rows[:, mine].astype(jnp.float32)
    rest = rest_rows[:, mine].astype(jnp.float32)
    summed = [
        here[:, b, :].astype(jnp.float32) + jnp.where(order[b] == 0, first, rest) for b in range(images)
    ]
    summed.append(jnp.zeros((special_out.shape[0] - images * special_count, width), jnp.float32))
    special_out[...] = jnp.concatenate(summed, axis=0).astype(jnp.bfloat16)
    for copy in copies[4:]:
        copy.wait()


def start_kernel(
    offsets, per_image, special_count, special_total, covisible, special, other_special, w_qkv, w_out,
    mask_out, weights_out, pairs_out, w_out_here, seen, copied,
):
    images = covisible.shape[0]
    patch_total = images * per_image
    moves = [(covisible, seen)]
    depth = w_qkv.shape[1] // 2
    for i in range(3):
        for j, rows in enumerate(halves(depth)):
            moves.append((w_qkv.at[i, rows], weights_out.at[i, pl.ds(j * depth, depth)]))
    moves.append((w_out, w_out_here))
    copies = [
        pltpu.make_async_copy(source, target, copied.at[i]) for i, (source, target) in enumerate(moves)
    ]
    for copy in copies:
        copy.start()
    copies[0].wait()
    lane = lax.broadcasted_iota(jnp.int32, (1, mask_out.shape[1]), 1)
    special_lane = lax.rem(lane - patch_total, special_total)
    image = jnp.where(
        lane < patch_total, lane // per_image, jnp.minimum(special_lane // special_count, images - 1)
    )
    for i, offset in enumerate(offsets):
        for b in range(images):
            row = jnp.zeros(lane.shape, jnp.float32)
            for a in range(images):
                hidden = seen[a, owner_at(offset) * images + b] <= 0
                row = jnp.where((image == a) & hidden, -jnp.inf, row)
            mask_out[i * images + b : i * images + b + 1, :] = row
    rows = jnp.concatenate([special[...], other_special[...]], axis=1)
    width = weights_out.shape[2]
    for copy in copies[1:-1]:
        copy.wait()
    for i in range(2):
        pairs_out[:, i * width : (i + 1) * width] = product(rows, weights_out[i + 1]).astype(jnp.bfloat16)
    copies[-1].wait()


def projector(own, other, weights):
    rows = jnp.concatenate([own, other], axis=1)

    def columns(which, quad):
        return product(rows, weights[which, :, quad * QUAD : (quad + 1) * QUAD])

    return columns


def attend(scores, masks, state):
    largest = state
    start = 0
    for count, mask in masks:
        part = jnp.max(scores[start : start + count], axis=0, keepdims=True)
        part = part if mask is None else part + mask
        largest = part if largest is None else jnp.maximum(largest, part)
        start += count
    weights, start = [], 0
    for count, mask in masks:
        level = largest if mask is None else largest - mask
        weights.append(jnp.exp2((scores[start : start + count] - level).astype(jnp.bfloat16)))
        start += count
    factor = None if state is None else jnp.exp2(state - largest)
    return largest, factor, jnp.concatenate(weights, axis=0)


def attend_all(columns, masks, queries_of, special_queries, state, pairs, rows, special_real):
    keys, values = {}, {}
    quads = pairs // 2

    def keys_of(quad):
        if quad not in keys:
            keys[quad] = columns(1, quad).astype(jnp.bfloat16)
        return keys[quad]

    def values_of(quad):
        if quad not in values:
            values[quad] = jnp.transpose(columns(2, quad).astype(jnp.bfloat16))
        return values[quad]

    def prepared(pair):
        if pair == pairs:
            scores = product(
                jnp.concatenate([keys_of(quad) for quad in range(quads)], axis=1), special_queries()
            )
        else:
            lanes = slice((pair % 2) * PAIR, (pair % 2 + 1) * PAIR)
            scores = product(keys_of(pair // 2)[:, lanes], queries_of(pair))
        if all(mask is not None for _, mask in masks):
            return scores
        parts, start = [], 0
        for count, mask in masks:
            part = scores[start : start + count]
            if mask is None:
                key_row = lax.broadcasted_iota(jnp.int32, (count, 1), 0)
                part = jnp.where(lax.rem(key_row, special_real[0]) < special_real[1], part, -jnp.inf)
            parts.append(part)
            start += count
        return jnp.concatenate(parts, axis=0)

    ones = jnp.ones((TILE_ROWS, sum(count for count, _ in masks)), jnp.bfloat16)
    both = [
        (count, None if mask is None else jnp.concatenate([mask[:, :rows]] * 2, axis=1))
        for count, mask in masks
    ]
    only = [(count, None if mask is None else mask[:, rows:]) for count, mask in masks]
    order = list(range(pairs))
    order.insert(pairs - 2, pairs)
    scores = prepared(order[0])
    for step, pair in enumerate(order):
        if pair < pairs:
            left = values_of(pair // 2)[(pair % 2) * PAIR : (pair % 2 + 1) * PAIR]
        else:
            left = jnp.concatenate([values_of(quad) for quad in range(quads)], axis=0)
        following = prepared(order[step + 1]) if step < pairs else None
        largest, factor, weights = attend(
            scores, both if pair < pairs else only, state and state.largest(pair)
        )
        added = product(jnp.concatenate([left, ones], axis=0), weights)
        height, subs = (HEAD_DIM, 2) if pair < pairs else (left.shape[0], 1)
        width = scores.shape[1] // subs
        for sub in range(subs):
            lanes = slice(sub * width, (sub + 1) * width)
            total = added[sub * height : (sub + 1) * height, lanes]
            weight = added[left.shape[0] : left.shape[0] + 1, lanes]
            if state is not None:
                total = total + state.total(pair, sub) * factor[:, lanes]
                weight = weight + state.weight(pair, sub) * factor[:, lanes]
            yield pair, sub, largest[:, lanes], total, weight
        scores = following


class State:
    def __init__(self, rows, refs):
        self.rows = rows
        self.largest_ref, self.weight_ref, self.total_ref, self.special_ref = refs

    def lanes(self, pair, sub):
        if pair == self.total_ref.shape[0]:
            return slice(0, self.special_ref.shape[1])
        return slice(sub * self.rows, (sub + 1) * self.rows)

    def largest(self, pair):
        stop = self.special_ref.shape[1] if pair == self.total_ref.shape[0] else 2 * self.rows
        return self.largest_ref[pair : pair + 1, 0:stop]

    def weight(self, pair, sub):
        return self.weight_ref[pair : pair + 1, self.lanes(pair, sub)]

    def total(self, pair, sub):
        if pair == self.total_ref.shape[0]:
            return self.special_ref[...]
        return self.total_ref[pair, :, self.lanes(pair, sub)]

    def put(self, pair, sub, largest, total, weight):
        lanes = self.lanes(pair, sub)
        self.largest_ref[pair : pair + 1, lanes] = largest
        self.weight_ref[pair : pair + 1, lanes] = weight
        if pair == self.total_ref.shape[0]:
            self.special_ref[...] = total
        else:
            self.total_ref[pair, :, lanes] = total


def first_kernel(
    images, mask, own, other, special, other_special, weights, queries_out, special_out, *state_out
):
    patch_total = own.shape[0]
    columns = projector(
        jnp.concatenate([own[...], special[...]], axis=0),
        jnp.concatenate([other[...], other_special[...]], axis=0),
        weights,
    )
    pairs = queries_out.shape[0]
    zero = jnp.zeros((HEAD_DIM, patch_total), jnp.bfloat16)
    made = {}

    def patch_columns(which, quad):
        return columns(which, quad)[:patch_total]

    def columns_of(quad):
        if quad not in made:
            queries = columns(0, quad) * (HEAD_DIM ** (-0.5) * LOG2_E)
            made[quad] = queries[patch_total:]
            turned = jnp.transpose(queries[:patch_total].astype(jnp.bfloat16))
            for i in range(2):
                first = i * PAIR
                upper = jnp.concatenate([turned[first : first + HEAD_DIM], zero], axis=1)
                lower = jnp.concatenate([zero, turned[first + HEAD_DIM : first + PAIR]], axis=1)
                queries_out[2 * quad + i] = jnp.concatenate([upper, lower], axis=0)
        return made[quad]

    def queries_of(pair):
        columns_of(pair // 2)
        return queries_out[pair]

    def special_queries():
        block = jnp.concatenate([columns_of(quad) for quad in range(pairs // 2)], axis=1)
        count = block.shape[0]
        block = jnp.concatenate([block] * (2 * pairs), axis=0)
        row = lax.broadcasted_iota(jnp.int32, block.shape, 0) // count
        lane = lax.broadcasted_iota(jnp.int32, block.shape, 1) // HEAD_DIM
        block = jnp.transpose(jnp.where(row == lane, block, 0.0).astype(jnp.bfloat16))
        special_out[...] = block
        return block

    per_image = patch_total // images
    masks = [(per_image, mask[b : b + 1, :]) for b in range(images)]
    state = State(patch_total, state_out)
    for result in attend_all(
        patch_columns, masks, queries_of, special_queries, None, pairs, patch_total, 0
    ):
        state.put(*result)


def joined(stretches, mask, refs):
    count = len(stretches)
    own = jnp.concatenate([ref[...] for ref in refs[:count]], axis=0)
    other = jnp.concatenate([ref[...] for ref in refs[count : 2 * count]], axis=0)
    masks = [(rows, mask[i : i + 1, :]) for part in stretches for rows, i in part]
    return own, other, masks, refs[2 * count :]


def given(pairs):
    width = pairs.shape[1] // 2

    def columns(which, quad):
        first = (which - 1) * width + quad * QUAD
        return pairs[:, first : first + QUAD]

    return columns


def later_kernel(stretches, mask, *refs):
    own, other, masks, refs = joined(stretches, mask, refs)
    weights, queries, special_queries = refs[:3]
    state_in, state_out = refs[3:7], refs[7:]
    pairs, rows = queries.shape[0], queries.shape[2] // 2
    state = State(rows, state_out)
    for result in attend_all(
        projector(own, other, weights), masks, lambda pair: queries[pair], lambda: special_queries[...],
        State(rows, state_in), pairs, rows, None,
    ):
        state.put(*result)


def half_kernel(count, *refs):
    weights, sums_out = refs[count:]
    rows = jnp.concatenate([ref[...] for ref in refs[:count]], axis=0)
    for i in range(2):
        sums_out[i] = product(rows, weights[i + 1, : rows.shape[1], :])


def begun(sums, other, weights):
    depth = other.shape[1]

    def columns(which, quad):
        lanes = slice(quad * QUAD, (quad + 1) * QUAD)
        return sums[which - 1, :, lanes] + product(other, weights[which, depth:, lanes])

    return columns


def begun_kernel(stretches, special_real, mask, sums, *refs):
    count = len(stretches)
    other = jnp.concatenate([ref[...] for ref in refs[:count]], axis=0)
    masks = [(rows, mask[i : i + 1, :]) for part in stretches for rows, i in part]
    weights, queries, special_queries, special_pairs = refs[count : count + 4]
    state_in, state_out = refs[count + 4 : count + 8], refs[count + 8 :]
    sources = [begun(sums, other, weights)]
    if special_real is not None:
        sources.append(given(special_pairs))
        masks.append((special_pairs.shape[0], None))
    pairs, rows = queries.shape[0], queries.shape[2] // 2

    def joint(which, quad):
        parts = [source(which, quad).astype(jnp.bfloat16) for source in sources]
        return jnp.concatenate(parts, axis=0)

    state = State(rows, state_out)
    for result in attend_all(
        joint, masks, lambda pair: queries[pair], lambda: special_queries[...],
        State(rows, state_in), pairs, rows, special_real,
    ):
        state.put(*result)


def last_kernel(
    special_real, mask, special_pairs, queries, special_queries, *refs
):
    state_in = refs[:4]
    w_here, kept_out, sent_out = refs[4:]
    masks = [(special_pairs.shape[0], None)]
    pairs, rows = queries.shape[0], queries.shape[2] // 2
    columns, waiting, out, special = [], [], None, None
    sides = halves(kept_out.shape[1])
    for pair, sub, _, total, weight in attend_all(
        given(special_pairs), masks, lambda pair: queries[pair], lambda: special_queries[...],
        State(rows, state_in), pairs, rows, special_real,
    ):
        share = total * (1.0 / weight)
        if pair == pairs:
            row = lax.broadcasted_iota(jnp.int32, share.shape, 0) // HEAD_DIM
            lane = lax.broadcasted_iota(jnp.int32, share.shape, 1) // TILE_ROWS
            share = jnp.transpose(jnp.where(row == lane, share, 0.0))
            share = sum(share[i * TILE_ROWS : (i + 1) * TILE_ROWS] for i in range(2 * pairs))
            special = share.astype(jnp.bfloat16)
        else:
            columns.append(share)
            if pair % 2 == 1 and sub == 1:
                quad = jnp.transpose(jnp.concatenate(columns, axis=0).astype(jnp.bfloat16))
                waiting.append((slice((pair // 2) * QUAD, (pair // 2 + 1) * QUAD), quad))
                columns = []
        if special is not None:
            for features, quad in waiting:
                quad = jnp.concatenate([quad, special[:, features]], axis=0)
                added = [product(quad, w_here[features, side]) for side in sides]
                out = added if out is None else [before + more for before, more in zip(out, added)]
            waiting = []
    sent_out[...] = out[1].astype(jnp.bfloat16)
    kept_out[...] = out[0]


def end_kernel(images, kept, received, patch_out, special_out):
    patch_total = patch_out.shape[0]
    special_count = special_out.shape[0]
    patch_out[...] = (kept[:patch_total, :] + received[:patch_total, :].astype(jnp.float32)).astype(
        jnp.bfloat16
    )
    rest = kept[patch_total:, :] + received[patch_total:, :].astype(jnp.float32)
    rows = [rest[b * special_count : (b + 1) * special_count][:, None, :] for b in range(images)]
    special_out[...] = jnp.concatenate(rows, axis=1).astype(jnp.bfloat16)


def call(kernel, out_shape, operands, in_specs=None, out_specs=None, scratch=(), flops=0):
    if in_specs:
        operands = [
            pltpu.with_memory_space_constraint(operand, pltpu.HBM) if spec is HBM else operand
            for operand, spec in zip(operands, in_specs)
        ]
    return pl.pallas_call(
        kernel,
        out_shape=out_shape,
        in_specs=in_specs or [VMEM] * len(operands),
        out_specs=out_specs or [VMEM] * len(out_shape),
        scratch_shapes=scratch,
        compiler_params=pltpu.CompilerParams(vmem_limit_bytes=VMEM_BYTES),
        cost_estimate=pl.CostEstimate(flops=flops, transcendentals=0, bytes_accessed=0),
    )(*operands)


def stack_kernel(first, second, out):
    count = first.shape[0]
    out[:count, :] = first[...]
    out[count:, :] = second[...]


def compact_kernel(block, real, first, second, out):
    rows = [
        part[start : start + real, :].astype(jnp.float32)
        for part in (first, second)
        for start in range(0, part.shape[0], block)
    ]
    padding = out.shape[0] - sum(part.shape[0] for part in rows)
    if padding:
        rows.append(jnp.zeros((padding, out.shape[1]), jnp.float32))
    out[...] = jnp.concatenate(rows, axis=0).astype(jnp.bfloat16)


def stacked(first, second, flops=0):
    shape = jax.ShapeDtypeStruct((2 * first.shape[0], first.shape[1]), first.dtype)
    return call(stack_kernel, [shape], (first, second), flops=flops)[0]


def after(array, *others):
    return lax.optimization_barrier((array, *others))[0]


def per_device(
    patch_rows, special_rows, role_first, role_rest, frame_order, covisible, w_qkv, w_out
):
    images, per_image, width = patch_rows.shape
    special_count = special_rows.shape[1]
    real_rows = images * special_count
    special_block = real_rows + -real_rows % TILE_ROWS
    owner_count = lax.axis_size("blk")
    reach = max(1, owner_count // 64)
    patch_total = images * per_image
    rows = patch_total + special_block
    heads = width // HEAD_DIM
    pairs = heads // 2
    paired = reach == 1 and owner_count % 2 == 0

    if paired:
        offsets = [0, (-1, 1), (1, -1)]
    else:
        offsets = [0] + [sign * d for d in range(1, reach + 1) for sign in (-1, 1)]
    mask_rows = -(-len(offsets) * images // 8) * 8
    bf16 = lambda *shape: jax.ShapeDtypeStruct(shape, jnp.bfloat16)
    f32 = lambda *shape: jax.ShapeDtypeStruct(shape, jnp.float32)
    state_shape = [
        f32(8, 2 * patch_total),
        f32(8, 2 * patch_total),
        f32(pairs, HEAD_DIM, 2 * patch_total),
        f32(width, heads * special_block),
    ]

    both = lambda part: (part, swapped(part, "head", 1))
    patches = patch_rows.reshape(patch_total, width)
    turned = jnp.transpose(special_rows, (1, 0, 2))
    power = owner_count >= 8 and owner_count & (owner_count - 1) == 0
    specials, own = call(
        rows_kernel,
        [
            bf16(special_block, width),
            bf16(patch_total, width),
        ],
        (frame_order, turned, role_first, role_rest, patches),
        in_specs=[HBM] * 5,
        scratch=[
            pltpu.SMEM(frame_order.shape, jnp.int32),
            pltpu.VMEM(turned.shape, jnp.bfloat16),
            pltpu.VMEM(role_first.shape, jnp.bfloat16),
            pltpu.VMEM(role_rest.shape, jnp.bfloat16),
            pltpu.SemaphoreType.DMA((5,)),
        ],
    )
    specials = both(specials)
    mask, weights, everywhere, w_here = call(
        functools.partial(start_kernel, offsets, per_image, special_count, special_block),
        [
            f32(mask_rows, patch_total + heads * special_block),
            bf16(*w_qkv.shape),
            bf16(special_block, 2 * width),
            bf16(*w_out.shape),
        ],
        (covisible, *specials, w_qkv, w_out),
        in_specs=[HBM, VMEM, VMEM, HBM, HBM],
        scratch=[pltpu.SMEM(covisible.shape, jnp.int32), pltpu.SemaphoreType.DMA((1 + 7,))],
    )
    if paired and power:
        everywhere = stacked(everywhere, swapped(everywhere, "blk", 2), FIRST)
    queries, special_queries, *state = call(
        functools.partial(first_kernel, images),
        [bf16(pairs, PAIR, 2 * patch_total), bf16(width, heads * special_block), *state_shape],
        (mask, own, swapped(patches, "head", 1), *specials, weights),
    )
    fixed = (weights, queries, special_queries)

    def later(stretches, parts, state):
        return call(
            functools.partial(later_kernel, stretches),
            state_shape,
            (mask, *[part[0] for part in parts], *[part[1] for part in parts], *fixed, *state),
        )

    image_rows = lambda owner: [(per_image, owner * images + b) for b in range(images)]
    def halved(part, gate):
        return [both(after(part, gate))]

    stretches = lambda owner: [image_rows(owner)]
    if paired:
        far = after(crossed(patches, "blk"), state[0])
        near = swapped(patches, "blk", 1)
        if power:
            everywhere = after(everywhere, far)
            bit = 4
            while 2 * bit < owner_count:
                everywhere = stacked(everywhere, swapped(everywhere, "blk", bit))
                bit *= 2
            arrived = swapped(everywhere, "blk", bit)
        state = later(stretches(1), halved(far, state[0]), state)
        if power:
            real = real_rows * owner_count // 2
            blocks = (real + -real % TILE_ROWS, real)
            (everywhere,) = call(
                functools.partial(compact_kernel, special_block, real_rows),
                [bf16(blocks[0], 2 * width)],
                (after(everywhere, state[0]), arrived),
                flops=FIRST,
            )
            arrived = swapped(everywhere, "blk", 1)
        parts = halved(near, state[0])
        (sums,) = call(
            functools.partial(half_kernel, len(parts)),
            [f32(2, patch_total, width)],
            (*[part[0] for part in parts], weights),
            flops=0,
        )
        state = call(
            functools.partial(begun_kernel, stretches(2), blocks if power else None),
            state_shape,
            (mask, sums, *[part[1] for part in parts], *fixed, everywhere, *state),
        )
        if power:
            everywhere = arrived
    else:
        for i, offset in enumerate(offsets[1:]):
            state = later(stretches(i + 1), halved(shifted(patches, "blk", -offset), state[0]), state)
    if not (paired and power):
        blocks = (special_block, real_rows)
        everywhere = lax.all_gather(everywhere, "blk", axis=0, tiled=True)
    kept, sent = call(
        functools.partial(last_kernel, blocks),
        [f32(rows, width), bf16(rows, width)],
        (mask, everywhere, queries, special_queries, *state, w_here),
    )
    received = swapped(sent, "head", 1)
    patch_out, special_out = call(
        functools.partial(end_kernel, images),
        [bf16(patch_total, width), bf16(special_count, images, width)],
        (kept, received),
        out_specs=[pl.BlockSpec(), pl.BlockSpec()],
    )
    return patch_out.reshape(patch_rows.shape), jnp.transpose(special_out, (1, 0, 2))


def solution(mesh):
    in_specs = (
        P(("scene", "blk"), None, "head"),
        P(("scene", "blk"), None, "head"),
        P(),
        P(),
        P(("scene", "blk")),
        P(("scene", "blk"), None),
        P(None, None, "head"),
        P("head", None),
    )
    out_specs = (P(("scene", "blk"), None, "head"), P(("scene", "blk"), None, "head"))
    return jax.shard_map(
        per_device, mesh=mesh, in_specs=in_specs, out_specs=out_specs, check_vma=False
    )
```
